32 devices in a mesh: fsdp: 16 (over z, y, core), tensor: 2 (over x).
Axes of the slice: x: 2, y: 2, z: 4, core: 2. Of those that a mesh axis runs over, the one named last changes fastest.
Arguments:
- reference_hidden_states: bfloat16 [2048, 8192], P('fsdp'), may hold values from -6 to 6
- policy_hidden_states: bfloat16 [2048, 8192], P('fsdp'), may hold values from -6 to 6
- readout_target_rows: bfloat16 [2048, 8192], P('fsdp'), may hold values from -6 to 6
- final_norm_gain: bfloat16 [8192], replicated, may hold values from 0.5 to 1.5
- query_projection_matrix: bfloat16 [8192, 4096], P('fsdp', 'tensor'), may hold values from -0.0625 to 0.0625
- key_projection_matrix: bfloat16 [8192, 1024], P('fsdp', 'tensor'), may hold values from -0.0625 to 0.0625
- value_projection_matrix: bfloat16 [8192, 1024], P('fsdp', 'tensor'), may hold values from -0.0625 to 0.0625
- output_projection_matrix: bfloat16 [4096, 8192], P('tensor', 'fsdp'), may hold values from -0.09375 to 0.09375
- query_adapter_inner: bfloat16 [8192, 64], replicated, may hold values from -0.0625 to 0.0625
- query_adapter_outer: bfloat16 [64, 4096], P(None, 'tensor'), may hold values from -0.75 to 0.75
- value_adapter_inner: bfloat16 [8192, 64], replicated, may hold values from -0.0625 to 0.0625
- value_adapter_outer: bfloat16 [64, 1024], P(None, 'tensor'), may hold values from -0.75 to 0.75
- prompt_length: int32 [16], P('fsdp'), may hold values from 16 to 64
- preference_pair_index: int32 [16], replicated, may hold values from 0 to 15, each once
Outputs:
- dpo_loss: float32 [], replicated
- query_a_grad: float32 [8192, 64], P('tensor')
- query_outer_gradient: float32 [64, 4096], P(None, 'tensor')
- value_a_grad: float32 [8192, 64], P('tensor')
- value_outer_gradient: float32 [64, 1024], P(None, 'tensor')
The draws below stay inside these ranges and needn't reach their ends.
Inputs may be any that keep to these rules, and one draw needn't show every extreme that they name: Pair i compares sequence preference_pair_index[2i] (chosen) with preference_pair_index[2i + 1] (rejected); every sequence appears exactly once.
All inputs are finite; a program needn't handle non-finite values.
Results may differ from the reference program's by a relative error of at most 0.018.
Values may be sent and summed in bfloat16 or wider, within the bound.
No kernel may reach another device: no remote copies, remote signals or barrier semaphores. Data moves between devices by JAX's collectives and lax.ppermute only.
A program may use at most 256 MiB of HBM per device.

```python
import jax
import jax.numpy as jnp
from jax import lax

MODEL_WIDTH = 8192
QUERY_HEADS = 32
KEY_VALUE_HEADS = 8
HEAD_SIZE = 128
ADAPTER_RANK = 64
L = 128
TOKENS = 2048
SEQS = 16
N_TENSOR = 2


state_offset = 0.1


readout_noise = 0.4


def base_normal(key):
    return jax.random.normal(key, (TOKENS, MODEL_WIDTH), jnp.float32)


def noise_normal(key):
    return jax.random.normal(key, (TOKENS, MODEL_WIDTH), jnp.float32)


def draw_policy_hidden_states(key, part):
    common = base_normal(key)
    return jnp.clip(common, -6.0, 6.0).astype(jnp.bfloat16)


def draw_reference_hidden_states(key, part):
    common = base_normal(key)
    own_key = jax.random.fold_in(key, 21)
    extra = noise_normal(own_key)
    return jnp.clip(jnp.clip(common, -6.0, 6.0) + state_offset * extra, -6.0, 6.0).astype(jnp.bfloat16)


def draw_readout_target_rows(key, part):
    common = base_normal(key)
    own_key = jax.random.fold_in(key, 37)
    extra = noise_normal(own_key)
    return jnp.clip(jnp.clip(common, -6.0, 6.0) + readout_noise * extra, -6.0, 6.0).astype(jnp.bfloat16)


def with_ends(drawn, stream_key, low, high):
    shape = drawn.shape
    index_at = [jax.random.randint(jax.random.fold_in(stream_key, axis), (), 0, shape[axis]) for axis in range(len(shape))]
    drawn = drawn.at[tuple(index_at)].set(low)
    longest = shape.index(max(shape))
    index_at[longest] = (index_at[longest] + 1) % shape[longest]
    return drawn.at[tuple(index_at)].set(high)


def block_scale(rng, dims, pieces, smallest, largest):
    def one(dim, parts):
        draws = jax.random.uniform(jax.random.fold_in(jax.random.fold_in(rng, 6), dim), (parts,), jnp.float32, smallest / len(pieces), largest / len(pieces))
        return jnp.repeat(jnp.exp(draws), dims[dim] // parts).reshape((-1,) + (1,) * (len(dims) - dim - 1))

    factor_of = one(*pieces[0])
    for cut in pieces[1:]:
        factor_of = factor_of * one(*cut)
    return factor_of


def centred(rng, dims, deviation, bound, shards=(), kind=jnp.bfloat16):
    result = deviation * jax.random.normal(rng, dims, jnp.float32)
    if shards:
        result = result * block_scale(rng, dims, shards, -0.22, 0.18)
    return jnp.clip(result, -bound, bound).astype(kind)


def setup_inputs(seed: int = 0) -> dict:
    arg_keys = jax.random.split(jax.random.key(seed), 15)
    return {
        "reference_hidden_states": draw_reference_hidden_states(jax.random.fold_in(arg_keys[14], 71), 0),
        "policy_hidden_states": draw_policy_hidden_states(jax.random.fold_in(arg_keys[14], 71), 0),
        "readout_target_rows": draw_readout_target_rows(jax.random.fold_in(arg_keys[14], 71), 0),
        "final_norm_gain": jnp.clip(1.0 + 0.1 * jax.random.normal(arg_keys[3], (MODEL_WIDTH,), jnp.float32), 0.5, 1.5).astype(jnp.bfloat16),
        "query_projection_matrix": centred(arg_keys[4], (MODEL_WIDTH, QUERY_HEADS * HEAD_SIZE), MODEL_WIDTH ** -0.5, 0.0625, ((0, 16), (1, 2))),
        "key_projection_matrix": centred(arg_keys[5], (MODEL_WIDTH, KEY_VALUE_HEADS * HEAD_SIZE), MODEL_WIDTH ** -0.5, 0.0625, ((0, 16), (1, 2))),
        "value_projection_matrix": centred(arg_keys[6], (MODEL_WIDTH, KEY_VALUE_HEADS * HEAD_SIZE), MODEL_WIDTH ** -0.5, 0.0625, ((0, 16), (1, 2))),
        "output_projection_matrix": centred(arg_keys[7], (QUERY_HEADS * HEAD_SIZE, MODEL_WIDTH), (QUERY_HEADS * HEAD_SIZE) ** -0.5, 0.09375, ((0, 2), (1, 16))),
        "query_adapter_inner": centred(arg_keys[8], (MODEL_WIDTH, ADAPTER_RANK), MODEL_WIDTH ** -0.5, 0.0625),
        "query_adapter_outer": centred(arg_keys[9], (ADAPTER_RANK, QUERY_HEADS * HEAD_SIZE), ADAPTER_RANK ** -0.5, 0.75, ((1, 2),)),
        "value_adapter_inner": centred(arg_keys[10], (MODEL_WIDTH, ADAPTER_RANK), MODEL_WIDTH ** -0.5, 0.0625),
        "value_adapter_outer": centred(arg_keys[11], (ADAPTER_RANK, KEY_VALUE_HEADS * HEAD_SIZE), ADAPTER_RANK ** -0.5, 0.75, ((1, 2),)),
        "prompt_length": with_ends(jax.random.randint(arg_keys[12], (SEQS,), L // 8, L // 2 + 1), jax.random.fold_in(arg_keys[12], 1), L // 8, (L // 2 + 1) - 1).astype(jnp.int32),
        "preference_pair_index": jax.random.permutation(arg_keys[13], SEQS).astype(jnp.int32),
    }


adapter_scale = 0.5
dpo_beta = 0.1
loss_scale = 256.0
rope_base = 500000.0
norm_eps = 1e-05

def rope_tables(length, head_dim):
    half_dim = head_dim // 2
    exponent = jnp.arange(half_dim, dtype=jnp.float32) * (2.0 / head_dim)
    inverse = jnp.power(jnp.float32(rope_base), -exponent)
    angles = jnp.arange(length, dtype=jnp.float32)[:, None] * inverse[None, :]
    cosine = jnp.concatenate([jnp.cos(angles), jnp.cos(angles)], 1)
    sine_table = jnp.concatenate([jnp.sin(angles), jnp.sin(angles)], 1)
    return (cosine, sine_table)

def rotate(values, cosine, sine_table):
    half_dim = values.shape[-1] // 2
    turned = jnp.concatenate([-values[..., half_dim:], values[..., :half_dim]], -1)
    return values * cosine[None, :, None, :] + turned * sine_table[None, :, None, :]

def rotate_back(gradient, cosine, sine_table):
    half_dim = gradient.shape[-1] // 2
    scaled = gradient * sine_table[None, :, None, :]
    turned = jnp.concatenate([scaled[..., half_dim:], -scaled[..., :half_dim]], -1)
    return gradient * cosine[None, :, None, :] + turned

def attend(queries, key_heads, value_heads):
    length = queries.shape[1]
    score_scale = queries.shape[-1] ** (-0.5)
    scores = jnp.einsum('slkgd,smkd->skglm', queries.astype(jnp.float32), key_heads.astype(jnp.float32)) * score_scale
    position = jnp.arange(length, dtype=jnp.int32)
    allowed = position[:, None] >= position[None, :]
    weights = jnp.where(allowed, jnp.exp(scores), 0.0)
    attention_prob = weights / lax.optimization_barrier(jnp.sum(weights, -1, keepdims=True))
    rounded = attention_prob.astype(jnp.bfloat16)
    mixed_heads = jnp.einsum('skglm,smkd->slkgd', rounded.astype(jnp.float32), value_heads.astype(jnp.float32)).astype(jnp.bfloat16)
    return (mixed_heads, attention_prob, rounded)

def attend_back(grad_mixed, key_heads, value_heads, attention_prob, rounded):
    score_scale = key_heads.shape[-1] ** (-0.5)
    grad_prob = jnp.einsum('slkgd,smkd->skglm', grad_mixed.astype(jnp.float32), value_heads.astype(jnp.float32))
    grad_values = jnp.einsum('skglm,slkgd->smkd', rounded.astype(jnp.float32), grad_mixed.astype(jnp.float32)).astype(jnp.bfloat16)
    grad_scores = (attention_prob * (grad_prob - lax.optimization_barrier(jnp.sum(grad_prob * attention_prob, -1, keepdims=True))) * score_scale).astype(jnp.bfloat16)
    grad_query = jnp.einsum('skglm,smkd->slkgd', grad_scores.astype(jnp.float32), key_heads.astype(jnp.float32))
    return (grad_query, grad_values)

def norm_forward(summed, states, readout_target_rows, final_norm_gain):
    hidden = states.astype(jnp.float32) + summed
    inverse_rms = lax.rsqrt(lax.optimization_barrier(jnp.mean(hidden * hidden, -1, keepdims=True)) + norm_eps)
    scaled = hidden * inverse_rms * final_norm_gain.astype(jnp.float32)[None, :]
    token_score = lax.optimization_barrier(jnp.sum(scaled * readout_target_rows.astype(jnp.float32), -1)) * hidden.shape[1] ** (-0.5)
    return (token_score, hidden, inverse_rms)

def norm_backward(token_grad, hidden, inverse_rms, readout_target_rows, final_norm_gain):
    weighted = final_norm_gain.astype(jnp.float32)[None, :] * readout_target_rows.astype(jnp.float32) * (token_grad[:, None] * hidden.shape[1] ** (-0.5))
    return inverse_rms * weighted - hidden * inverse_rms ** 3 * lax.optimization_barrier(jnp.mean(hidden * weighted, -1, keepdims=True))

def preference(seq_scores, preference_pair_index):
    pair_slots = preference_pair_index.shape[0]
    onehot = (preference_pair_index[:, None] == jnp.arange(pair_slots, dtype=jnp.int32)[None, :]).astype(jnp.float32)
    margin_each = seq_scores[1] - seq_scores[0]
    picked = lax.optimization_barrier(jnp.sum(onehot * margin_each[None, :], 1)).reshape(pair_slots // 2, 2)
    logits = dpo_beta * (picked[:, 0] - picked[:, 1])
    total_loss = jnp.sum(jax.nn.softplus(-logits))
    slopes = -dpo_beta * jax.nn.sigmoid(-logits)
    coefficient = jnp.stack([slopes, -slopes], 1).reshape(pair_slots)
    gradient = lax.optimization_barrier(jnp.sum(onehot * coefficient[:, None], 0))
    return (total_loss, gradient)

def reference(reference_hidden_states, policy_hidden_states, readout_target_rows, final_norm_gain, query_projection_matrix, key_projection_matrix, value_projection_matrix, output_projection_matrix, query_adapter_inner, query_adapter_outer, value_adapter_inner, value_adapter_outer, prompt_length, preference_pair_index):
    tokens = reference_hidden_states.shape[0]
    width = reference_hidden_states.shape[1]
    seq_count = tokens // L
    group_size = QUERY_HEADS // KEY_VALUE_HEADS
    cosine, sine_table = rope_tables(L, HEAD_SIZE)
    query_low_rank = jnp.dot(policy_hidden_states, query_adapter_inner, preferred_element_type=jnp.float32).astype(jnp.bfloat16)
    value_low_rank = jnp.dot(policy_hidden_states, value_adapter_inner, preferred_element_type=jnp.float32).astype(jnp.bfloat16)

    def attention_pass(states, with_adapter):
        query_before_adapter = jnp.dot(states, query_projection_matrix, preferred_element_type=jnp.float32)
        key_pre = jnp.dot(states, key_projection_matrix, preferred_element_type=jnp.float32)
        value_before_adapter = jnp.dot(states, value_projection_matrix, preferred_element_type=jnp.float32)
        if with_adapter:
            query_before_adapter = query_before_adapter + adapter_scale * jnp.dot(query_low_rank, query_adapter_outer, preferred_element_type=jnp.float32)
            value_before_adapter = value_before_adapter + adapter_scale * jnp.dot(value_low_rank, value_adapter_outer, preferred_element_type=jnp.float32)
        queries = rotate(query_before_adapter.reshape(seq_count, L, QUERY_HEADS, HEAD_SIZE), cosine, sine_table).astype(jnp.bfloat16).reshape(seq_count, L, KEY_VALUE_HEADS, group_size, HEAD_SIZE)
        key_heads = rotate(key_pre.reshape(seq_count, L, KEY_VALUE_HEADS, HEAD_SIZE), cosine, sine_table).astype(jnp.bfloat16)
        value_heads = value_before_adapter.reshape(seq_count, L, KEY_VALUE_HEADS, HEAD_SIZE).astype(jnp.bfloat16)
        mixed_heads, attention_prob, rounded = attend(queries, key_heads, value_heads)
        heads_out = mixed_heads.reshape(tokens, QUERY_HEADS * HEAD_SIZE)
        block_width = QUERY_HEADS * HEAD_SIZE // N_TENSOR
        summed = jnp.zeros((tokens, width), jnp.float32)
        for block_index in range(N_TENSOR):
            partial_value = jnp.dot(heads_out[:, block_index * block_width:(block_index + 1) * block_width], output_projection_matrix[block_index * block_width:(block_index + 1) * block_width], preferred_element_type=jnp.float32)
            summed = summed + lax.optimization_barrier(partial_value.astype(jnp.bfloat16)).astype(jnp.float32)
        return (summed, key_heads, value_heads, attention_prob, rounded)
    ref_result = attention_pass(reference_hidden_states, False)
    pol_result = attention_pass(policy_hidden_states, True)
    row_ids = jnp.arange(tokens, dtype=jnp.int32)
    seq_of = row_ids // L
    live_rows = (row_ids % L >= prompt_length[seq_of]).astype(jnp.float32)
    ref_score, ref_hidden, ref_inverse = norm_forward(ref_result[0], reference_hidden_states, readout_target_rows, final_norm_gain)
    pol_score, pol_hidden, pol_inverse = norm_forward(pol_result[0], policy_hidden_states, readout_target_rows, final_norm_gain)
    seq_scores = jnp.stack([lax.optimization_barrier(jnp.sum((ref_score * live_rows).reshape(seq_count, L), 1)), lax.optimization_barrier(jnp.sum((pol_score * live_rows).reshape(seq_count, L), 1))])
    total_loss, seq_grad = preference(seq_scores, preference_pair_index)
    token_grad = (loss_scale * seq_grad)[seq_of] * live_rows
    grad_hidden = norm_backward(token_grad, pol_hidden, pol_inverse, readout_target_rows, final_norm_gain).astype(jnp.bfloat16)
    grad_mixed = jnp.dot(grad_hidden, output_projection_matrix.T, preferred_element_type=jnp.float32).astype(jnp.bfloat16).reshape(seq_count, L, KEY_VALUE_HEADS, group_size, HEAD_SIZE)
    grad_query, grad_values = attend_back(grad_mixed, pol_result[1], pol_result[2], pol_result[3], pol_result[4])
    query_backward = rotate_back(grad_query.reshape(seq_count, L, QUERY_HEADS, HEAD_SIZE), cosine, sine_table).astype(jnp.bfloat16).reshape(tokens, QUERY_HEADS * HEAD_SIZE)
    value_backward = grad_values.reshape(tokens, KEY_VALUE_HEADS * HEAD_SIZE)
    query_outer_gradient = adapter_scale * jnp.dot(query_low_rank.T, query_backward, preferred_element_type=jnp.float32)
    value_outer_gradient = adapter_scale * jnp.dot(value_low_rank.T, value_backward, preferred_element_type=jnp.float32)
    adapter_rank_width = query_adapter_inner.shape[1]
    query_block = QUERY_HEADS * HEAD_SIZE // N_TENSOR
    value_block = KEY_VALUE_HEADS * HEAD_SIZE // N_TENSOR
    a_grads = jnp.zeros((width, 2 * adapter_rank_width), jnp.float32)
    for block_index in range(N_TENSOR):
        query_columns = slice(block_index * query_block, (block_index + 1) * query_block)
        value_columns = slice(block_index * value_block, (block_index + 1) * value_block)
        query_middle = (adapter_scale * jnp.dot(query_backward[:, query_columns], query_adapter_outer[:, query_columns].T, preferred_element_type=jnp.float32)).astype(jnp.bfloat16)
        value_middle = (adapter_scale * jnp.dot(value_backward[:, value_columns], value_adapter_outer[:, value_columns].T, preferred_element_type=jnp.float32)).astype(jnp.bfloat16)
        joined = jnp.concatenate([query_middle, value_middle], 1)
        a_grads = a_grads + jnp.dot(policy_hidden_states.T, joined, preferred_element_type=jnp.float32)
    return (total_loss, a_grads[:, :adapter_rank_width], query_outer_gradient, a_grads[:, adapter_rank_width:], value_outer_gradient)
```

```python
import functools

import jax
import jax.numpy as jnp
from jax import lax
from jax.experimental import pallas as pl
from jax.experimental.pallas import tpu as pltpu
from jax.sharding import PartitionSpec as P

QUERY_HEADS = 32
KEY_VALUE_HEADS = 8
HEAD_SIZE = 128
L = 128
GROUP = QUERY_HEADS // KEY_VALUE_HEADS
QCOLS = GROUP * HEAD_SIZE

adapter_scale = 0.5
dpo_beta = 0.1
loss_scale = 256.0
rope_base = 500000.0
norm_eps = 1e-05

F32 = jnp.float32
BF16 = jnp.bfloat16
ORD = (0, 2, 1, 3)
MB = 1 << 20


def rope_tables(length, head_dim):
    half_dim = head_dim // 2
    exponent = jnp.arange(half_dim, dtype=F32) * (2.0 / head_dim)
    inverse = jnp.power(F32(rope_base), -exponent)
    angles = jnp.arange(length, dtype=F32)[:, None] * inverse[None, :]
    cosine = jnp.concatenate([jnp.cos(angles), jnp.cos(angles)], 1)
    sine = jnp.concatenate([-jnp.sin(angles), jnp.sin(angles)], 1)
    return cosine, sine


def dot(a, b, dims=((1,), (0,))):
    return lax.dot_general(a, b, (dims, ((), ())), preferred_element_type=F32)


def params(limit_mb):
    return pltpu.CompilerParams(vmem_limit_bytes=limit_mb * MB)


def smem():
    return pl.BlockSpec(memory_space=pltpu.SMEM)


def whole_vmem():
    return pl.BlockSpec(memory_space=pltpu.VMEM)


def prep_body(parts, part, idx, ref, pol, tgt, gain, x0, x1, x2, x3, t0, t1, t2, t3, go):
    per_t = parts // (t0.shape[1] // part)
    for d, (xo, to) in enumerate(((x0, t0), (x1, t1), (x2, t2), (x3, t3))):
        for j in range(parts):
            src = pl.ds(pl.multiple_of(idx[d * parts + j] * part, part), part)
            xo[0, :, j * part : (j + 1) * part] = ref[:, src]
            xo[1, :, j * part : (j + 1) * part] = pol[:, src]
        for j in range(parts // per_t):
            at = idx[4 * parts + d * (parts // per_t) + j] * part
            src = pl.ds(pl.multiple_of(at, part), part)
            to[:, j * part : (j + 1) * part] = tgt[:, src]
            if d == 0:
                go[:, j * part : (j + 1) * part] = gain[:, src]


def prep(idx, ref, pol, tgt, gain, parts, part, t_parts):
    tokens = ref.shape[0]
    xs = jax.ShapeDtypeStruct((2, tokens, parts * part), BF16)
    ts = jax.ShapeDtypeStruct((tokens, t_parts * part), BF16)
    return pl.pallas_call(
        functools.partial(prep_body, parts, part),
        in_specs=[smem()] + [whole_vmem()] * 4,
        out_specs=[whole_vmem()] * 9,
        out_shape=[xs] * 4 + [ts] * 4 + [jax.ShapeDtypeStruct((1, t_parts * part), F32)],
        compiler_params=params(32),
    )(idx, ref, pol, tgt, gain)


def mm_body(x_ref, *refs):
    out_ref = refs[-1]
    total = None
    at = 0
    for w in refs[:-1]:
        depth = w.shape[0]
        term = dot(x_ref[0, :, at : at + depth], w[...])
        total = term if total is None else total + term
        at += depth
    out_ref[0] = total.astype(out_ref.dtype)


def mm(x, off, blocks, ws, out_dtype):
    _, rows, depth = x.shape
    cols = ws[0].shape[1]
    return pl.pallas_call(
        mm_body,
        grid=(blocks,),
        in_specs=[pl.BlockSpec((1, rows, depth), lambda i: (i + off, 0, 0))]
        + [pl.BlockSpec(w.shape, lambda i: (0, 0)) for w in ws],
        out_specs=pl.BlockSpec((1, rows, cols), lambda i: (i, 0, 0)),
        out_shape=jax.ShapeDtypeStruct((blocks, rows, cols), out_dtype),
        compiler_params=params(32),
        cost_estimate=pl.CostEstimate(
            flops=2 * blocks * rows * depth * cols,
            bytes_accessed=2 * (blocks * rows * (depth + cols) + depth * cols),
            transcendentals=0,
        ),
    )(x, *ws)


def back_body(blocks, part, has_acc, x_ref, *refs):
    n = x_ref.shape[1] // part
    ws = refs[:n]
    refs = refs[n:]
    total = None
    for j in range(n):
        term = dot(x_ref[:, j * part : (j + 1) * part], ws[j][...], ((1,), (1,)))
        total = term if total is None else total + term
    if has_acc:
        total = total + refs[0][...]
        keep, send = refs[1:]
        half = total.shape[0] // 2
        keep[...] = total[:half]
        send[...] = total[half:].astype(send.dtype)
    else:
        refs[0][...] = total


def back_mm(x, ws, acc, tile):
    rows, depth = x.shape
    part = ws[0].shape[1]
    heads = ws[0].shape[0]
    has_acc = acc is not None
    in_specs = [pl.BlockSpec((rows, depth), lambda i: (0, 0))]
    in_specs += [pl.BlockSpec((tile, part), lambda i: (i, 0)) for _ in ws]
    args = [x, *ws]
    if has_acc:
        in_specs.append(pl.BlockSpec((rows, tile), lambda i: (0, i)))
        args.append(acc)
        out_specs = [pl.BlockSpec((rows // 2, tile), lambda i: (0, i))] * 2
        out_shape = [
            jax.ShapeDtypeStruct((rows // 2, heads), F32),
            jax.ShapeDtypeStruct((rows // 2, heads), BF16),
        ]
    else:
        out_specs = pl.BlockSpec((rows, tile), lambda i: (0, i))
        out_shape = jax.ShapeDtypeStruct((rows, heads), F32)
    return pl.pallas_call(
        functools.partial(back_body, 4, part, has_acc),
        grid=(heads // tile,),
        in_specs=in_specs,
        out_specs=out_specs,
        out_shape=out_shape,
        compiler_params=params(32),
        cost_estimate=pl.CostEstimate(
            flops=2 * rows * depth * heads,
            bytes_accessed=2 * (rows * depth + depth * heads) + 4 * rows * heads,
            transcendentals=0,
        ),
    )(*args)


def causal(rows):
    at = lax.broadcasted_iota(jnp.int32, (rows, L), 0) % L
    return at >= lax.broadcasted_iota(jnp.int32, (rows, L), 1)


def probabilities(q4, keys):
    scores = dot(q4, keys, ((1,), (1,))) * (HEAD_SIZE**-0.5)
    weights = jnp.where(causal(q4.shape[0]), jnp.exp(scores), 0.0)
    return weights / jnp.sum(weights, -1, keepdims=True)


def stack_heads(values):
    return jnp.concatenate(
        [values[:, h * HEAD_SIZE : (h + 1) * HEAD_SIZE] for h in range(GROUP)], 0
    )


def attend_body(keep, rs, r2, low, qo, vo, cos_ref, sin_ref, mixed, saved):
    scale = jnp.where(pl.program_id(0) == 1, adapter_scale, 0.0).astype(F32)
    cosine = cos_ref[...]
    sine = sin_ref[...]
    pre = keep[0] + rs[0].astype(F32) + r2[...].astype(F32)
    rank = qo.shape[0]
    q_pre = pre[:, :QCOLS] + scale * dot(low[:, :rank], qo[...])
    k_pre = pre[:, QCOLS : QCOLS + HEAD_SIZE]
    v_pre = pre[:, QCOLS + HEAD_SIZE :] + scale * dot(low[:, rank:], vo[...])
    cos4 = jnp.concatenate([cosine] * GROUP, 0)
    sin4 = jnp.concatenate([sine] * GROUP, 0)
    q4 = stack_heads(q_pre)
    q4 = (q4 * cos4 + pltpu.roll(q4, HEAD_SIZE // 2, 1) * sin4).astype(BF16)
    keys = (k_pre * cosine + pltpu.roll(k_pre, HEAD_SIZE // 2, 1) * sine).astype(BF16)
    values = v_pre.astype(BF16)
    rounded = probabilities(q4, keys).astype(BF16)
    out = dot(rounded, values).astype(BF16)
    for h in range(GROUP):
        cols = slice(h * HEAD_SIZE, (h + 1) * HEAD_SIZE)
        mixed[:, cols] = out[h * L : (h + 1) * L]
        saved[:, cols] = q4[h * L : (h + 1) * L]
    saved[:, QCOLS : QCOLS + HEAD_SIZE] = keys
    saved[:, QCOLS + HEAD_SIZE :] = values


def attend(keep, rs, r2, low, qo, vo, cosine, sine):
    cols = keep.shape[2]
    fixed = lambda a: pl.BlockSpec(a.shape, lambda i: (0,) * a.ndim)
    return pl.pallas_call(
        attend_body,
        grid=(2,),
        in_specs=[
            pl.BlockSpec((1, L, cols), lambda i: (0, i, 0)),
            pl.BlockSpec((1, L, cols), lambda i: (0, i, 0)),
            pl.BlockSpec((L, cols), lambda i: (i, 0)),
            fixed(low),
            fixed(qo),
            fixed(vo),
            fixed(cosine),
            fixed(sine),
        ],
        out_specs=[
            pl.BlockSpec((L, QCOLS), lambda i: (i, 0)),
            pl.BlockSpec((L, cols), lambda i: (i, 0)),
        ],
        out_shape=[
            jax.ShapeDtypeStruct((2 * L, QCOLS), BF16),
            jax.ShapeDtypeStruct((2 * L, cols), BF16),
        ],
        compiler_params=params(32),
        cost_estimate=pl.CostEstimate(
            flops=2 * 2 * L * (L * QCOLS * 2 + cols * 64),
            bytes_accessed=2 * L * (cols * 10 + QCOLS * 2),
            transcendentals=2 * L * L * GROUP,
        ),
    )(keep, rs, r2, low, qo, vo, cosine, sine)


def attend_back_body(kv, keep, rs, r2, low, qo, vo, cos_ref, sin_ref, *refs):
    saved = refs[:kv]
    outer, mid = refs[kv:]
    rank = qo.shape[0]
    cos4 = jnp.concatenate([cos_ref[...]] * GROUP, 0)
    sin4 = jnp.concatenate([sin_ref[...]] * GROUP, 0)
    low_q = low[:, :rank]
    low_v = low[:, rank:]
    q_mid = jnp.zeros((L, rank), F32)
    v_mid = jnp.zeros((L, rank), F32)
    for j in range(kv):
        cols = slice(j * QCOLS, (j + 1) * QCOLS)
        grad = keep[0, :, cols] + rs[0, :, cols].astype(F32) + r2[:, cols].astype(F32)
        grad4 = stack_heads(grad.astype(BF16))
        q4 = stack_heads(saved[j][:, :QCOLS])
        keys = saved[j][:, QCOLS : QCOLS + HEAD_SIZE]
        values = saved[j][:, QCOLS + HEAD_SIZE :]
        prob = probabilities(q4, keys)
        grad_prob = dot(grad4, values, ((1,), (1,)))
        grad_values = dot(prob.astype(BF16), grad4, ((0,), (0,))).astype(BF16)
        inner = jnp.sum(grad_prob * prob, -1, keepdims=True)
        grad_scores = (prob * (grad_prob - inner) * (HEAD_SIZE**-0.5)).astype(BF16)
        grad_query = dot(grad_scores, keys)
        back4 = (grad_query * cos4 - pltpu.roll(grad_query, HEAD_SIZE // 2, 1) * sin4).astype(BF16)
        for h in range(GROUP):
            at = j * GROUP + h
            back = back4[h * L : (h + 1) * L]
            outer[at * rank : (at + 1) * rank] = adapter_scale * dot(low_q, back, ((0,), (0,)))
            q_mid += dot(back, qo[:, at * HEAD_SIZE : (at + 1) * HEAD_SIZE], ((1,), (1,)))
        at = kv * GROUP + j
        outer[at * rank : (at + 1) * rank] = adapter_scale * dot(low_v, grad_values, ((0,), (0,)))
        v_mid += dot(grad_values, vo[:, j * HEAD_SIZE : (j + 1) * HEAD_SIZE], ((1,), (1,)))
    mid[:, :rank] = (adapter_scale * q_mid).astype(BF16)
    mid[:, rank:] = (adapter_scale * v_mid).astype(BF16)


def attend_back(keep, rs, r2, low, qo, vo, cosine, sine, saved):
    kv = len(saved)
    rank = qo.shape[0]
    heads = kv * QCOLS
    fixed = lambda a: pl.BlockSpec(a.shape, lambda i: (0,) * a.ndim)
    return pl.pallas_call(
        functools.partial(attend_back_body, kv),
        grid=(1,),
        in_specs=[
            pl.BlockSpec((1, L, heads), lambda i: (0, 0, 0)),
            pl.BlockSpec((1, L, heads), lambda i: (0, 0, 0)),
            fixed(r2),
            fixed(low),
            fixed(qo),
            fixed(vo),
            fixed(cosine),
            fixed(sine),
        ]
        + [pl.BlockSpec((L, s.shape[1]), lambda i: (1, 0)) for s in saved],
        out_specs=[
            pl.BlockSpec((kv * (GROUP + 1) * rank, HEAD_SIZE), lambda i: (0, 0)),
            pl.BlockSpec((L, 2 * rank), lambda i: (0, 0)),
        ],
        out_shape=[
            jax.ShapeDtypeStruct((kv * (GROUP + 1) * rank, HEAD_SIZE), F32),
            jax.ShapeDtypeStruct((L, 2 * rank), BF16),
        ],
        compiler_params=params(32),
    )(keep, rs, r2, low, qo, vo, cosine, sine, *saved)


def stats_body(n, part, split, scal, xt, tgt, gain, *refs):
    keeps = refs[:n]
    recvs = refs[n : 2 * n]
    hidden_out, stats = refs[2 * n :]
    squares = jnp.zeros((2 * L, HEAD_SIZE), F32)
    products = jnp.zeros((2 * L, HEAD_SIZE), F32)
    for j in range(n):
        src = pl.ds(pl.multiple_of((j * split + scal[0]) * part, part), part)
        hidden = xt[0, :, src].astype(F32) + keeps[j][0].astype(F32) + recvs[j][0].astype(F32)
        cols = slice(j * part, (j + 1) * part)
        hidden_out[0, :, cols] = hidden[L:]
        weighted = gain[:, cols] * tgt[0, :, cols].astype(F32)
        product = hidden * jnp.concatenate([weighted, weighted], 0)
        square = hidden * hidden
        for s in range(part // HEAD_SIZE):
            lanes = slice(s * HEAD_SIZE, (s + 1) * HEAD_SIZE)
            squares += square[:, lanes]
            products += product[:, lanes]
    squares = jnp.broadcast_to(jnp.sum(squares, 1, keepdims=True), squares.shape).T
    products = jnp.broadcast_to(jnp.sum(products, 1, keepdims=True), products.shape).T
    at = lax.broadcasted_iota(jnp.int32, (1, 2 * L), 1) % L
    own = (at >= scal[1]) & (pl.program_id(0) == 0)
    live = jnp.where(own, 1.0, 0.0).astype(F32)
    stats[...] = jnp.concatenate(
        [squares[:1], products[:1], live, jnp.zeros((5, 2 * L), F32)], 0
    )


def norm_stats(scal, xt, tgt, gain, keeps, recvs, split):
    n = len(keeps)
    part = keeps[0].shape[2]
    block = pl.BlockSpec((1, 2 * L, part), lambda i: (i, 0, 0))
    return pl.pallas_call(
        functools.partial(stats_body, n, part, split),
        grid=(4,),
        in_specs=[
            smem(),
            pl.BlockSpec((1, 2 * L, xt.shape[2]), lambda i: (i, 0, 0)),
            pl.BlockSpec((1, L, n * part), lambda i: (i, 0, 0)),
            pl.BlockSpec((1, n * part), lambda i: (0, 0)),
        ]
        + [block] * (2 * n),
        out_specs=[
            pl.BlockSpec((1, L, n * part), lambda i: (i, 0, 0)),
            pl.BlockSpec((8, 2 * L), lambda i: (i, 0)),
        ],
        out_shape=[
            jax.ShapeDtypeStruct((4, L, n * part), F32),
            jax.ShapeDtypeStruct((32, 2 * L), F32),
        ],
        compiler_params=params(32),
    )(scal, xt, tgt, gain, *keeps, *recvs)


def score_body(width, masks, ids, own, *refs):
    recvs = refs[: len(masks)]
    total_out, margin_out = refs[len(masks) :]
    lane = lax.broadcasted_iota(jnp.int32, (8, 128), 1)
    margins = jnp.zeros((8, 128), F32)
    for p in range(4):
        total = own[8 * p : 8 * p + 8]
        for recv, m in zip(recvs, masks):
            q = ORD.index(ORD[p] ^ m)
            total = total + recv[8 * q : 8 * q + 8]
        total_out[8 * p : 8 * p + 8] = total
        inverse = lax.rsqrt(total[0:1] * (1.0 / width) + norm_eps)
        score = total[1:2] * inverse * (width**-0.5)
        score = jnp.where(total[2:3] > 0.5, score, 0.0)
        margin = jnp.sum(score[:, L:], 1, keepdims=True) - jnp.sum(score[:, :L], 1, keepdims=True)
        margins = margins + jnp.where(lane == ids[p], margin, 0.0)
    margin_out[...] = margins


def scores(ids, own, recvs, masks, width):
    return pl.pallas_call(
        functools.partial(score_body, width, masks),
        in_specs=[smem()] + [whole_vmem()] * (1 + len(recvs)),
        out_specs=[whole_vmem()] * 2,
        out_shape=[jax.ShapeDtypeStruct(own.shape, F32), jax.ShapeDtypeStruct((8, 128), F32)],
    )(ids, own, *recvs)


def grad_body(width, seqs, n_vec, ids, pairs, total, hidden, tgt, gain, *refs):
    vecs = refs[:n_vec]
    grad_out, loss_out, slope = refs[n_vec:]
    lane = lax.broadcasted_iota(jnp.int32, (8, 128), 1)

    @pl.when(pl.program_id(0) == 0)
    def _():
        margin = vecs[0][...]
        for v in vecs[1:]:
            margin = margin + v[...]
        logits = jnp.zeros((8, 128), F32)
        for i in range(seqs // 2):
            sign = jnp.where(lane == pairs[2 * i], 1.0, 0.0) - jnp.where(
                lane == pairs[2 * i + 1], 1.0, 0.0
            )
            logit = dpo_beta * jnp.sum(margin * sign, 1, keepdims=True)
            logits = logits + jnp.where(lane == i, logit, 0.0)
        soft = jnp.maximum(-logits, 0.0) + jnp.log1p(jnp.exp(-jnp.abs(logits)))
        used = lane < seqs // 2
        loss = jnp.sum(jnp.where(used, soft, 0.0), 1, keepdims=True)
        loss_out[...] = jnp.broadcast_to(loss, (8, 128))
        slopes = jnp.where(used, -dpo_beta / (1.0 + jnp.exp(logits)), 0.0)
        gradient = jnp.zeros((8, 128), F32)
        for i in range(seqs // 2):
            each = jnp.sum(jnp.where(lane == i, slopes, 0.0), 1, keepdims=True)
            sign = jnp.where(lane == pairs[2 * i], 1.0, 0.0) - jnp.where(
                lane == pairs[2 * i + 1], 1.0, 0.0
            )
            gradient = gradient + each * sign
        slope[...] = gradient * loss_scale

    mine = lane == ids[pl.program_id(0)]
    seq = jnp.sum(jnp.where(mine, slope[...], 0.0), 1, keepdims=True)[:1]
    rows = total[:, L:]
    token = jnp.where(rows[2:3] > 0.5, seq, 0.0) * (width**-0.5)
    inverse = lax.rsqrt(rows[0:1] * (1.0 / width) + norm_eps)
    first = inverse * token
    second = inverse * inverse * inverse * (token * rows[1:2] * (1.0 / width))
    first = jnp.broadcast_to(first, (L, L)).T
    second = jnp.broadcast_to(second, (L, L)).T
    for s in range(hidden.shape[2] // HEAD_SIZE):
        cols = slice(s * HEAD_SIZE, (s + 1) * HEAD_SIZE)
        weighted = gain[:, cols] * tgt[0, :, cols].astype(F32)
        grad_out[0, :, cols] = (first * weighted - second * hidden[0, :, cols]).astype(BF16)


def grad_hidden(ids, pairs, total, hidden, tgt, gain, vecs, width):
    n = hidden.shape[2]
    seqs = pairs.shape[0]
    return pl.pallas_call(
        functools.partial(grad_body, width, seqs, len(vecs)),
        grid=(4,),
        in_specs=[
            smem(),
            smem(),
            pl.BlockSpec((8, 2 * L), lambda i: (i, 0)),
            pl.BlockSpec((1, L, n), lambda i: (i, 0, 0)),
            pl.BlockSpec((1, L, n), lambda i: (i, 0, 0)),
            pl.BlockSpec((1, n), lambda i: (0, 0)),
        ]
        + [pl.BlockSpec((8, 128), lambda i: (0, 0)) for _ in vecs],
        out_specs=[
            pl.BlockSpec((1, L, n), lambda i: (i, 0, 0)),
            pl.BlockSpec((8, 128), lambda i: (0, 0)),
        ],
        out_shape=[
            jax.ShapeDtypeStruct((4, L, n), BF16),
            jax.ShapeDtypeStruct((8, 128), F32),
        ],
        scratch_shapes=[pltpu.VMEM((8, 128), F32)],
        compiler_params=params(32),
    )(ids, pairs, total, hidden, tgt, gain, *vecs)


def per_device(
    fsdp_size,
    tensor_size,
    ref_states,
    pol_states,
    target_rows,
    norm_gain,
    wq,
    wk,
    wv,
    wo,
    qa,
    qo,
    va,
    vo,
    prompt_length,
    pairs,
):
    tokens, width = ref_states.shape
    groups = fsdp_size // 4
    top = fsdp_size // 2
    split = 2 if tensor_size == 2 else 1
    kv_local = wk.shape[1] // HEAD_SIZE
    depth = wq.shape[0]
    part = depth // split
    rank = qa.shape[1]
    me = lax.axis_index("fsdp")
    x = lax.axis_index("tensor")
    side = x if split == 2 else 0

    def tmask(d):
        return (d & 1) | ((d >> 1) * top)

    def move(value, mask):
        return lax.ppermute(value, "fsdp", [(i, i ^ mask) for i in range(fsdp_size)])

    def swap_x(value):
        return lax.ppermute(value, "tensor", [(0, 1), (1, 0)])

    def move_both(value, mask, flip):
        pairs_list = [
            (2 * i + j, 2 * (i ^ mask) + (j ^ flip)) for i in range(fsdp_size) for j in range(2)
        ]
        return lax.ppermute(value, ("fsdp", "tensor"), pairs_list)

    parts = groups * split
    idx = []
    for d in range(4):
        for k in range(groups):
            for h in range(split):
                idx.append((me ^ tmask(d) ^ (k << 1)) * split + h)
    for d in range(4):
        for k in range(groups):
            idx.append((me ^ tmask(d) ^ (k << 1)) * split + side)
    idx = jnp.stack(idx).astype(jnp.int32)
    prepared = prep(
        idx,
        ref_states,
        pol_states,
        target_rows,
        norm_gain.astype(F32).reshape(1, width),
        parts,
        part,
        groups,
    )
    xs, ts, gain = prepared[:4], prepared[4:8], prepared[8]

    def gather(first, second):
        if groups != 4 or split != 2:
            both = first if second is None else jnp.concatenate([first, second], 0)
            return [both] + [move(both, k << 1) for k in range(1, groups)]
        both = jnp.concatenate([first, second], 0)
        by_y = move(both, 2)
        by_z = move(both, 4)
        half = first.shape[0]
        return [both, by_y, by_z, move(by_y[:half], 4), move(by_z[half:], 2)]

    wqkv = []
    for j in range(kv_local):
        shard = jnp.concatenate(
            [
                wq[:, j * QCOLS : (j + 1) * QCOLS],
                wk[:, j * HEAD_SIZE : (j + 1) * HEAD_SIZE],
                wv[:, j * HEAD_SIZE : (j + 1) * HEAD_SIZE],
            ],
            1,
        )
        wqkv.append(gather(shard[:part], shard[part:] if split == 2 else None))
    if split == 2:
        wo_keep = lax.dynamic_slice_in_dim(wo, x * part, part, 1)
        wo_send = lax.dynamic_slice_in_dim(wo, (1 - x) * part, part, 1)
        wo_all = gather(wo_keep, wo_send)
    else:
        wo_all = gather(wo, None)
    heads = wo.shape[0]

    received = [None] + [move(xs[d], tmask(d)) for d in (1, 2, 3)]
    received[0] = xs[0]
    xt = jnp.stack([received[d].reshape(2 * tokens, -1) for d in ORD])
    targets = [ts[0]] + [move(ts[d], tmask(d)) for d in (1, 2, 3)]
    tgt = jnp.stack([targets[d] for d in ORD])

    low = dot(pol_states, jnp.concatenate([qa, va], 1)).astype(BF16)
    cosine, sine = rope_tables(L, HEAD_SIZE)

    mixed_blocks = []
    saved = []
    for j in range(kv_local):
        send = mm(xt, 2, 2, wqkv[j], BF16)
        rs = move(send, 1)
        keep = mm(xt, 0, 2, wqkv[j], F32)
        far = (keep[1] + rs[1].astype(F32)).astype(BF16)
        r2 = move(far, top)
        mixed, kept = attend(
            keep,
            rs,
            r2,
            low,
            qo[:, j * QCOLS : (j + 1) * QCOLS],
            vo[:, j * HEAD_SIZE : (j + 1) * HEAD_SIZE],
            cosine,
            sine,
        )
        saved.append(kept)
        mz = move(mixed, top)
        pair = jnp.stack([mixed, mz])
        mixed_blocks.append(jnp.concatenate([pair, move(pair, 1)], 0))
    mixed_all = jnp.concatenate(mixed_blocks, 2)

    keeps, recvs, back_keep, back_send = [], [], [], []
    for k in range(groups):
        if split == 2:
            if k < 3:
                w_keep, w_send = wo_all[k][:heads], wo_all[k][heads:]
            else:
                w_keep, w_send = wo_all[3], wo_all[4]
            recvs.append(swap_x(mm(mixed_all, 0, 4, [w_send], BF16)))
            keeps.append(mm(mixed_all, 0, 4, [w_keep], BF16))
            back_send.append(w_send)
        else:
            w_keep = wo_all[k]
            keeps.append(lax.psum(mm(mixed_all, 0, 4, [w_keep], BF16), "tensor"))
            recvs.append(jnp.zeros_like(keeps[-1]))
        back_keep.append(w_keep)

    scal = jnp.stack([jnp.asarray(side, jnp.int32), prompt_length[0].astype(jnp.int32)])
    hidden, stats = norm_stats(scal, xt, tgt, gain, keeps, recvs, split)
    masks, got = [], []
    for flip in range(split):
        for d in range(4):
            if d or flip:
                masks.append(d)
                if split == 2:
                    got.append(move_both(stats, tmask(d), flip))
                else:
                    got.append(move(stats, tmask(d)))
    ids = jnp.stack([me ^ tmask(d) for d in ORD]).astype(jnp.int32)
    total, margin = scores(ids, stats, got, tuple(masks), width)
    vecs = [margin] + [move(margin, k << 1) for k in range(1, groups)]
    grad, loss = grad_hidden(ids, pairs, total, hidden, tgt, gain, vecs, width)

    tile = min(512, heads)
    grad_rows = grad.reshape(4 * L, -1)
    if split == 2:
        grad_other = swap_x(grad_rows)
        acc = back_mm(grad_rows, back_keep, None, tile)
        keep, send = back_mm(grad_other, back_send, acc, tile)
    else:
        keep, send = back_mm(grad_rows, back_keep, jnp.zeros((4 * L, heads), F32), tile)
    keep = keep.reshape(2, L, heads)
    rs = move(send, 1).reshape(2, L, heads)
    far = (keep[1] + rs[1].astype(F32)).astype(BF16)
    r2 = move(far, top)
    outer, mid = attend_back(keep, rs, r2, low, qo, vo, cosine, sine, saved)

    rows_each = width // tensor_size
    own_states = lax.dynamic_slice_in_dim(pol_states, x * rows_each, rows_each, 1)
    if split == 2:
        mid_other = swap_x(mid)
        a_grads = dot(
            jnp.concatenate([own_states, own_states], 0),
            jnp.concatenate([mid, mid_other], 0),
            ((0,), (0,)),
        )
    else:
        mid_all = lax.all_gather(mid, "tensor", axis=0, tiled=True)
        a_grads = dot(jnp.concatenate([own_states] * tensor_size, 0), mid_all, ((0,), (0,)))
    current = jnp.concatenate([a_grads, outer], 0)
    bits = []
    mask = 1
    while mask < fsdp_size:
        bits.append(mask)
        mask *= 2
    for mask in bits:
        half = current.shape[0] // 2
        bit = (me & mask) // mask
        away = lax.dynamic_slice_in_dim(current, (1 - bit) * half, half, 0).astype(BF16)
        stay = lax.dynamic_slice_in_dim(current, bit * half, half, 0)
        current = stay + move(away, mask).astype(F32)
    current = current.astype(BF16)
    for mask in reversed(bits):
        bit = (me & mask) // mask
        other = move(current, mask)
        current = jnp.where(
            bit == 0,
            jnp.concatenate([current, other], 0),
            jnp.concatenate([other, current], 0),
        )
    current = current.astype(F32)
    a_grads = current[:rows_each]
    q_rows = kv_local * GROUP * rank
    outer_q = current[rows_each : rows_each + q_rows].reshape(-1, rank, HEAD_SIZE)
    outer_v = current[rows_each + q_rows :].reshape(-1, rank, HEAD_SIZE)
    return (
        loss[0, 0],
        a_grads[:, :rank],
        outer_q.transpose(1, 0, 2).reshape(rank, -1),
        a_grads[:, rank:],
        outer_v.transpose(1, 0, 2).reshape(rank, -1),
    )


def solution(mesh):
    in_specs = (
        P("fsdp", None),
        P("fsdp", None),
        P("fsdp", None),
        P(),
        P("fsdp", "tensor"),
        P("fsdp", "tensor"),
        P("fsdp", "tensor"),
        P("tensor", "fsdp"),
        P(),
        P(None, "tensor"),
        P(),
        P(None, "tensor"),
        P("fsdp"),
        P(),
    )
    out_specs = (P(), P("tensor", None), P(None, "tensor"), P("tensor", None), P(None, "tensor"))
    body = functools.partial(per_device, mesh.shape["fsdp"], mesh.shape["tensor"])
    return jax.shard_map(body, mesh=mesh, in_specs=in_specs, out_specs=out_specs, check_vma=False)
```

```python
import functools

import jax
import jax.numpy as jnp
from jax import lax
from jax.experimental import pallas as pl
from jax.experimental.pallas import tpu as pltpu
from jax.sharding import PartitionSpec as P

QUERY_HEADS = 32
KEY_VALUE_HEADS = 8
HEAD_SIZE = 128
L = 128
GROUP = QUERY_HEADS // KEY_VALUE_HEADS
QCOLS = GROUP * HEAD_SIZE

adapter_scale = 0.5
dpo_beta = 0.1
loss_scale = 256.0
rope_base = 500000.0
norm_eps = 1e-05

F32 = jnp.float32
BF16 = jnp.bfloat16
ORD = (0, 2, 1, 3)
MB = 1 << 20


def rope_tables(length, head_dim):
    half_dim = head_dim // 2
    exponent = jnp.arange(half_dim, dtype=F32) * (2.0 / head_dim)
    inverse = jnp.power(F32(rope_base), -exponent)
    angles = jnp.arange(length, dtype=F32)[:, None] * inverse[None, :]
    cosine = jnp.concatenate([jnp.cos(angles), jnp.cos(angles)], 1)
    sine = jnp.concatenate([-jnp.sin(angles), jnp.sin(angles)], 1)
    return cosine, sine


def dot(a, b, dims=((1,), (0,))):
    return lax.dot_general(a, b, (dims, ((), ())), preferred_element_type=F32)


def params(limit_mb):
    return pltpu.CompilerParams(vmem_limit_bytes=limit_mb * MB)


def smem():
    return pl.BlockSpec(memory_space=pltpu.SMEM)


def whole_vmem():
    return pl.BlockSpec(memory_space=pltpu.VMEM)


def prep_body(parts, part, split, idx, ref, pol, tgt, gain, *outs):
    x0, x1, x2, x3, t0, t1, t2, t3, go = outs
    groups = parts // split
    for d, (xo, to) in enumerate(((x0, t0), (x1, t1), (x2, t2), (x3, t3))):
        for j in range(parts):
            src = pl.ds(pl.multiple_of(idx[d * parts + j] * part, part), part)
            cols = slice(j * part, (j + 1) * part)
            if xo.shape[0] == 2:
                xo[0, :, cols] = ref[:, src]
                xo[1, :, cols] = pol[:, src]
            else:
                @pl.when(idx[4 * parts + 4 * groups] == 0)
                def _():
                    xo[0, :, cols] = ref[:, src]

                @pl.when(idx[4 * parts + 4 * groups] != 0)
                def _():
                    xo[0, :, cols] = pol[:, src]

        for j in range(groups):
            at = idx[4 * parts + d * groups + j] * part
            src = pl.ds(pl.multiple_of(at, part), part)
            to[:, j * part : (j + 1) * part] = tgt[:, src]
            if d == 0:
                go[:, j * part : (j + 1) * part] = gain[:, src]


def prep(idx, ref, pol, tgt, gain, parts, part, split):
    tokens = ref.shape[0]
    xs = lambda n: jax.ShapeDtypeStruct((n, tokens, parts * part), BF16)
    far = 1 if split == 2 else 2
    width = parts // split * part
    return pl.pallas_call(
        functools.partial(prep_body, parts, part, split),
        in_specs=[smem()] + [whole_vmem()] * 4,
        out_specs=[whole_vmem()] * 9,
        out_shape=[xs(2), xs(2), xs(far), xs(far)]
        + [jax.ShapeDtypeStruct((tokens, width), BF16)] * 4
        + [jax.ShapeDtypeStruct((1, width), F32)],
        compiler_params=params(32),
    )(idx, ref, pol, tgt, gain)


def tile_of(cols):
    for tile in (256, 128):
        if cols % tile == 0:
            return tile
    return cols


def mm_body(x_ref, w_ref, out_ref):
    out_ref[...] = dot(x_ref[...], w_ref[...]).astype(out_ref.dtype)


def mm(x, half, w, out_dtype):
    rows, depth = x.shape[0] // 2, x.shape[1]
    cols = w.shape[1]
    tile = tile_of(cols)
    return pl.pallas_call(
        mm_body,
        grid=(cols // tile,),
        in_specs=[
            pl.BlockSpec((rows, depth), lambda i: (half, 0)),
            pl.BlockSpec((depth, tile), lambda i: (0, i)),
        ],
        out_specs=pl.BlockSpec((rows, tile), lambda i: (0, i)),
        out_shape=jax.ShapeDtypeStruct((rows, cols), out_dtype),
        compiler_params=params(32),
        cost_estimate=pl.CostEstimate(
            flops=2 * rows * depth * cols,
            bytes_accessed=2 * (rows * (depth + cols) + depth * cols),
            transcendentals=0,
        ),
    )(x, w)


def out_body(n, *refs):
    w_ref, out_ref = refs[2 * n :]
    rows = refs[0].shape[0]
    for side in range(2):
        total = None
        at = 0
        for ref in refs[side * n : (side + 1) * n]:
            depth = ref.shape[1]
            term = dot(ref[...], w_ref[0, 0, at : at + depth])
            total = term if total is None else total + term
            at += depth
        out_ref[0, side * rows : (side + 1) * rows] = total.astype(out_ref.dtype)


def out_mm(near, far, w_all, which, start, count):
    n = len(near)
    rows = near[0].shape[0]
    _, _, depth, cols = w_all.shape
    return pl.pallas_call(
        functools.partial(out_body, n),
        grid=(count,),
        in_specs=[pl.BlockSpec(a.shape, lambda i: (0, 0)) for a in (*near, *far)]
        + [pl.BlockSpec((1, 1, depth, cols), lambda i: (i + start, which, 0, 0))],
        out_specs=pl.BlockSpec((1, 2 * rows, cols), lambda i: (i, 0, 0)),
        out_shape=jax.ShapeDtypeStruct((count, 2 * rows, cols), BF16),
        compiler_params=params(32),
        cost_estimate=pl.CostEstimate(
            flops=4 * count * rows * depth * cols,
            bytes_accessed=2 * (2 * rows * depth + count * (2 * rows * cols + depth * cols)),
            transcendentals=0,
        ),
    )(*near, *far, w_all)


def back_body(n, part, has_acc, x_ref, *refs):
    ws = refs[:n]
    refs = refs[n:]
    total = None
    for j in range(n):
        term = dot(x_ref[:, j * part : (j + 1) * part], ws[j][0, 0], ((1,), (1,)))
        total = term if total is None else total + term
    if has_acc:
        total = total + refs[0][...]
        keep, send = refs[1:]
        half = total.shape[0] // 2
        keep[...] = total[:half]
        send[...] = total[half:].astype(send.dtype)
    else:
        refs[0][...] = total


def back_mm(x, half, w_all, which, acc):
    rows = x.shape[0] // (1 if half is None else 2)
    depth = x.shape[1]
    groups, _, heads, part = w_all.shape
    tile = min(512, heads)
    has_acc = acc is not None
    row = half or 0
    in_specs = [pl.BlockSpec((rows, depth), lambda i: (row, 0))]
    for k in range(groups):
        in_specs.append(
            pl.BlockSpec((1, 1, tile, part), functools.partial(lambda k, i: (k, which, i, 0), k))
        )
    args = [x] + [w_all] * groups
    if has_acc:
        in_specs.append(pl.BlockSpec((rows, tile), lambda i: (0, i)))
        args.append(acc)
        out_specs = [pl.BlockSpec((rows // 2, tile), lambda i: (0, i))] * 2
        out_shape = [
            jax.ShapeDtypeStruct((rows // 2, heads), F32),
            jax.ShapeDtypeStruct((rows // 2, heads), BF16),
        ]
    else:
        out_specs = pl.BlockSpec((rows, tile), lambda i: (0, i))
        out_shape = jax.ShapeDtypeStruct((rows, heads), F32)
    return pl.pallas_call(
        functools.partial(back_body, groups, part, has_acc),
        grid=(heads // tile,),
        in_specs=in_specs,
        out_specs=out_specs,
        out_shape=out_shape,
        compiler_params=params(32),
        cost_estimate=pl.CostEstimate(
            flops=2 * rows * depth * heads,
            bytes_accessed=2 * (rows * depth + depth * heads) + 4 * rows * heads,
            transcendentals=0,
        ),
    )(*args)


def causal(rows):
    at = lax.broadcasted_iota(jnp.int32, (rows, L), 0) % L
    return at >= lax.broadcasted_iota(jnp.int32, (rows, L), 1)


def probabilities(q4, keys):
    scores = dot(q4, keys, ((1,), (1,))) * (HEAD_SIZE**-0.5)
    weights = jnp.where(causal(q4.shape[0]), jnp.exp(scores), 0.0)
    return weights / jnp.sum(weights, -1, keepdims=True)


def stack_heads(values):
    return jnp.concatenate(
        [values[:, h * HEAD_SIZE : (h + 1) * HEAD_SIZE] for h in range(GROUP)], 0
    )


def attend_body(adapted, keep, rs, r2, low, qo, vo, cos_ref, sin_ref, mixed, *saved):
    cosine = cos_ref[...]
    sine = sin_ref[...]
    pre = keep[...] + rs[...].astype(F32) + r2[...].astype(F32)
    rank = qo.shape[0]
    q_pre = pre[:, :QCOLS]
    k_pre = pre[:, QCOLS : QCOLS + HEAD_SIZE]
    v_pre = pre[:, QCOLS + HEAD_SIZE :]
    if adapted:
        q_pre = q_pre + adapter_scale * dot(low[:, :rank], qo[...])
        v_pre = v_pre + adapter_scale * dot(low[:, rank:], vo[...])
    cos4 = jnp.concatenate([cosine] * GROUP, 0)
    sin4 = jnp.concatenate([sine] * GROUP, 0)
    q4 = stack_heads(q_pre)
    q4 = (q4 * cos4 + pltpu.roll(q4, HEAD_SIZE // 2, 1) * sin4).astype(BF16)
    keys = (k_pre * cosine + pltpu.roll(k_pre, HEAD_SIZE // 2, 1) * sine).astype(BF16)
    values = v_pre.astype(BF16)
    rounded = probabilities(q4, keys).astype(BF16)
    out = dot(rounded, values).astype(BF16)
    for h in range(GROUP):
        cols = slice(h * HEAD_SIZE, (h + 1) * HEAD_SIZE)
        mixed[:, cols] = out[h * L : (h + 1) * L]
        if saved:
            saved[0][:, cols] = q4[h * L : (h + 1) * L]
    if saved:
        saved[0][:, QCOLS : QCOLS + HEAD_SIZE] = keys
        saved[0][:, QCOLS + HEAD_SIZE :] = values


def attend(adapted, keep, rs, r2, low, qo, vo, start, cosine, sine):
    each = QCOLS + 2 * HEAD_SIZE
    count = r2.shape[1] // each
    rank = qo.shape[0]
    fixed = lambda a: pl.BlockSpec(a.shape, lambda i: (0,) * a.ndim)
    block = pl.BlockSpec((L, each), lambda i: (0, i))
    mixed_spec = pl.BlockSpec((L, QCOLS), lambda i: (0, i))
    mixed_shape = jax.ShapeDtypeStruct((L, count * QCOLS), BF16)
    return pl.pallas_call(
        functools.partial(attend_body, adapted),
        grid=(count,),
        in_specs=[
            block,
            block,
            block,
            fixed(low),
            pl.BlockSpec((rank, QCOLS), lambda i: (0, i + start)),
            pl.BlockSpec((rank, HEAD_SIZE), lambda i: (0, i + start)),
            fixed(cosine),
            fixed(sine),
        ],
        out_specs=[mixed_spec, block] if adapted else [mixed_spec],
        out_shape=[mixed_shape, jax.ShapeDtypeStruct((L, count * each), BF16)]
        if adapted
        else [mixed_shape],
        compiler_params=params(32),
        cost_estimate=pl.CostEstimate(
            flops=2 * count * L * QCOLS * (2 * L + 64),
            bytes_accessed=L * count * (each * 10 + QCOLS * 2),
            transcendentals=count * L * L * GROUP,
        ),
    )(keep, rs, r2, low, qo, vo, cosine, sine)


def outer_place(block, rank, kv):
    wide = (kv * (GROUP + 1) + 1) // 2
    return (block // wide) * rank, (block % wide) * HEAD_SIZE, wide


def attend_back_body(kv, splits, keep, rs, r2, low, qo, vo, cos_ref, sin_ref, *refs):
    saved = refs[:splits]
    outer, mid = refs[splits:]
    rank = qo.shape[0]
    each = QCOLS + 2 * HEAD_SIZE
    cos4 = jnp.concatenate([cos_ref[...]] * GROUP, 0)
    sin4 = jnp.concatenate([sin_ref[...]] * GROUP, 0)
    low_q = low[:, :rank]
    low_v = low[:, rank:]
    q_mid = jnp.zeros((L, rank), F32)
    v_mid = jnp.zeros((L, rank), F32)

    def put(block, value):
        row, col, _ = outer_place(block, rank, kv)
        outer[row : row + rank, col : col + HEAD_SIZE] = adapter_scale * value

    if (kv * (GROUP + 1)) % 2:
        put(kv * (GROUP + 1), jnp.zeros((rank, HEAD_SIZE), F32))
    for j in range(kv):
        cols = slice(j * QCOLS, (j + 1) * QCOLS)
        at = (j % (kv // splits)) * each
        kept = saved[j // (kv // splits)]
        grad = keep[:, cols] + rs[:, cols].astype(F32) + r2[:, cols].astype(F32)
        grad4 = stack_heads(grad.astype(BF16))
        q4 = stack_heads(kept[:, at : at + QCOLS])
        keys = kept[:, at + QCOLS : at + QCOLS + HEAD_SIZE]
        values = kept[:, at + QCOLS + HEAD_SIZE : at + each]
        prob = probabilities(q4, keys)
        grad_prob = dot(grad4, values, ((1,), (1,)))
        grad_values = dot(prob.astype(BF16), grad4, ((0,), (0,))).astype(BF16)
        inner = jnp.sum(grad_prob * prob, -1, keepdims=True)
        grad_scores = (prob * (grad_prob - inner) * (HEAD_SIZE**-0.5)).astype(BF16)
        grad_query = dot(grad_scores, keys)
        back4 = (grad_query * cos4 - pltpu.roll(grad_query, HEAD_SIZE // 2, 1) * sin4).astype(BF16)
        for h in range(GROUP):
            at = j * GROUP + h
            back = back4[h * L : (h + 1) * L]
            put(at, dot(low_q, back, ((0,), (0,))))
            q_mid += dot(back, qo[:, at * HEAD_SIZE : (at + 1) * HEAD_SIZE], ((1,), (1,)))
        put(kv * GROUP + j, dot(low_v, grad_values, ((0,), (0,))))
        v_mid += dot(grad_values, vo[:, j * HEAD_SIZE : (j + 1) * HEAD_SIZE], ((1,), (1,)))
    mid[:, :rank] = (adapter_scale * q_mid).astype(BF16)
    mid[:, rank:] = (adapter_scale * v_mid).astype(BF16)


def attend_back(keep, rs, r2, low, qo, vo, cosine, sine, saved):
    rank = qo.shape[0]
    kv = vo.shape[1] // HEAD_SIZE
    wide = outer_place(0, rank, kv)[2]
    return pl.pallas_call(
        functools.partial(attend_back_body, kv, len(saved)),
        in_specs=[whole_vmem()] * (8 + len(saved)),
        out_specs=[whole_vmem()] * 2,
        out_shape=[
            jax.ShapeDtypeStruct((2 * rank, wide * HEAD_SIZE), F32),
            jax.ShapeDtypeStruct((L, 2 * rank), BF16),
        ],
        compiler_params=params(32),
    )(keep, rs, r2, low, qo, vo, cosine, sine, *saved)


def adapter_body(n, rows_each, scal, states, outer, *refs):
    mids = refs[:n]
    away, stay = refs[n:]
    src = pl.ds(pl.multiple_of(scal[0] * rows_each, rows_each), rows_each)
    own = states[:, src]
    total = None
    for mid in mids:
        term = dot(mid[...], own, ((0,), (0,)))
        total = term if total is None else total + term
    half = total.shape[0] // 2
    for low in range(2):
        rows = slice(low * half, (low + 1) * half)

        @pl.when(scal[1] == low)
        def _():
            stay[:, :rows_each] = total[rows]
            stay[:, rows_each:] = outer[rows]

        @pl.when(scal[1] != low)
        def _():
            away[:, :rows_each] = total[rows].astype(BF16)
            away[:, rows_each:] = outer[rows].astype(BF16)


def adapter_products(scal, states, mids, outer, rows_each):
    half = outer.shape[0] // 2
    cols = rows_each + outer.shape[1]
    return pl.pallas_call(
        functools.partial(adapter_body, len(mids), rows_each),
        in_specs=[smem()] + [whole_vmem()] * (2 + len(mids)),
        out_specs=[whole_vmem()] * 2,
        out_shape=[
            jax.ShapeDtypeStruct((half, cols), BF16),
            jax.ShapeDtypeStruct((half, cols), F32),
        ],
        compiler_params=params(32),
    )(scal, states, outer, *mids)


def stats_body(counts, part, split, scal, xt_ref, xt_pol, tgt, gain, *refs):
    refs = list(refs)
    sums = []
    hidden_out, stats = refs[-2:]
    for which, count in enumerate(counts):
        xt = (xt_ref, xt_pol)[which]
        keeps, recvs = refs[:count], refs[count : 2 * count]
        refs = refs[2 * count :]
        squares = jnp.zeros((L, HEAD_SIZE), F32)
        products = jnp.zeros((L, HEAD_SIZE), F32)
        j = 0
        for keep, recv in zip(keeps, recvs):
            for i in range(keep.shape[0]):
                src = pl.ds(pl.multiple_of((j * split + scal[0]) * part, part), part)
                hidden = xt[:, src].astype(F32) + keep[i].astype(F32) + recv[i].astype(F32)
                cols = slice(j * part, (j + 1) * part)
                if which == 1:
                    hidden_out[0, :, cols] = hidden
                product = hidden * (gain[:, cols] * tgt[0, :, cols].astype(F32))
                square = hidden * hidden
                for s in range(part // HEAD_SIZE):
                    lanes = slice(s * HEAD_SIZE, (s + 1) * HEAD_SIZE)
                    squares += square[:, lanes]
                    products += product[:, lanes]
                j += 1
        sums.append(
            [
                jnp.broadcast_to(jnp.sum(v, 1, keepdims=True), v.shape).T[:1]
                for v in (squares, products)
            ]
        )
    at = lax.broadcasted_iota(jnp.int32, (1, 2 * L), 1) % L
    own = (at >= scal[1]) & (pl.program_id(0) == 0)
    live = jnp.where(own, 1.0, 0.0).astype(F32)
    both = [jnp.concatenate([sums[0][i], sums[1][i]], 1) for i in range(2)]
    stats[...] = jnp.concatenate([*both, live, jnp.zeros((5, 2 * L), F32)], 0)


def norm_stats(scal, xt_ref, xt_pol, tgt, gain, keeps, recvs, split):
    n = sum(a.shape[0] for a in keeps[0])
    part = keeps[0][0].shape[2]
    shared = []
    for which in range(2):
        for a in (*keeps[which], *recvs[which]):
            shared.append((a, pl.BlockSpec((a.shape[0], L, part), lambda i: (0, i, 0))))
    return pl.pallas_call(
        functools.partial(stats_body, tuple(len(k) for k in keeps), part, split),
        grid=(4,),
        in_specs=[
            smem(),
            pl.BlockSpec((L, xt_ref.shape[1]), lambda i: (i, 0)),
            pl.BlockSpec((L, xt_pol.shape[1]), lambda i: (i, 0)),
            pl.BlockSpec((1, L, n * part), lambda i: (i, 0, 0)),
            pl.BlockSpec((1, n * part), lambda i: (0, 0)),
        ]
        + [spec for _, spec in shared],
        out_specs=[
            pl.BlockSpec((1, L, n * part), lambda i: (i, 0, 0)),
            pl.BlockSpec((8, 2 * L), lambda i: (i, 0)),
        ],
        out_shape=[
            jax.ShapeDtypeStruct((4, L, n * part), F32),
            jax.ShapeDtypeStruct((32, 2 * L), F32),
        ],
        compiler_params=params(32),
    )(scal, xt_ref, xt_pol, tgt, gain, *[a for a, _ in shared])


def score_body(width, masks, ids, own, *refs):
    recvs = refs[: len(masks)]
    total_out, margin_out = refs[len(masks) :]
    lane = lax.broadcasted_iota(jnp.int32, (8, 128), 1)
    margins = jnp.zeros((8, 128), F32)
    for p in range(4):
        total = own[8 * p : 8 * p + 8]
        for recv, m in zip(recvs, masks):
            q = ORD.index(ORD[p] ^ m)
            total = total + recv[8 * q : 8 * q + 8]
        total_out[8 * p : 8 * p + 8] = total
        inverse = lax.rsqrt(total[0:1] * (1.0 / width) + norm_eps)
        score = total[1:2] * inverse * (width**-0.5)
        score = jnp.where(total[2:3] > 0.5, score, 0.0)
        margin = jnp.sum(score[:, L:], 1, keepdims=True) - jnp.sum(score[:, :L], 1, keepdims=True)
        margins = margins + jnp.where(lane == ids[p], margin, 0.0)
    margin_out[...] = margins


def scores(ids, own, recvs, masks, width):
    return pl.pallas_call(
        functools.partial(score_body, width, masks),
        in_specs=[smem()] + [whole_vmem()] * (1 + len(recvs)),
        out_specs=[whole_vmem()] * 2,
        out_shape=[jax.ShapeDtypeStruct(own.shape, F32), jax.ShapeDtypeStruct((8, 128), F32)],
    )(ids, own, *recvs)


def turn(i):
    return (2 * i + 1) % 5


def grad_body(width, seqs, n_vec, ids, pairs, total, hidden, tgt, gain, *refs):
    vecs = refs[:n_vec]
    grad_out, loss_out, slope = refs[n_vec:]
    lane = lax.broadcasted_iota(jnp.int32, (8, 128), 1)

    @pl.when(pl.program_id(0) == 0)
    def _():
        margin = vecs[0][...]
        for v in vecs[1:]:
            margin = margin + v[...]
        logits = jnp.zeros((8, 128), F32)
        for i in range(seqs // 2):
            sign = jnp.where(lane == pairs[2 * i], 1.0, 0.0) - jnp.where(
                lane == pairs[2 * i + 1], 1.0, 0.0
            )
            logit = dpo_beta * jnp.sum(margin * sign, 1, keepdims=True)
            logits = logits + jnp.where(lane == i, logit, 0.0)
        soft = jnp.maximum(-logits, 0.0) + jnp.log1p(jnp.exp(-jnp.abs(logits)))
        used = lane < seqs // 2
        loss = jnp.sum(jnp.where(used, soft, 0.0), 1, keepdims=True)
        loss_out[...] = jnp.broadcast_to(loss, (8, 128))
        slopes = jnp.where(used, -dpo_beta / (1.0 + jnp.exp(logits)), 0.0)
        gradient = jnp.zeros((8, 128), F32)
        for i in range(seqs // 2):
            each = jnp.sum(jnp.where(lane == i, slopes, 0.0), 1, keepdims=True)
            sign = jnp.where(lane == pairs[2 * i], 1.0, 0.0) - jnp.where(
                lane == pairs[2 * i + 1], 1.0, 0.0
            )
            gradient = gradient + each * sign
        slope[...] = gradient * loss_scale

    mine = lane == ids[turn(pl.program_id(0))]
    seq = jnp.sum(jnp.where(mine, slope[...], 0.0), 1, keepdims=True)[:1]
    rows = total[:, L:]
    token = jnp.where(rows[2:3] > 0.5, seq, 0.0) * (width**-0.5)
    inverse = lax.rsqrt(rows[0:1] * (1.0 / width) + norm_eps)
    first = inverse * token
    second = inverse * inverse * inverse * (token * rows[1:2] * (1.0 / width))
    first = jnp.broadcast_to(first, (L, L)).T
    second = jnp.broadcast_to(second, (L, L)).T
    for s in range(hidden.shape[2] // HEAD_SIZE):
        cols = slice(s * HEAD_SIZE, (s + 1) * HEAD_SIZE)
        weighted = gain[:, cols] * tgt[0, :, cols].astype(F32)
        grad_out[0, :, cols] = (first * weighted - second * hidden[0, :, cols]).astype(BF16)


def grad_hidden(ids, pairs, total, hidden, tgt, gain, vecs, width):
    n = hidden.shape[2]
    seqs = pairs.shape[0]
    return pl.pallas_call(
        functools.partial(grad_body, width, seqs, len(vecs)),
        grid=(4,),
        in_specs=[
            smem(),
            smem(),
            pl.BlockSpec((8, 2 * L), lambda i: (turn(i), 0)),
            pl.BlockSpec((1, L, n), lambda i: (turn(i), 0, 0)),
            pl.BlockSpec((1, L, n), lambda i: (turn(i), 0, 0)),
            pl.BlockSpec((1, n), lambda i: (0, 0)),
        ]
        + [pl.BlockSpec((8, 128), lambda i: (0, 0)) for _ in vecs],
        out_specs=[
            pl.BlockSpec((1, L, n), lambda i: (i, 0, 0)),
            pl.BlockSpec((8, 128), lambda i: (0, 0)),
        ],
        out_shape=[
            jax.ShapeDtypeStruct((4, L, n), BF16),
            jax.ShapeDtypeStruct((8, 128), F32),
        ],
        scratch_shapes=[pltpu.VMEM((8, 128), F32)],
        compiler_params=params(32),
    )(ids, pairs, total, hidden, tgt, gain, *vecs)


def per_device(
    fsdp_size,
    tensor_size,
    ref_states,
    pol_states,
    target_rows,
    norm_gain,
    wq,
    wk,
    wv,
    wo,
    qa,
    qo,
    va,
    vo,
    prompt_length,
    pairs,
):
    tokens, width = ref_states.shape
    groups = fsdp_size // 4
    top = fsdp_size // 2
    split = 2 if tensor_size == 2 else 1
    kv_local = wk.shape[1] // HEAD_SIZE
    depth = wq.shape[0]
    part = depth // split
    rank = qa.shape[1]
    me = lax.axis_index("fsdp")
    x = lax.axis_index("tensor")
    side = x if split == 2 else 0
    mine = me & (top | 1)

    def tmask(d):
        return (d & 1) | ((d >> 1) * top)

    def move(value, mask):
        return lax.ppermute(value, "fsdp", [(i, i ^ mask) for i in range(fsdp_size)])

    def swap_x(value):
        return lax.ppermute(value, "tensor", [(0, 1), (1, 0)])

    def move_both(value, mask, flip):
        pairs_list = [
            (2 * i + j, 2 * (i ^ mask) + (j ^ flip)) for i in range(fsdp_size) for j in range(2)
        ]
        return lax.ppermute(value, ("fsdp", "tensor"), pairs_list)

    squares = [[high + 2 * k + low for k in range(groups)] for high in (0, top) for low in (0, 1)]

    def gather(shard):
        return lax.all_gather(shard, "fsdp", axis=0, axis_index_groups=squares, tiled=False)

    halves = 2 if kv_local % 2 == 0 else 1
    per_half = kv_local // halves
    wqkv = []
    for h in range(halves):
        pieces = []
        for j in range(h * per_half, (h + 1) * per_half):
            pieces += [
                wq[:, j * QCOLS : (j + 1) * QCOLS],
                wk[:, j * HEAD_SIZE : (j + 1) * HEAD_SIZE],
                wv[:, j * HEAD_SIZE : (j + 1) * HEAD_SIZE],
            ]
        shard = jnp.concatenate(pieces, 1)
        wqkv.append(gather(shard).reshape(groups * depth, -1))
    if split == 2:
        wo_keep = lax.dynamic_slice_in_dim(wo, x * part, part, 1)
        wo_send = lax.dynamic_slice_in_dim(wo, (1 - x) * part, part, 1)
        wo_all = gather(jnp.stack([wo_keep, wo_send]))
    else:
        wo_all = gather(wo[None])
    heads = wo.shape[0]

    parts = groups * split
    idx = []
    for d in range(4):
        for k in range(groups):
            for h in range(split):
                idx.append(((mine ^ tmask(d)) + 2 * k) * split + h)
    for d in range(4):
        for k in range(groups):
            idx.append(((mine ^ tmask(d)) + 2 * k) * split + side)
    idx.append(x)
    idx = jnp.stack(idx).astype(jnp.int32)
    prepared = prep(
        idx,
        ref_states,
        pol_states,
        target_rows,
        norm_gain.astype(F32).reshape(1, width),
        parts,
        part,
        split,
    )
    xs, ts, gain = prepared[:4], prepared[4:8], prepared[8]
    far = [move(xs[d], tmask(d)) for d in (2, 3)]
    near = move(xs[1], 1)
    if split == 2:
        other = [swap_x(a) for a in far]
        blocks = []
        for which in range(2):
            direct = x == which
            got = [jnp.where(direct, a[0], b[0]) for a, b in zip(far, other)]
            blocks.append(jnp.concatenate([xs[0][which], got[0], near[which], got[1]], 0))
    else:
        blocks = [
            jnp.concatenate([xs[0][w], far[0][w], near[w], far[1][w]], 0) for w in range(2)
        ]

    low = dot(pol_states, jnp.concatenate([qa, va], 1)).astype(BF16)
    cosine, sine = rope_tables(L, HEAD_SIZE)

    keeps, recvs, saved = [], [], []
    for which in range(2):
        near_mixed, far_mixed = [], []
        for h in range(halves):
            send = mm(blocks[which], 1, wqkv[h], BF16)
            rs = move(send, 1)
            keep = mm(blocks[which], 0, wqkv[h], F32)
            over_z = (keep[L:] + rs[L:].astype(F32)).astype(BF16)
            r2 = move(over_z, top)
            result = attend(
                which == 1, keep, rs, r2, low, qo, vo, h * per_half, cosine, sine
            )
            if which == 1:
                saved.append(result[1])
            mz = move(result[0], top)
            pair = jnp.concatenate([result[0], mz], 0)
            near_mixed.append(pair)
            far_mixed.append(move(pair, 1))
        steps = 2 if split == 2 and which == 1 else 1
        each = groups // steps
        kept, got = [], []
        for s in range(steps):
            if split == 2:
                got.append(swap_x(out_mm(near_mixed, far_mixed, wo_all, 1, s * each, each)))
        for s in range(steps):
            product = out_mm(near_mixed, far_mixed, wo_all, 0, s * each, each)
            if split == 1:
                product = lax.psum(product, "tensor")
                got.append(jnp.zeros_like(product))
            kept.append(product)
        keeps.append(kept)
        recvs.append(got)
        last = far_mixed[-1]

    ts = [ts[0]] + list(lax.optimization_barrier((*ts[1:], last))[:3])
    targets = [ts[0]] + [move(ts[d], tmask(d)) for d in (1, 2, 3)]
    tgt = jnp.stack([targets[d] for d in ORD])

    scal = jnp.stack([jnp.asarray(side, jnp.int32), prompt_length[0].astype(jnp.int32)])
    hidden, stats = norm_stats(scal, blocks[0], blocks[1], tgt, gain, keeps, recvs, split)
    masks, got = [], []
    for flip in range(split):
        for d in range(4):
            if d or flip:
                masks.append(d)
                if split == 2:
                    got.append(move_both(stats, tmask(d), flip))
                else:
                    got.append(move(stats, tmask(d)))
    ids = jnp.stack([me ^ tmask(d) for d in ORD]).astype(jnp.int32)
    total, margin = scores(ids, stats, got, tuple(masks), width)
    vecs = [margin] + [move(margin, k << 1) for k in range(1, groups)]
    grad, loss = grad_hidden(ids, pairs, total, hidden, tgt, gain, vecs, width)

    grad_rows = grad.reshape(4 * L, -1)
    parts_back = []
    for half in range(2):
        if split == 2:
            other = swap_x(grad_rows[2 * L * half : 2 * L * (half + 1)])
            acc = back_mm(grad_rows, half, wo_all, 0, None)
            keep, send = back_mm(other, None, wo_all, 1, acc)
        else:
            acc = jnp.zeros((2 * L, heads), F32)
            keep, send = back_mm(grad_rows, half, wo_all, 0, acc)
        rs = move(send, 1)
        if half == 0:
            r2 = move((keep + rs.astype(F32)).astype(BF16), top)
    outer, mid = attend_back(keep, rs, r2, low, qo, vo, cosine, sine, saved)

    rows_each = width // tensor_size
    if split == 2:
        mids = [mid, swap_x(mid)]
    else:
        gathered = lax.all_gather(mid, "tensor", axis=0, tiled=False)
        mids = [gathered[i] for i in range(tensor_size)]
    scal = jnp.stack([x, me & 1]).astype(jnp.int32)
    away, current = adapter_products(scal, pol_states, mids, outer, rows_each)
    current = current + move(away, 1).astype(F32)
    g = (me // 2) % groups
    rows = current.shape[0] // groups
    pieces = [
        lax.dynamic_slice_in_dim(current, (g ^ k) * rows, rows, 0) for k in range(groups)
    ]
    current = pieces[0]
    for k in range(1, groups):
        current = current + move(pieces[k].astype(BF16), k << 1).astype(F32)
    rows //= 2
    high = me // top
    away = lax.dynamic_slice_in_dim(current, (1 - high) * rows, rows, 0).astype(BF16)
    current = lax.dynamic_slice_in_dim(current, high * rows, rows, 0)
    current = (current + move(away, top).astype(F32)).astype(BF16)

    def join(bit, own, other):
        return jnp.where(
            bit == 0, jnp.concatenate([own, other], 0), jnp.concatenate([other, own], 0)
        )

    current = join(high, current, move(current, top))
    pieces = [current] + [move(current, k << 1) for k in range(1, groups)]
    step = 1
    while step < groups:
        odd = (g & step) != 0
        pieces = [jnp.where(odd, pieces[k ^ step], pieces[k]) for k in range(groups)]
        step *= 2
    current = jnp.concatenate(pieces, 0)
    current = join(me & 1, current, move(current, 1)).astype(F32)
    a_grads = current[:, :rows_each]
    outer = current[:, rows_each:]
    outer = jnp.concatenate([outer[:rank], outer[rank:]], 1)
    return (
        loss[0, 0],
        a_grads[:rank].T,
        outer[:, : qo.shape[1]],
        a_grads[rank:].T,
        outer[:, qo.shape[1] : qo.shape[1] + vo.shape[1]],
    )


def solution(mesh):
    in_specs = (
        P("fsdp", None),
        P("fsdp", None),
        P("fsdp", None),
        P(),
        P("fsdp", "tensor"),
        P("fsdp", "tensor"),
        P("fsdp", "tensor"),
        P("tensor", "fsdp"),
        P(),
        P(None, "tensor"),
        P(),
        P(None, "tensor"),
        P("fsdp"),
        P(),
    )
    out_specs = (P(), P("tensor", None), P(None, "tensor"), P("tensor", None), P(None, "tensor"))
    body = functools.partial(per_device, mesh.shape["fsdp"], mesh.shape["tensor"])
    return jax.shard_map(body, mesh=mesh, in_specs=in_specs, out_specs=out_specs, check_vma=False)
```

```python
import functools

import jax
import jax.numpy as jnp
from jax import lax
from jax.experimental import pallas as pl
from jax.experimental.pallas import tpu as pltpu
from jax.sharding import PartitionSpec as P

QUERY_HEADS = 32
KEY_VALUE_HEADS = 8
HEAD_SIZE = 128
L = 128
GROUP = QUERY_HEADS // KEY_VALUE_HEADS
QCOLS = GROUP * HEAD_SIZE

adapter_scale = 0.5
dpo_beta = 0.1
loss_scale = 256.0
rope_base = 500000.0
norm_eps = 1e-05

F32 = jnp.float32
BF16 = jnp.bfloat16
ORD = (0, 2, 1, 3)
MB = 1 << 20


def rope_tables(length, head_dim):
    half_dim = head_dim // 2
    exponent = jnp.arange(half_dim, dtype=F32) * (2.0 / head_dim)
    inverse = jnp.power(F32(rope_base), -exponent)
    angles = jnp.arange(length, dtype=F32)[:, None] * inverse[None, :]
    cosine = jnp.concatenate([jnp.cos(angles), jnp.cos(angles)], 1)
    sine = jnp.concatenate([-jnp.sin(angles), jnp.sin(angles)], 1)
    return cosine, sine


def dot(a, b, dims=((1,), (0,))):
    return lax.dot_general(a, b, (dims, ((), ())), preferred_element_type=F32)


def params(limit_mb):
    return pltpu.CompilerParams(vmem_limit_bytes=limit_mb * MB)


def smem():
    return pl.BlockSpec(memory_space=pltpu.SMEM)


def whole_vmem():
    return pl.BlockSpec(memory_space=pltpu.VMEM)


def prep_body(parts, part, split, idx, ref, pol, tgt, gain, *outs):
    x0, x1, x2, x3, t0, t1, t2, t3, go = outs
    groups = parts // split
    for d, (xo, to) in enumerate(((x0, t0), (x1, t1), (x2, t2), (x3, t3))):
        for j in range(parts):
            src = pl.ds(pl.multiple_of(idx[d * parts + j] * part, part), part)
            cols = slice(j * part, (j + 1) * part)
            if xo.shape[0] == 2:
                xo[0, :, cols] = ref[:, src]
                xo[1, :, cols] = pol[:, src]
            else:
                @pl.when(idx[4 * parts + 4 * groups] == 0)
                def _():
                    xo[0, :, cols] = ref[:, src]

                @pl.when(idx[4 * parts + 4 * groups] != 0)
                def _():
                    xo[0, :, cols] = pol[:, src]

        for j in range(groups):
            at = idx[4 * parts + d * groups + j] * part
            src = pl.ds(pl.multiple_of(at, part), part)
            to[:, j * part : (j + 1) * part] = tgt[:, src]
            if d == 0:
                go[:, j * part : (j + 1) * part] = gain[:, src]


def prep(idx, ref, pol, tgt, gain, parts, part, split):
    tokens = ref.shape[0]
    xs = lambda n: jax.ShapeDtypeStruct((n, tokens, parts * part), BF16)
    far = 1 if split == 2 else 2
    width = parts // split * part
    return pl.pallas_call(
        functools.partial(prep_body, parts, part, split),
        in_specs=[smem()] + [whole_vmem()] * 4,
        out_specs=[whole_vmem()] * 9,
        out_shape=[xs(2), xs(2), xs(far), xs(far)]
        + [jax.ShapeDtypeStruct((tokens, width), BF16)] * 4
        + [jax.ShapeDtypeStruct((1, width), F32)],
        compiler_params=params(32),
    )(idx, ref, pol, tgt, gain)


def tile_of(cols):
    for tile in (256, 128):
        if cols % tile == 0:
            return tile
    return cols


def mm_body(x_ref, *refs):
    out_ref = refs[-1]
    total = None
    at = 0
    for w in refs[:-1]:
        depth = w.shape[0]
        term = dot(x_ref[:, at : at + depth], w[...])
        total = term if total is None else total + term
        at += depth
    out_ref[...] = total.astype(out_ref.dtype)


def mm(x, half, ws, out_dtype):
    rows, depth = x.shape[0] // 2, x.shape[1]
    cols = ws[0].shape[1]
    tile = tile_of(cols)
    return pl.pallas_call(
        mm_body,
        grid=(cols // tile,),
        in_specs=[pl.BlockSpec((rows, depth), lambda i: (half, 0))]
        + [pl.BlockSpec((w.shape[0], tile), lambda i: (0, i)) for w in ws],
        out_specs=pl.BlockSpec((rows, tile), lambda i: (0, i)),
        out_shape=jax.ShapeDtypeStruct((rows, cols), out_dtype),
        compiler_params=params(32),
        cost_estimate=pl.CostEstimate(
            flops=2 * rows * depth * cols,
            bytes_accessed=2 * (rows * (depth + cols) + depth * cols),
            transcendentals=0,
        ),
    )(x, *ws)


def out_body(n, x_ref, *refs):
    out_ref = refs[-1]
    for k in range(n):
        out_ref[k] = dot(x_ref[...], refs[k][0]).astype(out_ref.dtype)


def out_mm(x, ws, tile=256):
    n = len(ws)
    rows, depth = x.shape
    cols = ws[0][0].shape[2]
    at = lambda which: lambda i: (which, 0, 0)
    return pl.pallas_call(
        functools.partial(out_body, n),
        grid=(rows // tile,),
        in_specs=[pl.BlockSpec((tile, depth), lambda i: (i, 0))]
        + [pl.BlockSpec((1, depth, cols), at(which)) for _, which in ws],
        out_specs=pl.BlockSpec((n, tile, cols), lambda i: (0, i, 0)),
        out_shape=jax.ShapeDtypeStruct((n, rows, cols), BF16),
        compiler_params=params(32),
        cost_estimate=pl.CostEstimate(
            flops=2 * n * rows * depth * cols,
            bytes_accessed=2 * (rows * depth + n * (rows * cols + depth * cols)),
            transcendentals=0,
        ),
    )(x, *[w for w, _ in ws])


def back_body(n, part, has_acc, x_ref, *refs):
    ws = refs[:n]
    refs = refs[n:]
    total = None
    for j in range(n):
        term = dot(x_ref[:, j * part : (j + 1) * part], ws[j][0], ((1,), (1,)))
        total = term if total is None else total + term
    if has_acc:
        total = total + refs[0][...]
        keep, send = refs[1:]
        half = total.shape[0] // 2
        keep[...] = total[:half]
        send[...] = total[half:].astype(send.dtype)
    else:
        refs[0][...] = total


def back_mm(x, half, ws, acc):
    rows = x.shape[0] // (1 if half is None else 2)
    depth = x.shape[1]
    groups = len(ws)
    _, heads, part = ws[0][0].shape
    tile = min(512, heads)
    has_acc = acc is not None
    row = half or 0
    in_specs = [pl.BlockSpec((rows, depth), lambda i: (row, 0))]
    for _, which in ws:
        in_specs.append(
            pl.BlockSpec((1, tile, part), functools.partial(lambda which, i: (which, i, 0), which))
        )
    args = [x] + [w for w, _ in ws]
    if has_acc:
        in_specs.append(pl.BlockSpec((rows, tile), lambda i: (0, i)))
        args.append(acc)
        out_specs = [pl.BlockSpec((rows // 2, tile), lambda i: (0, i))] * 2
        out_shape = [
            jax.ShapeDtypeStruct((rows // 2, heads), F32),
            jax.ShapeDtypeStruct((rows // 2, heads), BF16),
        ]
    else:
        out_specs = pl.BlockSpec((rows, tile), lambda i: (0, i))
        out_shape = jax.ShapeDtypeStruct((rows, heads), F32)
    return pl.pallas_call(
        functools.partial(back_body, groups, part, has_acc),
        grid=(heads // tile,),
        in_specs=in_specs,
        out_specs=out_specs,
        out_shape=out_shape,
        compiler_params=params(32),
        cost_estimate=pl.CostEstimate(
            flops=2 * rows * depth * heads,
            bytes_accessed=2 * (rows * depth + depth * heads) + 4 * rows * heads,
            transcendentals=0,
        ),
    )(*args)


def causal(rows):
    at = lax.broadcasted_iota(jnp.int32, (rows, L), 0) % L
    return at >= lax.broadcasted_iota(jnp.int32, (rows, L), 1)


def probabilities(q4, keys):
    scores = dot(q4, keys, ((1,), (1,))) * (HEAD_SIZE**-0.5)
    weights = jnp.where(causal(q4.shape[0]), jnp.exp(scores), 0.0)
    return weights / jnp.sum(weights, -1, keepdims=True)


def stack_heads(values):
    return jnp.concatenate(
        [values[:, h * HEAD_SIZE : (h + 1) * HEAD_SIZE] for h in range(GROUP)], 0
    )


def attend_body(adapted, keep, rs, r2, low, qo, vo, cos_ref, sin_ref, mixed, *saved):
    cosine = cos_ref[...]
    sine = sin_ref[...]
    pre = keep[...] + rs[...].astype(F32) + r2[...].astype(F32)
    rank = qo.shape[0]
    q_pre = pre[:, :QCOLS]
    k_pre = pre[:, QCOLS : QCOLS + HEAD_SIZE]
    v_pre = pre[:, QCOLS + HEAD_SIZE :]
    if adapted:
        q_pre = q_pre + adapter_scale * dot(low[:, :rank], qo[...])
        v_pre = v_pre + adapter_scale * dot(low[:, rank:], vo[...])
    cos4 = jnp.concatenate([cosine] * GROUP, 0)
    sin4 = jnp.concatenate([sine] * GROUP, 0)
    q4 = stack_heads(q_pre)
    q4 = (q4 * cos4 + pltpu.roll(q4, HEAD_SIZE // 2, 1) * sin4).astype(BF16)
    keys = (k_pre * cosine + pltpu.roll(k_pre, HEAD_SIZE // 2, 1) * sine).astype(BF16)
    values = v_pre.astype(BF16)
    rounded = probabilities(q4, keys).astype(BF16)
    out = dot(rounded, values).astype(BF16)
    for h in range(GROUP):
        cols = slice(h * HEAD_SIZE, (h + 1) * HEAD_SIZE)
        mixed[:, cols] = out[h * L : (h + 1) * L]
        if saved:
            saved[0][:, cols] = q4[h * L : (h + 1) * L]
    if saved:
        saved[0][:, QCOLS : QCOLS + HEAD_SIZE] = keys
        saved[0][:, QCOLS + HEAD_SIZE :] = values


def attend(adapted, row, keep, rs, r2, low, qo, vo, start, cosine, sine):
    each = QCOLS + 2 * HEAD_SIZE
    count = r2.shape[1] // each
    rank = qo.shape[0]
    fixed = lambda a: pl.BlockSpec(a.shape, lambda i: (0,) * a.ndim)
    block = pl.BlockSpec((L, each), lambda i: (0, i))
    mixed_spec = pl.BlockSpec((L, QCOLS), lambda i: (0, i))
    mixed_shape = jax.ShapeDtypeStruct((L, count * QCOLS), BF16)
    return pl.pallas_call(
        functools.partial(attend_body, adapted),
        grid=(count,),
        in_specs=[
            pl.BlockSpec((L, each), lambda i: (row, i)),
            pl.BlockSpec((L, each), lambda i: (row, i)),
            block,
            fixed(low),
            pl.BlockSpec((rank, QCOLS), lambda i: (0, i + start)),
            pl.BlockSpec((rank, HEAD_SIZE), lambda i: (0, i + start)),
            fixed(cosine),
            fixed(sine),
        ],
        out_specs=[mixed_spec, block] if adapted else [mixed_spec],
        out_shape=[mixed_shape, jax.ShapeDtypeStruct((L, count * each), BF16)]
        if adapted
        else [mixed_shape],
        compiler_params=params(32),
        cost_estimate=pl.CostEstimate(
            flops=2 * count * L * QCOLS * (2 * L + 64),
            bytes_accessed=L * count * (each * 10 + QCOLS * 2),
            transcendentals=count * L * L * GROUP,
        ),
    )(keep, rs, r2, low, qo, vo, cosine, sine)


def outer_place(block, rank, kv):
    wide = (kv * (GROUP + 1) + 1) // 2
    return (block // wide) * rank, (block % wide) * HEAD_SIZE, wide


def attend_back_body(kv, splits, keep, rs, r2, low, qo, vo, cos_ref, sin_ref, *refs):
    saved = refs[:splits]
    outer, mid = refs[splits:]
    rank = qo.shape[0]
    each = QCOLS + 2 * HEAD_SIZE
    cos4 = jnp.concatenate([cos_ref[...]] * GROUP, 0)
    sin4 = jnp.concatenate([sin_ref[...]] * GROUP, 0)
    low_q = low[:, :rank]
    low_v = low[:, rank:]
    q_mid = jnp.zeros((L, rank), F32)
    v_mid = jnp.zeros((L, rank), F32)

    def put(block, value):
        row, col, _ = outer_place(block, rank, kv)
        outer[row : row + rank, col : col + HEAD_SIZE] = adapter_scale * value

    if (kv * (GROUP + 1)) % 2:
        put(kv * (GROUP + 1), jnp.zeros((rank, HEAD_SIZE), F32))
    for j in range(kv):
        cols = slice(j * QCOLS, (j + 1) * QCOLS)
        at = (j % (kv // splits)) * each
        kept = saved[j // (kv // splits)]
        grad = keep[:, cols] + rs[:, cols].astype(F32) + r2[:, cols].astype(F32)
        grad4 = stack_heads(grad.astype(BF16))
        q4 = stack_heads(kept[:, at : at + QCOLS])
        keys = kept[:, at + QCOLS : at + QCOLS + HEAD_SIZE]
        values = kept[:, at + QCOLS + HEAD_SIZE : at + each]
        prob = probabilities(q4, keys)
        grad_prob = dot(grad4, values, ((1,), (1,)))
        grad_values = dot(prob.astype(BF16), grad4, ((0,), (0,))).astype(BF16)
        inner = jnp.sum(grad_prob * prob, -1, keepdims=True)
        grad_scores = (prob * (grad_prob - inner) * (HEAD_SIZE**-0.5)).astype(BF16)
        grad_query = dot(grad_scores, keys)
        back4 = (grad_query * cos4 - pltpu.roll(grad_query, HEAD_SIZE // 2, 1) * sin4).astype(BF16)
        for h in range(GROUP):
            at = j * GROUP + h
            back = back4[h * L : (h + 1) * L]
            put(at, dot(low_q, back, ((0,), (0,))))
            q_mid += dot(back, qo[:, at * HEAD_SIZE : (at + 1) * HEAD_SIZE], ((1,), (1,)))
        put(kv * GROUP + j, dot(low_v, grad_values, ((0,), (0,))))
        v_mid += dot(grad_values, vo[:, j * HEAD_SIZE : (j + 1) * HEAD_SIZE], ((1,), (1,)))
    mid[:, :rank] = (adapter_scale * q_mid).astype(BF16)
    mid[:, rank:] = (adapter_scale * v_mid).astype(BF16)


def attend_back(keep, rs, r2, low, qo, vo, cosine, sine, saved):
    rank = qo.shape[0]
    kv = vo.shape[1] // HEAD_SIZE
    wide = outer_place(0, rank, kv)[2]
    return pl.pallas_call(
        functools.partial(attend_back_body, kv, len(saved)),
        in_specs=[whole_vmem()] * (8 + len(saved)),
        out_specs=[whole_vmem()] * 2,
        out_shape=[
            jax.ShapeDtypeStruct((2 * rank, wide * HEAD_SIZE), F32),
            jax.ShapeDtypeStruct((L, 2 * rank), BF16),
        ],
        compiler_params=params(32),
    )(keep, rs, r2, low, qo, vo, cosine, sine, *saved)


def adapter_body(n, rows_each, scal, states, outer, *refs):
    mids = refs[:n]
    away, stay = refs[n:]
    src = pl.ds(pl.multiple_of(scal[0] * rows_each, rows_each), rows_each)
    own = states[:, src]
    total = None
    for mid in mids:
        term = dot(mid[...], own, ((0,), (0,)))
        total = term if total is None else total + term
    half = total.shape[0] // 2
    for low in range(2):
        rows = slice(low * half, (low + 1) * half)

        @pl.when(scal[1] == low)
        def _():
            stay[:, :rows_each] = total[rows]
            stay[:, rows_each:] = outer[rows]

        @pl.when(scal[1] != low)
        def _():
            away[:, :rows_each] = total[rows].astype(BF16)
            away[:, rows_each:] = outer[rows].astype(BF16)


def adapter_products(scal, states, mids, outer, rows_each):
    half = outer.shape[0] // 2
    cols = rows_each + outer.shape[1]
    return pl.pallas_call(
        functools.partial(adapter_body, len(mids), rows_each),
        in_specs=[smem()] + [whole_vmem()] * (2 + len(mids)),
        out_specs=[whole_vmem()] * 2,
        out_shape=[
            jax.ShapeDtypeStruct((half, cols), BF16),
            jax.ShapeDtypeStruct((half, cols), F32),
        ],
        compiler_params=params(32),
    )(scal, states, outer, *mids)


def stats_body(counts, part, split, scal, xt_ref, xt_pol, tgt, gain, *refs):
    refs = list(refs)
    sums = []
    hidden_out, stats = refs[-2:]
    for which, count in enumerate(counts):
        xt = (xt_ref, xt_pol)[which]
        keeps, recvs = refs[:count], refs[count : 2 * count]
        refs = refs[2 * count :]
        squares = jnp.zeros((L, HEAD_SIZE), F32)
        products = jnp.zeros((L, HEAD_SIZE), F32)
        j = 0
        for keep, recv in zip(keeps, recvs):
            for i in range(keep.shape[0]):
                src = pl.ds(pl.multiple_of((j * split + scal[0]) * part, part), part)
                hidden = xt[:, src].astype(F32) + keep[i].astype(F32) + recv[i].astype(F32)
                cols = slice(j * part, (j + 1) * part)
                if which == 1:
                    hidden_out[0, :, cols] = hidden
                product = hidden * (gain[:, cols] * tgt[0, :, cols].astype(F32))
                square = hidden * hidden
                for s in range(part // HEAD_SIZE):
                    lanes = slice(s * HEAD_SIZE, (s + 1) * HEAD_SIZE)
                    squares += square[:, lanes]
                    products += product[:, lanes]
                j += 1
        sums.append(
            [
                jnp.broadcast_to(jnp.sum(v, 1, keepdims=True), v.shape).T[:1]
                for v in (squares, products)
            ]
        )
    at = lax.broadcasted_iota(jnp.int32, (1, 2 * L), 1) % L
    own = (at >= scal[1]) & (pl.program_id(0) == 0)
    live = jnp.where(own, 1.0, 0.0).astype(F32)
    both = [jnp.concatenate([sums[0][i], sums[1][i]], 1) for i in range(2)]
    stats[...] = jnp.concatenate([*both, live, jnp.zeros((5, 2 * L), F32)], 0)


def norm_stats(scal, xt, tgt, gain, keeps, recvs, split):
    n = sum(a.shape[0] for a in keeps[0])
    part = keeps[0][0].shape[2]
    shared = []
    for which in range(2):
        for a in (*keeps[which], *recvs[which]):
            shared.append((a, pl.BlockSpec((a.shape[0], L, part), lambda i: (0, i, 0))))
    return pl.pallas_call(
        functools.partial(stats_body, tuple(len(k) for k in keeps), part, split),
        grid=(4,),
        in_specs=[
            smem(),
            pl.BlockSpec((L, xt.shape[1]), lambda i: ((i // 2) * 4 + i % 2, 0)),
            pl.BlockSpec((L, xt.shape[1]), lambda i: ((i // 2) * 4 + 2 + i % 2, 0)),
            pl.BlockSpec((1, L, n * part), lambda i: (i, 0, 0)),
            pl.BlockSpec((1, n * part), lambda i: (0, 0)),
        ]
        + [spec for _, spec in shared],
        out_specs=[
            pl.BlockSpec((1, L, n * part), lambda i: (i, 0, 0)),
            pl.BlockSpec((8, 2 * L), lambda i: (i, 0)),
        ],
        out_shape=[
            jax.ShapeDtypeStruct((4, L, n * part), F32),
            jax.ShapeDtypeStruct((32, 2 * L), F32),
        ],
        compiler_params=params(32),
    )(scal, xt, xt, tgt, gain, *[a for a, _ in shared])


def score_body(width, masks, ids, own, *refs):
    recvs = refs[: len(masks)]
    total_out, margin_out = refs[len(masks) :]
    lane = lax.broadcasted_iota(jnp.int32, (8, 128), 1)
    margins = jnp.zeros((8, 128), F32)
    for p in range(4):
        total = own[8 * p : 8 * p + 8]
        for recv, m in zip(recvs, masks):
            q = ORD.index(ORD[p] ^ m)
            total = total + recv[8 * q : 8 * q + 8]
        total_out[8 * p : 8 * p + 8] = total
        inverse = lax.rsqrt(total[0:1] * (1.0 / width) + norm_eps)
        score = total[1:2] * inverse * (width**-0.5)
        score = jnp.where(total[2:3] > 0.5, score, 0.0)
        margin = jnp.sum(score[:, L:], 1, keepdims=True) - jnp.sum(score[:, :L], 1, keepdims=True)
        margins = margins + jnp.where(lane == ids[p], margin, 0.0)
    margin_out[...] = margins


def scores(ids, own, recvs, masks, width):
    return pl.pallas_call(
        functools.partial(score_body, width, masks),
        in_specs=[smem()] + [whole_vmem()] * (1 + len(recvs)),
        out_specs=[whole_vmem()] * 2,
        out_shape=[jax.ShapeDtypeStruct(own.shape, F32), jax.ShapeDtypeStruct((8, 128), F32)],
    )(ids, own, *recvs)


def turn(i):
    return (2 * i + 1) % 5


def grad_body(width, seqs, n_vec, ids, pairs, total, hidden, tgt, gain, *refs):
    vecs = refs[:n_vec]
    grad_out, loss_out, slope = refs[n_vec:]
    lane = lax.broadcasted_iota(jnp.int32, (8, 128), 1)

    @pl.when(pl.program_id(0) == 0)
    def _():
        margin = vecs[0][...]
        for v in vecs[1:]:
            margin = margin + v[...]
        logits = jnp.zeros((8, 128), F32)
        for i in range(seqs // 2):
            sign = jnp.where(lane == pairs[2 * i], 1.0, 0.0) - jnp.where(
                lane == pairs[2 * i + 1], 1.0, 0.0
            )
            logit = dpo_beta * jnp.sum(margin * sign, 1, keepdims=True)
            logits = logits + jnp.where(lane == i, logit, 0.0)
        soft = jnp.maximum(-logits, 0.0) + jnp.log1p(jnp.exp(-jnp.abs(logits)))
        used = lane < seqs // 2
        loss = jnp.sum(jnp.where(used, soft, 0.0), 1, keepdims=True)
        loss_out[...] = jnp.broadcast_to(loss, (8, 128))
        slopes = jnp.where(used, -dpo_beta / (1.0 + jnp.exp(logits)), 0.0)
        gradient = jnp.zeros((8, 128), F32)
        for i in range(seqs // 2):
            each = jnp.sum(jnp.where(lane == i, slopes, 0.0), 1, keepdims=True)
            sign = jnp.where(lane == pairs[2 * i], 1.0, 0.0) - jnp.where(
                lane == pairs[2 * i + 1], 1.0, 0.0
            )
            gradient = gradient + each * sign
        slope[...] = gradient * loss_scale

    mine = lane == ids[turn(pl.program_id(0))]
    seq = jnp.sum(jnp.where(mine, slope[...], 0.0), 1, keepdims=True)[:1]
    rows = total[:, L:]
    token = jnp.where(rows[2:3] > 0.5, seq, 0.0) * (width**-0.5)
    inverse = lax.rsqrt(rows[0:1] * (1.0 / width) + norm_eps)
    first = inverse * token
    second = inverse * inverse * inverse * (token * rows[1:2] * (1.0 / width))
    first = jnp.broadcast_to(first, (L, L)).T
    second = jnp.broadcast_to(second, (L, L)).T
    for s in range(hidden.shape[2] // HEAD_SIZE):
        cols = slice(s * HEAD_SIZE, (s + 1) * HEAD_SIZE)
        weighted = gain[:, cols] * tgt[0, :, cols].astype(F32)
        grad_out[0, :, cols] = (first * weighted - second * hidden[0, :, cols]).astype(BF16)


def grad_hidden(ids, pairs, total, hidden, tgt, gain, vecs, width):
    n = hidden.shape[2]
    seqs = pairs.shape[0]
    return pl.pallas_call(
        functools.partial(grad_body, width, seqs, len(vecs)),
        grid=(4,),
        in_specs=[
            smem(),
            smem(),
            pl.BlockSpec((8, 2 * L), lambda i: (turn(i), 0)),
            pl.BlockSpec((1, L, n), lambda i: (turn(i), 0, 0)),
            pl.BlockSpec((1, L, n), lambda i: (turn(i), 0, 0)),
            pl.BlockSpec((1, n), lambda i: (0, 0)),
        ]
        + [pl.BlockSpec((8, 128), lambda i: (0, 0)) for _ in vecs],
        out_specs=[
            pl.BlockSpec((1, L, n), lambda i: (i, 0, 0)),
            pl.BlockSpec((8, 128), lambda i: (0, 0)),
        ],
        out_shape=[
            jax.ShapeDtypeStruct((4, L, n), BF16),
            jax.ShapeDtypeStruct((8, 128), F32),
        ],
        scratch_shapes=[pltpu.VMEM((8, 128), F32)],
        compiler_params=params(32),
    )(ids, pairs, total, hidden, tgt, gain, *vecs)


def per_device(
    fsdp_size,
    tensor_size,
    ref_states,
    pol_states,
    target_rows,
    norm_gain,
    wq,
    wk,
    wv,
    wo,
    qa,
    qo,
    va,
    vo,
    prompt_length,
    pairs,
):
    tokens, width = ref_states.shape
    groups = fsdp_size // 4
    top = fsdp_size // 2
    split = 2 if tensor_size == 2 else 1
    kv_local = wk.shape[1] // HEAD_SIZE
    depth = wq.shape[0]
    part = depth // split
    rank = qa.shape[1]
    me = lax.axis_index("fsdp")
    x = lax.axis_index("tensor")
    side = x if split == 2 else 0

    def tmask(d):
        return (d & 1) | ((d >> 1) * top)

    def move(value, mask):
        return lax.ppermute(value, "fsdp", [(i, i ^ mask) for i in range(fsdp_size)])

    def swap_x(value):
        return lax.ppermute(value, "tensor", [(0, 1), (1, 0)])

    def move_both(value, mask, flip):
        pairs_list = [
            (2 * i + j, 2 * (i ^ mask) + (j ^ flip)) for i in range(fsdp_size) for j in range(2)
        ]
        return lax.ppermute(value, ("fsdp", "tensor"), pairs_list)

    def after(value, *others):
        return lax.optimization_barrier((value, *others))[0]

    parts = groups * split
    idx = []
    for d in range(4):
        for k in range(groups):
            for h in range(split):
                idx.append((me ^ tmask(d) ^ (k << 1)) * split + h)
    for d in range(4):
        for k in range(groups):
            idx.append((me ^ tmask(d) ^ (k << 1)) * split + side)
    idx.append(x)
    idx = jnp.stack(idx).astype(jnp.int32)
    prepared = prep(
        idx,
        ref_states,
        pol_states,
        target_rows,
        norm_gain.astype(F32).reshape(1, width),
        parts,
        part,
        split,
    )
    xs, ts, gain = prepared[:4], prepared[4:8], prepared[8]
    near = move(xs[1], 1)
    far = [move(xs[2], top)]
    far.append(move(after(xs[3], far[0]), top | 1))

    def gather(shard):
        if groups != 4 or split != 2:
            return [shard] + [move(shard, k << 1) for k in range(1, groups)]
        half = shard.shape[0] // 2
        by_y = move(shard, 2)
        by_z = move(shard, 4)
        return [shard, by_y, by_z, move(by_y[:half], 4), move(by_z[half:], 2)]

    halves = 2 if kv_local % 2 == 0 else 1
    per_half = kv_local // halves
    wqkv = []
    queue = (xs[2],)
    for h in range(halves):
        pieces = []
        for j in range(h * per_half, (h + 1) * per_half):
            pieces += [
                wq[:, j * QCOLS : (j + 1) * QCOLS],
                wk[:, j * HEAD_SIZE : (j + 1) * HEAD_SIZE],
                wv[:, j * HEAD_SIZE : (j + 1) * HEAD_SIZE],
            ]
        wqkv.append(gather(after(jnp.concatenate(pieces, 1), *queue)))
        queue = tuple(wqkv[-1][3:])
    heads = wo.shape[0]
    if split == 2:
        wo_keep = lax.dynamic_slice_in_dim(wo, x * part, part, 1)
        wo_send = lax.dynamic_slice_in_dim(wo, (1 - x) * part, part, 1)
        shards = gather(after(jnp.concatenate([wo_keep, wo_send], 0), *queue))
        both = [w.reshape(2, heads, part) for w in shards[:3]]
        wo_keep = [(w, 0) for w in both] + [(shards[3][None], 0)]
        wo_send = [(w, 1) for w in both] + [(shards[4][None], 0)]
    else:
        wo_keep = [(w[None], 0) for w in gather(wo)]

    if split == 2:
        other = [swap_x(a) for a in far]
        far = [
            [jnp.where(x == which, a[0], b[0]) for which in range(2)] for a, b in zip(far, other)
        ]
    states = jnp.concatenate(
        [
            *(xs[0][0], far[0][0], xs[0][1], far[0][1]),
            *(near[0], far[1][0], near[1], far[1][1]),
        ],
        0,
    )

    low = dot(pol_states, jnp.concatenate([qa, va], 1)).astype(BF16)
    cosine, sine = rope_tables(L, HEAD_SIZE)

    saved = []
    mixed = [[], []]
    for h in range(halves):
        send = mm(states, 1, wqkv[h], BF16)
        rs = move(send, 1)
        keep = mm(states, 0, wqkv[h], F32)
        for which in range(2):
            rows = slice((2 * which + 1) * L, (2 * which + 2) * L)
            r2 = move((keep[rows] + rs[rows].astype(F32)).astype(BF16), top)
            result = attend(
                which == 1, 2 * which, keep, rs, r2, low, qo, vo, h * per_half, cosine, sine
            )
            if which == 1:
                saved.append(result[1])
            mz = move(result[0], top)
            pair = jnp.concatenate([result[0], mz], 0)
            last = move(pair, 1)
            mixed[which].append(jnp.concatenate([pair, last], 0))

    keeps, recvs = [], []
    for which in range(2):
        rows = jnp.concatenate(mixed[which], 1)
        steps = 2 if groups % 2 == 0 else 1
        each = groups // steps
        kept, got = [], []
        for s in range(steps):
            if split == 2:
                got.append(swap_x(out_mm(rows, wo_send[s * each : (s + 1) * each])))
        for s in range(steps):
            product = out_mm(rows, wo_keep[s * each : (s + 1) * each])
            if split == 1:
                product = lax.psum(product, "tensor")
                got.append(jnp.zeros_like(product))
            kept.append(product)
        keeps.append(kept)
        recvs.append(got)

    ts = [ts[0]] + list(lax.optimization_barrier((*ts[1:], last))[:3])
    targets = [ts[0]] + [move(ts[d], tmask(d)) for d in (1, 2, 3)]
    tgt = jnp.stack([targets[d] for d in ORD])

    scal = jnp.stack([jnp.asarray(side, jnp.int32), prompt_length[0].astype(jnp.int32)])
    hidden, stats = norm_stats(scal, states, tgt, gain, keeps, recvs, split)
    masks, got = [], []
    for flip in range(split):
        for d in range(4):
            if d or flip:
                masks.append(d)
                if split == 2:
                    got.append(move_both(stats, tmask(d), flip))
                else:
                    got.append(move(stats, tmask(d)))
    ids = jnp.stack([me ^ tmask(d) for d in ORD]).astype(jnp.int32)
    total, margin = scores(ids, stats, got, tuple(masks), width)
    vecs = [margin] + [move(margin, k << 1) for k in range(1, groups)]
    grad, loss = grad_hidden(ids, pairs, total, hidden, tgt, gain, vecs, width)

    grad_rows = grad.reshape(4 * L, -1)
    other = None
    for half in range(2):
        if split == 2:
            leaving = grad_rows[2 * L * half : 2 * L * (half + 1)]
            other = swap_x(leaving if half == 0 else after(leaving, other))
            acc = back_mm(grad_rows, half, wo_keep, None)
            keep, send = back_mm(other, None, wo_send, acc)
        else:
            acc = jnp.zeros((2 * L, heads), F32)
            keep, send = back_mm(grad_rows, half, wo_keep, acc)
        rs = move(send, 1)
        if half == 0:
            r2 = move((keep + rs.astype(F32)).astype(BF16), top)
    outer, mid = attend_back(keep, rs, r2, low, qo, vo, cosine, sine, saved)

    rows_each = width // tensor_size
    if split == 2:
        mids = [mid, swap_x(mid)]
    else:
        gathered = lax.all_gather(mid, "tensor", axis=0, tiled=False)
        mids = [gathered[i] for i in range(tensor_size)]
    scal = jnp.stack([x, me & 1]).astype(jnp.int32)
    away, current = adapter_products(scal, pol_states, mids, outer, rows_each)
    current = current + move(away, 1).astype(F32)
    g = (me // 2) % groups
    rows = current.shape[0] // groups
    pieces = [
        lax.dynamic_slice_in_dim(current, (g ^ k) * rows, rows, 0) for k in range(groups)
    ]
    current = pieces[0]
    for k in range(1, groups):
        current = current + move(pieces[k].astype(BF16), k << 1).astype(F32)
    rows //= 2
    high = me // top
    away = lax.dynamic_slice_in_dim(current, (1 - high) * rows, rows, 0).astype(BF16)
    current = lax.dynamic_slice_in_dim(current, high * rows, rows, 0)
    current = (current + move(away, top).astype(F32)).astype(BF16)

    def join(bit, own, other):
        return jnp.where(
            bit == 0, jnp.concatenate([own, other], 0), jnp.concatenate([other, own], 0)
        )

    current = join(high, current, move(current, top))
    pieces = [current] + [move(current, k << 1) for k in range(1, groups)]
    step = 1
    while step < groups:
        odd = (g & step) != 0
        pieces = [jnp.where(odd, pieces[k ^ step], pieces[k]) for k in range(groups)]
        step *= 2
    current = jnp.concatenate(pieces, 0)
    current = join(me & 1, current, move(current, 1)).astype(F32)
    a_grads = current[:, :rows_each]
    outer = current[:, rows_each:]
    outer = jnp.concatenate([outer[:rank], outer[rank:]], 1)
    return (
        loss[0, 0],
        a_grads[:rank].T,
        outer[:, : qo.shape[1]],
        a_grads[rank:].T,
        outer[:, qo.shape[1] : qo.shape[1] + vo.shape[1]],
    )


def solution(mesh):
    in_specs = (
        P("fsdp", None),
        P("fsdp", None),
        P("fsdp", None),
        P(),
        P("fsdp", "tensor"),
        P("fsdp", "tensor"),
        P("fsdp", "tensor"),
        P("tensor", "fsdp"),
        P(),
        P(None, "tensor"),
        P(),
        P(None, "tensor"),
        P("fsdp"),
        P(),
    )
    out_specs = (P(), P("tensor", None), P(None, "tensor"), P("tensor", None), P(None, "tensor"))
    body = functools.partial(per_device, mesh.shape["fsdp"], mesh.shape["tensor"])
    return jax.shard_map(body, mesh=mesh, in_specs=in_specs, out_specs=out_specs, check_vma=False)
```

```python
import functools

import jax
import jax.numpy as jnp
from jax import lax
from jax.experimental import pallas as pl
from jax.experimental.pallas import tpu as pltpu
from jax.sharding import PartitionSpec as P

QUERY_HEADS = 32
KEY_VALUE_HEADS = 8
HEAD_SIZE = 128
L = 128
GROUP = QUERY_HEADS // KEY_VALUE_HEADS
QCOLS = GROUP * HEAD_SIZE

adapter_scale = 0.5
dpo_beta = 0.1
loss_scale = 256.0
rope_base = 500000.0
norm_eps = 1e-05

F32 = jnp.float32
BF16 = jnp.bfloat16
ORD = (0, 2, 1, 3)
MB = 1 << 20


def rope_tables(length, head_dim):
    half_dim = head_dim // 2
    exponent = jnp.arange(half_dim, dtype=F32) * (2.0 / head_dim)
    inverse = jnp.power(F32(rope_base), -exponent)
    angles = jnp.arange(length, dtype=F32)[:, None] * inverse[None, :]
    cosine = jnp.concatenate([jnp.cos(angles), jnp.cos(angles)], 1)
    sine = jnp.concatenate([-jnp.sin(angles), jnp.sin(angles)], 1)
    return cosine, sine


def dot(a, b, dims=((1,), (0,))):
    return lax.dot_general(a, b, (dims, ((), ())), preferred_element_type=F32)


def params(limit_mb):
    return pltpu.CompilerParams(vmem_limit_bytes=limit_mb * MB)


def smem():
    return pl.BlockSpec(memory_space=pltpu.SMEM)


def whole_vmem():
    return pl.BlockSpec(memory_space=pltpu.VMEM)


def prep_body(parts, part, split, idx, ref, pol, tgt, gain, *outs):
    x0, x1, x2, x3, t0, t1, t2, t3, go = outs
    groups = parts // split
    for d, (xo, to) in enumerate(((x0, t0), (x1, t1), (x2, t2), (x3, t3))):
        for j in range(parts):
            src = pl.ds(pl.multiple_of(idx[d * parts + j] * part, part), part)
            cols = slice(j * part, (j + 1) * part)
            if xo.shape[0] == 2:
                xo[0, :, cols] = ref[:, src]
                xo[1, :, cols] = pol[:, src]
            else:
                @pl.when(idx[4 * parts + 4 * groups] == 0)
                def _():
                    xo[0, :, cols] = ref[:, src]

                @pl.when(idx[4 * parts + 4 * groups] != 0)
                def _():
                    xo[0, :, cols] = pol[:, src]

        for j in range(groups):
            at = idx[4 * parts + d * groups + j] * part
            src = pl.ds(pl.multiple_of(at, part), part)
            to[:, j * part : (j + 1) * part] = tgt[:, src]
            if d == 0:
                go[:, j * part : (j + 1) * part] = gain[:, src]


def prep(idx, ref, pol, tgt, gain, parts, part, split):
    tokens = ref.shape[0]
    xs = lambda n: jax.ShapeDtypeStruct((n, tokens, parts * part), BF16)
    far = 1 if split == 2 else 2
    width = parts // split * part
    return pl.pallas_call(
        functools.partial(prep_body, parts, part, split),
        in_specs=[smem()] + [whole_vmem()] * 4,
        out_specs=[whole_vmem()] * 9,
        out_shape=[xs(2), xs(2), xs(far), xs(far)]
        + [jax.ShapeDtypeStruct((tokens, width), BF16)] * 4
        + [jax.ShapeDtypeStruct((1, width), F32)],
        compiler_params=params(32),
    )(idx, ref, pol, tgt, gain)


def tile_of(cols):
    for tile in (256, 128):
        if cols % tile == 0:
            return tile
    return cols


def mm_body(x_ref, *refs):
    out_ref = refs[-1]
    total = None
    at = 0
    for w in refs[:-1]:
        depth = w.shape[0]
        term = dot(x_ref[:, at : at + depth], w[...])
        total = term if total is None else total + term
        at += depth
    out_ref[...] = total.astype(out_ref.dtype)


def mm(x, half, ws, out_dtype):
    rows, depth = x.shape[0] // 2, x.shape[1]
    cols = ws[0].shape[1]
    tile = tile_of(cols)
    return pl.pallas_call(
        mm_body,
        grid=(cols // tile,),
        in_specs=[pl.BlockSpec((rows, depth), lambda i: (half, 0))]
        + [pl.BlockSpec((w.shape[0], tile), lambda i: (0, i)) for w in ws],
        out_specs=pl.BlockSpec((rows, tile), lambda i: (0, i)),
        out_shape=jax.ShapeDtypeStruct((rows, cols), out_dtype),
        compiler_params=params(32),
        cost_estimate=pl.CostEstimate(
            flops=2 * rows * depth * cols,
            bytes_accessed=2 * (rows * (depth + cols) + depth * cols),
            transcendentals=0,
        ),
    )(x, *ws)


def out_body(n, x_ref, *refs):
    out_ref = refs[-1]
    for k in range(n):
        out_ref[k] = dot(x_ref[...], refs[k][0]).astype(out_ref.dtype)


def out_mm(x, ws, tile=256):
    n = len(ws)
    rows, depth = x.shape
    cols = ws[0][0].shape[2]
    at = lambda which: lambda i: (which, 0, 0)
    return pl.pallas_call(
        functools.partial(out_body, n),
        grid=(rows // tile,),
        in_specs=[pl.BlockSpec((tile, depth), lambda i: (i, 0))]
        + [pl.BlockSpec((1, depth, cols), at(which)) for _, which in ws],
        out_specs=pl.BlockSpec((n, tile, cols), lambda i: (0, i, 0)),
        out_shape=jax.ShapeDtypeStruct((n, rows, cols), BF16),
        compiler_params=params(32),
        cost_estimate=pl.CostEstimate(
            flops=2 * n * rows * depth * cols,
            bytes_accessed=2 * (rows * depth + n * (rows * cols + depth * cols)),
            transcendentals=0,
        ),
    )(x, *[w for w, _ in ws])


def back_body(n, part, has_acc, x_ref, *refs):
    ws = refs[:n]
    refs = refs[n:]
    total = None
    for j in range(n):
        term = dot(x_ref[:, j * part : (j + 1) * part], ws[j][0], ((1,), (1,)))
        total = term if total is None else total + term
    if has_acc:
        total = total + refs[0][...]
        keep, send = refs[1:]
        half = total.shape[0] // 2
        keep[...] = total[:half]
        send[...] = total[half:].astype(send.dtype)
    else:
        refs[0][...] = total


def back_mm(x, half, ws, acc):
    rows = x.shape[0] // (1 if half is None else 2)
    depth = x.shape[1]
    groups = len(ws)
    _, heads, part = ws[0][0].shape
    tile = min(512, heads)
    has_acc = acc is not None
    row = half or 0
    in_specs = [pl.BlockSpec((rows, depth), lambda i: (row, 0))]
    for _, which in ws:
        in_specs.append(
            pl.BlockSpec((1, tile, part), functools.partial(lambda which, i: (which, i, 0), which))
        )
    args = [x] + [w for w, _ in ws]
    if has_acc:
        in_specs.append(pl.BlockSpec((rows, tile), lambda i: (0, i)))
        args.append(acc)
        out_specs = [pl.BlockSpec((rows // 2, tile), lambda i: (0, i))] * 2
        out_shape = [
            jax.ShapeDtypeStruct((rows // 2, heads), F32),
            jax.ShapeDtypeStruct((rows // 2, heads), BF16),
        ]
    else:
        out_specs = pl.BlockSpec((rows, tile), lambda i: (0, i))
        out_shape = jax.ShapeDtypeStruct((rows, heads), F32)
    return pl.pallas_call(
        functools.partial(back_body, groups, part, has_acc),
        grid=(heads // tile,),
        in_specs=in_specs,
        out_specs=out_specs,
        out_shape=out_shape,
        compiler_params=params(32),
        cost_estimate=pl.CostEstimate(
            flops=2 * rows * depth * heads,
            bytes_accessed=2 * (rows * depth + depth * heads) + 4 * rows * heads,
            transcendentals=0,
        ),
    )(*args)


def causal(rows):
    at = lax.broadcasted_iota(jnp.int32, (rows, L), 0) % L
    return at >= lax.broadcasted_iota(jnp.int32, (rows, L), 1)


def probabilities(q4, keys):
    scores = dot(q4, keys, ((1,), (1,))) * (HEAD_SIZE**-0.5)
    weights = jnp.where(causal(q4.shape[0]), jnp.exp(scores), 0.0)
    return weights / jnp.sum(weights, -1, keepdims=True)


def stack_heads(values):
    return jnp.concatenate(
        [values[:, h * HEAD_SIZE : (h + 1) * HEAD_SIZE] for h in range(GROUP)], 0
    )


def attend_body(adapted, keep, rs, r2, low, qo, vo, cos_ref, sin_ref, mixed, *saved):
    cosine = cos_ref[...]
    sine = sin_ref[...]
    pre = keep[...] + rs[...].astype(F32) + r2[...].astype(F32)
    rank = qo.shape[0]
    q_pre = pre[:, :QCOLS]
    k_pre = pre[:, QCOLS : QCOLS + HEAD_SIZE]
    v_pre = pre[:, QCOLS + HEAD_SIZE :]
    if adapted:
        q_pre = q_pre + adapter_scale * dot(low[:, :rank], qo[...])
        v_pre = v_pre + adapter_scale * dot(low[:, rank:], vo[...])
    cos4 = jnp.concatenate([cosine] * GROUP, 0)
    sin4 = jnp.concatenate([sine] * GROUP, 0)
    q4 = stack_heads(q_pre)
    q4 = (q4 * cos4 + pltpu.roll(q4, HEAD_SIZE // 2, 1) * sin4).astype(BF16)
    keys = (k_pre * cosine + pltpu.roll(k_pre, HEAD_SIZE // 2, 1) * sine).astype(BF16)
    values = v_pre.astype(BF16)
    rounded = probabilities(q4, keys).astype(BF16)
    out = dot(rounded, values).astype(BF16)
    for h in range(GROUP):
        cols = slice(h * HEAD_SIZE, (h + 1) * HEAD_SIZE)
        mixed[:, cols] = out[h * L : (h + 1) * L]
        if saved:
            saved[0][:, cols] = q4[h * L : (h + 1) * L]
    if saved:
        saved[0][:, QCOLS : QCOLS + HEAD_SIZE] = keys
        saved[0][:, QCOLS + HEAD_SIZE :] = values


def attend(adapted, row, keep, rs, r2, low, qo, vo, start, cosine, sine):
    each = QCOLS + 2 * HEAD_SIZE
    count = r2.shape[1] // each
    rank = qo.shape[0]
    fixed = lambda a: pl.BlockSpec(a.shape, lambda i: (0,) * a.ndim)
    block = pl.BlockSpec((L, each), lambda i: (0, i))
    mixed_spec = pl.BlockSpec((L, QCOLS), lambda i: (0, i))
    mixed_shape = jax.ShapeDtypeStruct((L, count * QCOLS), BF16)
    return pl.pallas_call(
        functools.partial(attend_body, adapted),
        grid=(count,),
        in_specs=[
            pl.BlockSpec((L, each), lambda i: (row, i)),
            pl.BlockSpec((L, each), lambda i: (row, i)),
            block,
            fixed(low),
            pl.BlockSpec((rank, QCOLS), lambda i: (0, i + start)),
            pl.BlockSpec((rank, HEAD_SIZE), lambda i: (0, i + start)),
            fixed(cosine),
            fixed(sine),
        ],
        out_specs=[mixed_spec, block] if adapted else [mixed_spec],
        out_shape=[mixed_shape, jax.ShapeDtypeStruct((L, count * each), BF16)]
        if adapted
        else [mixed_shape],
        compiler_params=params(32),
        cost_estimate=pl.CostEstimate(
            flops=2 * count * L * QCOLS * (2 * L + 64),
            bytes_accessed=L * count * (each * 10 + QCOLS * 2),
            transcendentals=count * L * L * GROUP,
        ),
    )(keep, rs, r2, low, qo, vo, cosine, sine)


def outer_place(block, rank, kv):
    wide = (kv * (GROUP + 1) + 1) // 2
    return (block // wide) * rank, (block % wide) * HEAD_SIZE, wide


def attend_back_body(kv, splits, keep, rs, r2, low, qo, vo, cos_ref, sin_ref, *refs):
    saved = refs[:splits]
    outer, mid = refs[splits:]
    rank = qo.shape[0]
    each = QCOLS + 2 * HEAD_SIZE
    cos4 = jnp.concatenate([cos_ref[...]] * GROUP, 0)
    sin4 = jnp.concatenate([sin_ref[...]] * GROUP, 0)
    low_q = low[:, :rank]
    low_v = low[:, rank:]
    q_mid = jnp.zeros((L, rank), F32)
    v_mid = jnp.zeros((L, rank), F32)

    def put(block, value):
        row, col, _ = outer_place(block, rank, kv)
        outer[row : row + rank, col : col + HEAD_SIZE] = adapter_scale * value

    if (kv * (GROUP + 1)) % 2:
        put(kv * (GROUP + 1), jnp.zeros((rank, HEAD_SIZE), F32))
    for j in range(kv):
        cols = slice(j * QCOLS, (j + 1) * QCOLS)
        at = (j % (kv // splits)) * each
        kept = saved[j // (kv // splits)]
        grad = keep[:, cols] + rs[:, cols].astype(F32) + r2[:, cols].astype(F32)
        grad4 = stack_heads(grad.astype(BF16))
        q4 = stack_heads(kept[:, at : at + QCOLS])
        keys = kept[:, at + QCOLS : at + QCOLS + HEAD_SIZE]
        values = kept[:, at + QCOLS + HEAD_SIZE : at + each]
        prob = probabilities(q4, keys)
        grad_prob = dot(grad4, values, ((1,), (1,)))
        grad_values = dot(prob.astype(BF16), grad4, ((0,), (0,))).astype(BF16)
        inner = jnp.sum(grad_prob * prob, -1, keepdims=True)
        grad_scores = (prob * (grad_prob - inner) * (HEAD_SIZE**-0.5)).astype(BF16)
        grad_query = dot(grad_scores, keys)
        back4 = (grad_query * cos4 - pltpu.roll(grad_query, HEAD_SIZE // 2, 1) * sin4).astype(BF16)
        for h in range(GROUP):
            at = j * GROUP + h
            back = back4[h * L : (h + 1) * L]
            put(at, dot(low_q, back, ((0,), (0,))))
            q_mid += dot(back, qo[:, at * HEAD_SIZE : (at + 1) * HEAD_SIZE], ((1,), (1,)))
        put(kv * GROUP + j, dot(low_v, grad_values, ((0,), (0,))))
        v_mid += dot(grad_values, vo[:, j * HEAD_SIZE : (j + 1) * HEAD_SIZE], ((1,), (1,)))
    mid[:, :rank] = (adapter_scale * q_mid).astype(BF16)
    mid[:, rank:] = (adapter_scale * v_mid).astype(BF16)


def attend_back(keep, rs, r2, low, qo, vo, cosine, sine, saved):
    rank = qo.shape[0]
    kv = vo.shape[1] // HEAD_SIZE
    wide = outer_place(0, rank, kv)[2]
    return pl.pallas_call(
        functools.partial(attend_back_body, kv, len(saved)),
        in_specs=[whole_vmem()] * (8 + len(saved)),
        out_specs=[whole_vmem()] * 2,
        out_shape=[
            jax.ShapeDtypeStruct((2 * rank, wide * HEAD_SIZE), F32),
            jax.ShapeDtypeStruct((L, 2 * rank), BF16),
        ],
        compiler_params=params(32),
    )(keep, rs, r2, low, qo, vo, cosine, sine, *saved)


def adapter_body(n, rows_each, scal, states, outer, *refs):
    mids = refs[:n]
    away, stay = refs[n:]
    src = pl.ds(pl.multiple_of(scal[0] * rows_each, rows_each), rows_each)
    own = states[:, src]
    total = None
    for mid in mids:
        term = dot(mid[...], own, ((0,), (0,)))
        total = term if total is None else total + term
    half = total.shape[0] // 2
    for low in range(2):
        rows = slice(low * half, (low + 1) * half)

        @pl.when(scal[1] == low)
        def _():
            stay[:, :rows_each] = total[rows]
            stay[:, rows_each:] = outer[rows]

        @pl.when(scal[1] != low)
        def _():
            away[:, :rows_each] = total[rows].astype(BF16)
            away[:, rows_each:] = outer[rows].astype(BF16)


def adapter_products(scal, states, mids, outer, rows_each):
    half = outer.shape[0] // 2
    cols = rows_each + outer.shape[1]
    return pl.pallas_call(
        functools.partial(adapter_body, len(mids), rows_each),
        in_specs=[smem()] + [whole_vmem()] * (2 + len(mids)),
        out_specs=[whole_vmem()] * 2,
        out_shape=[
            jax.ShapeDtypeStruct((half, cols), BF16),
            jax.ShapeDtypeStruct((half, cols), F32),
        ],
        compiler_params=params(32),
    )(scal, states, outer, *mids)


def stats_body(counts, part, split, scal, xt_ref, xt_pol, tgt, gain, *refs):
    refs = list(refs)
    sums = []
    hidden_out, stats = refs[-2:]
    for which, count in enumerate(counts):
        xt = (xt_ref, xt_pol)[which]
        keeps, recvs = refs[:count], refs[count : 2 * count]
        refs = refs[2 * count :]
        squares = jnp.zeros((L, HEAD_SIZE), F32)
        products = jnp.zeros((L, HEAD_SIZE), F32)
        j = 0
        for keep, recv in zip(keeps, recvs):
            for i in range(keep.shape[0]):
                src = pl.ds(pl.multiple_of((j * split + scal[0]) * part, part), part)
                hidden = xt[:, src].astype(F32) + keep[i].astype(F32) + recv[i].astype(F32)
                cols = slice(j * part, (j + 1) * part)
                if which == 1:
                    hidden_out[0, :, cols] = hidden
                product = hidden * (gain[:, cols] * tgt[0, :, cols].astype(F32))
                square = hidden * hidden
                for s in range(part // HEAD_SIZE):
                    lanes = slice(s * HEAD_SIZE, (s + 1) * HEAD_SIZE)
                    squares += square[:, lanes]
                    products += product[:, lanes]
                j += 1
        sums.append(
            [
                jnp.broadcast_to(jnp.sum(v, 1, keepdims=True), v.shape).T[:1]
                for v in (squares, products)
            ]
        )
    at = lax.broadcasted_iota(jnp.int32, (1, 2 * L), 1) % L
    own = (at >= scal[1]) & (pl.program_id(0) == 0)
    live = jnp.where(own, 1.0, 0.0).astype(F32)
    both = [jnp.concatenate([sums[0][i], sums[1][i]], 1) for i in range(2)]
    stats[...] = jnp.concatenate([*both, live, jnp.zeros((5, 2 * L), F32)], 0)


def norm_stats(scal, xt, tgt, gain, keeps, recvs, split):
    n = sum(a.shape[0] for a in keeps[0])
    part = keeps[0][0].shape[2]
    shared = []
    for which in range(2):
        for a in (*keeps[which], *recvs[which]):
            shared.append((a, pl.BlockSpec((a.shape[0], L, part), lambda i: (0, i, 0))))
    return pl.pallas_call(
        functools.partial(stats_body, tuple(len(k) for k in keeps), part, split),
        grid=(4,),
        in_specs=[
            smem(),
            pl.BlockSpec((L, xt.shape[1]), lambda i: ((i // 2) * 4 + i % 2, 0)),
            pl.BlockSpec((L, xt.shape[1]), lambda i: ((i // 2) * 4 + 2 + i % 2, 0)),
            pl.BlockSpec((1, L, n * part), lambda i: (i, 0, 0)),
            pl.BlockSpec((1, n * part), lambda i: (0, 0)),
        ]
        + [spec for _, spec in shared],
        out_specs=[
            pl.BlockSpec((1, L, n * part), lambda i: (i, 0, 0)),
            pl.BlockSpec((8, 2 * L), lambda i: (i, 0)),
        ],
        out_shape=[
            jax.ShapeDtypeStruct((4, L, n * part), F32),
            jax.ShapeDtypeStruct((32, 2 * L), F32),
        ],
        compiler_params=params(32),
    )(scal, xt, xt, tgt, gain, *[a for a, _ in shared])


def score_body(width, masks, ids, own, *refs):
    recvs = refs[: len(masks)]
    total_out, margin_out = refs[len(masks) :]
    lane = lax.broadcasted_iota(jnp.int32, (8, 128), 1)
    margins = jnp.zeros((8, 128), F32)
    for p in range(4):
        total = own[8 * p : 8 * p + 8]
        for recv, m in zip(recvs, masks):
            q = ORD.index(ORD[p] ^ m)
            total = total + recv[8 * q : 8 * q + 8]
        total_out[8 * p : 8 * p + 8] = total
        inverse = lax.rsqrt(total[0:1] * (1.0 / width) + norm_eps)
        score = total[1:2] * inverse * (width**-0.5)
        score = jnp.where(total[2:3] > 0.5, score, 0.0)
        margin = jnp.sum(score[:, L:], 1, keepdims=True) - jnp.sum(score[:, :L], 1, keepdims=True)
        margins = margins + jnp.where(lane == ids[p], margin, 0.0)
    margin_out[...] = margins


def scores(ids, own, recvs, masks, width):
    return pl.pallas_call(
        functools.partial(score_body, width, masks),
        in_specs=[smem()] + [whole_vmem()] * (1 + len(recvs)),
        out_specs=[whole_vmem()] * 2,
        out_shape=[jax.ShapeDtypeStruct(own.shape, F32), jax.ShapeDtypeStruct((8, 128), F32)],
    )(ids, own, *recvs)


def turn(i):
    return (2 * i + 1) % 5


def grad_body(width, seqs, n_vec, ids, pairs, total, hidden, tgt, gain, *refs):
    vecs = refs[:n_vec]
    grad_out, loss_out, slope = refs[n_vec:]
    lane = lax.broadcasted_iota(jnp.int32, (8, 128), 1)

    @pl.when(pl.program_id(0) == 0)
    def _():
        margin = vecs[0][...]
        for v in vecs[1:]:
            margin = margin + v[...]
        logits = jnp.zeros((8, 128), F32)
        for i in range(seqs // 2):
            sign = jnp.where(lane == pairs[2 * i], 1.0, 0.0) - jnp.where(
                lane == pairs[2 * i + 1], 1.0, 0.0
            )
            logit = dpo_beta * jnp.sum(margin * sign, 1, keepdims=True)
            logits = logits + jnp.where(lane == i, logit, 0.0)
        soft = jnp.maximum(-logits, 0.0) + jnp.log1p(jnp.exp(-jnp.abs(logits)))
        used = lane < seqs // 2
        loss = jnp.sum(jnp.where(used, soft, 0.0), 1, keepdims=True)
        loss_out[...] = jnp.broadcast_to(loss, (8, 128))
        slopes = jnp.where(used, -dpo_beta / (1.0 + jnp.exp(logits)), 0.0)
        gradient = jnp.zeros((8, 128), F32)
        for i in range(seqs // 2):
            each = jnp.sum(jnp.where(lane == i, slopes, 0.0), 1, keepdims=True)
            sign = jnp.where(lane == pairs[2 * i], 1.0, 0.0) - jnp.where(
                lane == pairs[2 * i + 1], 1.0, 0.0
            )
            gradient = gradient + each * sign
        slope[...] = gradient * loss_scale

    mine = lane == ids[turn(pl.program_id(0))]
    seq = jnp.sum(jnp.where(mine, slope[...], 0.0), 1, keepdims=True)[:1]
    rows = total[:, L:]
    token = jnp.where(rows[2:3] > 0.5, seq, 0.0) * (width**-0.5)
    inverse = lax.rsqrt(rows[0:1] * (1.0 / width) + norm_eps)
    first = inverse * token
    second = inverse * inverse * inverse * (token * rows[1:2] * (1.0 / width))
    first = jnp.broadcast_to(first, (L, L)).T
    second = jnp.broadcast_to(second, (L, L)).T
    for s in range(hidden.shape[2] // HEAD_SIZE):
        cols = slice(s * HEAD_SIZE, (s + 1) * HEAD_SIZE)
        weighted = gain[:, cols] * tgt[0, :, cols].astype(F32)
        grad_out[0, :, cols] = (first * weighted - second * hidden[0, :, cols]).astype(BF16)


def grad_hidden(ids, pairs, total, hidden, tgt, gain, vecs, width):
    n = hidden.shape[2]
    seqs = pairs.shape[0]
    return pl.pallas_call(
        functools.partial(grad_body, width, seqs, len(vecs)),
        grid=(4,),
        in_specs=[
            smem(),
            smem(),
            pl.BlockSpec((8, 2 * L), lambda i: (turn(i), 0)),
            pl.BlockSpec((1, L, n), lambda i: (turn(i), 0, 0)),
            pl.BlockSpec((1, L, n), lambda i: (turn(i), 0, 0)),
            pl.BlockSpec((1, n), lambda i: (0, 0)),
        ]
        + [pl.BlockSpec((8, 128), lambda i: (0, 0)) for _ in vecs],
        out_specs=[
            pl.BlockSpec((1, L, n), lambda i: (i, 0, 0)),
            pl.BlockSpec((8, 128), lambda i: (0, 0)),
        ],
        out_shape=[
            jax.ShapeDtypeStruct((4, L, n), BF16),
            jax.ShapeDtypeStruct((8, 128), F32),
        ],
        scratch_shapes=[pltpu.VMEM((8, 128), F32)],
        compiler_params=params(32),
    )(ids, pairs, total, hidden, tgt, gain, *vecs)


def per_device(
    fsdp_size,
    tensor_size,
    ref_states,
    pol_states,
    target_rows,
    norm_gain,
    wq,
    wk,
    wv,
    wo,
    qa,
    qo,
    va,
    vo,
    prompt_length,
    pairs,
):
    tokens, width = ref_states.shape
    groups = fsdp_size // 4
    near_z = fsdp_size // 4
    bits = []
    bit = 2
    while bit < fsdp_size:
        if bit != near_z:
            bits.append(bit)
        bit *= 2
    split = 2 if tensor_size == 2 else 1
    kv_local = wk.shape[1] // HEAD_SIZE
    depth = wq.shape[0]
    part = depth // split
    rank = qa.shape[1]
    me = lax.axis_index("fsdp")
    x = lax.axis_index("tensor")
    side = x if split == 2 else 0

    def tmask(d):
        return (d & 1) | ((d >> 1) * near_z)

    def gmask(k):
        return sum(bit for i, bit in enumerate(bits) if (k >> i) & 1)

    def move(value, mask):
        return lax.ppermute(value, "fsdp", [(i, i ^ mask) for i in range(fsdp_size)])

    def swap_x(value):
        return lax.ppermute(value, "tensor", [(0, 1), (1, 0)])

    def move_both(value, mask, flip):
        pairs_list = [
            (2 * i + j, 2 * (i ^ mask) + (j ^ flip)) for i in range(fsdp_size) for j in range(2)
        ]
        return lax.ppermute(value, ("fsdp", "tensor"), pairs_list)

    def after(value, *others):
        return lax.optimization_barrier((value, *others))[0]

    halves = 2 if kv_local % 2 == 0 else 1
    per_half = kv_local // halves
    wide = groups == 4 and split == 2

    def shard_of(h, *queue):
        q, k, v = wq, wk, wv
        if queue:
            q, k, v = lax.optimization_barrier((wq, wk, wv, *queue))[:3]
        pieces = []
        for j in range(h * per_half, (h + 1) * per_half):
            pieces += [
                q[:, j * QCOLS : (j + 1) * QCOLS],
                k[:, j * HEAD_SIZE : (j + 1) * HEAD_SIZE],
                v[:, j * HEAD_SIZE : (j + 1) * HEAD_SIZE],
            ]
        return jnp.concatenate(pieces, 1)

    def gather(shard):
        return [shard] + [move(shard, gmask(k)) for k in range(1, groups)]

    heads = wo.shape[0]
    if wide:
        over_y, over_z = gmask(1), gmask(2)
        shard = shard_of(0)
        z0 = move(shard, over_z)
        y0 = move(shard, over_y)
        wqkv = [[shard, y0, z0, move(z0, over_y)]]

    parts = groups * split
    idx = []
    for d in range(4):
        for k in range(groups):
            for h in range(split):
                idx.append((me ^ tmask(d) ^ gmask(k)) * split + h)
    for d in range(4):
        for k in range(groups):
            idx.append((me ^ tmask(d) ^ gmask(k)) * split + side)
    idx.append(x)
    idx = jnp.stack(idx).astype(jnp.int32)
    prepared = prep(
        idx,
        ref_states,
        pol_states,
        target_rows,
        norm_gain.astype(F32).reshape(1, width),
        parts,
        part,
        split,
    )
    xs, ts, gain = prepared[:4], prepared[4:8], prepared[8]
    near = move(xs[1], 1)
    far = [move(xs[2], near_z)]
    far.append(move(after(xs[3], far[0]), near_z | 1))

    if split == 2:
        other = [swap_x(a) for a in far]
        far = [
            [jnp.where(x == which, a[0], b[0]) for which in range(2)] for a, b in zip(far, other)
        ]
    states = jnp.concatenate(
        [
            *(xs[0][0], far[0][0], xs[0][1], far[0][1]),
            *(near[0], far[1][0], near[1], far[1][1]),
        ],
        0,
    )

    low = dot(pol_states, jnp.concatenate([qa, va], 1)).astype(BF16)
    cosine, sine = rope_tables(L, HEAD_SIZE)

    saved = []
    mixed = [[], []]
    for h in range(halves):
        if wide:
            if h == 1:
                shard = shard_of(1, y0)
                y1 = move(shard, over_y)
                z1 = move(after(shard, z0), over_z)
                wqkv.append([shard, y1, z1, move(after(z1, send, keep), over_y)])
                wo_b = after(wo, keep, y1)
                wo_keep = lax.dynamic_slice_in_dim(wo_b, x * part, part, 1)
                wo_send = lax.dynamic_slice_in_dim(wo_b, (1 - x) * part, part, 1)
                ys = move(wo_send, over_y)
                zs = move(after(wo_send, z1), over_z)
        elif h == 0:
            wqkv = [gather(shard_of(i)) for i in range(halves)]
            wo_keep = [(w[None], 0) for w in gather(wo)]
        send = mm(states, 1, wqkv[h], BF16)
        rs = move(send, 1)
        keep = mm(states, 0, wqkv[h], F32)
        for which in range(2):
            rows = slice((2 * which + 1) * L, (2 * which + 2) * L)
            r2 = move((keep[rows] + rs[rows].astype(F32)).astype(BF16), near_z)
            result = attend(
                which == 1, 2 * which, keep, rs, r2, low, qo, vo, h * per_half, cosine, sine
            )
            if which == 1:
                saved.append(result[1])
            mz = move(result[0], near_z)
            pair = jnp.concatenate([result[0], mz], 0)
            last = move(pair, 1)
            mixed[which].append(jnp.concatenate([pair, last], 0))
    if wide:
        sends = [wo_send, ys, zs, move(after(zs, keep), over_y)]
        yk = move(after(wo_keep, sends[3]), over_y)
        zk = move(after(wo_keep, zs, keep), over_z)
        wo_keep = [(w[None], 0) for w in (wo_keep, yk, zk, move(after(zk, yk), over_y))]
        wo_send = [(w[None], 0) for w in sends]

    keeps, recvs = [], []
    for which in range(2):
        rows = jnp.concatenate(mixed[which], 1)
        steps = 2 if groups % 2 == 0 else 1
        each = groups // steps
        kept, got = [], []
        for s in range(steps):
            if split == 2:
                got.append(swap_x(out_mm(rows, wo_send[s * each : (s + 1) * each])))
        for s in range(steps):
            product = out_mm(rows, wo_keep[s * each : (s + 1) * each])
            if split == 1:
                product = lax.psum(product, "tensor")
                got.append(jnp.zeros_like(product))
            kept.append(product)
        keeps.append(kept)
        recvs.append(got)

    ts = [ts[0]] + list(lax.optimization_barrier((*ts[1:], last))[:3])
    targets = [ts[0]] + [move(ts[d], tmask(d)) for d in (1, 2, 3)]
    tgt = jnp.stack([targets[d] for d in ORD])

    scal = jnp.stack([jnp.asarray(side, jnp.int32), prompt_length[0].astype(jnp.int32)])
    hidden, stats = norm_stats(scal, states, tgt, gain, keeps, recvs, split)
    masks, got = [], []
    for flip in range(split):
        for d in range(4):
            if d or flip:
                masks.append(d)
                if split == 2:
                    got.append(move_both(stats, tmask(d), flip))
                else:
                    got.append(move(stats, tmask(d)))
    ids = jnp.stack([me ^ tmask(d) for d in ORD]).astype(jnp.int32)
    total, margin = scores(ids, stats, got, tuple(masks), width)
    vecs = [margin] + [move(margin, gmask(k)) for k in range(1, groups)]
    grad, loss = grad_hidden(ids, pairs, total, hidden, tgt, gain, vecs, width)

    grad_rows = grad.reshape(4 * L, -1)
    other = None
    for half in range(2):
        if split == 2:
            leaving = grad_rows[2 * L * half : 2 * L * (half + 1)]
            other = swap_x(leaving if half == 0 else after(leaving, other))
            acc = back_mm(grad_rows, half, wo_keep, None)
            keep, send = back_mm(other, None, wo_send, acc)
        else:
            acc = jnp.zeros((2 * L, heads), F32)
            keep, send = back_mm(grad_rows, half, wo_keep, acc)
        rs = move(send, 1)
        if half == 0:
            r2 = move((keep + rs.astype(F32)).astype(BF16), near_z)
    outer, mid = attend_back(keep, rs, r2, low, qo, vo, cosine, sine, saved)

    rows_each = width // tensor_size
    if split == 2:
        mids = [mid, swap_x(mid)]
    else:
        gathered = lax.all_gather(mid, "tensor", axis=0, tiled=False)
        mids = [gathered[i] for i in range(tensor_size)]
    scal = jnp.stack([x, me & 1]).astype(jnp.int32)
    away, current = adapter_products(scal, pol_states, mids, outer, rows_each)
    current = current + move(away, 1).astype(F32)
    top = fsdp_size // 2
    g = (me // 2) % groups
    rows = current.shape[0] // groups
    pieces = [
        lax.dynamic_slice_in_dim(current, (g ^ k) * rows, rows, 0) for k in range(groups)
    ]
    current = pieces[0]
    for k in range(1, groups):
        current = current + move(pieces[k].astype(BF16), k << 1).astype(F32)
    rows //= 2
    high = me // top
    away = lax.dynamic_slice_in_dim(current, (1 - high) * rows, rows, 0).astype(BF16)
    current = lax.dynamic_slice_in_dim(current, high * rows, rows, 0)
    current = (current + move(away, top).astype(F32)).astype(BF16)

    def join(bit, own, other):
        return jnp.where(
            bit == 0, jnp.concatenate([own, other], 0), jnp.concatenate([other, own], 0)
        )

    current = join(high, current, move(current, top))
    pieces = [current] + [move(current, k << 1) for k in range(1, groups)]
    step = 1
    while step < groups:
        odd = (g & step) != 0
        pieces = [jnp.where(odd, pieces[k ^ step], pieces[k]) for k in range(groups)]
        step *= 2
    current = jnp.concatenate(pieces, 0)
    current = join(me & 1, current, move(current, 1)).astype(F32)
    a_grads = current[:, :rows_each]
    outer = current[:, rows_each:]
    outer = jnp.concatenate([outer[:rank], outer[rank:]], 1)
    return (
        loss[0, 0],
        a_grads[:rank].T,
        outer[:, : qo.shape[1]],
        a_grads[rank:].T,
        outer[:, qo.shape[1] : qo.shape[1] + vo.shape[1]],
    )


def solution(mesh):
    in_specs = (
        P("fsdp", None),
        P("fsdp", None),
        P("fsdp", None),
        P(),
        P("fsdp", "tensor"),
        P("fsdp", "tensor"),
        P("fsdp", "tensor"),
        P("tensor", "fsdp"),
        P(),
        P(None, "tensor"),
        P(),
        P(None, "tensor"),
        P("fsdp"),
        P(),
    )
    out_specs = (P(), P("tensor", None), P(None, "tensor"), P("tensor", None), P(None, "tensor"))
    body = functools.partial(per_device, mesh.shape["fsdp"], mesh.shape["tensor"])
    return jax.shard_map(body, mesh=mesh, in_specs=in_specs, out_specs=out_specs, check_vma=False)
```

```python
import functools

import jax
import jax.numpy as jnp
from jax import lax
from jax.experimental import pallas as pl
from jax.experimental.pallas import tpu as pltpu
from jax.sharding import PartitionSpec as P

QUERY_HEADS = 32
KEY_VALUE_HEADS = 8
HEAD_SIZE = 128
L = 128
GROUP = QUERY_HEADS // KEY_VALUE_HEADS
QCOLS = GROUP * HEAD_SIZE

adapter_scale = 0.5
dpo_beta = 0.1
loss_scale = 256.0
rope_base = 500000.0
norm_eps = 1e-05

F32 = jnp.float32
BF16 = jnp.bfloat16
ORD = (0, 2, 1, 3)
MB = 1 << 20


def rope_tables(length, head_dim):
    half_dim = head_dim // 2
    exponent = jnp.arange(half_dim, dtype=F32) * (2.0 / head_dim)
    inverse = jnp.power(F32(rope_base), -exponent)
    angles = jnp.arange(length, dtype=F32)[:, None] * inverse[None, :]
    cosine = jnp.concatenate([jnp.cos(angles), jnp.cos(angles)], 1)
    sine = jnp.concatenate([-jnp.sin(angles), jnp.sin(angles)], 1)
    return cosine, sine


def dot(a, b, dims=((1,), (0,))):
    return lax.dot_general(a, b, (dims, ((), ())), preferred_element_type=F32)


def params(limit_mb):
    return pltpu.CompilerParams(vmem_limit_bytes=limit_mb * MB)


def smem():
    return pl.BlockSpec(memory_space=pltpu.SMEM)


def whole_vmem():
    return pl.BlockSpec(memory_space=pltpu.VMEM)


def prep_body(parts, part, split, idx, ref, pol, tgt, gain, *outs):
    x0, x1, x2, x3, t0, t1, t2, t3, go = outs
    groups = parts // split
    for d, (xo, to) in enumerate(((x0, t0), (x1, t1), (x2, t2), (x3, t3))):
        for j in range(parts):
            src = pl.ds(pl.multiple_of(idx[d * parts + j] * part, part), part)
            cols = slice(j * part, (j + 1) * part)
            if xo.shape[0] == 2:
                xo[0, :, cols] = ref[:, src]
                xo[1, :, cols] = pol[:, src]
            else:
                @pl.when(idx[4 * parts + 4 * groups] == 0)
                def _():
                    xo[0, :, cols] = ref[:, src]

                @pl.when(idx[4 * parts + 4 * groups] != 0)
                def _():
                    xo[0, :, cols] = pol[:, src]

        for j in range(groups):
            at = idx[4 * parts + d * groups + j] * part
            src = pl.ds(pl.multiple_of(at, part), part)
            to[:, j * part : (j + 1) * part] = tgt[:, src]
            if d == 0:
                go[:, j * part : (j + 1) * part] = gain[:, src]


def prep(idx, ref, pol, tgt, gain, parts, part, split):
    tokens = ref.shape[0]
    xs = lambda n: jax.ShapeDtypeStruct((n, tokens, parts * part), BF16)
    far = 1 if split == 2 else 2
    width = parts // split * part
    return pl.pallas_call(
        functools.partial(prep_body, parts, part, split),
        in_specs=[smem()] + [whole_vmem()] * 4,
        out_specs=[whole_vmem()] * 9,
        out_shape=[xs(2), xs(2), xs(far), xs(far)]
        + [jax.ShapeDtypeStruct((tokens, width), BF16)] * 4
        + [jax.ShapeDtypeStruct((1, width), F32)],
        compiler_params=params(32),
    )(idx, ref, pol, tgt, gain)


def tile_of(cols):
    for tile in (256, 128):
        if cols % tile == 0:
            return tile
    return cols


def mm_body(x_ref, *refs):
    out_ref = refs[-1]
    total = None
    at = 0
    for w in refs[:-1]:
        depth = w.shape[0]
        term = dot(x_ref[:, at : at + depth], w[...])
        total = term if total is None else total + term
        at += depth
    out_ref[...] = total.astype(out_ref.dtype)


def mm(x, half, ws, out_dtype):
    rows, depth = x.shape[0] // 2, x.shape[1]
    cols = ws[0].shape[1]
    tile = tile_of(cols)
    return pl.pallas_call(
        mm_body,
        grid=(cols // tile,),
        in_specs=[pl.BlockSpec((rows, depth), lambda i: (half, 0))]
        + [pl.BlockSpec((w.shape[0], tile), lambda i: (0, i)) for w in ws],
        out_specs=pl.BlockSpec((rows, tile), lambda i: (0, i)),
        out_shape=jax.ShapeDtypeStruct((rows, cols), out_dtype),
        compiler_params=params(32),
        cost_estimate=pl.CostEstimate(
            flops=2 * rows * depth * cols,
            bytes_accessed=2 * (rows * (depth + cols) + depth * cols),
            transcendentals=0,
        ),
    )(x, *ws)


def out_body(n, x_ref, *refs):
    out_ref = refs[-1]
    for k in range(n):
        out_ref[k] = dot(x_ref[...], refs[k][0]).astype(out_ref.dtype)


def out_mm(x, ws, tile=256):
    n = len(ws)
    rows, depth = x.shape
    cols = ws[0][0].shape[2]
    at = lambda which: lambda i: (which, 0, 0)
    return pl.pallas_call(
        functools.partial(out_body, n),
        grid=(rows // tile,),
        in_specs=[pl.BlockSpec((tile, depth), lambda i: (i, 0))]
        + [pl.BlockSpec((1, depth, cols), at(which)) for _, which in ws],
        out_specs=pl.BlockSpec((n, tile, cols), lambda i: (0, i, 0)),
        out_shape=jax.ShapeDtypeStruct((n, rows, cols), BF16),
        compiler_params=params(32),
        cost_estimate=pl.CostEstimate(
            flops=2 * n * rows * depth * cols,
            bytes_accessed=2 * (rows * depth + n * (rows * cols + depth * cols)),
            transcendentals=0,
        ),
    )(x, *[w for w, _ in ws])


def back_body(n, part, has_acc, x_ref, *refs):
    ws = refs[:n]
    refs = refs[n:]
    total = None
    for j in range(n):
        term = dot(x_ref[:, j * part : (j + 1) * part], ws[j][0], ((1,), (1,)))
        total = term if total is None else total + term
    if has_acc:
        total = total + refs[0][...]
        keep, send = refs[1:]
        half = total.shape[0] // 2
        keep[...] = total[:half]
        send[...] = total[half:].astype(send.dtype)
    else:
        refs[0][...] = total


def back_mm(x, half, ws, acc):
    rows = x.shape[0] // (1 if half is None else 2)
    depth = x.shape[1]
    groups = len(ws)
    _, heads, part = ws[0][0].shape
    tile = min(512, heads)
    has_acc = acc is not None
    row = half or 0
    in_specs = [pl.BlockSpec((rows, depth), lambda i: (row, 0))]
    for _, which in ws:
        in_specs.append(
            pl.BlockSpec((1, tile, part), functools.partial(lambda which, i: (which, i, 0), which))
        )
    args = [x] + [w for w, _ in ws]
    if has_acc:
        in_specs.append(pl.BlockSpec((rows, tile), lambda i: (0, i)))
        args.append(acc)
        out_specs = [pl.BlockSpec((rows // 2, tile), lambda i: (0, i))] * 2
        out_shape = [
            jax.ShapeDtypeStruct((rows // 2, heads), F32),
            jax.ShapeDtypeStruct((rows // 2, heads), BF16),
        ]
    else:
        out_specs = pl.BlockSpec((rows, tile), lambda i: (0, i))
        out_shape = jax.ShapeDtypeStruct((rows, heads), F32)
    return pl.pallas_call(
        functools.partial(back_body, groups, part, has_acc),
        grid=(heads // tile,),
        in_specs=in_specs,
        out_specs=out_specs,
        out_shape=out_shape,
        compiler_params=params(32),
        cost_estimate=pl.CostEstimate(
            flops=2 * rows * depth * heads,
            bytes_accessed=2 * (rows * depth + depth * heads) + 4 * rows * heads,
            transcendentals=0,
        ),
    )(*args)


def causal(rows):
    at = lax.broadcasted_iota(jnp.int32, (rows, L), 0) % L
    return at >= lax.broadcasted_iota(jnp.int32, (rows, L), 1)


def probabilities(q4, keys):
    scores = dot(q4, keys, ((1,), (1,))) * (HEAD_SIZE**-0.5)
    weights = jnp.where(causal(q4.shape[0]), jnp.exp(scores), 0.0)
    return weights / jnp.sum(weights, -1, keepdims=True)


def stack_heads(values):
    return jnp.concatenate(
        [values[:, h * HEAD_SIZE : (h + 1) * HEAD_SIZE] for h in range(GROUP)], 0
    )


def attend_body(keep, rs, r2, low, qo, vo, cos_ref, sin_ref, mixed, saved):
    scale = jnp.where(pl.program_id(0) == 1, adapter_scale, 0.0).astype(F32)
    cosine = cos_ref[...]
    sine = sin_ref[...]
    pre = keep[...] + rs[...].astype(F32) + r2[...].astype(F32)
    rank = qo.shape[0]
    q_pre = pre[:, :QCOLS] + scale * dot(low[:, :rank], qo[...])
    k_pre = pre[:, QCOLS : QCOLS + HEAD_SIZE]
    v_pre = pre[:, QCOLS + HEAD_SIZE :] + scale * dot(low[:, rank:], vo[...])
    cos4 = jnp.concatenate([cosine] * GROUP, 0)
    sin4 = jnp.concatenate([sine] * GROUP, 0)
    q4 = stack_heads(q_pre)
    q4 = (q4 * cos4 + pltpu.roll(q4, HEAD_SIZE // 2, 1) * sin4).astype(BF16)
    keys = (k_pre * cosine + pltpu.roll(k_pre, HEAD_SIZE // 2, 1) * sine).astype(BF16)
    values = v_pre.astype(BF16)
    rounded = probabilities(q4, keys).astype(BF16)
    out = dot(rounded, values).astype(BF16)
    for h in range(GROUP):
        cols = slice(h * HEAD_SIZE, (h + 1) * HEAD_SIZE)
        mixed[:, cols] = out[h * L : (h + 1) * L]
        saved[:, cols] = q4[h * L : (h + 1) * L]
    saved[:, QCOLS : QCOLS + HEAD_SIZE] = keys
    saved[:, QCOLS + HEAD_SIZE :] = values


def attend(keep, rs, r2, low, qo, vo, group, cosine, sine):
    each = QCOLS + 2 * HEAD_SIZE
    rank = qo.shape[0]
    fixed = lambda a: pl.BlockSpec(a.shape, lambda i: (0,) * a.ndim)
    return pl.pallas_call(
        attend_body,
        grid=(2,),
        in_specs=[
            pl.BlockSpec((L, each), lambda i: (2 * i, 0)),
            pl.BlockSpec((L, each), lambda i: (2 * i, 0)),
            pl.BlockSpec((L, each), lambda i: (i, 0)),
            fixed(low),
            pl.BlockSpec((rank, QCOLS), lambda i: (0, group)),
            pl.BlockSpec((rank, HEAD_SIZE), lambda i: (0, group)),
            fixed(cosine),
            fixed(sine),
        ],
        out_specs=[
            pl.BlockSpec((L, QCOLS), lambda i: (i, 0)),
            pl.BlockSpec((L, each), lambda i: (0, 0)),
        ],
        out_shape=[
            jax.ShapeDtypeStruct((2 * L, QCOLS), BF16),
            jax.ShapeDtypeStruct((L, each), BF16),
        ],
        compiler_params=params(32),
        cost_estimate=pl.CostEstimate(
            flops=4 * L * QCOLS * (2 * L + 64),
            bytes_accessed=2 * L * (each * 10 + QCOLS * 2),
            transcendentals=2 * L * L * GROUP,
        ),
    )(keep, rs, r2, low, qo, vo, cosine, sine)


def outer_place(block, rank, kv):
    wide = (kv * (GROUP + 1) + 1) // 2
    return (block // wide) * rank, (block % wide) * HEAD_SIZE, wide


def attend_back_body(kv, splits, keep, rs, r2, low, qo, vo, cos_ref, sin_ref, *refs):
    saved = refs[:splits]
    outer, mid = refs[splits:]
    rank = qo.shape[0]
    each = QCOLS + 2 * HEAD_SIZE
    cos4 = jnp.concatenate([cos_ref[...]] * GROUP, 0)
    sin4 = jnp.concatenate([sin_ref[...]] * GROUP, 0)
    low_q = low[:, :rank]
    low_v = low[:, rank:]
    q_mid = jnp.zeros((L, rank), F32)
    v_mid = jnp.zeros((L, rank), F32)

    def put(block, value):
        row, col, _ = outer_place(block, rank, kv)
        outer[row : row + rank, col : col + HEAD_SIZE] = adapter_scale * value

    if (kv * (GROUP + 1)) % 2:
        put(kv * (GROUP + 1), jnp.zeros((rank, HEAD_SIZE), F32))
    for j in range(kv):
        cols = slice(j * QCOLS, (j + 1) * QCOLS)
        at = (j % (kv // splits)) * each
        kept = saved[j // (kv // splits)]
        grad = keep[:, cols] + rs[:, cols].astype(F32) + r2[:, cols].astype(F32)
        grad4 = stack_heads(grad.astype(BF16))
        q4 = stack_heads(kept[:, at : at + QCOLS])
        keys = kept[:, at + QCOLS : at + QCOLS + HEAD_SIZE]
        values = kept[:, at + QCOLS + HEAD_SIZE : at + each]
        prob = probabilities(q4, keys)
        grad_prob = dot(grad4, values, ((1,), (1,)))
        grad_values = dot(prob.astype(BF16), grad4, ((0,), (0,))).astype(BF16)
        inner = jnp.sum(grad_prob * prob, -1, keepdims=True)
        grad_scores = (prob * (grad_prob - inner) * (HEAD_SIZE**-0.5)).astype(BF16)
        grad_query = dot(grad_scores, keys)
        back4 = (grad_query * cos4 - pltpu.roll(grad_query, HEAD_SIZE // 2, 1) * sin4).astype(BF16)
        for h in range(GROUP):
            at = j * GROUP + h
            back = back4[h * L : (h + 1) * L]
            put(at, dot(low_q, back, ((0,), (0,))))
            q_mid += dot(back, qo[:, at * HEAD_SIZE : (at + 1) * HEAD_SIZE], ((1,), (1,)))
        put(kv * GROUP + j, dot(low_v, grad_values, ((0,), (0,))))
        v_mid += dot(grad_values, vo[:, j * HEAD_SIZE : (j + 1) * HEAD_SIZE], ((1,), (1,)))
    mid[:, :rank] = (adapter_scale * q_mid).astype(BF16)
    mid[:, rank:] = (adapter_scale * v_mid).astype(BF16)


def attend_back(keep, rs, r2, low, qo, vo, cosine, sine, saved):
    rank = qo.shape[0]
    kv = vo.shape[1] // HEAD_SIZE
    wide = outer_place(0, rank, kv)[2]
    return pl.pallas_call(
        functools.partial(attend_back_body, kv, len(saved)),
        in_specs=[whole_vmem()] * (8 + len(saved)),
        out_specs=[whole_vmem()] * 2,
        out_shape=[
            jax.ShapeDtypeStruct((2 * rank, wide * HEAD_SIZE), F32),
            jax.ShapeDtypeStruct((L, 2 * rank), BF16),
        ],
        compiler_params=params(32),
    )(keep, rs, r2, low, qo, vo, cosine, sine, *saved)


def adapter_body(n, rows_each, scal, states, outer, *refs):
    mids = refs[:n]
    away, stay = refs[n:]
    src = pl.ds(pl.multiple_of(scal[0] * rows_each, rows_each), rows_each)
    own = states[:, src]
    total = None
    for mid in mids:
        term = dot(mid[...], own, ((0,), (0,)))
        total = term if total is None else total + term
    half = total.shape[0] // 2
    for low in range(2):
        rows = slice(low * half, (low + 1) * half)

        @pl.when(scal[1] == low)
        def _():
            stay[:, :rows_each] = total[rows]
            stay[:, rows_each:] = outer[rows]

        @pl.when(scal[1] != low)
        def _():
            away[:, :rows_each] = total[rows].astype(BF16)
            away[:, rows_each:] = outer[rows].astype(BF16)


def adapter_products(scal, states, mids, outer, rows_each):
    half = outer.shape[0] // 2
    cols = rows_each + outer.shape[1]
    return pl.pallas_call(
        functools.partial(adapter_body, len(mids), rows_each),
        in_specs=[smem()] + [whole_vmem()] * (2 + len(mids)),
        out_specs=[whole_vmem()] * 2,
        out_shape=[
            jax.ShapeDtypeStruct((half, cols), BF16),
            jax.ShapeDtypeStruct((half, cols), F32),
        ],
        compiler_params=params(32),
    )(scal, states, outer, *mids)


def stats_body(count, part, split, scal, xt_ref, xt_pol, tgt, gain, *refs):
    refs = list(refs)
    sums = []
    hidden_out, stats = refs[-2:]
    for which in range(2):
        xt = (xt_ref, xt_pol)[which]
        keeps, recvs = refs[:count], refs[count : 2 * count]
        refs = refs[2 * count :]
        squares = jnp.zeros((L, HEAD_SIZE), F32)
        products = jnp.zeros((L, HEAD_SIZE), F32)
        j = 0
        for keep, recv in zip(keeps, recvs):
            for i in range(keep.shape[0]):
                src = pl.ds(pl.multiple_of((j * split + scal[0]) * part, part), part)
                hidden = xt[:, src].astype(F32) + keep[i].astype(F32) + recv[i].astype(F32)
                cols = slice(j * part, (j + 1) * part)
                if which == 1:
                    hidden_out[0, :, cols] = hidden
                product = hidden * (gain[:, cols] * tgt[0, :, cols].astype(F32))
                square = hidden * hidden
                for s in range(part // HEAD_SIZE):
                    lanes = slice(s * HEAD_SIZE, (s + 1) * HEAD_SIZE)
                    squares += square[:, lanes]
                    products += product[:, lanes]
                j += 1
        sums.append(
            [
                jnp.broadcast_to(jnp.sum(v, 1, keepdims=True), v.shape).T[:1]
                for v in (squares, products)
            ]
        )
    at = lax.broadcasted_iota(jnp.int32, (1, 2 * L), 1) % L
    own = (at >= scal[1]) & (pl.program_id(0) == 0)
    live = jnp.where(own, 1.0, 0.0).astype(F32)
    both = [jnp.concatenate([sums[0][i], sums[1][i]], 1) for i in range(2)]
    stats[...] = jnp.concatenate([*both, live, jnp.zeros((5, 2 * L), F32)], 0)


def norm_stats(scal, xt, tgt, gain, keeps, recvs, split):
    n = sum(a.shape[0] for a in keeps)
    part = keeps[0].shape[2]
    shared = []
    for which in range(2):
        at = functools.partial(lambda which, i: (0, 2 * i + which, 0), which)
        for a in (*keeps, *recvs):
            shared.append((a, pl.BlockSpec((a.shape[0], L, part), at)))
    return pl.pallas_call(
        functools.partial(stats_body, len(keeps), part, split),
        grid=(4,),
        in_specs=[
            smem(),
            pl.BlockSpec((L, xt.shape[1]), lambda i: ((i // 2) * 4 + i % 2, 0)),
            pl.BlockSpec((L, xt.shape[1]), lambda i: ((i // 2) * 4 + 2 + i % 2, 0)),
            pl.BlockSpec((1, L, n * part), lambda i: (i, 0, 0)),
            pl.BlockSpec((1, n * part), lambda i: (0, 0)),
        ]
        + [spec for _, spec in shared],
        out_specs=[
            pl.BlockSpec((1, L, n * part), lambda i: (i, 0, 0)),
            pl.BlockSpec((8, 2 * L), lambda i: (i, 0)),
        ],
        out_shape=[
            jax.ShapeDtypeStruct((4, L, n * part), F32),
            jax.ShapeDtypeStruct((32, 2 * L), F32),
        ],
        compiler_params=params(32),
    )(scal, xt, xt, tgt, gain, *[a for a, _ in shared])


def score_body(width, masks, ids, own, *refs):
    recvs = refs[: len(masks)]
    total_out, margin_out = refs[len(masks) :]
    lane = lax.broadcasted_iota(jnp.int32, (8, 128), 1)
    margins = jnp.zeros((8, 128), F32)
    for p in range(4):
        total = own[8 * p : 8 * p + 8]
        for recv, m in zip(recvs, masks):
            q = ORD.index(ORD[p] ^ m)
            total = total + recv[8 * q : 8 * q + 8]
        total_out[8 * p : 8 * p + 8] = total
        inverse = lax.rsqrt(total[0:1] * (1.0 / width) + norm_eps)
        score = total[1:2] * inverse * (width**-0.5)
        score = jnp.where(total[2:3] > 0.5, score, 0.0)
        margin = jnp.sum(score[:, L:], 1, keepdims=True) - jnp.sum(score[:, :L], 1, keepdims=True)
        margins = margins + jnp.where(lane == ids[p], margin, 0.0)
    margin_out[...] = margins


def scores(ids, own, recvs, masks, width):
    return pl.pallas_call(
        functools.partial(score_body, width, masks),
        in_specs=[smem()] + [whole_vmem()] * (1 + len(recvs)),
        out_specs=[whole_vmem()] * 2,
        out_shape=[jax.ShapeDtypeStruct(own.shape, F32), jax.ShapeDtypeStruct((8, 128), F32)],
    )(ids, own, *recvs)


def turn(i):
    return (2 * i + 1) % 5


def grad_body(width, seqs, n_vec, ids, pairs, total, hidden, tgt, gain, *refs):
    vecs = refs[:n_vec]
    grad_out, loss_out, slope = refs[n_vec:]
    lane = lax.broadcasted_iota(jnp.int32, (8, 128), 1)

    @pl.when(pl.program_id(0) == 0)
    def _():
        margin = vecs[0][...]
        for v in vecs[1:]:
            margin = margin + v[...]
        logits = jnp.zeros((8, 128), F32)
        for i in range(seqs // 2):
            sign = jnp.where(lane == pairs[2 * i], 1.0, 0.0) - jnp.where(
                lane == pairs[2 * i + 1], 1.0, 0.0
            )
            logit = dpo_beta * jnp.sum(margin * sign, 1, keepdims=True)
            logits = logits + jnp.where(lane == i, logit, 0.0)
        soft = jnp.maximum(-logits, 0.0) + jnp.log1p(jnp.exp(-jnp.abs(logits)))
        used = lane < seqs // 2
        loss = jnp.sum(jnp.where(used, soft, 0.0), 1, keepdims=True)
        loss_out[...] = jnp.broadcast_to(loss, (8, 128))
        slopes = jnp.where(used, -dpo_beta / (1.0 + jnp.exp(logits)), 0.0)
        gradient = jnp.zeros((8, 128), F32)
        for i in range(seqs // 2):
            each = jnp.sum(jnp.where(lane == i, slopes, 0.0), 1, keepdims=True)
            sign = jnp.where(lane == pairs[2 * i], 1.0, 0.0) - jnp.where(
                lane == pairs[2 * i + 1], 1.0, 0.0
            )
            gradient = gradient + each * sign
        slope[...] = gradient * loss_scale

    mine = lane == ids[turn(pl.program_id(0))]
    seq = jnp.sum(jnp.where(mine, slope[...], 0.0), 1, keepdims=True)[:1]
    rows = total[:, L:]
    token = jnp.where(rows[2:3] > 0.5, seq, 0.0) * (width**-0.5)
    inverse = lax.rsqrt(rows[0:1] * (1.0 / width) + norm_eps)
    first = inverse * token
    second = inverse * inverse * inverse * (token * rows[1:2] * (1.0 / width))
    first = jnp.broadcast_to(first, (L, L)).T
    second = jnp.broadcast_to(second, (L, L)).T
    for s in range(hidden.shape[2] // HEAD_SIZE):
        cols = slice(s * HEAD_SIZE, (s + 1) * HEAD_SIZE)
        weighted = gain[:, cols] * tgt[0, :, cols].astype(F32)
        grad_out[0, :, cols] = (first * weighted - second * hidden[0, :, cols]).astype(BF16)


def grad_hidden(ids, pairs, total, hidden, tgt, gain, vecs, width):
    n = hidden.shape[2]
    seqs = pairs.shape[0]
    return pl.pallas_call(
        functools.partial(grad_body, width, seqs, len(vecs)),
        grid=(4,),
        in_specs=[
            smem(),
            smem(),
            pl.BlockSpec((8, 2 * L), lambda i: (turn(i), 0)),
            pl.BlockSpec((1, L, n), lambda i: (turn(i), 0, 0)),
            pl.BlockSpec((1, L, n), lambda i: (turn(i), 0, 0)),
            pl.BlockSpec((1, n), lambda i: (0, 0)),
        ]
        + [pl.BlockSpec((8, 128), lambda i: (0, 0)) for _ in vecs],
        out_specs=[
            pl.BlockSpec((1, L, n), lambda i: (i, 0, 0)),
            pl.BlockSpec((8, 128), lambda i: (0, 0)),
        ],
        out_shape=[
            jax.ShapeDtypeStruct((4, L, n), BF16),
            jax.ShapeDtypeStruct((8, 128), F32),
        ],
        scratch_shapes=[pltpu.VMEM((8, 128), F32)],
        compiler_params=params(32),
    )(ids, pairs, total, hidden, tgt, gain, *vecs)


def per_device(
    fsdp_size,
    tensor_size,
    ref_states,
    pol_states,
    target_rows,
    norm_gain,
    wq,
    wk,
    wv,
    wo,
    qa,
    qo,
    va,
    vo,
    prompt_length,
    pairs,
):
    tokens, width = ref_states.shape
    groups = fsdp_size // 4
    near_z = fsdp_size // 4
    bits = []
    bit = 2
    while bit < fsdp_size:
        if bit != near_z:
            bits.append(bit)
        bit *= 2
    split = 2 if tensor_size == 2 and fsdp_size == 16 else 1
    kv_local = wk.shape[1] // HEAD_SIZE
    depth = wq.shape[0]
    part = depth // split
    rank = qa.shape[1]
    me = lax.axis_index("fsdp")
    x = lax.axis_index("tensor")
    side = x if split == 2 else 0

    def tmask(d):
        return (d & 1) | ((d >> 1) * near_z)

    def gmask(k):
        return sum(bit for i, bit in enumerate(bits) if (k >> i) & 1)

    def move(value, mask):
        return lax.ppermute(value, "fsdp", [(i, i ^ mask) for i in range(fsdp_size)])

    def swap_x(value):
        return lax.ppermute(value, "tensor", [(0, 1), (1, 0)])

    def move_both(value, mask, flip):
        pairs_list = [
            (2 * i + j, 2 * (i ^ mask) + (j ^ flip)) for i in range(fsdp_size) for j in range(2)
        ]
        return lax.ppermute(value, ("fsdp", "tensor"), pairs_list)

    def after(value, *others):
        return lax.optimization_barrier((value, *others))[0]

    wide = groups == 4 and split == 2
    heads = wo.shape[0]

    def shard_of(j, *queue):
        q, k, v = wq, wk, wv
        if queue:
            q, k, v = lax.optimization_barrier((wq, wk, wv, *queue))[:3]
        pieces = [
            q[:, j * QCOLS : (j + 1) * QCOLS],
            k[:, j * HEAD_SIZE : (j + 1) * HEAD_SIZE],
            v[:, j * HEAD_SIZE : (j + 1) * HEAD_SIZE],
        ]
        return jnp.concatenate(pieces, 1)

    def gather(shard):
        return [shard] + [move(shard, gmask(k)) for k in range(1, groups)]

    if wide:
        over_y, over_z = gmask(1), gmask(2)
        shards = [shard_of(0)]
        zs = [move(shards[0], over_z)]
        ys = [move(shards[0], over_y)]
        corners = []

    parts = groups * split
    idx = []
    for d in range(4):
        for k in range(groups):
            for h in range(split):
                idx.append((me ^ tmask(d) ^ gmask(k)) * split + h)
    for d in range(4):
        for k in range(groups):
            idx.append((me ^ tmask(d) ^ gmask(k)) * split + side)
    idx.append(x)
    idx = jnp.stack(idx).astype(jnp.int32)
    if wide:
        idx = after(idx, shards[0])
    prepared = prep(
        idx,
        ref_states,
        pol_states,
        target_rows,
        norm_gain.astype(F32).reshape(1, width),
        parts,
        part,
        split,
    )
    xs, ts, gain = prepared[:4], prepared[4:8], prepared[8]
    near = move(xs[1], 1)
    far = [move(xs[2], near_z)]
    far.append(move(xs[3], near_z | 1))

    if split == 2:
        other = [swap_x(a) for a in far]
        far = [
            [jnp.where(x == which, a[0], b[0]) for which in range(2)] for a, b in zip(far, other)
        ]
    states = jnp.concatenate(
        [
            *(xs[0][0], far[0][0], xs[0][1], far[0][1]),
            *(near[0], far[1][0], near[1], far[1][1]),
        ],
        0,
    )

    low = dot(pol_states, jnp.concatenate([qa, va], 1)).astype(BF16)
    cosine, sine = rope_tables(L, HEAD_SIZE)

    def next_shard(j, *queue):
        if j < kv_local:
            shards.append(shard_of(j, ys[-1] if j == 1 else corners[-1], *queue))
        elif j == kv_local:
            own = after(wo, corners[-1], *queue)
            shards.append(lax.dynamic_slice_in_dim(own, (1 - x) * part, part, 1))
        else:
            own = after(wo, corners[-1], *queue)
            shards.append(lax.dynamic_slice_in_dim(own, x * part, part, 1))
        ys.append(move(shards[j], over_y))
        zs.append(move(after(shards[j], zs[-1], *queue), over_z))
        corners.append(move(after(zs[j - 1], ys[j], *queue), over_y))

    saved, mixed = [], []
    queue = ()
    for j in range(kv_local):
        if wide:
            next_shard(j + 1, *queue)
            ws = [shards[j], ys[j], zs[j], corners[j]]
        else:
            ws = gather(shard_of(j))
        send = mm(states, 1, ws, BF16)
        rs = move(send, 1)
        keep = mm(states, 0, ws, F32)
        over = [keep[(2 * w + 1) * L : (2 * w + 2) * L] for w in range(2)]
        came = [rs[(2 * w + 1) * L : (2 * w + 2) * L] for w in range(2)]
        over = (jnp.concatenate(over, 0) + jnp.concatenate(came, 0).astype(F32)).astype(BF16)
        r2 = move(over, near_z)
        queue = (over,)
        if wide and j + 1 < kv_local:
            r2 = after(r2, zs[j + 1])
        result, kept = attend(keep, rs, r2, low, qo, vo, j, cosine, sine)
        saved.append(kept)
        pair = jnp.concatenate([result, move(result, near_z)], 0)
        last = move(pair, 1)
        mixed.append(jnp.concatenate([pair, last], 0))
        states = after(states, last)
    rows = jnp.concatenate(mixed, 1)

    keeps, recvs = [], []
    if wide:
        next_shard(kv_local + 1, *queue)
        j = kv_local
        wo_send = [(w[None], 0) for w in (shards[j], ys[j], zs[j], corners[j])]
        first = out_mm(rows, wo_send[:3])
        recvs.append(swap_x(first))
        corner = move(after(zs[j + 1], corners[j], first), over_y)
        recvs.append(swap_x(out_mm(rows, wo_send[3:])))
        wo_keep = [(w[None], 0) for w in (shards[j + 1], ys[j + 1], zs[j + 1], corner)]
        keeps.append(out_mm(rows, wo_keep[:3]))
        keeps.append(out_mm(rows, wo_keep[3:]))
    else:
        wo_keep = [(w[None], 0) for w in gather(wo)]
        product = out_mm(rows, wo_keep)
        if tensor_size > 1:
            product = lax.psum(product, "tensor")
        keeps.append(product)
        recvs.append(jnp.zeros_like(product))

    ts = [ts[0]] + list(lax.optimization_barrier((*ts[1:], last))[:3])
    targets = [ts[0]] + [move(ts[d], tmask(d)) for d in (1, 2, 3)]
    tgt = jnp.stack([targets[d] for d in ORD])

    scal = jnp.stack([jnp.asarray(side, jnp.int32), prompt_length[0].astype(jnp.int32)])
    hidden, stats = norm_stats(scal, states, tgt, gain, keeps, recvs, split)
    masks, got = [], []
    for flip in range(split):
        for d in range(4):
            if d or flip:
                masks.append(d)
                if split == 2:
                    got.append(move_both(stats, tmask(d), flip))
                else:
                    got.append(move(stats, tmask(d)))
    ids = jnp.stack([me ^ tmask(d) for d in ORD]).astype(jnp.int32)
    total, margin = scores(ids, stats, got, tuple(masks), width)
    vecs = [margin] + [move(margin, gmask(k)) for k in range(1, groups)]
    grad, loss = grad_hidden(ids, pairs, total, hidden, tgt, gain, vecs, width)

    grad_rows = grad.reshape(4 * L, -1)
    other = None
    for half in range(2):
        if split == 2:
            leaving = grad_rows[2 * L * half : 2 * L * (half + 1)]
            other = swap_x(leaving if half == 0 else after(leaving, other))
            acc = back_mm(grad_rows, half, wo_keep, None)
            if half == 1:
                other = after(other, over)
            keep, send = back_mm(other, None, wo_send, acc)
        else:
            acc = jnp.zeros((2 * L, heads), F32)
            keep, send = back_mm(grad_rows, half, wo_keep, acc)
        rs = move(send, 1)
        if half == 0:
            over = (keep + rs.astype(F32)).astype(BF16)
            r2 = move(over, near_z)
    outer, mid = attend_back(keep, rs, r2, low, qo, vo, cosine, sine, saved)

    rows_each = width // tensor_size
    if split == 2:
        mids = [mid, swap_x(mid)]
    elif tensor_size == 1:
        mids = [mid]
    else:
        gathered = lax.all_gather(mid, "tensor", axis=0, tiled=False)
        mids = [gathered[i] for i in range(tensor_size)]
    scal = jnp.stack([x, me & 1]).astype(jnp.int32)
    away, current = adapter_products(scal, pol_states, mids, outer, rows_each)
    current = current + move(away, 1).astype(F32)
    top = fsdp_size // 2
    g = (me // 2) % groups
    rows = current.shape[0] // groups
    pieces = [
        lax.dynamic_slice_in_dim(current, (g ^ k) * rows, rows, 0) for k in range(groups)
    ]
    current = pieces[0]
    for k in range(1, groups):
        current = current + move(pieces[k].astype(BF16), k << 1).astype(F32)
    rows //= 2
    high = me // top
    away = lax.dynamic_slice_in_dim(current, (1 - high) * rows, rows, 0).astype(BF16)
    current = lax.dynamic_slice_in_dim(current, high * rows, rows, 0)
    current = (current + move(away, top).astype(F32)).astype(BF16)

    def join(bit, own, other):
        return jnp.where(
            bit == 0, jnp.concatenate([own, other], 0), jnp.concatenate([other, own], 0)
        )

    current = join(high, current, move(current, top))
    pieces = [current] + [move(current, k << 1) for k in range(1, groups)]
    step = 1
    while step < groups:
        odd = (g & step) != 0
        pieces = [jnp.where(odd, pieces[k ^ step], pieces[k]) for k in range(groups)]
        step *= 2
    current = jnp.concatenate(pieces, 0)
    current = join(me & 1, current, move(current, 1)).astype(F32)
    a_grads = current[:, :rows_each]
    outer = current[:, rows_each:]
    outer = jnp.concatenate([outer[:rank], outer[rank:]], 1)
    return (
        loss[0, 0],
        a_grads[:rank].T,
        outer[:, : qo.shape[1]],
        a_grads[rank:].T,
        outer[:, qo.shape[1] : qo.shape[1] + vo.shape[1]],
    )


def solution(mesh):
    in_specs = (
        P("fsdp", None),
        P("fsdp", None),
        P("fsdp", None),
        P(),
        P("fsdp", "tensor"),
        P("fsdp", "tensor"),
        P("fsdp", "tensor"),
        P("tensor", "fsdp"),
        P(),
        P(None, "tensor"),
        P(),
        P(None, "tensor"),
        P("fsdp"),
        P(),
    )
    out_specs = (P(), P("tensor", None), P(None, "tensor"), P("tensor", None), P(None, "tensor"))
    body = functools.partial(per_device, mesh.shape["fsdp"], mesh.shape["tensor"])
    return jax.shard_map(body, mesh=mesh, in_specs=in_specs, out_specs=out_specs, check_vma=False)
```

```python
import functools

import jax
import jax.numpy as jnp
from jax import lax
from jax.experimental import pallas as pl
from jax.experimental.pallas import tpu as pltpu
from jax.sharding import PartitionSpec as P

QUERY_HEADS = 32
KEY_VALUE_HEADS = 8
HEAD_SIZE = 128
L = 128
GROUP = QUERY_HEADS // KEY_VALUE_HEADS
QCOLS = GROUP * HEAD_SIZE

adapter_scale = 0.5
dpo_beta = 0.1
loss_scale = 256.0
rope_base = 500000.0
norm_eps = 1e-05

F32 = jnp.float32
BF16 = jnp.bfloat16
ORD = (0, 2, 1, 3)
MB = 1 << 20
SMALL = pl.CostEstimate(flops=1, bytes_accessed=1, transcendentals=0)


def rope_tables(length, head_dim):
    half_dim = head_dim // 2
    exponent = jnp.arange(half_dim, dtype=F32) * (2.0 / head_dim)
    inverse = jnp.power(F32(rope_base), -exponent)
    angles = jnp.arange(length, dtype=F32)[:, None] * inverse[None, :]
    cosine = jnp.concatenate([jnp.cos(angles), jnp.cos(angles)], 1)
    sine = jnp.concatenate([-jnp.sin(angles), jnp.sin(angles)], 1)
    return cosine, sine


def dot(a, b, dims=((1,), (0,))):
    return lax.dot_general(a, b, (dims, ((), ())), preferred_element_type=F32)


def params(limit_mb):
    return pltpu.CompilerParams(vmem_limit_bytes=limit_mb * MB)


def smem():
    return pl.BlockSpec(memory_space=pltpu.SMEM)


def whole_vmem():
    return pl.BlockSpec(memory_space=pltpu.VMEM)


def prep_body(parts, part, split, idx, ref, pol, tgt, gain, *outs):
    x0, x1, x2, x3, t0, t1, t2, t3, go = outs
    groups = parts // split
    for d, (xo, to) in enumerate(((x0, t0), (x1, t1), (x2, t2), (x3, t3))):
        for j in range(parts):
            src = pl.ds(pl.multiple_of(idx[d * parts + j] * part, part), part)
            cols = slice(j * part, (j + 1) * part)
            if xo.shape[0] == 2:
                xo[0, :, cols] = ref[:, src]
                xo[1, :, cols] = pol[:, src]
            else:
                @pl.when(idx[4 * parts + 4 * groups] == 0)
                def _():
                    xo[0, :, cols] = ref[:, src]

                @pl.when(idx[4 * parts + 4 * groups] != 0)
                def _():
                    xo[0, :, cols] = pol[:, src]

        for j in range(groups):
            at = idx[4 * parts + d * groups + j] * part
            src = pl.ds(pl.multiple_of(at, part), part)
            to[:, j * part : (j + 1) * part] = tgt[:, src]
            if d == 0:
                go[:, j * part : (j + 1) * part] = gain[:, src]


def prep(idx, ref, pol, tgt, gain, parts, part, split):
    tokens = ref.shape[0]
    xs = lambda n: jax.ShapeDtypeStruct((n, tokens, parts * part), BF16)
    far = 1 if split == 2 else 2
    width = parts // split * part
    return pl.pallas_call(
        functools.partial(prep_body, parts, part, split),
        in_specs=[smem()] + [whole_vmem()] * 4,
        out_specs=[whole_vmem()] * 9,
        out_shape=[xs(2), xs(2), xs(far), xs(far)]
        + [jax.ShapeDtypeStruct((tokens, width), BF16)] * 4
        + [jax.ShapeDtypeStruct((1, width), F32)],
        compiler_params=params(32),
        cost_estimate=SMALL,
    )(idx, ref, pol, tgt, gain)


def tile_of(cols):
    for tile in (256, 128):
        if cols % tile == 0:
            return tile
    return cols


def mm_body(count, x_ref, *refs):
    ws, outs = refs[:count], refs[count:]
    total = None
    at = 0
    for w in ws:
        depth = w.shape[0]
        term = dot(x_ref[:, at : at + depth], w[...])
        total = term if total is None else total + term
        at += depth
    rows = total.shape[0] // 2
    for i, out_ref in enumerate(outs):
        out_ref[...] = total[i * rows : (i + 1) * rows].astype(out_ref.dtype)


def mm(x, half, ws, out_dtype):
    rows, depth = x.shape[0] // 2, x.shape[1]
    cols = ws[0].shape[1]
    tile = tile_of(cols)
    return pl.pallas_call(
        functools.partial(mm_body, len(ws)),
        grid=(cols // tile,),
        in_specs=[pl.BlockSpec((rows, depth), lambda i: (half, 0))]
        + [pl.BlockSpec((w.shape[0], tile), lambda i: (0, i)) for w in ws],
        out_specs=[pl.BlockSpec((rows // 2, tile), lambda i: (0, i))] * 2,
        out_shape=[jax.ShapeDtypeStruct((rows // 2, cols), out_dtype)] * 2,
        compiler_params=params(32),
        cost_estimate=SMALL,
    )(x, *ws)


def out_body(n, counts, *refs):
    ws = refs[4 * n : -1]
    out_ref = refs[-1]
    rows = refs[0].shape[0]
    for j in range(n):
        x = jnp.concatenate([refs[p * n + j][...] for p in range(4)], 0)
        depth = x.shape[1]
        at = 0
        for k, count in enumerate(counts):
            row = j * depth
            piece = at
            while row >= ws[piece].shape[0]:
                row -= ws[piece].shape[0]
                piece += 1
            at += count
            term = dot(x, ws[piece][row : row + depth])
            if j:
                term = term + out_ref[k]
            out_ref[k] = term


def out_store(n, counts, *refs):
    out_body(n, counts, *refs[:-2], refs[-1])
    refs[-2][...] = refs[-1][...].astype(BF16)


def out_mm(parts, ws):
    n = len(parts[0])
    rows = parts[0][0].shape[0]
    cols = ws[0][0].shape[1]
    flat = [piece for w in ws for piece in w]
    inputs = [a for part in parts for a in part] + flat
    return pl.pallas_call(
        functools.partial(out_store, n, tuple(len(w) for w in ws)),
        in_specs=[whole_vmem()] * len(inputs),
        out_specs=whole_vmem(),
        out_shape=jax.ShapeDtypeStruct((len(ws), 4 * rows, cols), BF16),
        scratch_shapes=[pltpu.VMEM((len(ws), 4 * rows, cols), F32)],
        compiler_params=params(32),
        cost_estimate=SMALL,
    )(*inputs)


def back_body(counts, part, has_acc, x_ref, *refs):
    total = None
    at = 0
    for j, count in enumerate(counts):
        w = refs[at][...]
        if count == 2:
            w = jnp.where(pl.program_id(0) < pl.num_programs(0) // 2, w, refs[at + 1][...])
        at += count
        term = dot(x_ref[:, j * part : (j + 1) * part], w, ((1,), (1,)))
        total = term if total is None else total + term
    refs = refs[at:]
    if has_acc:
        total = total + refs[0][...]
        keep, send = refs[1:]
        half = total.shape[0] // 2
        keep[...] = total[:half]
        send[...] = total[half:].astype(send.dtype)
    else:
        refs[0][...] = total


def back_mm(x, half, ws, acc):
    rows = x.shape[0] // (1 if half is None else 2)
    depth = x.shape[1]
    part = ws[0][0].shape[1]
    heads = sum(piece.shape[0] for piece in ws[0])
    tile = min(512, heads)
    steps = heads // tile
    has_acc = acc is not None
    row = half or 0
    in_specs = [pl.BlockSpec((rows, depth), lambda i: (row, 0))]
    for w in ws:
        if len(w) == 1:
            in_specs.append(pl.BlockSpec((tile, part), lambda i: (i, 0)))
        else:
            in_specs.append(pl.BlockSpec((tile, part), lambda i: (jnp.minimum(i, steps // 2 - 1), 0)))
            in_specs.append(pl.BlockSpec((tile, part), lambda i: (jnp.maximum(i - steps // 2, 0), 0)))
    args = [x] + [piece for w in ws for piece in w]
    if has_acc:
        in_specs.append(pl.BlockSpec((rows, tile), lambda i: (0, i)))
        args.append(acc)
        out_specs = [pl.BlockSpec((rows // 2, tile), lambda i: (0, i))] * 2
        out_shape = [
            jax.ShapeDtypeStruct((rows // 2, heads), F32),
            jax.ShapeDtypeStruct((rows // 2, heads), BF16),
        ]
    else:
        out_specs = pl.BlockSpec((rows, tile), lambda i: (0, i))
        out_shape = jax.ShapeDtypeStruct((rows, heads), F32)
    return pl.pallas_call(
        functools.partial(back_body, tuple(len(w) for w in ws), part, has_acc),
        grid=(steps,),
        in_specs=in_specs,
        out_specs=out_specs,
        out_shape=out_shape,
        compiler_params=params(32),
        cost_estimate=SMALL,
    )(*args)


def causal(rows):
    at = lax.broadcasted_iota(jnp.int32, (rows, L), 0) % L
    return at >= lax.broadcasted_iota(jnp.int32, (rows, L), 1)


def probabilities(q4, keys):
    scores = dot(q4, keys, ((1,), (1,))) * (HEAD_SIZE**-0.5)
    weights = jnp.where(causal(q4.shape[0]), jnp.exp(scores), 0.0)
    return weights / jnp.sum(weights, -1, keepdims=True)


def stack_heads(values):
    return jnp.concatenate(
        [values[:, h * HEAD_SIZE : (h + 1) * HEAD_SIZE] for h in range(GROUP)], 0
    )


def attend_body(adapted, keep, rs, r2, low, qo, vo, cos_ref, sin_ref, mixed, *saved):
    cosine = cos_ref[...]
    sine = sin_ref[...]
    pre = keep[...] + rs[...].astype(F32) + r2[...].astype(F32)
    rank = qo.shape[0]
    q_pre = pre[:, :QCOLS]
    k_pre = pre[:, QCOLS : QCOLS + HEAD_SIZE]
    v_pre = pre[:, QCOLS + HEAD_SIZE :]
    if adapted:
        q_pre = q_pre + adapter_scale * dot(low[:, :rank], qo[...])
        v_pre = v_pre + adapter_scale * dot(low[:, rank:], vo[...])
    cos4 = jnp.concatenate([cosine] * GROUP, 0)
    sin4 = jnp.concatenate([sine] * GROUP, 0)
    q4 = stack_heads(q_pre)
    q4 = (q4 * cos4 + pltpu.roll(q4, HEAD_SIZE // 2, 1) * sin4).astype(BF16)
    keys = (k_pre * cosine + pltpu.roll(k_pre, HEAD_SIZE // 2, 1) * sine).astype(BF16)
    values = v_pre.astype(BF16)
    rounded = probabilities(q4, keys).astype(BF16)
    out = dot(rounded, values).astype(BF16)
    for h in range(GROUP):
        cols = slice(h * HEAD_SIZE, (h + 1) * HEAD_SIZE)
        mixed[:, cols] = out[h * L : (h + 1) * L]
        if saved:
            saved[0][:, cols] = q4[h * L : (h + 1) * L]
    if saved:
        saved[0][:, QCOLS : QCOLS + HEAD_SIZE] = keys
        saved[0][:, QCOLS + HEAD_SIZE :] = values


def attend(adapted, keep, rs, r2, low, qo, vo, group, cosine, sine):
    each = QCOLS + 2 * HEAD_SIZE
    rank = qo.shape[0]
    top = lambda a: pl.BlockSpec((L, a.shape[1]), lambda i: (0, 0))
    return pl.pallas_call(
        functools.partial(attend_body, adapted),
        grid=(1,),
        in_specs=[
            top(keep),
            top(rs),
            top(r2),
            top(low),
            pl.BlockSpec((rank, QCOLS), lambda i: (0, group)),
            pl.BlockSpec((rank, HEAD_SIZE), lambda i: (0, group)),
            top(cosine),
            top(sine),
        ],
        out_specs=[pl.BlockSpec((L, w), lambda i: (0, 0)) for w in (QCOLS, each)[: 1 + adapted]],
        out_shape=[jax.ShapeDtypeStruct((L, w), BF16) for w in (QCOLS, each)[: 1 + adapted]],
        compiler_params=params(32),
        cost_estimate=SMALL,
    )(keep, rs, r2, low, qo, vo, cosine, sine)


def outer_place(block, rank, kv):
    wide = (kv * (GROUP + 1) + 1) // 2
    return (block // wide) * rank, (block % wide) * HEAD_SIZE, wide


def attend_back_body(kv, splits, keep, rs, r2, low, qo, vo, cos_ref, sin_ref, *refs):
    saved = refs[:splits]
    outer, mid = refs[splits:]
    rank = qo.shape[0]
    each = QCOLS + 2 * HEAD_SIZE
    cos4 = jnp.concatenate([cos_ref[...]] * GROUP, 0)
    sin4 = jnp.concatenate([sin_ref[...]] * GROUP, 0)
    low_q = low[:, :rank]
    low_v = low[:, rank:]
    q_mid = jnp.zeros((L, rank), F32)
    v_mid = jnp.zeros((L, rank), F32)

    def put(block, value):
        row, col, _ = outer_place(block, rank, kv)
        outer[row : row + rank, col : col + HEAD_SIZE] = adapter_scale * value

    if (kv * (GROUP + 1)) % 2:
        put(kv * (GROUP + 1), jnp.zeros((rank, HEAD_SIZE), F32))
    for j in range(kv):
        cols = slice(j * QCOLS, (j + 1) * QCOLS)
        at = (j % (kv // splits)) * each
        kept = saved[j // (kv // splits)]
        grad = keep[:, cols] + rs[:, cols].astype(F32) + r2[:, cols].astype(F32)
        grad4 = stack_heads(grad.astype(BF16))
        q4 = stack_heads(kept[:, at : at + QCOLS])
        keys = kept[:, at + QCOLS : at + QCOLS + HEAD_SIZE]
        values = kept[:, at + QCOLS + HEAD_SIZE : at + each]
        prob = probabilities(q4, keys)
        grad_prob = dot(grad4, values, ((1,), (1,)))
        grad_values = dot(prob.astype(BF16), grad4, ((0,), (0,))).astype(BF16)
        inner = jnp.sum(grad_prob * prob, -1, keepdims=True)
        grad_scores = (prob * (grad_prob - inner) * (HEAD_SIZE**-0.5)).astype(BF16)
        grad_query = dot(grad_scores, keys)
        back4 = (grad_query * cos4 - pltpu.roll(grad_query, HEAD_SIZE // 2, 1) * sin4).astype(BF16)
        for h in range(GROUP):
            at = j * GROUP + h
            back = back4[h * L : (h + 1) * L]
            put(at, dot(low_q, back, ((0,), (0,))))
            q_mid += dot(back, qo[:, at * HEAD_SIZE : (at + 1) * HEAD_SIZE], ((1,), (1,)))
        put(kv * GROUP + j, dot(low_v, grad_values, ((0,), (0,))))
        v_mid += dot(grad_values, vo[:, j * HEAD_SIZE : (j + 1) * HEAD_SIZE], ((1,), (1,)))
    mid[:, :rank] = (adapter_scale * q_mid).astype(BF16)
    mid[:, rank:] = (adapter_scale * v_mid).astype(BF16)


def attend_back(keep, rs, r2, low, qo, vo, cosine, sine, saved):
    rank = qo.shape[0]
    kv = vo.shape[1] // HEAD_SIZE
    wide = outer_place(0, rank, kv)[2]
    return pl.pallas_call(
        functools.partial(attend_back_body, kv, len(saved)),
        in_specs=[whole_vmem()] * (8 + len(saved)),
        out_specs=[whole_vmem()] * 2,
        out_shape=[
            jax.ShapeDtypeStruct((2 * rank, wide * HEAD_SIZE), F32),
            jax.ShapeDtypeStruct((L, 2 * rank), BF16),
        ],
        compiler_params=params(32),
        cost_estimate=SMALL,
    )(keep, rs, r2, low, qo, vo, cosine, sine, *saved)


def adapter_body(n, rows_each, scal, states, outer, *refs):
    mids = refs[:n]
    away, stay = refs[n:]
    src = pl.ds(pl.multiple_of(scal[0] * rows_each, rows_each), rows_each)
    own = states[:, src]
    total = None
    for mid in mids:
        term = dot(mid[...], own, ((0,), (0,)))
        total = term if total is None else total + term
    half = total.shape[0] // 2
    for low in range(2):
        rows = slice(low * half, (low + 1) * half)

        @pl.when(scal[1] == low)
        def _():
            stay[:, :rows_each] = total[rows]
            stay[:, rows_each:] = outer[rows]

        @pl.when(scal[1] != low)
        def _():
            away[:, :rows_each] = total[rows].astype(BF16)
            away[:, rows_each:] = outer[rows].astype(BF16)


def adapter_products(scal, states, mids, outer, rows_each):
    half = outer.shape[0] // 2
    cols = rows_each + outer.shape[1]
    return pl.pallas_call(
        functools.partial(adapter_body, len(mids), rows_each),
        in_specs=[smem()] + [whole_vmem()] * (2 + len(mids)),
        out_specs=[whole_vmem()] * 2,
        out_shape=[
            jax.ShapeDtypeStruct((half, cols), BF16),
            jax.ShapeDtypeStruct((half, cols), F32),
        ],
        compiler_params=params(32),
        cost_estimate=SMALL,
    )(scal, states, outer, *mids)


def stats_body(counts, part, split, scal, xt_ref, xt_pol, tgt, gain, *refs):
    refs = list(refs)
    sums = []
    hidden_out, stats = refs[-2:]
    for which in range(2):
        xt = (xt_ref, xt_pol)[which]
        count = sum(counts)
        keeps = [r[i] for r in refs[: counts[0]] for i in range(r.shape[0])]
        recvs = [r[i] for r in refs[counts[0] : count] for i in range(r.shape[0])]
        refs = refs[count:]
        squares = jnp.zeros((L, HEAD_SIZE), F32)
        products = jnp.zeros((L, HEAD_SIZE), F32)
        for j, (keep, recv) in enumerate(zip(keeps, recvs)):
            src = pl.ds(pl.multiple_of((j * split + scal[0]) * part, part), part)
            hidden = xt[:, src].astype(F32) + keep.astype(F32) + recv.astype(F32)
            cols = slice(j * part, (j + 1) * part)
            if which == 1:
                hidden_out[0, :, cols] = hidden
            product = hidden * (gain[:, cols] * tgt[0, :, cols].astype(F32))
            square = hidden * hidden
            for s in range(part // HEAD_SIZE):
                lanes = slice(s * HEAD_SIZE, (s + 1) * HEAD_SIZE)
                squares += square[:, lanes]
                products += product[:, lanes]
        sums.append(
            [
                jnp.broadcast_to(jnp.sum(v, 1, keepdims=True), v.shape).T[:1]
                for v in (squares, products)
            ]
        )
    at = lax.broadcasted_iota(jnp.int32, (1, 2 * L), 1) % L
    own = (at >= scal[1]) & (pl.program_id(0) == 0)
    live = jnp.where(own, 1.0, 0.0).astype(F32)
    both = [jnp.concatenate([sums[0][i], sums[1][i]], 1) for i in range(2)]
    stats[...] = jnp.concatenate([*both, live, jnp.zeros((5, 2 * L), F32)], 0)


def norm_stats(scal, xt, tgt, gain, keeps, recvs, split):
    n = sum(a.shape[0] for a in keeps)
    part = keeps[0].shape[2]
    shared = []
    for which in range(2):
        at = functools.partial(
            lambda which, i: (0, (i // 2) * 4 + which * 2 + i % 2, 0), which
        )
        for a in (*keeps, *recvs):
            shared.append((a, pl.BlockSpec((a.shape[0], L, part), at)))
    return pl.pallas_call(
        functools.partial(stats_body, (len(keeps), len(recvs)), part, split),
        grid=(4,),
        in_specs=[
            smem(),
            pl.BlockSpec((L, xt.shape[1]), lambda i: ((i // 2) * 4 + i % 2, 0)),
            pl.BlockSpec((L, xt.shape[1]), lambda i: ((i // 2) * 4 + 2 + i % 2, 0)),
            pl.BlockSpec((1, L, n * part), lambda i: (i, 0, 0)),
            pl.BlockSpec((1, n * part), lambda i: (0, 0)),
        ]
        + [spec for _, spec in shared],
        out_specs=[
            pl.BlockSpec((1, L, n * part), lambda i: (i, 0, 0)),
            pl.BlockSpec((8, 2 * L), lambda i: (i, 0)),
        ],
        out_shape=[
            jax.ShapeDtypeStruct((4, L, n * part), F32),
            jax.ShapeDtypeStruct((32, 2 * L), F32),
        ],
        compiler_params=params(32),
        cost_estimate=SMALL,
    )(scal, xt, xt, tgt, gain, *[a for a, _ in shared])


def score_body(width, masks, ids, own, *refs):
    recvs = refs[: len(masks)]
    total_out, margin_out = refs[len(masks) :]
    lane = lax.broadcasted_iota(jnp.int32, (8, 128), 1)
    margins = jnp.zeros((8, 128), F32)
    for p in range(4):
        total = own[8 * p : 8 * p + 8]
        for recv, m in zip(recvs, masks):
            q = ORD.index(ORD[p] ^ m)
            total = total + recv[8 * q : 8 * q + 8]
        total_out[8 * p : 8 * p + 8] = total
        inverse = lax.rsqrt(total[0:1] * (1.0 / width) + norm_eps)
        score = total[1:2] * inverse * (width**-0.5)
        score = jnp.where(total[2:3] > 0.5, score, 0.0)
        margin = jnp.sum(score[:, L:], 1, keepdims=True) - jnp.sum(score[:, :L], 1, keepdims=True)
        margins = margins + jnp.where(lane == ids[p], margin, 0.0)
    margin_out[...] = margins


def scores(ids, own, recvs, masks, width):
    return pl.pallas_call(
        functools.partial(score_body, width, masks),
        in_specs=[smem()] + [whole_vmem()] * (1 + len(recvs)),
        out_specs=[whole_vmem()] * 2,
        out_shape=[jax.ShapeDtypeStruct(own.shape, F32), jax.ShapeDtypeStruct((8, 128), F32)],
        cost_estimate=SMALL,
    )(ids, own, *recvs)


def turn(i):
    return (2 * i + 1) % 5


def grad_body(width, seqs, n_vec, ids, pairs, total, hidden, tgt, gain, *refs):
    vecs = refs[:n_vec]
    grad_out, loss_out, slope = refs[n_vec:]
    lane = lax.broadcasted_iota(jnp.int32, (8, 128), 1)

    @pl.when(pl.program_id(0) == 0)
    def _():
        margin = vecs[0][...]
        for v in vecs[1:]:
            margin = margin + v[...]
        logits = jnp.zeros((8, 128), F32)
        for i in range(seqs // 2):
            sign = jnp.where(lane == pairs[2 * i], 1.0, 0.0) - jnp.where(
                lane == pairs[2 * i + 1], 1.0, 0.0
            )
            logit = dpo_beta * jnp.sum(margin * sign, 1, keepdims=True)
            logits = logits + jnp.where(lane == i, logit, 0.0)
        soft = jnp.maximum(-logits, 0.0) + jnp.log1p(jnp.exp(-jnp.abs(logits)))
        used = lane < seqs // 2
        loss = jnp.sum(jnp.where(used, soft, 0.0), 1, keepdims=True)
        loss_out[...] = jnp.broadcast_to(loss, (8, 128))
        slopes = jnp.where(used, -dpo_beta / (1.0 + jnp.exp(logits)), 0.0)
        gradient = jnp.zeros((8, 128), F32)
        for i in range(seqs // 2):
            each = jnp.sum(jnp.where(lane == i, slopes, 0.0), 1, keepdims=True)
            sign = jnp.where(lane == pairs[2 * i], 1.0, 0.0) - jnp.where(
                lane == pairs[2 * i + 1], 1.0, 0.0
            )
            gradient = gradient + each * sign
        slope[...] = gradient * loss_scale

    mine = lane == ids[turn(pl.program_id(0))]
    seq = jnp.sum(jnp.where(mine, slope[...], 0.0), 1, keepdims=True)[:1]
    rows = total[:, L:]
    token = jnp.where(rows[2:3] > 0.5, seq, 0.0) * (width**-0.5)
    inverse = lax.rsqrt(rows[0:1] * (1.0 / width) + norm_eps)
    first = inverse * token
    second = inverse * inverse * inverse * (token * rows[1:2] * (1.0 / width))
    first = jnp.broadcast_to(first, (L, L)).T
    second = jnp.broadcast_to(second, (L, L)).T
    for s in range(hidden.shape[2] // HEAD_SIZE):
        cols = slice(s * HEAD_SIZE, (s + 1) * HEAD_SIZE)
        weighted = gain[:, cols] * tgt[0, :, cols].astype(F32)
        grad_out[0, :, cols] = (first * weighted - second * hidden[0, :, cols]).astype(BF16)


def grad_hidden(ids, pairs, total, hidden, tgt, gain, vecs, width):
    n = hidden.shape[2]
    seqs = pairs.shape[0]
    return pl.pallas_call(
        functools.partial(grad_body, width, seqs, len(vecs)),
        grid=(4,),
        in_specs=[
            smem(),
            smem(),
            pl.BlockSpec((8, 2 * L), lambda i: (turn(i), 0)),
            pl.BlockSpec((1, L, n), lambda i: (turn(i), 0, 0)),
            pl.BlockSpec((1, L, n), lambda i: (turn(i), 0, 0)),
            pl.BlockSpec((1, n), lambda i: (0, 0)),
        ]
        + [pl.BlockSpec((8, 128), lambda i: (0, 0)) for _ in vecs],
        out_specs=[
            pl.BlockSpec((1, L, n), lambda i: (i, 0, 0)),
            pl.BlockSpec((8, 128), lambda i: (0, 0)),
        ],
        out_shape=[
            jax.ShapeDtypeStruct((4, L, n), BF16),
            jax.ShapeDtypeStruct((8, 128), F32),
        ],
        scratch_shapes=[pltpu.VMEM((8, 128), F32)],
        compiler_params=params(32),
        cost_estimate=SMALL,
    )(ids, pairs, total, hidden, tgt, gain, *vecs)


def per_device(
    fsdp_size,
    tensor_size,
    ref_states,
    pol_states,
    target_rows,
    norm_gain,
    wq,
    wk,
    wv,
    wo,
    qa,
    qo,
    va,
    vo,
    prompt_length,
    pairs,
):
    tokens, width = ref_states.shape
    groups = fsdp_size // 4
    near_z = fsdp_size // 4
    bits = []
    bit = 2
    while bit < fsdp_size:
        if bit != near_z:
            bits.append(bit)
        bit *= 2
    split = 2 if tensor_size == 2 and fsdp_size == 16 else 1
    kv_local = wk.shape[1] // HEAD_SIZE
    depth = wq.shape[0]
    part = depth // split
    rank = qa.shape[1]
    me = lax.axis_index("fsdp")
    x = lax.axis_index("tensor")
    side = x if split == 2 else 0

    def tmask(d):
        return (d & 1) | ((d >> 1) * near_z)

    def gmask(k):
        return sum(bit for i, bit in enumerate(bits) if (k >> i) & 1)

    def move(value, mask):
        return lax.ppermute(value, "fsdp", [(i, i ^ mask) for i in range(fsdp_size)])

    def swap_x(value):
        return lax.ppermute(value, "tensor", [(0, 1), (1, 0)])

    def move_both(value, mask, flip):
        pairs_list = [
            (2 * i + j, 2 * (i ^ mask) + (j ^ flip)) for i in range(fsdp_size) for j in range(2)
        ]
        return lax.ppermute(value, ("fsdp", "tensor"), pairs_list)

    def after(value, *others):
        return lax.optimization_barrier((value, *others))[0]

    wide = groups == 4 and split == 2
    heads = wo.shape[0]

    def shard_of(j, *queue):
        q, k, v = wq, wk, wv
        if queue:
            q, k, v = lax.optimization_barrier((wq, wk, wv, *queue))[:3]
        pieces = [
            q[:, j * QCOLS : (j + 1) * QCOLS],
            k[:, j * HEAD_SIZE : (j + 1) * HEAD_SIZE],
            v[:, j * HEAD_SIZE : (j + 1) * HEAD_SIZE],
        ]
        return jnp.concatenate(pieces, 1)

    def gather(shard):
        return [shard] + [move(shard, gmask(k)) for k in range(1, groups)]

    if wide:
        over_y, over_z = gmask(1), gmask(2)
        shards = [shard_of(0)]
        zs = [move(shards[0], over_z)]
        ys = [move(shards[0], over_y)]
        corners = []

    parts = groups * split
    idx = []
    for d in range(4):
        for k in range(groups):
            for h in range(split):
                idx.append((me ^ tmask(d) ^ gmask(k)) * split + h)
    for d in range(4):
        for k in range(groups):
            idx.append((me ^ tmask(d) ^ gmask(k)) * split + side)
    idx.append(x)
    idx = jnp.stack(idx).astype(jnp.int32)
    if wide:
        idx = after(idx, shards[0])
    prepared = prep(
        idx,
        ref_states,
        pol_states,
        target_rows,
        norm_gain.astype(F32).reshape(1, width),
        parts,
        part,
        split,
    )
    xs, ts, gain = prepared[:4], prepared[4:8], prepared[8]
    near = move(xs[1], 1)
    far = [move(xs[2], near_z)]
    far.append(move(xs[3], near_z | 1))

    if split == 2:
        other = [swap_x(a) for a in far]
        far = [
            [jnp.where(x == which, a[0], b[0]) for which in range(2)] for a, b in zip(far, other)
        ]
    states = jnp.concatenate(
        [
            *(xs[0][0], far[0][0], xs[0][1], far[0][1]),
            *(near[0], far[1][0], near[1], far[1][1]),
        ],
        0,
    )

    low = dot(pol_states, jnp.concatenate([qa, va], 1)).astype(BF16)
    cosine, sine = rope_tables(L, HEAD_SIZE)

    def own_columns(at, piece, *queue):
        return lax.dynamic_slice(
            after(wo, *queue), (piece * (heads // 2), at * part), (heads // 2, part)
        )

    def own_piece(step, *queue):
        at = (1 - x) if step < 2 else x
        return lax.dynamic_slice(
            after(wo, *queue), ((step % 2) * (heads // 2), at * part), (heads // 2, part)
        )

    def next_shard(j, *more):
        early = zs[j - 2 :][:1] if j >= 2 else []
        shards.append(
            shard_of(j, *early) if j < kv_local else own_piece(j - kv_local, *early)
        )
        queue = (zs[j - 1], ys[j - 1], *more)
        ys.append(move(after(shards[j], *queue), over_y))
        zs.append(move(after(shards[j], *queue), over_z))
        corners.append(move(after(*queue), over_y))

    saved = []
    parts_mixed = [[], [], [], []]
    if wide:
        next_shard(1)
    for j in range(kv_local):
        if wide:
            next_shard(j + 2)
            ws = [shards[j], ys[j], zs[j], corners[j]]
            states = after(states, zs[j + 1], ys[j + 1])
        else:
            ws = gather(shard_of(j))
        sends = mm(states, 1, ws, BF16)
        came = [move(send, 1) for send in sends]
        keeps = mm(states, 0, ws, F32)
        ends, overs = [], []
        for which in range(2):
            over = (keeps[which][L:] + came[which][L:].astype(F32)).astype(BF16)
            overs.append(over)
            r2 = move(over, near_z)
            result = attend(
                which == 1, keeps[which], came[which], r2, low, qo, vo, j, cosine, sine
            )
            saved += result[1:]
            pair = jnp.concatenate([result[0], move(result[0], near_z)], 0)
            if wide:
                pair = after(pair, zs[j + 2], ys[j + 2])
            parts_mixed[which].append(pair)
            ends.append(move(pair, 1))
            parts_mixed[2 + which].append(ends[-1])
        states = after(states, *ends)
    last = ends[-1]

    keeps, recvs = [], []
    if wide:
        for step in (2, 3):
            next_shard(kv_local + step, *overs)
        corners.append(move(after(zs[-1], ys[-1]), over_y))
        pieces = [shards[kv_local:], ys[kv_local:], zs[kv_local:], corners[kv_local:]]
        wo_send = [a[:2] for a in pieces]
        wo_keep = [a[2:] for a in pieces]
        recvs.append(swap_x(out_mm(parts_mixed, wo_send[:2])))
        recvs.append(swap_x(out_mm(parts_mixed, wo_send[2:])))
        keeps.append(out_mm(parts_mixed, wo_keep[:3]))
        keeps.append(out_mm(parts_mixed, wo_keep[3:]))
    else:
        wo_keep = [[w] for w in gather(wo)]
        product = out_mm(parts_mixed, wo_keep)
        if tensor_size > 1:
            product = lax.psum(product, "tensor")
        keeps.append(product)
        recvs.append(jnp.zeros_like(product))

    ts = [ts[0]] + list(lax.optimization_barrier((*ts[1:], last))[:3])
    targets = [ts[0]] + [move(ts[d], tmask(d)) for d in (1, 2, 3)]
    tgt = jnp.stack([targets[d] for d in ORD])

    scal = jnp.stack([jnp.asarray(side, jnp.int32), prompt_length[0].astype(jnp.int32)])
    hidden, stats = norm_stats(scal, states, tgt, gain, keeps, recvs, split)
    masks, got = [], []
    for flip in range(split):
        for d in range(4):
            if d or flip:
                masks.append(d)
                if split == 2:
                    got.append(move_both(stats, tmask(d), flip))
                else:
                    got.append(move(stats, tmask(d)))
    ids = jnp.stack([me ^ tmask(d) for d in ORD]).astype(jnp.int32)
    total, margin = scores(ids, stats, got, tuple(masks), width)
    vecs = [margin] + [move(margin, gmask(k)) for k in range(1, groups)]
    grad, loss = grad_hidden(ids, pairs, total, hidden, tgt, gain, vecs, width)

    grad_rows = grad.reshape(4 * L, -1)
    other = None
    for half in range(2):
        if split == 2:
            leaving = grad_rows[2 * L * half : 2 * L * (half + 1)]
            other = swap_x(leaving if half == 0 else after(leaving, other))
            acc = back_mm(grad_rows, half, wo_keep, None)
            if half == 1:
                other = after(other, over)
            keep, send = back_mm(other, None, wo_send, acc)
        else:
            acc = jnp.zeros((2 * L, heads), F32)
            keep, send = back_mm(grad_rows, half, wo_keep, acc)
        rs = move(send, 1)
        if half == 0:
            over = (keep + rs.astype(F32)).astype(BF16)
            r2 = move(over, near_z)
    outer, mid = attend_back(keep, rs, r2, low, qo, vo, cosine, sine, saved)

    rows_each = width // tensor_size
    if split == 2:
        mids = [mid, swap_x(mid)]
    elif tensor_size == 1:
        mids = [mid]
    else:
        gathered = lax.all_gather(mid, "tensor", axis=0, tiled=False)
        mids = [gathered[i] for i in range(tensor_size)]
    scal = jnp.stack([x, me & 1]).astype(jnp.int32)
    away, current = adapter_products(scal, pol_states, mids, outer, rows_each)
    current = current + move(away, 1).astype(F32)
    top = fsdp_size // 2
    g = (me // 2) % groups
    rows = current.shape[0] // groups
    pieces = [
        lax.dynamic_slice_in_dim(current, (g ^ k) * rows, rows, 0) for k in range(groups)
    ]
    current = pieces[0]
    for k in range(1, groups):
        current = current + move(pieces[k].astype(BF16), k << 1).astype(F32)
    rows //= 2
    high = me // top
    away = lax.dynamic_slice_in_dim(current, (1 - high) * rows, rows, 0).astype(BF16)
    current = lax.dynamic_slice_in_dim(current, high * rows, rows, 0)
    current = (current + move(away, top).astype(F32)).astype(BF16)

    def join(bit, own, other):
        return jnp.where(
            bit == 0, jnp.concatenate([own, other], 0), jnp.concatenate([other, own], 0)
        )

    current = join(high, current, move(current, top))
    pieces = [current] + [move(current, k << 1) for k in range(1, groups)]
    step = 1
    while step < groups:
        odd = (g & step) != 0
        pieces = [jnp.where(odd, pieces[k ^ step], pieces[k]) for k in range(groups)]
        step *= 2
    current = jnp.concatenate(pieces, 0)
    current = join(me & 1, current, move(current, 1)).astype(F32)
    a_grads = current[:, :rows_each]
    outer = current[:, rows_each:]
    outer = jnp.concatenate([outer[:rank], outer[rank:]], 1)
    return (
        loss[0, 0],
        a_grads[:rank].T,
        outer[:, : qo.shape[1]],
        a_grads[rank:].T,
        outer[:, qo.shape[1] : qo.shape[1] + vo.shape[1]],
    )


def solution(mesh):
    in_specs = (
        P("fsdp", None),
        P("fsdp", None),
        P("fsdp", None),
        P(),
        P("fsdp", "tensor"),
        P("fsdp", "tensor"),
        P("fsdp", "tensor"),
        P("tensor", "fsdp"),
        P(),
        P(None, "tensor"),
        P(),
        P(None, "tensor"),
        P("fsdp"),
        P(),
    )
    out_specs = (P(), P("tensor", None), P(None, "tensor"), P("tensor", None), P(None, "tensor"))
    body = functools.partial(per_device, mesh.shape["fsdp"], mesh.shape["tensor"])
    return jax.shard_map(body, mesh=mesh, in_specs=in_specs, out_specs=out_specs, check_vma=False)
```

```python
import functools

import jax
import jax.numpy as jnp
from jax import lax
from jax.experimental import pallas as pl
from jax.experimental.pallas import tpu as pltpu
from jax.sharding import PartitionSpec as P

QUERY_HEADS = 32
KEY_VALUE_HEADS = 8
HEAD_SIZE = 128
L = 128
GROUP = QUERY_HEADS // KEY_VALUE_HEADS
QCOLS = GROUP * HEAD_SIZE

adapter_scale = 0.5
dpo_beta = 0.1
loss_scale = 256.0
rope_base = 500000.0
norm_eps = 1e-05

F32 = jnp.float32
BF16 = jnp.bfloat16
ORD = (0, 2, 1, 3)
MB = 1 << 20
SMALL = pl.CostEstimate(flops=1, bytes_accessed=1, transcendentals=0)


def rope_tables(length, head_dim):
    half_dim = head_dim // 2
    exponent = jnp.arange(half_dim, dtype=F32) * (2.0 / head_dim)
    inverse = jnp.power(F32(rope_base), -exponent)
    angles = jnp.arange(length, dtype=F32)[:, None] * inverse[None, :]
    cosine = jnp.concatenate([jnp.cos(angles), jnp.cos(angles)], 1)
    sine = jnp.concatenate([-jnp.sin(angles), jnp.sin(angles)], 1)
    return cosine, sine


def dot(a, b, dims=((1,), (0,))):
    return lax.dot_general(a, b, (dims, ((), ())), preferred_element_type=F32)


def params(limit_mb):
    return pltpu.CompilerParams(vmem_limit_bytes=limit_mb * MB)


def smem():
    return pl.BlockSpec(memory_space=pltpu.SMEM)


def full(a):
    return pl.BlockSpec(a.shape, lambda i: (0,) * len(a.shape))


def prep_body(parts, part, split, idx, ref, pol, tgt, gain, *outs):
    x0, x1, x2, x3, t0, t1, t2, t3, go = outs
    groups = parts // split
    for d, (xo, to) in enumerate(((x0, t0), (x1, t1), (x2, t2), (x3, t3))):
        for j in range(parts):
            src = pl.ds(pl.multiple_of(idx[d * parts + j] * part, part), part)
            cols = slice(j * part, (j + 1) * part)
            if xo.shape[0] == 2:
                xo[0, :, cols] = ref[:, src]
                xo[1, :, cols] = pol[:, src]
            else:
                @pl.when(idx[4 * parts + 4 * groups] == 0)
                def _():
                    xo[0, :, cols] = ref[:, src]

                @pl.when(idx[4 * parts + 4 * groups] != 0)
                def _():
                    xo[0, :, cols] = pol[:, src]

        for j in range(groups):
            at = idx[4 * parts + d * groups + j] * part
            src = pl.ds(pl.multiple_of(at, part), part)
            to[:, j * part : (j + 1) * part] = tgt[:, src]
            if d == 0:
                go[:, j * part : (j + 1) * part] = gain[:, src]


def prep(idx, ref, pol, tgt, gain, parts, part, split):
    tokens = ref.shape[0]
    xs = lambda n: jax.ShapeDtypeStruct((n, tokens, parts * part), BF16)
    far = 1 if split == 2 else 2
    width = parts // split * part
    shapes = [xs(2), xs(2), xs(far), xs(far)]
    shapes += [jax.ShapeDtypeStruct((tokens, width), BF16)] * 4
    shapes += [jax.ShapeDtypeStruct((1, width), F32)]
    return pl.pallas_call(
        functools.partial(prep_body, parts, part, split),
        grid=(1,),
        in_specs=[smem()] + [full(a) for a in (ref, pol, tgt, gain)],
        out_specs=[full(a) for a in shapes],
        out_shape=shapes,
        compiler_params=params(32),
        cost_estimate=SMALL,
    )(idx, ref, pol, tgt, gain)


def tile_of(cols):
    for tile in (256, 128):
        if cols % tile == 0:
            return tile
    return cols


def mm_body(count, x_ref, *refs):
    ws, outs = refs[:count], refs[count:]
    total = None
    at = 0
    for w in ws:
        depth = w.shape[0]
        term = dot(x_ref[:, at : at + depth], w[...])
        total = term if total is None else total + term
        at += depth
    rows = total.shape[0] // 2
    for i, out_ref in enumerate(outs):
        out_ref[...] = total[i * rows : (i + 1) * rows].astype(out_ref.dtype)


def mm(x, half, ws, out_dtype):
    rows, depth = x.shape[0] // 2, x.shape[1]
    cols = ws[0].shape[1]
    tile = tile_of(cols)
    return pl.pallas_call(
        functools.partial(mm_body, len(ws)),
        grid=(cols // tile,),
        in_specs=[pl.BlockSpec((rows, depth), lambda i: (half, 0))]
        + [pl.BlockSpec((w.shape[0], tile), lambda i: (0, i)) for w in ws],
        out_specs=[pl.BlockSpec((rows // 2, tile), lambda i: (0, i))] * 2,
        out_shape=[jax.ShapeDtypeStruct((rows // 2, cols), out_dtype)] * 2,
        compiler_params=params(32),
        cost_estimate=SMALL,
    )(x, *ws)


def out_body(n, row_parts, counts, *refs):
    ws = refs[row_parts * n : -2]
    out_ref, total = refs[-2:]
    for j in range(n):
        x = jnp.concatenate([refs[p * n + j][...] for p in range(row_parts)], 0)
        depth = x.shape[1]
        at = 0
        for k, count in enumerate(counts):
            row = j * depth
            piece = at
            while row >= ws[piece].shape[0]:
                row -= ws[piece].shape[0]
                piece += 1
            at += count
            term = dot(x, ws[piece][row : row + depth])
            if j:
                term = term + total[k]
            if j == n - 1:
                out_ref[k] = term.astype(BF16)
            else:
                total[k] = term


def out_mm(parts, ws):
    n = len(parts[0])
    rows = sum(part[0].shape[0] for part in parts)
    cols = ws[0][0].shape[1]
    flat = [piece for w in ws for piece in w]
    inputs = [a for part in parts for a in part] + flat
    out_shape = jax.ShapeDtypeStruct((len(ws), rows, cols), BF16)
    return pl.pallas_call(
        functools.partial(out_body, n, len(parts), tuple(len(w) for w in ws)),
        grid=(1,),
        in_specs=[full(a) for a in inputs],
        out_specs=full(out_shape),
        out_shape=out_shape,
        scratch_shapes=[pltpu.VMEM(out_shape.shape, F32)],
        compiler_params=params(40),
        cost_estimate=SMALL,
    )(*inputs)


def back_body(counts, part, has_acc, x_ref, *refs):
    total = None
    at = 0
    for j, count in enumerate(counts):
        w = refs[at][...]
        if count == 2:
            w = jnp.where(pl.program_id(0) < pl.num_programs(0) // 2, w, refs[at + 1][...])
        at += count
        term = dot(x_ref[:, j * part : (j + 1) * part], w, ((1,), (1,)))
        total = term if total is None else total + term
    refs = refs[at:]
    if has_acc:
        total = total + refs[0][...]
        keep, send = refs[1:]
        half = total.shape[0] // 2
        keep[...] = total[:half]
        send[...] = total[half:].astype(send.dtype)
    else:
        refs[0][...] = total


def back_mm(x, half, ws, acc):
    rows = x.shape[0] // (1 if half is None else 2)
    depth = x.shape[1]
    part = ws[0][0].shape[1]
    heads = sum(piece.shape[0] for piece in ws[0])
    tile = min(512, heads)
    steps = heads // tile
    has_acc = acc is not None
    row = half or 0
    in_specs = [pl.BlockSpec((rows, depth), lambda i: (row, 0))]
    for w in ws:
        if len(w) == 1:
            in_specs.append(pl.BlockSpec((tile, part), lambda i: (i, 0)))
        else:
            in_specs.append(pl.BlockSpec((tile, part), lambda i: (jnp.minimum(i, steps // 2 - 1), 0)))
            in_specs.append(pl.BlockSpec((tile, part), lambda i: (jnp.maximum(i - steps // 2, 0), 0)))
    args = [x] + [piece for w in ws for piece in w]
    if has_acc:
        in_specs.append(pl.BlockSpec((rows, tile), lambda i: (0, i)))
        args.append(acc)
        out_specs = [pl.BlockSpec((rows // 2, tile), lambda i: (0, i))] * 2
        out_shape = [
            jax.ShapeDtypeStruct((rows // 2, heads), F32),
            jax.ShapeDtypeStruct((rows // 2, heads), BF16),
        ]
    else:
        out_specs = pl.BlockSpec((rows, tile), lambda i: (0, i))
        out_shape = jax.ShapeDtypeStruct((rows, heads), F32)
    return pl.pallas_call(
        functools.partial(back_body, tuple(len(w) for w in ws), part, has_acc),
        grid=(steps,),
        in_specs=in_specs,
        out_specs=out_specs,
        out_shape=out_shape,
        compiler_params=params(32),
        cost_estimate=SMALL,
    )(*args)


def causal(rows):
    at = lax.broadcasted_iota(jnp.int32, (rows, L), 0) % L
    return at >= lax.broadcasted_iota(jnp.int32, (rows, L), 1)


def probabilities(q4, keys):
    scores = dot(q4, keys, ((1,), (1,))) * (HEAD_SIZE**-0.5)
    weights = jnp.where(causal(q4.shape[0]), jnp.exp(scores), 0.0)
    return weights / jnp.sum(weights, -1, keepdims=True)


def stack_heads(values):
    return jnp.concatenate(
        [values[:, h * HEAD_SIZE : (h + 1) * HEAD_SIZE] for h in range(GROUP)], 0
    )


def attend_body(adapted, keep, rs, r2, low, qo, vo, cos_ref, sin_ref, mixed, *saved):
    cosine = cos_ref[...]
    sine = sin_ref[...]
    pre = keep[...] + rs[...].astype(F32) + r2[...].astype(F32)
    rank = qo.shape[0]
    q_pre = pre[:, :QCOLS]
    k_pre = pre[:, QCOLS : QCOLS + HEAD_SIZE]
    v_pre = pre[:, QCOLS + HEAD_SIZE :]
    if adapted:
        q_pre = q_pre + adapter_scale * dot(low[:, :rank], qo[...])
        v_pre = v_pre + adapter_scale * dot(low[:, rank:], vo[...])
    cos4 = jnp.concatenate([cosine] * GROUP, 0)
    sin4 = jnp.concatenate([sine] * GROUP, 0)
    q4 = stack_heads(q_pre)
    q4 = (q4 * cos4 + pltpu.roll(q4, HEAD_SIZE // 2, 1) * sin4).astype(BF16)
    keys = (k_pre * cosine + pltpu.roll(k_pre, HEAD_SIZE // 2, 1) * sine).astype(BF16)
    values = v_pre.astype(BF16)
    rounded = probabilities(q4, keys).astype(BF16)
    out = dot(rounded, values).astype(BF16)
    for h in range(GROUP):
        cols = slice(h * HEAD_SIZE, (h + 1) * HEAD_SIZE)
        mixed[:, cols] = out[h * L : (h + 1) * L]
        if saved:
            saved[0][:, cols] = q4[h * L : (h + 1) * L]
    if saved:
        saved[0][:, QCOLS : QCOLS + HEAD_SIZE] = keys
        saved[0][:, QCOLS + HEAD_SIZE :] = values


def attend(adapted, keep, rs, r2, low, qo, vo, group, cosine, sine):
    each = QCOLS + 2 * HEAD_SIZE
    rank = qo.shape[0]
    top = lambda a: pl.BlockSpec((L, a.shape[1]), lambda i: (0, 0))
    return pl.pallas_call(
        functools.partial(attend_body, adapted),
        grid=(1,),
        in_specs=[
            top(keep),
            top(rs),
            top(r2),
            top(low),
            pl.BlockSpec((rank, QCOLS), lambda i: (0, group)),
            pl.BlockSpec((rank, HEAD_SIZE), lambda i: (0, group)),
            top(cosine),
            top(sine),
        ],
        out_specs=[pl.BlockSpec((L, w), lambda i: (0, 0)) for w in (QCOLS, each)[: 1 + adapted]],
        out_shape=[jax.ShapeDtypeStruct((L, w), BF16) for w in (QCOLS, each)[: 1 + adapted]],
        compiler_params=params(32),
        cost_estimate=SMALL,
    )(keep, rs, r2, low, qo, vo, cosine, sine)


def outer_place(block, rank, kv):
    wide = (kv * (GROUP + 1) + 1) // 2
    return (block // wide) * rank, (block % wide) * HEAD_SIZE, wide


def attend_back_body(kv, splits, keep, rs, r2, low, qo, vo, cos_ref, sin_ref, *refs):
    saved = refs[:splits]
    outer, mid = refs[splits:]
    rank = qo.shape[0]
    each = QCOLS + 2 * HEAD_SIZE
    cos4 = jnp.concatenate([cos_ref[...]] * GROUP, 0)
    sin4 = jnp.concatenate([sin_ref[...]] * GROUP, 0)
    low_q = low[:, :rank]
    low_v = low[:, rank:]
    q_mid = jnp.zeros((L, rank), F32)
    v_mid = jnp.zeros((L, rank), F32)

    def put(block, value):
        row, col, _ = outer_place(block, rank, kv)
        outer[row : row + rank, col : col + HEAD_SIZE] = adapter_scale * value

    if (kv * (GROUP + 1)) % 2:
        put(kv * (GROUP + 1), jnp.zeros((rank, HEAD_SIZE), F32))
    for j in range(kv):
        cols = slice(j * QCOLS, (j + 1) * QCOLS)
        at = (j % (kv // splits)) * each
        kept = saved[j // (kv // splits)]
        grad = keep[:, cols] + rs[:, cols].astype(F32) + r2[:, cols].astype(F32)
        grad4 = stack_heads(grad.astype(BF16))
        q4 = stack_heads(kept[:, at : at + QCOLS])
        keys = kept[:, at + QCOLS : at + QCOLS + HEAD_SIZE]
        values = kept[:, at + QCOLS + HEAD_SIZE : at + each]
        prob = probabilities(q4, keys)
        grad_prob = dot(grad4, values, ((1,), (1,)))
        grad_values = dot(prob.astype(BF16), grad4, ((0,), (0,))).astype(BF16)
        inner = jnp.sum(grad_prob * prob, -1, keepdims=True)
        grad_scores = (prob * (grad_prob - inner) * (HEAD_SIZE**-0.5)).astype(BF16)
        grad_query = dot(grad_scores, keys)
        back4 = (grad_query * cos4 - pltpu.roll(grad_query, HEAD_SIZE // 2, 1) * sin4).astype(BF16)
        for h in range(GROUP):
            at = j * GROUP + h
            back = back4[h * L : (h + 1) * L]
            put(at, dot(low_q, back, ((0,), (0,))))
            q_mid += dot(back, qo[:, at * HEAD_SIZE : (at + 1) * HEAD_SIZE], ((1,), (1,)))
        put(kv * GROUP + j, dot(low_v, grad_values, ((0,), (0,))))
        v_mid += dot(grad_values, vo[:, j * HEAD_SIZE : (j + 1) * HEAD_SIZE], ((1,), (1,)))
    mid[:, :rank] = (adapter_scale * q_mid).astype(BF16)
    mid[:, rank:] = (adapter_scale * v_mid).astype(BF16)


def attend_back(keep, rs, r2, low, qo, vo, cosine, sine, saved):
    rank = qo.shape[0]
    kv = vo.shape[1] // HEAD_SIZE
    wide = outer_place(0, rank, kv)[2]
    inputs = (keep, rs, r2, low, qo, vo, cosine, sine, *saved)
    shapes = [
        jax.ShapeDtypeStruct((2 * rank, wide * HEAD_SIZE), F32),
        jax.ShapeDtypeStruct((L, 2 * rank), BF16),
    ]
    return pl.pallas_call(
        functools.partial(attend_back_body, kv, len(saved)),
        grid=(1,),
        in_specs=[full(a) for a in inputs],
        out_specs=[full(a) for a in shapes],
        out_shape=shapes,
        compiler_params=params(32),
        cost_estimate=SMALL,
    )(*inputs)


def adapter_body(n, rows_each, scal, states, outer, *refs):
    mids = refs[:n]
    away, stay = refs[n:]
    src = pl.ds(pl.multiple_of(scal[0] * rows_each, rows_each), rows_each)
    own = states[:, src]
    total = None
    for mid in mids:
        term = dot(mid[...], own, ((0,), (0,)))
        total = term if total is None else total + term
    half = total.shape[0] // 2
    for low in range(2):
        rows = slice(low * half, (low + 1) * half)

        @pl.when(scal[1] == low)
        def _():
            stay[:, :rows_each] = total[rows]
            stay[:, rows_each:] = outer[rows]

        @pl.when(scal[1] != low)
        def _():
            away[:, :rows_each] = total[rows].astype(BF16)
            away[:, rows_each:] = outer[rows].astype(BF16)


def adapter_products(scal, states, mids, outer, rows_each):
    half = outer.shape[0] // 2
    cols = rows_each + outer.shape[1]
    shapes = [jax.ShapeDtypeStruct((half, cols), BF16), jax.ShapeDtypeStruct((half, cols), F32)]
    return pl.pallas_call(
        functools.partial(adapter_body, len(mids), rows_each),
        grid=(1,),
        in_specs=[smem()] + [full(a) for a in (states, outer, *mids)],
        out_specs=[full(a) for a in shapes],
        out_shape=shapes,
        compiler_params=params(32),
        cost_estimate=SMALL,
    )(scal, states, outer, *mids)


def stats_body(counts, part, split, scal, xt_ref, xt_pol, tgt, gain, *refs):
    refs = list(refs)
    sums = []
    hidden_out, stats = refs[-2:]
    for which in range(2):
        xt = (xt_ref, xt_pol)[which]
        count = sum(counts)
        keeps = [r[i] for r in refs[: counts[0]] for i in range(r.shape[0])]
        recvs = [r[i] for r in refs[counts[0] : count] for i in range(r.shape[0])]
        refs = refs[count:]
        squares = jnp.zeros((L, HEAD_SIZE), F32)
        products = jnp.zeros((L, HEAD_SIZE), F32)
        for j, (keep, recv) in enumerate(zip(keeps, recvs)):
            src = pl.ds(pl.multiple_of((j * split + scal[0]) * part, part), part)
            hidden = xt[:, src].astype(F32) + keep.astype(F32) + recv.astype(F32)
            cols = slice(j * part, (j + 1) * part)
            if which == 1:
                hidden_out[0, :, cols] = hidden
            product = hidden * (gain[:, cols] * tgt[0, :, cols].astype(F32))
            square = hidden * hidden
            for s in range(part // HEAD_SIZE):
                lanes = slice(s * HEAD_SIZE, (s + 1) * HEAD_SIZE)
                squares += square[:, lanes]
                products += product[:, lanes]
        sums.append(
            [
                jnp.broadcast_to(jnp.sum(v, 1, keepdims=True), v.shape).T[:1]
                for v in (squares, products)
            ]
        )
    at = lax.broadcasted_iota(jnp.int32, (1, 2 * L), 1) % L
    own = (at >= scal[1]) & (pl.program_id(0) == 0)
    live = jnp.where(own, 1.0, 0.0).astype(F32)
    both = [jnp.concatenate([sums[0][i], sums[1][i]], 1) for i in range(2)]
    stats[...] = jnp.concatenate([*both, live, jnp.zeros((5, 2 * L), F32)], 0)


def norm_stats(scal, xt, tgt, gain, keeps, recvs, split):
    n = sum(a.shape[0] for a in keeps)
    part = keeps[0].shape[2]
    shared = []
    for which in range(2):
        at = functools.partial(lambda which, i: (0, 2 * i + which, 0), which)
        for a in (*keeps, *recvs):
            shared.append((a, pl.BlockSpec((a.shape[0], L, part), at)))
    return pl.pallas_call(
        functools.partial(stats_body, (len(keeps), len(recvs)), part, split),
        grid=(4,),
        in_specs=[
            smem(),
            pl.BlockSpec((L, xt.shape[1]), lambda i: ((i // 2) * 4 + i % 2, 0)),
            pl.BlockSpec((L, xt.shape[1]), lambda i: ((i // 2) * 4 + 2 + i % 2, 0)),
            pl.BlockSpec((1, L, n * part), lambda i: (i, 0, 0)),
            pl.BlockSpec((1, n * part), lambda i: (0, 0)),
        ]
        + [spec for _, spec in shared],
        out_specs=[
            pl.BlockSpec((1, L, n * part), lambda i: (i, 0, 0)),
            pl.BlockSpec((8, 2 * L), lambda i: (i, 0)),
        ],
        out_shape=[
            jax.ShapeDtypeStruct((4, L, n * part), F32),
            jax.ShapeDtypeStruct((32, 2 * L), F32),
        ],
        compiler_params=params(32),
        cost_estimate=SMALL,
    )(scal, xt, xt, tgt, gain, *[a for a, _ in shared])


def score_body(width, masks, ids, own, *refs):
    recvs = refs[: len(masks)]
    total_out, margin_out = refs[len(masks) :]
    lane = lax.broadcasted_iota(jnp.int32, (8, 128), 1)
    margins = jnp.zeros((8, 128), F32)
    for p in range(4):
        total = own[8 * p : 8 * p + 8]
        for recv, m in zip(recvs, masks):
            q = ORD.index(ORD[p] ^ m)
            total = total + recv[8 * q : 8 * q + 8]
        total_out[8 * p : 8 * p + 8] = total
        inverse = lax.rsqrt(total[0:1] * (1.0 / width) + norm_eps)
        score = total[1:2] * inverse * (width**-0.5)
        score = jnp.where(total[2:3] > 0.5, score, 0.0)
        margin = jnp.sum(score[:, L:], 1, keepdims=True) - jnp.sum(score[:, :L], 1, keepdims=True)
        margins = margins + jnp.where(lane == ids[p], margin, 0.0)
    margin_out[...] = margins


def scores(ids, own, recvs, masks, width):
    shapes = [jax.ShapeDtypeStruct(own.shape, F32), jax.ShapeDtypeStruct((8, 128), F32)]
    return pl.pallas_call(
        functools.partial(score_body, width, masks),
        grid=(1,),
        in_specs=[smem()] + [full(a) for a in (own, *recvs)],
        out_specs=[full(a) for a in shapes],
        out_shape=shapes,
        cost_estimate=SMALL,
    )(ids, own, *recvs)


def turn(i):
    return (2 * i + 1) % 5


def grad_body(width, seqs, n_vec, ids, pairs, total, hidden, tgt, gain, *refs):
    vecs = refs[:n_vec]
    grad_out, loss_out, slope = refs[n_vec:]
    lane = lax.broadcasted_iota(jnp.int32, (8, 128), 1)

    @pl.when(pl.program_id(0) == 0)
    def _():
        margin = vecs[0][...]
        for v in vecs[1:]:
            margin = margin + v[...]
        logits = jnp.zeros((8, 128), F32)
        for i in range(seqs // 2):
            sign = jnp.where(lane == pairs[2 * i], 1.0, 0.0) - jnp.where(
                lane == pairs[2 * i + 1], 1.0, 0.0
            )
            logit = dpo_beta * jnp.sum(margin * sign, 1, keepdims=True)
            logits = logits + jnp.where(lane == i, logit, 0.0)
        soft = jnp.maximum(-logits, 0.0) + jnp.log1p(jnp.exp(-jnp.abs(logits)))
        used = lane < seqs // 2
        loss = jnp.sum(jnp.where(used, soft, 0.0), 1, keepdims=True)
        loss_out[...] = jnp.broadcast_to(loss, (8, 128))
        slopes = jnp.where(used, -dpo_beta / (1.0 + jnp.exp(logits)), 0.0)
        gradient = jnp.zeros((8, 128), F32)
        for i in range(seqs // 2):
            each = jnp.sum(jnp.where(lane == i, slopes, 0.0), 1, keepdims=True)
            sign = jnp.where(lane == pairs[2 * i], 1.0, 0.0) - jnp.where(
                lane == pairs[2 * i + 1], 1.0, 0.0
            )
            gradient = gradient + each * sign
        slope[...] = gradient * loss_scale

    mine = lane == ids[turn(pl.program_id(0))]
    seq = jnp.sum(jnp.where(mine, slope[...], 0.0), 1, keepdims=True)[:1]
    rows = total[:, L:]
    token = jnp.where(rows[2:3] > 0.5, seq, 0.0) * (width**-0.5)
    inverse = lax.rsqrt(rows[0:1] * (1.0 / width) + norm_eps)
    first = inverse * token
    second = inverse * inverse * inverse * (token * rows[1:2] * (1.0 / width))
    first = jnp.broadcast_to(first, (L, L)).T
    second = jnp.broadcast_to(second, (L, L)).T
    for s in range(hidden.shape[2] // HEAD_SIZE):
        cols = slice(s * HEAD_SIZE, (s + 1) * HEAD_SIZE)
        weighted = gain[:, cols] * tgt[0, :, cols].astype(F32)
        grad_out[0, :, cols] = (first * weighted - second * hidden[0, :, cols]).astype(BF16)


def grad_hidden(ids, pairs, total, hidden, tgt, gain, vecs, width):
    n = hidden.shape[2]
    seqs = pairs.shape[0]
    return pl.pallas_call(
        functools.partial(grad_body, width, seqs, len(vecs)),
        grid=(4,),
        in_specs=[
            smem(),
            smem(),
            pl.BlockSpec((8, 2 * L), lambda i: (turn(i), 0)),
            pl.BlockSpec((1, L, n), lambda i: (turn(i), 0, 0)),
            pl.BlockSpec((1, L, n), lambda i: (turn(i), 0, 0)),
            pl.BlockSpec((1, n), lambda i: (0, 0)),
        ]
        + [pl.BlockSpec((8, 128), lambda i: (0, 0)) for _ in vecs],
        out_specs=[
            pl.BlockSpec((1, L, n), lambda i: (i, 0, 0)),
            pl.BlockSpec((8, 128), lambda i: (0, 0)),
        ],
        out_shape=[
            jax.ShapeDtypeStruct((4, L, n), BF16),
            jax.ShapeDtypeStruct((8, 128), F32),
        ],
        scratch_shapes=[pltpu.VMEM((8, 128), F32)],
        compiler_params=params(32),
        cost_estimate=SMALL,
    )(ids, pairs, total, hidden, tgt, gain, *vecs)


def per_device(
    fsdp_size,
    tensor_size,
    ref_states,
    pol_states,
    target_rows,
    norm_gain,
    wq,
    wk,
    wv,
    wo,
    qa,
    qo,
    va,
    vo,
    prompt_length,
    pairs,
):
    tokens, width = ref_states.shape
    groups = fsdp_size // 4
    near_z = fsdp_size // 4
    bits = []
    bit = 2
    while bit < fsdp_size:
        if bit != near_z:
            bits.append(bit)
        bit *= 2
    split = 2 if tensor_size == 2 and fsdp_size == 16 else 1
    kv_local = wk.shape[1] // HEAD_SIZE
    depth = wq.shape[0]
    part = depth // split
    rank = qa.shape[1]
    me = lax.axis_index("fsdp")
    x = lax.axis_index("tensor")
    side = x if split == 2 else 0

    def tmask(d):
        return (d & 1) | ((d >> 1) * near_z)

    def gmask(k):
        return sum(bit for i, bit in enumerate(bits) if (k >> i) & 1)

    def move(value, mask):
        return lax.ppermute(value, "fsdp", [(i, i ^ mask) for i in range(fsdp_size)])

    def swap_x(value):
        return lax.ppermute(value, "tensor", [(0, 1), (1, 0)])

    def move_both(value, mask, flip):
        pairs_list = [
            (2 * i + j, 2 * (i ^ mask) + (j ^ flip)) for i in range(fsdp_size) for j in range(2)
        ]
        return lax.ppermute(value, ("fsdp", "tensor"), pairs_list)

    def after(value, *others):
        return lax.optimization_barrier((value, *others))[0]

    wide = groups == 4 and split == 2
    heads = wo.shape[0]

    def shard_of(j, *queue):
        q, k, v = wq, wk, wv
        if queue:
            q, k, v = lax.optimization_barrier((wq, wk, wv, *queue))[:3]
        pieces = [
            q[:, j * QCOLS : (j + 1) * QCOLS],
            k[:, j * HEAD_SIZE : (j + 1) * HEAD_SIZE],
            v[:, j * HEAD_SIZE : (j + 1) * HEAD_SIZE],
        ]
        return jnp.concatenate(pieces, 1)

    def gather(shard):
        return [shard] + [move(shard, gmask(k)) for k in range(1, groups)]

    if wide:
        over_y, over_z = gmask(1), gmask(2)
        shards = [shard_of(0)]
        zs = [move(shards[0], over_z)]
        ys = [move(shards[0], over_y)]
        corners = []

    parts = groups * split
    idx = []
    for d in range(4):
        for k in range(groups):
            for h in range(split):
                idx.append((me ^ tmask(d) ^ gmask(k)) * split + h)
    for d in range(4):
        for k in range(groups):
            idx.append((me ^ tmask(d) ^ gmask(k)) * split + side)
    idx.append(x)
    idx = jnp.stack(idx).astype(jnp.int32)
    if wide:
        idx = after(idx, shards[0])
    prepared = prep(
        idx,
        ref_states,
        pol_states,
        target_rows,
        norm_gain.astype(F32).reshape(1, width),
        parts,
        part,
        split,
    )
    xs, ts, gain = prepared[:4], prepared[4:8], prepared[8]
    near = move(xs[1], 1)
    far = [move(xs[2], near_z)]
    far.append(move(xs[3], near_z | 1))

    targets = [ts[0]] + [move(after(ts[d], *far), tmask(d)) for d in (1, 2, 3)]
    if split == 2:
        other = [swap_x(a) for a in far]
        far = [
            [jnp.where(x == which, a[0], b[0]) for which in range(2)] for a, b in zip(far, other)
        ]
    states = jnp.concatenate(
        [
            *(xs[0][0], far[0][0], xs[0][1], far[0][1]),
            *(near[0], far[1][0], near[1], far[1][1]),
        ],
        0,
    )

    states = after(states, *targets[1:])
    tgt = jnp.stack([targets[d] for d in ORD])

    low = dot(pol_states, jnp.concatenate([qa, va], 1)).astype(BF16)
    cosine, sine = rope_tables(L, HEAD_SIZE)

    def own_columns(at, piece, *queue):
        return lax.dynamic_slice(
            after(wo, *queue), (piece * (heads // 2), at * part), (heads // 2, part)
        )

    def own_piece(step, *queue):
        at = (1 - x) if step < 2 else x
        return lax.dynamic_slice(
            after(wo, *queue), ((step % 2) * (heads // 2), at * part), (heads // 2, part)
        )

    def next_shard(j, *more):
        early = zs[j - 2 :][:1] if j >= 2 else []
        shards.append(
            shard_of(j, *early) if j < kv_local else own_piece(j - kv_local, *early)
        )
        queue = (zs[j - 1], ys[j - 1], *more)
        ys.append(move(after(shards[j], *queue), over_y))
        zs.append(move(after(shards[j], *queue), over_z))
        corners.append(move(after(*queue), over_y))

    saved = []
    parts_mixed = [[], [], []]

    def mix(j, keeps, came, sums, *queue):
        results = []
        for which in range(2):
            total = sums[which * L : (which + 1) * L]
            result = attend(
                which == 1, keeps[which], came[which], total, low, qo, vo, j, cosine, sine
            )
            saved.extend(result[1:])
            results.append(result[0])
        result = jnp.concatenate(results, 0)
        return result, move(after(result, *queue) if queue else result, near_z)

    def spread(result, other):
        far = move(jnp.concatenate([result, other], 0), 1)
        for part_mixed, value in zip(parts_mixed, (result, other, far)):
            part_mixed.append(value)
        return far

    if wide:
        next_shard(1)
    before = None
    ends = []
    for j in range(kv_local):
        if wide:
            next_shard(j + 2)
            ws = [shards[j], ys[j], zs[j], corners[j]]
            states = after(states, zs[j + 1], ys[j + 1], corners[j])
        else:
            ws = gather(shard_of(j))
        sends = mm(states, 1, ws, BF16)
        came = [move(send, 1) for send in sends]
        keeps = mm(states, 0, ws, F32)
        over = jnp.concatenate(
            [(keeps[which][L:] + came[which][L:].astype(F32)).astype(BF16) for which in range(2)], 0
        )
        sums = move(over, near_z)
        if before is not None:
            result, other = mix(j - 1, *before, *came, *ends)
            states = after(states, other)
            ends = [spread(result, other)]
        states = after(states, sums)
        before = (keeps, came, sums)
    last = spread(*mix(kv_local - 1, *before, *ends))

    keeps, recvs = [], []
    if wide:
        for step in (2, 3):
            next_shard(kv_local + step, over)
        corners.append(move(after(zs[-1], ys[-1]), over_y))
        pieces = [shards[kv_local:], ys[kv_local:], zs[kv_local:], corners[kv_local:]]
        wo_send = [a[:2] for a in pieces]
        wo_keep = [a[2:] for a in pieces]
        recvs.append(swap_x(out_mm(parts_mixed, wo_send[:2])))
        recvs.append(swap_x(out_mm(parts_mixed, wo_send[2:])))
        keeps.append(out_mm(parts_mixed, wo_keep[:3]))
        keeps.append(out_mm(parts_mixed, wo_keep[3:]))
    else:
        wo_keep = [[w] for w in gather(wo)]
        product = out_mm(parts_mixed, wo_keep)
        if tensor_size > 1:
            product = lax.psum(product, "tensor")
        keeps.append(product)
        recvs.append(jnp.zeros_like(product))

    scal = jnp.stack([jnp.asarray(side, jnp.int32), prompt_length[0].astype(jnp.int32)])
    hidden, stats = norm_stats(scal, states, tgt, gain, keeps, recvs, split)
    masks, got = [], []
    for flip in range(split):
        for d in range(4):
            if d or flip:
                masks.append(d)
                if split == 2:
                    got.append(move_both(stats, tmask(d), flip))
                else:
                    got.append(move(stats, tmask(d)))
    ids = jnp.stack([me ^ tmask(d) for d in ORD]).astype(jnp.int32)
    total, margin = scores(ids, stats, got, tuple(masks), width)
    vecs = [margin] + [move(margin, gmask(k)) for k in range(1, groups)]
    grad, loss = grad_hidden(ids, pairs, total, hidden, tgt, gain, vecs, width)

    grad_rows = grad.reshape(4 * L, -1)
    other = None
    for half in range(2):
        if split == 2:
            leaving = grad_rows[2 * L * half : 2 * L * (half + 1)]
            other = swap_x(leaving if half == 0 else after(leaving, other))
            acc = back_mm(grad_rows, half, wo_keep, None)
            keep, send = back_mm(other, None, wo_send, acc)
        else:
            acc = jnp.zeros((2 * L, heads), F32)
            keep, send = back_mm(grad_rows, half, wo_keep, acc)
        rs = move(send if half == 0 else after(send, r2), 1)
        if half == 0:
            over = (keep + rs.astype(F32)).astype(BF16)
            r2 = move(over, near_z)
    outer, mid = attend_back(keep, rs, r2, low, qo, vo, cosine, sine, saved)

    rows_each = width // tensor_size
    if split == 2:
        mids = [mid, swap_x(mid)]
    elif tensor_size == 1:
        mids = [mid]
    else:
        gathered = lax.all_gather(mid, "tensor", axis=0, tiled=False)
        mids = [gathered[i] for i in range(tensor_size)]
    scal = jnp.stack([x, me & 1]).astype(jnp.int32)
    away, current = adapter_products(scal, pol_states, mids, outer, rows_each)
    current = current + move(away, 1).astype(F32)
    top = fsdp_size // 2
    g = (me // 2) % groups
    rows = current.shape[0] // groups
    pieces = [
        lax.dynamic_slice_in_dim(current, (g ^ k) * rows, rows, 0) for k in range(groups)
    ]
    current = pieces[0]
    for k in range(1, groups):
        current = current + move(pieces[k].astype(BF16), k << 1).astype(F32)
    rows //= 2
    high = me // top
    away = lax.dynamic_slice_in_dim(current, (1 - high) * rows, rows, 0).astype(BF16)
    current = lax.dynamic_slice_in_dim(current, high * rows, rows, 0)
    current = (current + move(away, top).astype(F32)).astype(BF16)

    def join(bit, own, other):
        return jnp.where(
            bit == 0, jnp.concatenate([own, other], 0), jnp.concatenate([other, own], 0)
        )

    current = join(high, current, move(current, top))
    pieces = [current] + [move(current, k << 1) for k in range(1, groups)]
    step = 1
    while step < groups:
        odd = (g & step) != 0
        pieces = [jnp.where(odd, pieces[k ^ step], pieces[k]) for k in range(groups)]
        step *= 2
    current = jnp.concatenate(pieces, 0)
    current = join(me & 1, current, move(current, 1)).astype(F32)
    a_grads = current[:, :rows_each]
    outer = current[:, rows_each:]
    outer = jnp.concatenate([outer[:rank], outer[rank:]], 1)
    return (
        loss[0, 0],
        a_grads[:rank].T,
        outer[:, : qo.shape[1]],
        a_grads[rank:].T,
        outer[:, qo.shape[1] : qo.shape[1] + vo.shape[1]],
    )


def solution(mesh):
    in_specs = (
        P("fsdp", None),
        P("fsdp", None),
        P("fsdp", None),
        P(),
        P("fsdp", "tensor"),
        P("fsdp", "tensor"),
        P("fsdp", "tensor"),
        P("tensor", "fsdp"),
        P(),
        P(None, "tensor"),
        P(),
        P(None, "tensor"),
        P("fsdp"),
        P(),
    )
    out_specs = (P(), P("tensor", None), P(None, "tensor"), P("tensor", None), P(None, "tensor"))
    body = functools.partial(per_device, mesh.shape["fsdp"], mesh.shape["tensor"])
    return jax.shard_map(body, mesh=mesh, in_specs=in_specs, out_specs=out_specs, check_vma=False)
```

```python
import functools

import jax
import jax.numpy as jnp
from jax import lax
from jax.experimental import pallas as pl
from jax.experimental.pallas import tpu as pltpu
from jax.sharding import PartitionSpec as P

QUERY_HEADS = 32
KEY_VALUE_HEADS = 8
HEAD_SIZE = 128
L = 128
GROUP = QUERY_HEADS // KEY_VALUE_HEADS
QCOLS = GROUP * HEAD_SIZE

adapter_scale = 0.5
dpo_beta = 0.1
loss_scale = 256.0
rope_base = 500000.0
norm_eps = 1e-05

F32 = jnp.float32
BF16 = jnp.bfloat16
ORD = (0, 2, 1, 3)
MB = 1 << 20
SMALL = pl.CostEstimate(flops=1, bytes_accessed=1, transcendentals=0)


def rope_tables(length, head_dim):
    half_dim = head_dim // 2
    exponent = jnp.arange(half_dim, dtype=F32) * (2.0 / head_dim)
    inverse = jnp.power(F32(rope_base), -exponent)
    angles = jnp.arange(length, dtype=F32)[:, None] * inverse[None, :]
    cosine = jnp.concatenate([jnp.cos(angles), jnp.cos(angles)], 1)
    sine = jnp.concatenate([-jnp.sin(angles), jnp.sin(angles)], 1)
    return cosine, sine


def dot(a, b, dims=((1,), (0,))):
    return lax.dot_general(a, b, (dims, ((), ())), preferred_element_type=F32)


def params(limit_mb):
    return pltpu.CompilerParams(vmem_limit_bytes=limit_mb * MB)


def smem():
    return pl.BlockSpec(memory_space=pltpu.SMEM)


def full(a):
    return pl.BlockSpec(a.shape, lambda i: (0,) * len(a.shape))


def prep_body(parts, part, split, idx, ref, pol, tgt, gain, *outs):
    x0, x1, x2, x3, t0, t1, t2, t3, go = outs
    groups = parts // split
    for d, (xo, to) in enumerate(((x0, t0), (x1, t1), (x2, t2), (x3, t3))):
        for j in range(parts):
            src = pl.ds(pl.multiple_of(idx[d * parts + j] * part, part), part)
            cols = slice(j * part, (j + 1) * part)
            if xo.shape[0] == 2:
                xo[0, :, cols] = ref[:, src]
                xo[1, :, cols] = pol[:, src]
            else:
                @pl.when(idx[4 * parts + 4 * groups] == 0)
                def _():
                    xo[0, :, cols] = ref[:, src]

                @pl.when(idx[4 * parts + 4 * groups] != 0)
                def _():
                    xo[0, :, cols] = pol[:, src]

        for j in range(groups):
            at = idx[4 * parts + d * groups + j] * part
            src = pl.ds(pl.multiple_of(at, part), part)
            to[:, j * part : (j + 1) * part] = tgt[:, src]
            if d == 0:
                go[:, j * part : (j + 1) * part] = gain[:, src]


def prep(idx, ref, pol, tgt, gain, parts, part, split):
    tokens = ref.shape[0]
    xs = lambda n: jax.ShapeDtypeStruct((n, tokens, parts * part), BF16)
    far = 1 if split == 2 else 2
    width = parts // split * part
    shapes = [xs(2), xs(2), xs(far), xs(far)]
    shapes += [jax.ShapeDtypeStruct((tokens, width), BF16)] * 4
    shapes += [jax.ShapeDtypeStruct((1, width), F32)]
    return pl.pallas_call(
        functools.partial(prep_body, parts, part, split),
        grid=(1,),
        in_specs=[smem()] + [full(a) for a in (ref, pol, tgt, gain)],
        out_specs=[full(a) for a in shapes],
        out_shape=shapes,
        compiler_params=params(60),
        cost_estimate=SMALL,
    )(idx, ref, pol, tgt, gain)


def tile_of(cols):
    for tile in (256, 128):
        if cols % tile == 0:
            return tile
    return cols


def mm_body(count, x_ref, *refs):
    ws, outs = refs[:count], refs[count:]
    total = None
    at = 0
    for w in ws:
        depth = w.shape[0]
        term = dot(x_ref[:, at : at + depth], w[...])
        total = term if total is None else total + term
        at += depth
    rows = total.shape[0] // 2
    for i, out_ref in enumerate(outs):
        out_ref[...] = total[i * rows : (i + 1) * rows].astype(out_ref.dtype)


def mm(x, half, ws, out_dtype):
    rows, depth = x.shape[0] // 2, x.shape[1]
    cols = ws[0].shape[1]
    tile = tile_of(cols)
    return pl.pallas_call(
        functools.partial(mm_body, len(ws)),
        grid=(cols // tile,),
        in_specs=[pl.BlockSpec((rows, depth), lambda i: (half, 0))]
        + [pl.BlockSpec((w.shape[0], tile), lambda i: (0, i)) for w in ws],
        out_specs=[pl.BlockSpec((rows // 2, tile), lambda i: (0, i))] * 2,
        out_shape=[jax.ShapeDtypeStruct((rows // 2, cols), out_dtype)] * 2,
        compiler_params=params(60),
        cost_estimate=SMALL,
    )(x, *ws)


def out_body(n, row_parts, counts, *refs):
    ws = refs[row_parts * n : -2]
    out_ref, total = refs[-2:]
    for j in range(n):
        x = jnp.concatenate([refs[p * n + j][...] for p in range(row_parts)], 0)
        depth = x.shape[1]
        at = 0
        for k, count in enumerate(counts):
            row = j * depth
            piece = at
            while row >= ws[piece].shape[0]:
                row -= ws[piece].shape[0]
                piece += 1
            at += count
            term = dot(x, ws[piece][row : row + depth])
            if j:
                term = term + total[k]
            if j == n - 1:
                out_ref[k] = term.astype(BF16)
            else:
                total[k] = term


def out_mm(parts, ws):
    n = len(parts[0])
    rows = sum(part[0].shape[0] for part in parts)
    cols = ws[0][0].shape[1]
    flat = [piece for w in ws for piece in w]
    inputs = [a for part in parts for a in part] + flat
    out_shape = jax.ShapeDtypeStruct((len(ws), rows, cols), BF16)
    return pl.pallas_call(
        functools.partial(out_body, n, len(parts), tuple(len(w) for w in ws)),
        grid=(1,),
        in_specs=[full(a) for a in inputs],
        out_specs=full(out_shape),
        out_shape=out_shape,
        scratch_shapes=[pltpu.VMEM(out_shape.shape, F32)],
        compiler_params=params(60),
        cost_estimate=SMALL,
    )(*inputs)


def back_body(counts, part, has_acc, x_ref, *refs):
    total = None
    at = 0
    for j, count in enumerate(counts):
        w = refs[at][...]
        if count == 2:
            w = jnp.where(pl.program_id(0) < pl.num_programs(0) // 2, w, refs[at + 1][...])
        at += count
        term = dot(x_ref[:, j * part : (j + 1) * part], w, ((1,), (1,)))
        total = term if total is None else total + term
    refs = refs[at:]
    if has_acc:
        total = total + refs[0][...]
        keep, send = refs[1:]
        half = total.shape[0] // 2
        keep[...] = total[:half]
        send[...] = total[half:].astype(send.dtype)
    else:
        refs[0][...] = total


def back_mm(x, half, ws, acc):
    rows = x.shape[0] // (1 if half is None else 2)
    depth = x.shape[1]
    part = ws[0][0].shape[1]
    heads = sum(piece.shape[0] for piece in ws[0])
    tile = min(512, heads)
    steps = heads // tile
    has_acc = acc is not None
    row = half or 0
    in_specs = [pl.BlockSpec((rows, depth), lambda i: (row, 0))]
    for w in ws:
        if len(w) == 1:
            in_specs.append(pl.BlockSpec((tile, part), lambda i: (i, 0)))
        else:
            in_specs.append(pl.BlockSpec((tile, part), lambda i: (jnp.minimum(i, steps // 2 - 1), 0)))
            in_specs.append(pl.BlockSpec((tile, part), lambda i: (jnp.maximum(i - steps // 2, 0), 0)))
    args = [x] + [piece for w in ws for piece in w]
    if has_acc:
        in_specs.append(pl.BlockSpec((rows, tile), lambda i: (0, i)))
        args.append(acc)
        out_specs = [pl.BlockSpec((rows // 2, tile), lambda i: (0, i))] * 2
        out_shape = [
            jax.ShapeDtypeStruct((rows // 2, heads), F32),
            jax.ShapeDtypeStruct((rows // 2, heads), BF16),
        ]
    else:
        out_specs = pl.BlockSpec((rows, tile), lambda i: (0, i))
        out_shape = jax.ShapeDtypeStruct((rows, heads), F32)
    return pl.pallas_call(
        functools.partial(back_body, tuple(len(w) for w in ws), part, has_acc),
        grid=(steps,),
        in_specs=in_specs,
        out_specs=out_specs,
        out_shape=out_shape,
        compiler_params=params(60),
        cost_estimate=SMALL,
    )(*args)


def causal(rows):
    at = lax.broadcasted_iota(jnp.int32, (rows, L), 0) % L
    return at >= lax.broadcasted_iota(jnp.int32, (rows, L), 1)


def probabilities(q4, keys):
    scores = dot(q4, keys, ((1,), (1,))) * (HEAD_SIZE**-0.5)
    weights = jnp.where(causal(q4.shape[0]), jnp.exp(scores), 0.0)
    return weights / jnp.sum(weights, -1, keepdims=True)


def stack_heads(values):
    return jnp.concatenate(
        [values[:, h * HEAD_SIZE : (h + 1) * HEAD_SIZE] for h in range(GROUP)], 0
    )


def attend_body(adapted, keep, rs, r2, low, qo, vo, cos_ref, sin_ref, mixed, *saved):
    cosine = cos_ref[...]
    sine = sin_ref[...]
    pre = keep[...] + rs[...].astype(F32) + r2[...].astype(F32)
    rank = qo.shape[0]
    q_pre = pre[:, :QCOLS]
    k_pre = pre[:, QCOLS : QCOLS + HEAD_SIZE]
    v_pre = pre[:, QCOLS + HEAD_SIZE :]
    if adapted:
        q_pre = q_pre + adapter_scale * dot(low[:, :rank], qo[...])
        v_pre = v_pre + adapter_scale * dot(low[:, rank:], vo[...])
    cos4 = jnp.concatenate([cosine] * GROUP, 0)
    sin4 = jnp.concatenate([sine] * GROUP, 0)
    q4 = stack_heads(q_pre)
    q4 = (q4 * cos4 + pltpu.roll(q4, HEAD_SIZE // 2, 1) * sin4).astype(BF16)
    keys = (k_pre * cosine + pltpu.roll(k_pre, HEAD_SIZE // 2, 1) * sine).astype(BF16)
    values = v_pre.astype(BF16)
    rounded = probabilities(q4, keys).astype(BF16)
    out = dot(rounded, values).astype(BF16)
    for h in range(GROUP):
        cols = slice(h * HEAD_SIZE, (h + 1) * HEAD_SIZE)
        mixed[:, cols] = out[h * L : (h + 1) * L]
        if saved:
            saved[0][:, cols] = q4[h * L : (h + 1) * L]
    if saved:
        saved[0][:, QCOLS : QCOLS + HEAD_SIZE] = keys
        saved[0][:, QCOLS + HEAD_SIZE :] = values


def attend(adapted, keep, rs, r2, low, qo, vo, group, cosine, sine):
    each = QCOLS + 2 * HEAD_SIZE
    rank = qo.shape[0]
    top = lambda a: pl.BlockSpec((L, a.shape[1]), lambda i: (0, 0))
    return pl.pallas_call(
        functools.partial(attend_body, adapted),
        grid=(1,),
        in_specs=[
            top(keep),
            top(rs),
            top(r2),
            top(low),
            pl.BlockSpec((rank, QCOLS), lambda i: (0, group)),
            pl.BlockSpec((rank, HEAD_SIZE), lambda i: (0, group)),
            top(cosine),
            top(sine),
        ],
        out_specs=[pl.BlockSpec((L, w), lambda i: (0, 0)) for w in (QCOLS, each)[: 1 + adapted]],
        out_shape=[jax.ShapeDtypeStruct((L, w), BF16) for w in (QCOLS, each)[: 1 + adapted]],
        compiler_params=params(16),
        cost_estimate=SMALL,
    )(keep, rs, r2, low, qo, vo, cosine, sine)


def outer_place(block, rank, kv):
    wide = (kv * (GROUP + 1) + 1) // 2
    return (block // wide) * rank, (block % wide) * HEAD_SIZE, wide


def attend_back_body(kv, splits, keep, rs, r2, low, qo, vo, cos_ref, sin_ref, *refs):
    saved = refs[:splits]
    outer, mid = refs[splits:]
    rank = qo.shape[0]
    each = QCOLS + 2 * HEAD_SIZE
    cos4 = jnp.concatenate([cos_ref[...]] * GROUP, 0)
    sin4 = jnp.concatenate([sin_ref[...]] * GROUP, 0)
    low_q = low[:, :rank]
    low_v = low[:, rank:]
    q_mid = jnp.zeros((L, rank), F32)
    v_mid = jnp.zeros((L, rank), F32)

    def put(block, value):
        row, col, _ = outer_place(block, rank, kv)
        outer[row : row + rank, col : col + HEAD_SIZE] = adapter_scale * value

    if (kv * (GROUP + 1)) % 2:
        put(kv * (GROUP + 1), jnp.zeros((rank, HEAD_SIZE), F32))
    for j in range(kv):
        cols = slice(j * QCOLS, (j + 1) * QCOLS)
        at = (j % (kv // splits)) * each
        kept = saved[j // (kv // splits)]
        grad = keep[:, cols] + rs[:, cols].astype(F32) + r2[:, cols].astype(F32)
        grad4 = stack_heads(grad.astype(BF16))
        q4 = stack_heads(kept[:, at : at + QCOLS])
        keys = kept[:, at + QCOLS : at + QCOLS + HEAD_SIZE]
        values = kept[:, at + QCOLS + HEAD_SIZE : at + each]
        prob = probabilities(q4, keys)
        grad_prob = dot(grad4, values, ((1,), (1,)))
        grad_values = dot(prob.astype(BF16), grad4, ((0,), (0,))).astype(BF16)
        inner = jnp.sum(grad_prob * prob, -1, keepdims=True)
        grad_scores = (prob * (grad_prob - inner) * (HEAD_SIZE**-0.5)).astype(BF16)
        grad_query = dot(grad_scores, keys)
        back4 = (grad_query * cos4 - pltpu.roll(grad_query, HEAD_SIZE // 2, 1) * sin4).astype(BF16)
        for h in range(GROUP):
            at = j * GROUP + h
            back = back4[h * L : (h + 1) * L]
            put(at, dot(low_q, back, ((0,), (0,))))
            q_mid += dot(back, qo[:, at * HEAD_SIZE : (at + 1) * HEAD_SIZE], ((1,), (1,)))
        put(kv * GROUP + j, dot(low_v, grad_values, ((0,), (0,))))
        v_mid += dot(grad_values, vo[:, j * HEAD_SIZE : (j + 1) * HEAD_SIZE], ((1,), (1,)))
    mid[:, :rank] = (adapter_scale * q_mid).astype(BF16)
    mid[:, rank:] = (adapter_scale * v_mid).astype(BF16)


def attend_back(keep, rs, r2, low, qo, vo, cosine, sine, saved):
    rank = qo.shape[0]
    kv = vo.shape[1] // HEAD_SIZE
    wide = outer_place(0, rank, kv)[2]
    inputs = (keep, rs, r2, low, qo, vo, cosine, sine, *saved)
    shapes = [
        jax.ShapeDtypeStruct((2 * rank, wide * HEAD_SIZE), F32),
        jax.ShapeDtypeStruct((L, 2 * rank), BF16),
    ]
    return pl.pallas_call(
        functools.partial(attend_back_body, kv, len(saved)),
        grid=(1,),
        in_specs=[full(a) for a in inputs],
        out_specs=[full(a) for a in shapes],
        out_shape=shapes,
        compiler_params=params(60),
        cost_estimate=SMALL,
    )(*inputs)


def adapter_body(n, rows_each, scal, states, outer, *refs):
    mids = refs[:n]
    away, stay = refs[n:]
    src = pl.ds(pl.multiple_of(scal[0] * rows_each, rows_each), rows_each)
    own = states[:, src]
    total = None
    for mid in mids:
        term = dot(mid[...], own, ((0,), (0,)))
        total = term if total is None else total + term
    half = total.shape[0] // 2
    for low in range(2):
        rows = slice(low * half, (low + 1) * half)

        @pl.when(scal[1] == low)
        def _():
            stay[:, :rows_each] = total[rows]
            stay[:, rows_each:] = outer[rows]

        @pl.when(scal[1] != low)
        def _():
            away[:, :rows_each] = total[rows].astype(BF16)
            away[:, rows_each:] = outer[rows].astype(BF16)


def adapter_products(scal, states, mids, outer, rows_each):
    half = outer.shape[0] // 2
    cols = rows_each + outer.shape[1]
    shapes = [jax.ShapeDtypeStruct((half, cols), BF16), jax.ShapeDtypeStruct((half, cols), F32)]
    return pl.pallas_call(
        functools.partial(adapter_body, len(mids), rows_each),
        grid=(1,),
        in_specs=[smem()] + [full(a) for a in (states, outer, *mids)],
        out_specs=[full(a) for a in shapes],
        out_shape=shapes,
        compiler_params=params(60),
        cost_estimate=SMALL,
    )(scal, states, outer, *mids)


def stats_body(counts, part, split, scal, xt_ref, xt_pol, tgt, gain, *refs):
    refs = list(refs)
    sums = []
    hidden_out, stats = refs[-2:]
    for which in range(2):
        xt = (xt_ref, xt_pol)[which]
        count = sum(counts)
        keeps = [r[i] for r in refs[: counts[0]] for i in range(r.shape[0])]
        recvs = [r[i] for r in refs[counts[0] : count] for i in range(r.shape[0])]
        refs = refs[count:]
        squares = jnp.zeros((L, HEAD_SIZE), F32)
        products = jnp.zeros((L, HEAD_SIZE), F32)
        for j, (keep, recv) in enumerate(zip(keeps, recvs)):
            src = pl.ds(pl.multiple_of((j * split + scal[0]) * part, part), part)
            hidden = xt[:, src].astype(F32) + keep.astype(F32) + recv.astype(F32)
            cols = slice(j * part, (j + 1) * part)
            if which == 1:
                hidden_out[0, :, cols] = hidden
            product = hidden * (gain[:, cols] * tgt[0, :, cols].astype(F32))
            square = hidden * hidden
            for s in range(part // HEAD_SIZE):
                lanes = slice(s * HEAD_SIZE, (s + 1) * HEAD_SIZE)
                squares += square[:, lanes]
                products += product[:, lanes]
        sums.append(
            [
                jnp.broadcast_to(jnp.sum(v, 1, keepdims=True), v.shape).T[:1]
                for v in (squares, products)
            ]
        )
    at = lax.broadcasted_iota(jnp.int32, (1, 2 * L), 1) % L
    own = (at >= scal[1]) & (pl.program_id(0) == 0)
    live = jnp.where(own, 1.0, 0.0).astype(F32)
    both = [jnp.concatenate([sums[0][i], sums[1][i]], 1) for i in range(2)]
    stats[...] = jnp.concatenate([*both, live, jnp.zeros((5, 2 * L), F32)], 0)


def norm_stats(scal, xt, tgt, gain, keeps, recvs, split):
    n = sum(a.shape[0] for a in keeps)
    part = keeps[0].shape[2]
    shared = []
    for which in range(2):
        at = functools.partial(lambda which, i: (0, 2 * i + which, 0), which)
        for a in (*keeps, *recvs):
            shared.append((a, pl.BlockSpec((a.shape[0], L, part), at)))
    return pl.pallas_call(
        functools.partial(stats_body, (len(keeps), len(recvs)), part, split),
        grid=(4,),
        in_specs=[
            smem(),
            pl.BlockSpec((L, xt.shape[1]), lambda i: ((i // 2) * 4 + i % 2, 0)),
            pl.BlockSpec((L, xt.shape[1]), lambda i: ((i // 2) * 4 + 2 + i % 2, 0)),
            pl.BlockSpec((1, L, n * part), lambda i: (i, 0, 0)),
            pl.BlockSpec((1, n * part), lambda i: (0, 0)),
        ]
        + [spec for _, spec in shared],
        out_specs=[
            pl.BlockSpec((1, L, n * part), lambda i: (i, 0, 0)),
            pl.BlockSpec((8, 2 * L), lambda i: (i, 0)),
        ],
        out_shape=[
            jax.ShapeDtypeStruct((4, L, n * part), F32),
            jax.ShapeDtypeStruct((32, 2 * L), F32),
        ],
        compiler_params=params(60),
        cost_estimate=SMALL,
    )(scal, xt, xt, tgt, gain, *[a for a, _ in shared])


def score_body(width, masks, ids, own, *refs):
    recvs = refs[: len(masks)]
    total_out, margin_out = refs[len(masks) :]
    lane = lax.broadcasted_iota(jnp.int32, (8, 128), 1)
    margins = jnp.zeros((8, 128), F32)
    for p in range(4):
        total = own[8 * p : 8 * p + 8]
        for recv, m in zip(recvs, masks):
            q = ORD.index(ORD[p] ^ m)
            total = total + recv[8 * q : 8 * q + 8]
        total_out[8 * p : 8 * p + 8] = total
        inverse = lax.rsqrt(total[0:1] * (1.0 / width) + norm_eps)
        score = total[1:2] * inverse * (width**-0.5)
        score = jnp.where(total[2:3] > 0.5, score, 0.0)
        margin = jnp.sum(score[:, L:], 1, keepdims=True) - jnp.sum(score[:, :L], 1, keepdims=True)
        margins = margins + jnp.where(lane == ids[p], margin, 0.0)
    margin_out[...] = margins


def scores(ids, own, recvs, masks, width):
    shapes = [jax.ShapeDtypeStruct(own.shape, F32), jax.ShapeDtypeStruct((8, 128), F32)]
    return pl.pallas_call(
        functools.partial(score_body, width, masks),
        grid=(1,),
        in_specs=[smem()] + [full(a) for a in (own, *recvs)],
        out_specs=[full(a) for a in shapes],
        out_shape=shapes,
        cost_estimate=SMALL,
    )(ids, own, *recvs)


def turn(i):
    return (2 * i + 1) % 5


def grad_body(width, seqs, n_vec, ids, pairs, total, hidden, tgt, gain, *refs):
    vecs = refs[:n_vec]
    grad_out, loss_out, slope = refs[n_vec:]
    lane = lax.broadcasted_iota(jnp.int32, (8, 128), 1)

    @pl.when(pl.program_id(0) == 0)
    def _():
        margin = vecs[0][...]
        for v in vecs[1:]:
            margin = margin + v[...]
        logits = jnp.zeros((8, 128), F32)
        for i in range(seqs // 2):
            sign = jnp.where(lane == pairs[2 * i], 1.0, 0.0) - jnp.where(
                lane == pairs[2 * i + 1], 1.0, 0.0
            )
            logit = dpo_beta * jnp.sum(margin * sign, 1, keepdims=True)
            logits = logits + jnp.where(lane == i, logit, 0.0)
        soft = jnp.maximum(-logits, 0.0) + jnp.log1p(jnp.exp(-jnp.abs(logits)))
        used = lane < seqs // 2
        loss = jnp.sum(jnp.where(used, soft, 0.0), 1, keepdims=True)
        loss_out[...] = jnp.broadcast_to(loss, (8, 128))
        slopes = jnp.where(used, -dpo_beta / (1.0 + jnp.exp(logits)), 0.0)
        gradient = jnp.zeros((8, 128), F32)
        for i in range(seqs // 2):
            each = jnp.sum(jnp.where(lane == i, slopes, 0.0), 1, keepdims=True)
            sign = jnp.where(lane == pairs[2 * i], 1.0, 0.0) - jnp.where(
                lane == pairs[2 * i + 1], 1.0, 0.0
            )
            gradient = gradient + each * sign
        slope[...] = gradient * loss_scale

    mine = lane == ids[turn(pl.program_id(0))]
    seq = jnp.sum(jnp.where(mine, slope[...], 0.0), 1, keepdims=True)[:1]
    rows = total[:, L:]
    token = jnp.where(rows[2:3] > 0.5, seq, 0.0) * (width**-0.5)
    inverse = lax.rsqrt(rows[0:1] * (1.0 / width) + norm_eps)
    first = inverse * token
    second = inverse * inverse * inverse * (token * rows[1:2] * (1.0 / width))
    first = jnp.broadcast_to(first, (L, L)).T
    second = jnp.broadcast_to(second, (L, L)).T
    for s in range(hidden.shape[2] // HEAD_SIZE):
        cols = slice(s * HEAD_SIZE, (s + 1) * HEAD_SIZE)
        weighted = gain[:, cols] * tgt[0, :, cols].astype(F32)
        grad_out[0, :, cols] = (first * weighted - second * hidden[0, :, cols]).astype(BF16)


def grad_hidden(ids, pairs, total, hidden, tgt, gain, vecs, width):
    n = hidden.shape[2]
    seqs = pairs.shape[0]
    return pl.pallas_call(
        functools.partial(grad_body, width, seqs, len(vecs)),
        grid=(4,),
        in_specs=[
            smem(),
            smem(),
            pl.BlockSpec((8, 2 * L), lambda i: (turn(i), 0)),
            pl.BlockSpec((1, L, n), lambda i: (turn(i), 0, 0)),
            pl.BlockSpec((1, L, n), lambda i: (turn(i), 0, 0)),
            pl.BlockSpec((1, n), lambda i: (0, 0)),
        ]
        + [pl.BlockSpec((8, 128), lambda i: (0, 0)) for _ in vecs],
        out_specs=[
            pl.BlockSpec((1, L, n), lambda i: (i, 0, 0)),
            pl.BlockSpec((8, 128), lambda i: (0, 0)),
        ],
        out_shape=[
            jax.ShapeDtypeStruct((4, L, n), BF16),
            jax.ShapeDtypeStruct((8, 128), F32),
        ],
        scratch_shapes=[pltpu.VMEM((8, 128), F32)],
        compiler_params=params(60),
        cost_estimate=SMALL,
    )(ids, pairs, total, hidden, tgt, gain, *vecs)


def per_device(
    fsdp_size,
    tensor_size,
    ref_states,
    pol_states,
    target_rows,
    norm_gain,
    wq,
    wk,
    wv,
    wo,
    qa,
    qo,
    va,
    vo,
    prompt_length,
    pairs,
):
    tokens, width = ref_states.shape
    groups = fsdp_size // 4
    near_z = fsdp_size // 4
    bits = []
    bit = 2
    while bit < fsdp_size:
        if bit != near_z:
            bits.append(bit)
        bit *= 2
    split = 2 if tensor_size == 2 and fsdp_size == 16 else 1
    kv_local = wk.shape[1] // HEAD_SIZE
    depth = wq.shape[0]
    part = depth // split
    rank = qa.shape[1]
    me = lax.axis_index("fsdp")
    x = lax.axis_index("tensor")
    side = x if split == 2 else 0

    def tmask(d):
        return (d & 1) | ((d >> 1) * near_z)

    def gmask(k):
        return sum(bit for i, bit in enumerate(bits) if (k >> i) & 1)

    def move(value, mask):
        return lax.ppermute(value, "fsdp", [(i, i ^ mask) for i in range(fsdp_size)])

    def swap_x(value):
        return lax.ppermute(value, "tensor", [(0, 1), (1, 0)])

    def move_both(value, mask, flip):
        pairs_list = [
            (2 * i + j, 2 * (i ^ mask) + (j ^ flip)) for i in range(fsdp_size) for j in range(2)
        ]
        return lax.ppermute(value, ("fsdp", "tensor"), pairs_list)

    def after(value, *others):
        return lax.optimization_barrier((value, *others))[0]

    wide = groups == 4 and split == 2
    heads = wo.shape[0]

    def shard_of(j, *queue):
        q, k, v = wq, wk, wv
        if queue:
            q, k, v = lax.optimization_barrier((wq, wk, wv, *queue))[:3]
        pieces = [
            q[:, j * QCOLS : (j + 1) * QCOLS],
            k[:, j * HEAD_SIZE : (j + 1) * HEAD_SIZE],
            v[:, j * HEAD_SIZE : (j + 1) * HEAD_SIZE],
        ]
        return jnp.concatenate(pieces, 1)

    def gather(shard):
        return [shard] + [move(shard, gmask(k)) for k in range(1, groups)]

    if wide:
        over_y, over_z = gmask(1), gmask(2)
        shards = [shard_of(0)]
        zs = [move(shards[0], over_z)]
        ys = [move(shards[0], over_y)]
        corners = []

    parts = groups * split
    idx = []
    for d in range(4):
        for k in range(groups):
            for h in range(split):
                idx.append((me ^ tmask(d) ^ gmask(k)) * split + h)
    for d in range(4):
        for k in range(groups):
            idx.append((me ^ tmask(d) ^ gmask(k)) * split + side)
    idx.append(x)
    idx = jnp.stack(idx).astype(jnp.int32)
    if wide:
        idx = after(idx, shards[0])
    prepared = prep(
        idx,
        ref_states,
        pol_states,
        target_rows,
        norm_gain.astype(F32).reshape(1, width),
        parts,
        part,
        split,
    )
    xs, ts, gain = prepared[:4], prepared[4:8], prepared[8]
    near = move(xs[1], 1)
    far = [move(xs[2], near_z)]
    far.append(move(xs[3], near_z | 1))

    targets = [ts[0]] + [move(after(ts[d], *far), tmask(d)) for d in (1, 2, 3)]
    if split == 2:
        other = [swap_x(a) for a in far]
        far = [
            [jnp.where(x == which, a[0], b[0]) for which in range(2)] for a, b in zip(far, other)
        ]
    states = jnp.concatenate(
        [
            *(xs[0][0], far[0][0], xs[0][1], far[0][1]),
            *(near[0], far[1][0], near[1], far[1][1]),
        ],
        0,
    )

    states = after(states, *targets[1:])
    tgt = jnp.stack([targets[d] for d in ORD])

    low = dot(pol_states, jnp.concatenate([qa, va], 1)).astype(BF16)
    cosine, sine = rope_tables(L, HEAD_SIZE)

    def own_columns(at, piece, *queue):
        return lax.dynamic_slice(
            after(wo, *queue), (piece * (heads // 2), at * part), (heads // 2, part)
        )

    def own_piece(step, *queue):
        at = (1 - x) if step < 2 else x
        return lax.dynamic_slice(
            after(wo, *queue), ((step % 2) * (heads // 2), at * part), (heads // 2, part)
        )

    def next_shard(j, *more):
        early = zs[j - 2 :][:1] if j >= 2 else []
        shards.append(
            shard_of(j, *early) if j < kv_local else own_piece(j - kv_local, *early)
        )
        queue = (zs[j - 1], ys[j - 1], *more)
        ys.append(move(after(shards[j], *queue), over_y))
        zs.append(move(after(shards[j], *queue), over_z))
        corners.append(move(after(*queue), over_y))

    saved = []
    parts_mixed = [[], [], []]

    def mix(j, keeps, came, sums, *queue):
        results = []
        for which in range(2):
            total = sums[which * L : (which + 1) * L]
            result = attend(
                which == 1, keeps[which], came[which], total, low, qo, vo, j, cosine, sine
            )
            saved.extend(result[1:])
            results.append(result[0])
        result = jnp.concatenate(results, 0)
        return result, move(after(result, *queue) if queue else result, near_z)

    def spread(result, other):
        far = move(jnp.concatenate([result, other], 0), 1)
        for part_mixed, value in zip(parts_mixed, (result, other, far)):
            part_mixed.append(value)
        return far

    if wide:
        next_shard(1)
    before = None
    ends = []
    for j in range(kv_local):
        if wide:
            next_shard(j + 2)
            states = after(states, zs[j + 1], ys[j + 1], corners[j])
            ws = [shards[j], ys[j], zs[j], corners[j]]
        else:
            ws = gather(shard_of(j))
        sends = mm(states, 1, ws, BF16)
        came = [move(send, 1) for send in sends]
        keeps = mm(states, 0, ws, F32)
        over = jnp.concatenate(
            [(keeps[which][L:] + came[which][L:].astype(F32)).astype(BF16) for which in range(2)], 0
        )
        if before is not None:
            result, other = mix(j - 1, *before, *came, *ends)
            if j + 1 < kv_local:
                over = after(over, other)
            states = after(states, other)
            ends = [spread(result, other)]
        sums = move(over, near_z)
        if wide and j + 1 == kv_local:
            sums = after(sums, zs[j + 2], ys[j + 2])
        before = (keeps, came, sums)
    last = spread(*mix(kv_local - 1, *before, *ends))

    keeps, recvs = [], []
    if wide:
        next_shard(kv_local + 2, over)
        first = [a[kv_local : kv_local + 2] for a in (shards, ys, zs, corners)]
        product = out_mm(parts_mixed, first[:2])
        recvs.append(swap_x(product))
        next_shard(kv_local + 3, product)
        recvs.append(swap_x(out_mm(parts_mixed, first[2:])))
        corners.append(move(after(zs[-1], ys[-1]), over_y))
        wo_send, wo_keep = first, [a[kv_local + 2 :] for a in (shards, ys, zs, corners)]
        keeps.append(out_mm(parts_mixed, wo_keep[:3]))
        keeps.append(out_mm(parts_mixed, wo_keep[3:]))
    else:
        wo_keep = [[w] for w in gather(wo)]
        product = out_mm(parts_mixed, wo_keep)
        if tensor_size > 1:
            product = lax.psum(product, "tensor")
        keeps.append(product)
        recvs.append(jnp.zeros_like(product))

    scal = jnp.stack([jnp.asarray(side, jnp.int32), prompt_length[0].astype(jnp.int32)])
    hidden, stats = norm_stats(scal, states, tgt, gain, keeps, recvs, split)
    masks, got = [], []
    for flip in range(split):
        for d in range(4):
            if d or flip:
                masks.append(d)
                if split == 2:
                    got.append(move_both(stats, tmask(d), flip))
                else:
                    got.append(move(stats, tmask(d)))
    ids = jnp.stack([me ^ tmask(d) for d in ORD]).astype(jnp.int32)
    total, margin = scores(ids, stats, got, tuple(masks), width)
    vecs = [margin] + [move(margin, gmask(k)) for k in range(1, groups)]
    grad, loss = grad_hidden(ids, pairs, total, hidden, tgt, gain, vecs, width)

    grad_rows = grad.reshape(4 * L, -1)
    other = None
    for half in range(2):
        if split == 2:
            leaving = grad_rows[2 * L * half : 2 * L * (half + 1)]
            other = swap_x(leaving if half == 0 else after(leaving, other))
            acc = back_mm(grad_rows, half, wo_keep, None)
            keep, send = back_mm(other, None, wo_send, acc)
        else:
            acc = jnp.zeros((2 * L, heads), F32)
            keep, send = back_mm(grad_rows, half, wo_keep, acc)
        rs = move(send if half == 0 else after(send, r2), 1)
        if half == 0:
            over = (keep + rs.astype(F32)).astype(BF16)
            r2 = move(over, near_z)
    outer, mid = attend_back(keep, rs, r2, low, qo, vo, cosine, sine, saved)

    rows_each = width // tensor_size
    if split == 2:
        mids = [mid, swap_x(mid)]
    elif tensor_size == 1:
        mids = [mid]
    else:
        gathered = lax.all_gather(mid, "tensor", axis=0, tiled=False)
        mids = [gathered[i] for i in range(tensor_size)]
    scal = jnp.stack([x, me & 1]).astype(jnp.int32)
    away, current = adapter_products(scal, pol_states, mids, outer, rows_each)
    current = current + move(away, 1).astype(F32)
    top = fsdp_size // 2
    g = (me // 2) % groups
    rows = current.shape[0] // groups
    pieces = [
        lax.dynamic_slice_in_dim(current, (g ^ k) * rows, rows, 0) for k in range(groups)
    ]
    current = pieces[0]
    for k in range(1, groups):
        current = current + move(pieces[k].astype(BF16), k << 1).astype(F32)
    rows //= 2
    high = me // top
    away = lax.dynamic_slice_in_dim(current, (1 - high) * rows, rows, 0).astype(BF16)
    current = lax.dynamic_slice_in_dim(current, high * rows, rows, 0)
    current = (current + move(away, top).astype(F32)).astype(BF16)

    def join(bit, own, other):
        return jnp.where(
            bit == 0, jnp.concatenate([own, other], 0), jnp.concatenate([other, own], 0)
        )

    current = join(high, current, move(current, top))
    pieces = [current] + [move(current, k << 1) for k in range(1, groups)]
    step = 1
    while step < groups:
        odd = (g & step) != 0
        pieces = [jnp.where(odd, pieces[k ^ step], pieces[k]) for k in range(groups)]
        step *= 2
    current = jnp.concatenate(pieces, 0)
    current = join(me & 1, current, move(current, 1)).astype(F32)
    a_grads = current[:, :rows_each]
    outer = current[:, rows_each:]
    outer = jnp.concatenate([outer[:rank], outer[rank:]], 1)
    return (
        loss[0, 0],
        a_grads[:rank].T,
        outer[:, : qo.shape[1]],
        a_grads[rank:].T,
        outer[:, qo.shape[1] : qo.shape[1] + vo.shape[1]],
    )


def solution(mesh):
    in_specs = (
        P("fsdp", None),
        P("fsdp", None),
        P("fsdp", None),
        P(),
        P("fsdp", "tensor"),
        P("fsdp", "tensor"),
        P("fsdp", "tensor"),
        P("tensor", "fsdp"),
        P(),
        P(None, "tensor"),
        P(),
        P(None, "tensor"),
        P("fsdp"),
        P(),
    )
    out_specs = (P(), P("tensor", None), P(None, "tensor"), P("tensor", None), P(None, "tensor"))
    body = functools.partial(per_device, mesh.shape["fsdp"], mesh.shape["tensor"])
    return jax.shard_map(body, mesh=mesh, in_specs=in_specs, out_specs=out_specs, check_vma=False)
```

```python
import functools

import jax
import jax.numpy as jnp
from jax import lax
from jax.experimental import pallas as pl
from jax.experimental.pallas import tpu as pltpu
from jax.sharding import PartitionSpec as P

QUERY_HEADS = 32
KEY_VALUE_HEADS = 8
HEAD_SIZE = 128
L = 128
GROUP = QUERY_HEADS // KEY_VALUE_HEADS
QCOLS = GROUP * HEAD_SIZE

adapter_scale = 0.5
dpo_beta = 0.1
loss_scale = 256.0
rope_base = 500000.0
norm_eps = 1e-05

F32 = jnp.float32
BF16 = jnp.bfloat16
ORD = (0, 2, 1, 3)
MB = 1 << 20
SMALL = pl.CostEstimate(flops=1, bytes_accessed=1, transcendentals=0)


def rope_tables(length, head_dim):
    half_dim = head_dim // 2
    exponent = jnp.arange(half_dim, dtype=F32) * (2.0 / head_dim)
    inverse = jnp.power(F32(rope_base), -exponent)
    angles = jnp.arange(length, dtype=F32)[:, None] * inverse[None, :]
    cosine = jnp.concatenate([jnp.cos(angles), jnp.cos(angles)], 1)
    sine = jnp.concatenate([-jnp.sin(angles), jnp.sin(angles)], 1)
    return cosine, sine


def dot(a, b, dims=((1,), (0,))):
    return lax.dot_general(a, b, (dims, ((), ())), preferred_element_type=F32)


def params(limit_mb):
    return pltpu.CompilerParams(vmem_limit_bytes=limit_mb * MB)


def smem():
    return pl.BlockSpec(memory_space=pltpu.SMEM)


def full(a):
    return pl.BlockSpec(a.shape, lambda i: (0,) * len(a.shape))


def prep_body(parts, part, split, idx, ref, pol, tgt, gain, *outs):
    x0, x1, x2, x3, t0, t1, t2, t3, go = outs[-9:]
    groups = parts // split
    for d, (xo, to) in enumerate(((x0, t0), (x1, t1), (x2, t2), (x3, t3))):
        for j in range(parts):
            src = pl.ds(pl.multiple_of(idx[d * parts + j] * part, part), part)
            cols = slice(j * part, (j + 1) * part)
            if xo.shape[0] == 2:
                xo[0, :, cols] = ref[:, src]
                xo[1, :, cols] = pol[:, src]
            else:
                @pl.when(idx[4 * parts + 4 * groups] == 0)
                def _():
                    xo[0, :, cols] = ref[:, src]

                @pl.when(idx[4 * parts + 4 * groups] != 0)
                def _():
                    xo[0, :, cols] = pol[:, src]

        for j in range(groups):
            at = idx[4 * parts + d * groups + j] * part
            src = pl.ds(pl.multiple_of(at, part), part)
            to[:, j * part : (j + 1) * part] = tgt[:, src]
            if d == 0:
                go[:, j * part : (j + 1) * part] = gain[:, src]


def prep(idx, ref, pol, tgt, gain, parts, part, split, marks=()):
    tokens = ref.shape[0]
    xs = lambda n: jax.ShapeDtypeStruct((n, tokens, parts * part), BF16)
    far = 1 if split == 2 else 2
    width = parts // split * part
    shapes = [xs(2), xs(2), xs(far), xs(far)]
    shapes += [jax.ShapeDtypeStruct((tokens, width), BF16)] * 4
    shapes += [jax.ShapeDtypeStruct((1, width), F32)]
    return pl.pallas_call(
        functools.partial(prep_body, parts, part, split),
        in_specs=[smem()] + [pl.BlockSpec(memory_space=pltpu.VMEM)] * (4 + len(marks)),
        out_specs=[pl.BlockSpec(memory_space=pltpu.VMEM)] * 9,
        out_shape=shapes,
        compiler_params=params(32),
        cost_estimate=SMALL,
    )(idx, ref, pol, tgt, gain, *marks)


def tile_of(cols):
    for tile in (256, 128):
        if cols % tile == 0:
            return tile
    return cols


def mm_body(count, x_ref, *refs):
    ws, outs = refs[:count], refs[-2:]
    total = None
    at = 0
    for w in ws:
        depth = w.shape[0]
        term = dot(x_ref[:, at : at + depth], w[...])
        total = term if total is None else total + term
        at += depth
    rows = total.shape[0] // 2
    for i, out_ref in enumerate(outs):
        out_ref[...] = total[i * rows : (i + 1) * rows].astype(out_ref.dtype)


def mm(x, half, ws, out_dtype, marks=()):
    rows, depth = x.shape[0] // 2, x.shape[1]
    cols = ws[0].shape[1]
    tile = tile_of(cols)
    return pl.pallas_call(
        functools.partial(mm_body, len(ws)),
        grid=(cols // tile,),
        in_specs=[pl.BlockSpec((rows, depth), lambda i: (half, 0))]
        + [pl.BlockSpec((w.shape[0], tile), lambda i: (0, i)) for w in ws]
        + [full(a) for a in marks],
        out_specs=[pl.BlockSpec((rows // 2, tile), lambda i: (0, i))] * 2,
        out_shape=[jax.ShapeDtypeStruct((rows // 2, cols), out_dtype)] * 2,
        compiler_params=params(32),
        cost_estimate=SMALL,
    )(x, *ws, *marks)


def out_body(n, row_parts, counts, *refs):
    ws = refs[row_parts * n :][: sum(counts)]
    out_ref, total = refs[-2:]
    for j in range(n):
        x = jnp.concatenate([refs[p * n + j][...] for p in range(row_parts)], 0)
        depth = x.shape[1]
        at = 0
        for k, count in enumerate(counts):
            row = j * depth
            piece = at
            while row >= ws[piece].shape[0]:
                row -= ws[piece].shape[0]
                piece += 1
            at += count
            term = dot(x, ws[piece][row : row + depth])
            if j:
                term = term + total[k]
            if j == n - 1:
                out_ref[k] = term.astype(BF16)
            else:
                total[k] = term


def out_mm(parts, ws, marks=()):
    n = len(parts[0])
    rows = sum(part[0].shape[0] for part in parts)
    cols = ws[0][0].shape[1]
    flat = [piece for w in ws for piece in w]
    inputs = [a for part in parts for a in part] + flat + list(marks)
    out_shape = jax.ShapeDtypeStruct((len(ws), rows, cols), BF16)
    return pl.pallas_call(
        functools.partial(out_body, n, len(parts), tuple(len(w) for w in ws)),
        grid=(1,),
        in_specs=[full(a) for a in inputs],
        out_specs=full(out_shape),
        out_shape=out_shape,
        scratch_shapes=[pltpu.VMEM(out_shape.shape, F32)],
        compiler_params=params(32),
        cost_estimate=SMALL,
    )(*inputs)


def back_body(counts, part, has_acc, x_ref, *refs):
    total = None
    at = 0
    for j, count in enumerate(counts):
        w = refs[at][...]
        if count == 2:
            w = jnp.where(pl.program_id(0) < pl.num_programs(0) // 2, w, refs[at + 1][...])
        at += count
        term = dot(x_ref[:, j * part : (j + 1) * part], w, ((1,), (1,)))
        total = term if total is None else total + term
    refs = refs[at:]
    if has_acc:
        total = total + refs[0][...]
        keep, send = refs[1:]
        half = total.shape[0] // 2
        keep[...] = total[:half]
        send[...] = total[half:].astype(send.dtype)
    else:
        refs[0][...] = total


def back_mm(x, half, ws, acc):
    rows = x.shape[0] // (1 if half is None else 2)
    depth = x.shape[1]
    part = ws[0][0].shape[1]
    heads = sum(piece.shape[0] for piece in ws[0])
    tile = min(512, heads)
    steps = heads // tile
    has_acc = acc is not None
    row = half or 0
    in_specs = [pl.BlockSpec((rows, depth), lambda i: (row, 0))]
    for w in ws:
        if len(w) == 1:
            in_specs.append(pl.BlockSpec((tile, part), lambda i: (i, 0)))
        else:
            in_specs.append(pl.BlockSpec((tile, part), lambda i: (jnp.minimum(i, steps // 2 - 1), 0)))
            in_specs.append(pl.BlockSpec((tile, part), lambda i: (jnp.maximum(i - steps // 2, 0), 0)))
    args = [x] + [piece for w in ws for piece in w]
    if has_acc:
        in_specs.append(pl.BlockSpec((rows, tile), lambda i: (0, i)))
        args.append(acc)
        out_specs = [pl.BlockSpec((rows // 2, tile), lambda i: (0, i))] * 2
        out_shape = [
            jax.ShapeDtypeStruct((rows // 2, heads), F32),
            jax.ShapeDtypeStruct((rows // 2, heads), BF16),
        ]
    else:
        out_specs = pl.BlockSpec((rows, tile), lambda i: (0, i))
        out_shape = jax.ShapeDtypeStruct((rows, heads), F32)
    return pl.pallas_call(
        functools.partial(back_body, tuple(len(w) for w in ws), part, has_acc),
        grid=(steps,),
        in_specs=in_specs,
        out_specs=out_specs,
        out_shape=out_shape,
        compiler_params=params(32),
        cost_estimate=SMALL,
    )(*args)


def causal(rows):
    at = lax.broadcasted_iota(jnp.int32, (rows, L), 0) % L
    return at >= lax.broadcasted_iota(jnp.int32, (rows, L), 1)


def probabilities(q4, keys):
    scores = dot(q4, keys, ((1,), (1,))) * (HEAD_SIZE**-0.5)
    weights = jnp.where(causal(q4.shape[0]), jnp.exp(scores), 0.0)
    return weights / jnp.sum(weights, -1, keepdims=True)


def stack_heads(values):
    return jnp.concatenate(
        [values[:, h * HEAD_SIZE : (h + 1) * HEAD_SIZE] for h in range(GROUP)], 0
    )


def attend_body(adapted, keep, rs, r2, low, qo, vo, cos_ref, sin_ref, *refs):
    mixed, *saved = refs[-1 - adapted :]
    cosine = cos_ref[...]
    sine = sin_ref[...]
    pre = keep[...] + rs[...].astype(F32) + r2[...].astype(F32)
    rank = qo.shape[0]
    q_pre = pre[:, :QCOLS]
    k_pre = pre[:, QCOLS : QCOLS + HEAD_SIZE]
    v_pre = pre[:, QCOLS + HEAD_SIZE :]
    if adapted:
        q_pre = q_pre + adapter_scale * dot(low[:, :rank], qo[...])
        v_pre = v_pre + adapter_scale * dot(low[:, rank:], vo[...])
    cos4 = jnp.concatenate([cosine] * GROUP, 0)
    sin4 = jnp.concatenate([sine] * GROUP, 0)
    q4 = stack_heads(q_pre)
    q4 = (q4 * cos4 + pltpu.roll(q4, HEAD_SIZE // 2, 1) * sin4).astype(BF16)
    keys = (k_pre * cosine + pltpu.roll(k_pre, HEAD_SIZE // 2, 1) * sine).astype(BF16)
    values = v_pre.astype(BF16)
    rounded = probabilities(q4, keys).astype(BF16)
    out = dot(rounded, values).astype(BF16)
    for h in range(GROUP):
        cols = slice(h * HEAD_SIZE, (h + 1) * HEAD_SIZE)
        mixed[:, cols] = out[h * L : (h + 1) * L]
        if saved:
            saved[0][:, cols] = q4[h * L : (h + 1) * L]
    if saved:
        saved[0][:, QCOLS : QCOLS + HEAD_SIZE] = keys
        saved[0][:, QCOLS + HEAD_SIZE :] = values


def attend(adapted, keep, rs, r2, low, qo, vo, group, cosine, sine, marks=()):
    each = QCOLS + 2 * HEAD_SIZE
    rank = qo.shape[0]
    top = lambda a: pl.BlockSpec((L, a.shape[1]), lambda i: (0, 0))
    return pl.pallas_call(
        functools.partial(attend_body, adapted),
        grid=(1,),
        in_specs=[
            top(keep),
            top(rs),
            top(r2),
            top(low),
            pl.BlockSpec((rank, QCOLS), lambda i: (0, group)),
            pl.BlockSpec((rank, HEAD_SIZE), lambda i: (0, group)),
            top(cosine),
            top(sine),
        ]
        + [full(a) for a in marks],
        out_specs=[pl.BlockSpec((L, w), lambda i: (0, 0)) for w in (QCOLS, each)[: 1 + adapted]],
        out_shape=[jax.ShapeDtypeStruct((L, w), BF16) for w in (QCOLS, each)[: 1 + adapted]],
        compiler_params=params(32),
        cost_estimate=SMALL,
    )(keep, rs, r2, low, qo, vo, cosine, sine, *marks)


def outer_place(block, rank, kv):
    wide = (kv * (GROUP + 1) + 1) // 2
    return (block // wide) * rank, (block % wide) * HEAD_SIZE, wide


def attend_back_body(kv, splits, keep, rs, r2, low, qo, vo, cos_ref, sin_ref, *refs):
    saved = refs[:splits]
    outer, mid = refs[splits:]
    rank = qo.shape[0]
    each = QCOLS + 2 * HEAD_SIZE
    cos4 = jnp.concatenate([cos_ref[...]] * GROUP, 0)
    sin4 = jnp.concatenate([sin_ref[...]] * GROUP, 0)
    low_q = low[:, :rank]
    low_v = low[:, rank:]
    q_mid = jnp.zeros((L, rank), F32)
    v_mid = jnp.zeros((L, rank), F32)

    def put(block, value):
        row, col, _ = outer_place(block, rank, kv)
        outer[row : row + rank, col : col + HEAD_SIZE] = adapter_scale * value

    if (kv * (GROUP + 1)) % 2:
        put(kv * (GROUP + 1), jnp.zeros((rank, HEAD_SIZE), F32))
    for j in range(kv):
        cols = slice(j * QCOLS, (j + 1) * QCOLS)
        at = (j % (kv // splits)) * each
        kept = saved[j // (kv // splits)]
        grad = keep[:, cols] + rs[:, cols].astype(F32) + r2[:, cols].astype(F32)
        grad4 = stack_heads(grad.astype(BF16))
        q4 = stack_heads(kept[:, at : at + QCOLS])
        keys = kept[:, at + QCOLS : at + QCOLS + HEAD_SIZE]
        values = kept[:, at + QCOLS + HEAD_SIZE : at + each]
        prob = probabilities(q4, keys)
        grad_prob = dot(grad4, values, ((1,), (1,)))
        grad_values = dot(prob.astype(BF16), grad4, ((0,), (0,))).astype(BF16)
        inner = jnp.sum(grad_prob * prob, -1, keepdims=True)
        grad_scores = (prob * (grad_prob - inner) * (HEAD_SIZE**-0.5)).astype(BF16)
        grad_query = dot(grad_scores, keys)
        back4 = (grad_query * cos4 - pltpu.roll(grad_query, HEAD_SIZE // 2, 1) * sin4).astype(BF16)
        for h in range(GROUP):
            at = j * GROUP + h
            back = back4[h * L : (h + 1) * L]
            put(at, dot(low_q, back, ((0,), (0,))))
            q_mid += dot(back, qo[:, at * HEAD_SIZE : (at + 1) * HEAD_SIZE], ((1,), (1,)))
        put(kv * GROUP + j, dot(low_v, grad_values, ((0,), (0,))))
        v_mid += dot(grad_values, vo[:, j * HEAD_SIZE : (j + 1) * HEAD_SIZE], ((1,), (1,)))
    mid[:, :rank] = (adapter_scale * q_mid).astype(BF16)
    mid[:, rank:] = (adapter_scale * v_mid).astype(BF16)


def attend_back(keep, rs, r2, low, qo, vo, cosine, sine, saved):
    rank = qo.shape[0]
    kv = vo.shape[1] // HEAD_SIZE
    wide = outer_place(0, rank, kv)[2]
    inputs = (keep, rs, r2, low, qo, vo, cosine, sine, *saved)
    shapes = [
        jax.ShapeDtypeStruct((2 * rank, wide * HEAD_SIZE), F32),
        jax.ShapeDtypeStruct((L, 2 * rank), BF16),
    ]
    return pl.pallas_call(
        functools.partial(attend_back_body, kv, len(saved)),
        grid=(1,),
        in_specs=[full(a) for a in inputs],
        out_specs=[full(a) for a in shapes],
        out_shape=shapes,
        compiler_params=params(32),
        cost_estimate=SMALL,
    )(*inputs)


def adapter_body(n, rows_each, scal, states, outer, *refs):
    mids = refs[:n]
    away, stay = refs[n:]
    src = pl.ds(pl.multiple_of(scal[0] * rows_each, rows_each), rows_each)
    own = states[:, src]
    total = None
    for mid in mids:
        term = dot(mid[...], own, ((0,), (0,)))
        total = term if total is None else total + term
    half = total.shape[0] // 2
    for low in range(2):
        rows = slice(low * half, (low + 1) * half)

        @pl.when(scal[1] == low)
        def _():
            stay[:, :rows_each] = total[rows]
            stay[:, rows_each:] = outer[rows]

        @pl.when(scal[1] != low)
        def _():
            away[:, :rows_each] = total[rows].astype(BF16)
            away[:, rows_each:] = outer[rows].astype(BF16)


def adapter_products(scal, states, mids, outer, rows_each):
    half = outer.shape[0] // 2
    cols = rows_each + outer.shape[1]
    shapes = [jax.ShapeDtypeStruct((half, cols), BF16), jax.ShapeDtypeStruct((half, cols), F32)]
    return pl.pallas_call(
        functools.partial(adapter_body, len(mids), rows_each),
        grid=(1,),
        in_specs=[smem()] + [full(a) for a in (states, outer, *mids)],
        out_specs=[full(a) for a in shapes],
        out_shape=shapes,
        compiler_params=params(32),
        cost_estimate=SMALL,
    )(scal, states, outer, *mids)


def stats_body(counts, part, split, scal, xt_ref, xt_pol, tgt, gain, *refs):
    refs = list(refs)
    sums = []
    hidden_out, stats = refs[-2:]
    for which in range(2):
        xt = (xt_ref, xt_pol)[which]
        count = sum(counts)
        keeps = [r[i] for r in refs[: counts[0]] for i in range(r.shape[0])]
        recvs = [r[i] for r in refs[counts[0] : count] for i in range(r.shape[0])]
        refs = refs[count:]
        squares = jnp.zeros((L, HEAD_SIZE), F32)
        products = jnp.zeros((L, HEAD_SIZE), F32)
        for j, (keep, recv) in enumerate(zip(keeps, recvs)):
            src = pl.ds(pl.multiple_of((j * split + scal[0]) * part, part), part)
            hidden = xt[:, src].astype(F32) + keep.astype(F32) + recv.astype(F32)
            cols = slice(j * part, (j + 1) * part)
            if which == 1:
                hidden_out[0, :, cols] = hidden
            product = hidden * (gain[:, cols] * tgt[0, :, cols].astype(F32))
            square = hidden * hidden
            for s in range(part // HEAD_SIZE):
                lanes = slice(s * HEAD_SIZE, (s + 1) * HEAD_SIZE)
                squares += square[:, lanes]
                products += product[:, lanes]
        sums.append(
            [
                jnp.broadcast_to(jnp.sum(v, 1, keepdims=True), v.shape).T[:1]
                for v in (squares, products)
            ]
        )
    at = lax.broadcasted_iota(jnp.int32, (1, 2 * L), 1) % L
    own = (at >= scal[1]) & (pl.program_id(0) == 0)
    live = jnp.where(own, 1.0, 0.0).astype(F32)
    both = [jnp.concatenate([sums[0][i], sums[1][i]], 1) for i in range(2)]
    stats[...] = jnp.concatenate([*both, live, jnp.zeros((5, 2 * L), F32)], 0)


def norm_stats(scal, xt, tgt, gain, keeps, recvs, split):
    n = sum(a.shape[0] for a in keeps)
    part = keeps[0].shape[2]
    shared = []
    for which in range(2):
        at = functools.partial(lambda which, i: (0, 2 * i + which, 0), which)
        for a in (*keeps, *recvs):
            shared.append((a, pl.BlockSpec((a.shape[0], L, part), at)))
    return pl.pallas_call(
        functools.partial(stats_body, (len(keeps), len(recvs)), part, split),
        grid=(4,),
        in_specs=[
            smem(),
            pl.BlockSpec((L, xt.shape[1]), lambda i: ((i // 2) * 4 + i % 2, 0)),
            pl.BlockSpec((L, xt.shape[1]), lambda i: ((i // 2) * 4 + 2 + i % 2, 0)),
            pl.BlockSpec((1, L, n * part), lambda i: (i, 0, 0)),
            pl.BlockSpec((1, n * part), lambda i: (0, 0)),
        ]
        + [spec for _, spec in shared],
        out_specs=[
            pl.BlockSpec((1, L, n * part), lambda i: (i, 0, 0)),
            pl.BlockSpec((8, 2 * L), lambda i: (i, 0)),
        ],
        out_shape=[
            jax.ShapeDtypeStruct((4, L, n * part), F32),
            jax.ShapeDtypeStruct((32, 2 * L), F32),
        ],
        compiler_params=params(32),
        cost_estimate=SMALL,
    )(scal, xt, xt, tgt, gain, *[a for a, _ in shared])


def score_body(width, masks, ids, own, *refs):
    recvs = refs[: len(masks)]
    total_out, margin_out = refs[len(masks) :]
    lane = lax.broadcasted_iota(jnp.int32, (8, 128), 1)
    margins = jnp.zeros((8, 128), F32)
    for p in range(4):
        total = own[8 * p : 8 * p + 8]
        for recv, m in zip(recvs, masks):
            q = ORD.index(ORD[p] ^ m)
            total = total + recv[8 * q : 8 * q + 8]
        total_out[8 * p : 8 * p + 8] = total
        inverse = lax.rsqrt(total[0:1] * (1.0 / width) + norm_eps)
        score = total[1:2] * inverse * (width**-0.5)
        score = jnp.where(total[2:3] > 0.5, score, 0.0)
        margin = jnp.sum(score[:, L:], 1, keepdims=True) - jnp.sum(score[:, :L], 1, keepdims=True)
        margins = margins + jnp.where(lane == ids[p], margin, 0.0)
    margin_out[...] = margins


def scores(ids, own, recvs, masks, width):
    shapes = [jax.ShapeDtypeStruct(own.shape, F32), jax.ShapeDtypeStruct((8, 128), F32)]
    return pl.pallas_call(
        functools.partial(score_body, width, masks),
        grid=(1,),
        in_specs=[smem()] + [full(a) for a in (own, *recvs)],
        out_specs=[full(a) for a in shapes],
        out_shape=shapes,
        cost_estimate=SMALL,
    )(ids, own, *recvs)


def turn(i):
    return (2 * i + 1) % 5


def grad_body(width, seqs, n_vec, ids, pairs, total, hidden, tgt, gain, *refs):
    vecs = refs[:n_vec]
    grad_out, loss_out, slope = refs[n_vec:]
    lane = lax.broadcasted_iota(jnp.int32, (8, 128), 1)

    @pl.when(pl.program_id(0) == 0)
    def _():
        margin = vecs[0][...]
        for v in vecs[1:]:
            margin = margin + v[...]
        logits = jnp.zeros((8, 128), F32)
        for i in range(seqs // 2):
            sign = jnp.where(lane == pairs[2 * i], 1.0, 0.0) - jnp.where(
                lane == pairs[2 * i + 1], 1.0, 0.0
            )
            logit = dpo_beta * jnp.sum(margin * sign, 1, keepdims=True)
            logits = logits + jnp.where(lane == i, logit, 0.0)
        soft = jnp.maximum(-logits, 0.0) + jnp.log1p(jnp.exp(-jnp.abs(logits)))
        used = lane < seqs // 2
        loss = jnp.sum(jnp.where(used, soft, 0.0), 1, keepdims=True)
        loss_out[...] = jnp.broadcast_to(loss, (8, 128))
        slopes = jnp.where(used, -dpo_beta / (1.0 + jnp.exp(logits)), 0.0)
        gradient = jnp.zeros((8, 128), F32)
        for i in range(seqs // 2):
            each = jnp.sum(jnp.where(lane == i, slopes, 0.0), 1, keepdims=True)
            sign = jnp.where(lane == pairs[2 * i], 1.0, 0.0) - jnp.where(
                lane == pairs[2 * i + 1], 1.0, 0.0
            )
            gradient = gradient + each * sign
        slope[...] = gradient * loss_scale

    mine = lane == ids[turn(pl.program_id(0))]
    seq = jnp.sum(jnp.where(mine, slope[...], 0.0), 1, keepdims=True)[:1]
    rows = total[:, L:]
    token = jnp.where(rows[2:3] > 0.5, seq, 0.0) * (width**-0.5)
    inverse = lax.rsqrt(rows[0:1] * (1.0 / width) + norm_eps)
    first = inverse * token
    second = inverse * inverse * inverse * (token * rows[1:2] * (1.0 / width))
    first = jnp.broadcast_to(first, (L, L)).T
    second = jnp.broadcast_to(second, (L, L)).T
    for s in range(hidden.shape[2] // HEAD_SIZE):
        cols = slice(s * HEAD_SIZE, (s + 1) * HEAD_SIZE)
        weighted = gain[:, cols] * tgt[0, :, cols].astype(F32)
        grad_out[0, :, cols] = (first * weighted - second * hidden[0, :, cols]).astype(BF16)


def grad_hidden(ids, pairs, total, hidden, tgt, gain, vecs, width):
    n = hidden.shape[2]
    seqs = pairs.shape[0]
    return pl.pallas_call(
        functools.partial(grad_body, width, seqs, len(vecs)),
        grid=(4,),
        in_specs=[
            smem(),
            smem(),
            pl.BlockSpec((8, 2 * L), lambda i: (turn(i), 0)),
            pl.BlockSpec((1, L, n), lambda i: (turn(i), 0, 0)),
            pl.BlockSpec((1, L, n), lambda i: (turn(i), 0, 0)),
            pl.BlockSpec((1, n), lambda i: (0, 0)),
        ]
        + [pl.BlockSpec((8, 128), lambda i: (0, 0)) for _ in vecs],
        out_specs=[
            pl.BlockSpec((1, L, n), lambda i: (i, 0, 0)),
            pl.BlockSpec((8, 128), lambda i: (0, 0)),
        ],
        out_shape=[
            jax.ShapeDtypeStruct((4, L, n), BF16),
            jax.ShapeDtypeStruct((8, 128), F32),
        ],
        scratch_shapes=[pltpu.VMEM((8, 128), F32)],
        compiler_params=params(32),
        cost_estimate=SMALL,
    )(ids, pairs, total, hidden, tgt, gain, *vecs)


def per_device(
    fsdp_size,
    tensor_size,
    ref_states,
    pol_states,
    target_rows,
    norm_gain,
    wq,
    wk,
    wv,
    wo,
    qa,
    qo,
    va,
    vo,
    prompt_length,
    pairs,
):
    tokens, width = ref_states.shape
    groups = fsdp_size // 4
    near_z = fsdp_size // 4
    bits = []
    bit = 2
    while bit < fsdp_size:
        if bit != near_z:
            bits.append(bit)
        bit *= 2
    split = 2 if tensor_size == 2 and fsdp_size == 16 else 1
    kv_local = wk.shape[1] // HEAD_SIZE
    depth = wq.shape[0]
    part = depth // split
    rank = qa.shape[1]
    me = lax.axis_index("fsdp")
    x = lax.axis_index("tensor")
    side = x if split == 2 else 0

    def tmask(d):
        return (d & 1) | ((d >> 1) * near_z)

    def gmask(k):
        return sum(bit for i, bit in enumerate(bits) if (k >> i) & 1)

    def move(value, mask):
        return lax.ppermute(value, "fsdp", [(i, i ^ mask) for i in range(fsdp_size)])

    def swap_x(value):
        return lax.ppermute(value, "tensor", [(0, 1), (1, 0)])

    def move_both(value, mask, flip):
        pairs_list = [
            (2 * i + j, 2 * (i ^ mask) + (j ^ flip)) for i in range(fsdp_size) for j in range(2)
        ]
        return lax.ppermute(value, ("fsdp", "tensor"), pairs_list)

    def after(value, *others):
        return lax.optimization_barrier((value, *others))[0]

    def marker(*queue):
        return move(after(cosine[:16].astype(BF16), *queue), 2)

    cosine, sine = rope_tables(L, HEAD_SIZE)

    wide = groups == 4 and split == 2
    heads = wo.shape[0]

    def shard_of(j, *queue):
        q, k, v = wq, wk, wv
        if queue:
            q, k, v = lax.optimization_barrier((wq, wk, wv, *queue))[:3]
        pieces = [
            q[:, j * QCOLS : (j + 1) * QCOLS],
            k[:, j * HEAD_SIZE : (j + 1) * HEAD_SIZE],
            v[:, j * HEAD_SIZE : (j + 1) * HEAD_SIZE],
        ]
        return jnp.concatenate(pieces, 1)

    def gather(shard):
        return [shard] + [move(shard, gmask(k)) for k in range(1, groups)]

    if wide:
        over_y, over_z = gmask(1), gmask(2)
        shards = [shard_of(0)]
        zs = [move(shards[0], over_z)]
        ys = [move(shards[0], over_y)]
        corners = []

    parts = groups * split
    idx = []
    for d in range(4):
        for k in range(groups):
            for h in range(split):
                idx.append((me ^ tmask(d) ^ gmask(k)) * split + h)
    for d in range(4):
        for k in range(groups):
            idx.append((me ^ tmask(d) ^ gmask(k)) * split + side)
    idx.append(x)
    idx = jnp.stack(idx).astype(jnp.int32)
    marks = ()
    prepared = prep(
        idx,
        ref_states,
        pol_states,
        target_rows,
        norm_gain.astype(F32).reshape(1, width),
        parts,
        part,
        split,
        marks,
    )
    xs, ts, gain = prepared[:4], prepared[4:8], prepared[8]
    near = move(xs[1], 1)
    far = [move(xs[2], near_z)]
    far.append(move(xs[3], near_z | 1))

    targets = [ts[0]] + [move(after(ts[d], *far), tmask(d)) for d in (1, 2, 3)]
    if split == 2:
        other = [swap_x(a) for a in far]
        far = [
            [jnp.where(x == which, a[0], b[0]) for which in range(2)] for a, b in zip(far, other)
        ]
    states = jnp.concatenate(
        [
            *(xs[0][0], far[0][0], xs[0][1], far[0][1]),
            *(near[0], far[1][0], near[1], far[1][1]),
        ],
        0,
    )

    states = after(states, *targets[1:])
    tgt = jnp.stack([targets[d] for d in ORD])

    low = dot(pol_states, jnp.concatenate([qa, va], 1)).astype(BF16)
    cosine, sine = rope_tables(L, HEAD_SIZE)

    def own_columns(at, piece, *queue):
        return lax.dynamic_slice(
            after(wo, *queue), (piece * (heads // 2), at * part), (heads // 2, part)
        )

    def own_piece(step, *queue):
        at = (1 - x) if step < 2 else x
        return lax.dynamic_slice(
            after(wo, *queue), ((step % 2) * (heads // 2), at * part), (heads // 2, part)
        )

    def make_shard(j, *queue):
        if j < kv_local:
            shards.append(shard_of(j, *queue))
        elif j < kv_local + 4:
            shards.append(own_piece(j - kv_local, *queue))

    def next_shard(j, *more):
        queue = (zs[j - 1], ys[j - 1], *more)
        ys.append(move(after(shards[j], *queue), over_y))
        zs.append(move(after(shards[j], *queue), over_z))
        corners.append(move(after(*queue), over_y))

    saved = []
    parts_mixed = [[], [], []]

    def mix(j, keeps, came, sums, *queue, marks=()):
        results = []
        for which in range(2):
            total = sums[which * L : (which + 1) * L]
            result = attend(
                *(which == 1, keeps[which], came[which], total, low, qo, vo, j, cosine, sine),
                marks=marks,
            )
            saved.extend(result[1:])
            results.append(result[0])
        result = jnp.concatenate(results, 0)
        return result, move(after(result, *queue) if queue else result, near_z)

    def spread(result, other):
        far = move(jnp.concatenate([result, other], 0), 1)
        for part_mixed, value in zip(parts_mixed, (result, other, far)):
            part_mixed.append(value)
        return far

    if wide:
        make_shard(1, shards[0])
        next_shard(1)
        make_shard(2, zs[0])
    before = None
    ends = []
    for j in range(kv_local):
        if wide:
            marks = (marker(zs[j + 1], ys[j + 1]),)
            ws = [shards[j], ys[j], zs[j], corners[j]]
        else:
            ws = gather(shard_of(j))
        sends = mm(states, 1, ws, BF16, marks)
        came = [move(send, 1) for send in sends]
        keeps = mm(states, 0, ws, F32)
        if wide:
            next_shard(j + 2)
            make_shard(j + 3, zs[j + 1])
        over = jnp.concatenate(
            [(keeps[which][L:] + came[which][L:].astype(F32)).astype(BF16) for which in range(2)], 0
        )
        if before is not None:
            result, other = mix(j - 1, *before, *came, *ends)
            if j + 1 < kv_local:
                over = after(over, other)
            states = after(states, other)
            ends = [spread(result, other)]
        if wide:
            over = after(over, shards[-1])
        sums = move(over, near_z)
        if wide and j + 1 == kv_local:
            marks = (marker(zs[j + 2], ys[j + 2]),)
            make_shard(kv_local + 3, zs[-2])
        before = (keeps, came, sums)
    last = spread(*mix(kv_local - 1, *before, *ends, marks=marks))

    keeps, recvs = [], []
    if wide:
        next_shard(kv_local + 2, over)
        first = [a[kv_local : kv_local + 2] for a in (shards, ys, zs, corners)]
        marks = (marker(zs[-1], ys[-1]),)
        recvs.append(swap_x(out_mm(parts_mixed, first[:2], marks)))
        next_shard(kv_local + 3)
        recvs.append(swap_x(out_mm(parts_mixed, first[2:])))
        corners.append(move(after(zs[-1], ys[-1]), over_y))
        wo_send, wo_keep = first, [a[kv_local + 2 :] for a in (shards, ys, zs, corners)]
        keeps.append(out_mm(parts_mixed, wo_keep[:3]))
        keeps.append(out_mm(parts_mixed, wo_keep[3:]))
    else:
        wo_keep = [[w] for w in gather(wo)]
        product = out_mm(parts_mixed, wo_keep)
        if tensor_size > 1:
            product = lax.psum(product, "tensor")
        keeps.append(product)
        recvs.append(jnp.zeros_like(product))

    scal = jnp.stack([jnp.asarray(side, jnp.int32), prompt_length[0].astype(jnp.int32)])
    hidden, stats = norm_stats(scal, states, tgt, gain, keeps, recvs, split)
    masks, got = [], []
    for flip in range(split):
        for d in range(4):
            if d or flip:
                masks.append(d)
                if split == 2:
                    got.append(move_both(stats, tmask(d), flip))
                else:
                    got.append(move(stats, tmask(d)))
    ids = jnp.stack([me ^ tmask(d) for d in ORD]).astype(jnp.int32)
    total, margin = scores(ids, stats, got, tuple(masks), width)
    vecs = [margin] + [move(margin, gmask(k)) for k in range(1, groups)]
    grad, loss = grad_hidden(ids, pairs, total, hidden, tgt, gain, vecs, width)

    grad_rows = grad.reshape(4 * L, -1)
    other = None
    for half in range(2):
        if split == 2:
            leaving = grad_rows[2 * L * half : 2 * L * (half + 1)]
            other = swap_x(leaving if half == 0 else after(leaving, other))
            acc = back_mm(grad_rows, half, wo_keep, None)
            keep, send = back_mm(other, None, wo_send, acc)
        else:
            acc = jnp.zeros((2 * L, heads), F32)
            keep, send = back_mm(grad_rows, half, wo_keep, acc)
        rs = move(send if half == 0 else after(send, r2), 1)
        if half == 0:
            over = (keep + rs.astype(F32)).astype(BF16)
            r2 = move(over, near_z)
    outer, mid = attend_back(keep, rs, r2, low, qo, vo, cosine, sine, saved)

    rows_each = width // tensor_size
    if split == 2:
        mids = [mid, swap_x(mid)]
    elif tensor_size == 1:
        mids = [mid]
    else:
        gathered = lax.all_gather(mid, "tensor", axis=0, tiled=False)
        mids = [gathered[i] for i in range(tensor_size)]
    scal = jnp.stack([x, me & 1]).astype(jnp.int32)
    away, current = adapter_products(scal, pol_states, mids, outer, rows_each)
    current = current + move(away, 1).astype(F32)
    top = fsdp_size // 2
    g = (me // 2) % groups
    rows = current.shape[0] // groups
    pieces = [
        lax.dynamic_slice_in_dim(current, (g ^ k) * rows, rows, 0) for k in range(groups)
    ]
    current = pieces[0]
    for k in range(1, groups):
        current = current + move(pieces[k].astype(BF16), k << 1).astype(F32)
    rows //= 2
    high = me // top
    away = lax.dynamic_slice_in_dim(current, (1 - high) * rows, rows, 0).astype(BF16)
    current = lax.dynamic_slice_in_dim(current, high * rows, rows, 0)
    current = (current + move(away, top).astype(F32)).astype(BF16)

    def join(bit, own, other):
        return jnp.where(
            bit == 0, jnp.concatenate([own, other], 0), jnp.concatenate([other, own], 0)
        )

    current = join(high, current, move(current, top))
    pieces = [current] + [move(current, k << 1) for k in range(1, groups)]
    step = 1
    while step < groups:
        odd = (g & step) != 0
        pieces = [jnp.where(odd, pieces[k ^ step], pieces[k]) for k in range(groups)]
        step *= 2
    current = jnp.concatenate(pieces, 0)
    current = join(me & 1, current, move(current, 1)).astype(F32)
    a_grads = current[:, :rows_each]
    outer = current[:, rows_each:]
    outer = jnp.concatenate([outer[:rank], outer[rank:]], 1)
    return (
        loss[0, 0],
        a_grads[:rank].T,
        outer[:, : qo.shape[1]],
        a_grads[rank:].T,
        outer[:, qo.shape[1] : qo.shape[1] + vo.shape[1]],
    )


def solution(mesh):
    in_specs = (
        P("fsdp", None),
        P("fsdp", None),
        P("fsdp", None),
        P(),
        P("fsdp", "tensor"),
        P("fsdp", "tensor"),
        P("fsdp", "tensor"),
        P("tensor", "fsdp"),
        P(),
        P(None, "tensor"),
        P(),
        P(None, "tensor"),
        P("fsdp"),
        P(),
    )
    out_specs = (P(), P("tensor", None), P(None, "tensor"), P("tensor", None), P(None, "tensor"))
    body = functools.partial(per_device, mesh.shape["fsdp"], mesh.shape["tensor"])
    return jax.shard_map(body, mesh=mesh, in_specs=in_specs, out_specs=out_specs, check_vma=False)
```

```python
import functools

import jax
import jax.numpy as jnp
from jax import lax
from jax.experimental import pallas as pl
from jax.experimental.pallas import tpu as pltpu
from jax.sharding import PartitionSpec as P

QUERY_HEADS = 32
KEY_VALUE_HEADS = 8
HEAD_SIZE = 128
L = 128
GROUP = QUERY_HEADS // KEY_VALUE_HEADS
QCOLS = GROUP * HEAD_SIZE

adapter_scale = 0.5
dpo_beta = 0.1
loss_scale = 256.0
rope_base = 500000.0
norm_eps = 1e-05

F32 = jnp.float32
BF16 = jnp.bfloat16
ORD = (0, 2, 1, 3)
MB = 1 << 20
SMALL = pl.CostEstimate(flops=1, bytes_accessed=1, transcendentals=0)


def rope_tables(length, head_dim):
    half_dim = head_dim // 2
    exponent = jnp.arange(half_dim, dtype=F32) * (2.0 / head_dim)
    inverse = jnp.power(F32(rope_base), -exponent)
    angles = jnp.arange(length, dtype=F32)[:, None] * inverse[None, :]
    cosine = jnp.concatenate([jnp.cos(angles), jnp.cos(angles)], 1)
    sine = jnp.concatenate([-jnp.sin(angles), jnp.sin(angles)], 1)
    return cosine, sine


def dot(a, b, dims=((1,), (0,))):
    return lax.dot_general(a, b, (dims, ((), ())), preferred_element_type=F32)


def params(limit_mb):
    return pltpu.CompilerParams(vmem_limit_bytes=limit_mb * MB)


def smem():
    return pl.BlockSpec(memory_space=pltpu.SMEM)


def full(a):
    return pl.BlockSpec(a.shape, lambda i: (0,) * len(a.shape))


def prep_body(parts, part, split, idx, ref, pol, tgt, gain, *outs):
    x0, x1, x2, x3, t0, t1, t2, t3, go = outs[-9:]
    groups = parts // split
    for d, (xo, to) in enumerate(((x0, t0), (x1, t1), (x2, t2), (x3, t3))):
        for j in range(parts):
            src = pl.ds(pl.multiple_of(idx[d * parts + j] * part, part), part)
            cols = slice(j * part, (j + 1) * part)
            if xo.shape[0] == 2:
                xo[0, :, cols] = ref[:, src]
                xo[1, :, cols] = pol[:, src]
            else:
                @pl.when(idx[4 * parts + 4 * groups] == 0)
                def _():
                    xo[0, :, cols] = ref[:, src]

                @pl.when(idx[4 * parts + 4 * groups] != 0)
                def _():
                    xo[0, :, cols] = pol[:, src]

        for j in range(groups):
            at = idx[4 * parts + d * groups + j] * part
            src = pl.ds(pl.multiple_of(at, part), part)
            to[:, j * part : (j + 1) * part] = tgt[:, src]
            if d == 0:
                go[:, j * part : (j + 1) * part] = gain[:, src]


def prep(idx, ref, pol, tgt, gain, parts, part, split, marks=()):
    tokens = ref.shape[0]
    xs = lambda n: jax.ShapeDtypeStruct((n, tokens, parts * part), BF16)
    far = 1 if split == 2 else 2
    width = parts // split * part
    shapes = [xs(2), xs(2), xs(far), xs(far)]
    shapes += [jax.ShapeDtypeStruct((tokens, width), BF16)] * 4
    shapes += [jax.ShapeDtypeStruct((1, width), F32)]
    return pl.pallas_call(
        functools.partial(prep_body, parts, part, split),
        in_specs=[smem()] + [pl.BlockSpec(memory_space=pltpu.VMEM)] * (4 + len(marks)),
        out_specs=[pl.BlockSpec(memory_space=pltpu.VMEM)] * 9,
        out_shape=shapes,
        compiler_params=params(32),
        cost_estimate=SMALL,
    )(idx, ref, pol, tgt, gain, *marks)


def tile_of(cols):
    for tile in (256, 128):
        if cols % tile == 0:
            return tile
    return cols


def mm_body(count, x_ref, *refs):
    ws, outs = refs[:count], refs[-2:]
    total = None
    at = 0
    for w in ws:
        depth = w.shape[0]
        term = dot(x_ref[:, at : at + depth], w[...])
        total = term if total is None else total + term
        at += depth
    rows = total.shape[0] // 2
    for i, out_ref in enumerate(outs):
        out_ref[...] = total[i * rows : (i + 1) * rows].astype(out_ref.dtype)


def mm(x, half, ws, out_dtype, marks=()):
    rows, depth = x.shape[0] // 2, x.shape[1]
    cols = ws[0].shape[1]
    tile = tile_of(cols)
    return pl.pallas_call(
        functools.partial(mm_body, len(ws)),
        grid=(cols // tile,),
        in_specs=[pl.BlockSpec((rows, depth), lambda i: (half, 0))]
        + [pl.BlockSpec((w.shape[0], tile), lambda i: (0, i)) for w in ws]
        + [full(a) for a in marks],
        out_specs=[pl.BlockSpec((rows // 2, tile), lambda i: (0, i))] * 2,
        out_shape=[jax.ShapeDtypeStruct((rows // 2, cols), out_dtype)] * 2,
        compiler_params=params(32),
        cost_estimate=SMALL,
    )(x, *ws, *marks)


def out_body(n, row_parts, counts, *refs):
    ws = refs[row_parts * n :][: sum(counts)]
    out_ref, total = refs[-2:]
    for j in range(n):
        x = jnp.concatenate([refs[p * n + j][...] for p in range(row_parts)], 0)
        depth = x.shape[1]
        at = 0
        for k, count in enumerate(counts):
            row = j * depth
            piece = at
            while row >= ws[piece].shape[0]:
                row -= ws[piece].shape[0]
                piece += 1
            at += count
            term = dot(x, ws[piece][row : row + depth])
            if j:
                term = term + total[k]
            if j == n - 1:
                out_ref[k] = term.astype(BF16)
            else:
                total[k] = term


def out_mm(parts, ws, marks=()):
    n = len(parts[0])
    rows = sum(part[0].shape[0] for part in parts)
    cols = ws[0][0].shape[1]
    flat = [piece for w in ws for piece in w]
    inputs = [a for part in parts for a in part] + flat + list(marks)
    out_shape = jax.ShapeDtypeStruct((len(ws), rows, cols), BF16)
    return pl.pallas_call(
        functools.partial(out_body, n, len(parts), tuple(len(w) for w in ws)),
        grid=(1,),
        in_specs=[full(a) for a in inputs],
        out_specs=full(out_shape),
        out_shape=out_shape,
        scratch_shapes=[pltpu.VMEM(out_shape.shape, F32)],
        compiler_params=params(32),
        cost_estimate=SMALL,
    )(*inputs)


def back_body(counts, part, has_acc, x_ref, *refs):
    total = None
    at = 0
    for j, count in enumerate(counts):
        w = refs[at][...]
        if count == 2:
            w = jnp.where(pl.program_id(0) < pl.num_programs(0) // 2, w, refs[at + 1][...])
        at += count
        term = dot(x_ref[:, j * part : (j + 1) * part], w, ((1,), (1,)))
        total = term if total is None else total + term
    refs = refs[at:]
    if has_acc:
        total = total + refs[0][...]
        keep, send = refs[1:]
        half = total.shape[0] // 2
        keep[...] = total[:half]
        send[...] = total[half:].astype(send.dtype)
    else:
        refs[0][...] = total


def back_mm(x, half, ws, acc):
    rows = x.shape[0] // (1 if half is None else 2)
    depth = x.shape[1]
    part = ws[0][0].shape[1]
    heads = sum(piece.shape[0] for piece in ws[0])
    tile = min(512, heads)
    steps = heads // tile
    has_acc = acc is not None
    row = half or 0
    in_specs = [pl.BlockSpec((rows, depth), lambda i: (row, 0))]
    for w in ws:
        if len(w) == 1:
            in_specs.append(pl.BlockSpec((tile, part), lambda i: (i, 0)))
        else:
            in_specs.append(pl.BlockSpec((tile, part), lambda i: (jnp.minimum(i, steps // 2 - 1), 0)))
            in_specs.append(pl.BlockSpec((tile, part), lambda i: (jnp.maximum(i - steps // 2, 0), 0)))
    args = [x] + [piece for w in ws for piece in w]
    if has_acc:
        in_specs.append(pl.BlockSpec((rows, tile), lambda i: (0, i)))
        args.append(acc)
        out_specs = [pl.BlockSpec((rows // 2, tile), lambda i: (0, i))] * 2
        out_shape = [
            jax.ShapeDtypeStruct((rows // 2, heads), F32),
            jax.ShapeDtypeStruct((rows // 2, heads), BF16),
        ]
    else:
        out_specs = pl.BlockSpec((rows, tile), lambda i: (0, i))
        out_shape = jax.ShapeDtypeStruct((rows, heads), F32)
    return pl.pallas_call(
        functools.partial(back_body, tuple(len(w) for w in ws), part, has_acc),
        grid=(steps,),
        in_specs=in_specs,
        out_specs=out_specs,
        out_shape=out_shape,
        compiler_params=params(32),
        cost_estimate=SMALL,
    )(*args)


def causal(rows):
    at = lax.broadcasted_iota(jnp.int32, (rows, L), 0) % L
    return at >= lax.broadcasted_iota(jnp.int32, (rows, L), 1)


def probabilities(q4, keys):
    scores = dot(q4, keys, ((1,), (1,))) * (HEAD_SIZE**-0.5)
    weights = jnp.where(causal(q4.shape[0]), jnp.exp(scores), 0.0)
    return weights / jnp.sum(weights, -1, keepdims=True)


def stack_heads(values):
    return jnp.concatenate(
        [values[:, h * HEAD_SIZE : (h + 1) * HEAD_SIZE] for h in range(GROUP)], 0
    )


def attend_body(adapted, keep, rs, r2, low, qo, vo, cos_ref, sin_ref, *refs):
    mixed, *saved = refs[-1 - adapted :]
    cosine = cos_ref[...]
    sine = sin_ref[...]
    pre = keep[...] + rs[...].astype(F32) + r2[...].astype(F32)
    rank = qo.shape[0]
    q_pre = pre[:, :QCOLS]
    k_pre = pre[:, QCOLS : QCOLS + HEAD_SIZE]
    v_pre = pre[:, QCOLS + HEAD_SIZE :]
    if adapted:
        q_pre = q_pre + adapter_scale * dot(low[:, :rank], qo[...])
        v_pre = v_pre + adapter_scale * dot(low[:, rank:], vo[...])
    cos4 = jnp.concatenate([cosine] * GROUP, 0)
    sin4 = jnp.concatenate([sine] * GROUP, 0)
    q4 = stack_heads(q_pre)
    q4 = (q4 * cos4 + pltpu.roll(q4, HEAD_SIZE // 2, 1) * sin4).astype(BF16)
    keys = (k_pre * cosine + pltpu.roll(k_pre, HEAD_SIZE // 2, 1) * sine).astype(BF16)
    values = v_pre.astype(BF16)
    rounded = probabilities(q4, keys).astype(BF16)
    out = dot(rounded, values).astype(BF16)
    for h in range(GROUP):
        cols = slice(h * HEAD_SIZE, (h + 1) * HEAD_SIZE)
        mixed[:, cols] = out[h * L : (h + 1) * L]
        if saved:
            saved[0][:, cols] = q4[h * L : (h + 1) * L]
    if saved:
        saved[0][:, QCOLS : QCOLS + HEAD_SIZE] = keys
        saved[0][:, QCOLS + HEAD_SIZE :] = values


def attend(adapted, keep, rs, r2, low, qo, vo, group, cosine, sine, marks=()):
    each = QCOLS + 2 * HEAD_SIZE
    rank = qo.shape[0]
    top = lambda a: pl.BlockSpec((L, a.shape[1]), lambda i: (0, 0))
    return pl.pallas_call(
        functools.partial(attend_body, adapted),
        grid=(1,),
        in_specs=[
            top(keep),
            top(rs),
            top(r2),
            top(low),
            pl.BlockSpec((rank, QCOLS), lambda i: (0, group)),
            pl.BlockSpec((rank, HEAD_SIZE), lambda i: (0, group)),
            top(cosine),
            top(sine),
        ]
        + [full(a) for a in marks],
        out_specs=[pl.BlockSpec((L, w), lambda i: (0, 0)) for w in (QCOLS, each)[: 1 + adapted]],
        out_shape=[jax.ShapeDtypeStruct((L, w), BF16) for w in (QCOLS, each)[: 1 + adapted]],
        compiler_params=params(32),
        cost_estimate=SMALL,
    )(keep, rs, r2, low, qo, vo, cosine, sine, *marks)


def outer_place(block, rank, kv):
    wide = (kv * (GROUP + 1) + 1) // 2
    return (block // wide) * rank, (block % wide) * HEAD_SIZE, wide


def attend_back_body(kv, splits, keep, rs, r2, low, qo, vo, cos_ref, sin_ref, *refs):
    saved = refs[:splits]
    outer, mid = refs[splits:]
    rank = qo.shape[0]
    each = QCOLS + 2 * HEAD_SIZE
    cos4 = jnp.concatenate([cos_ref[...]] * GROUP, 0)
    sin4 = jnp.concatenate([sin_ref[...]] * GROUP, 0)
    low_q = low[:, :rank]
    low_v = low[:, rank:]
    q_mid = jnp.zeros((L, rank), F32)
    v_mid = jnp.zeros((L, rank), F32)

    def put(block, value):
        row, col, _ = outer_place(block, rank, kv)
        outer[row : row + rank, col : col + HEAD_SIZE] = adapter_scale * value

    if (kv * (GROUP + 1)) % 2:
        put(kv * (GROUP + 1), jnp.zeros((rank, HEAD_SIZE), F32))
    for j in range(kv):
        cols = slice(j * QCOLS, (j + 1) * QCOLS)
        at = (j % (kv // splits)) * each
        kept = saved[j // (kv // splits)]
        grad = keep[:, cols] + rs[:, cols].astype(F32) + r2[:, cols].astype(F32)
        grad4 = stack_heads(grad.astype(BF16))
        q4 = stack_heads(kept[:, at : at + QCOLS])
        keys = kept[:, at + QCOLS : at + QCOLS + HEAD_SIZE]
        values = kept[:, at + QCOLS + HEAD_SIZE : at + each]
        prob = probabilities(q4, keys)
        grad_prob = dot(grad4, values, ((1,), (1,)))
        grad_values = dot(prob.astype(BF16), grad4, ((0,), (0,))).astype(BF16)
        inner = jnp.sum(grad_prob * prob, -1, keepdims=True)
        grad_scores = (prob * (grad_prob - inner) * (HEAD_SIZE**-0.5)).astype(BF16)
        grad_query = dot(grad_scores, keys)
        back4 = (grad_query * cos4 - pltpu.roll(grad_query, HEAD_SIZE // 2, 1) * sin4).astype(BF16)
        for h in range(GROUP):
            at = j * GROUP + h
            back = back4[h * L : (h + 1) * L]
            put(at, dot(low_q, back, ((0,), (0,))))
            q_mid += dot(back, qo[:, at * HEAD_SIZE : (at + 1) * HEAD_SIZE], ((1,), (1,)))
        put(kv * GROUP + j, dot(low_v, grad_values, ((0,), (0,))))
        v_mid += dot(grad_values, vo[:, j * HEAD_SIZE : (j + 1) * HEAD_SIZE], ((1,), (1,)))
    mid[:, :rank] = (adapter_scale * q_mid).astype(BF16)
    mid[:, rank:] = (adapter_scale * v_mid).astype(BF16)


def attend_back(keep, rs, r2, low, qo, vo, cosine, sine, saved):
    rank = qo.shape[0]
    kv = vo.shape[1] // HEAD_SIZE
    wide = outer_place(0, rank, kv)[2]
    inputs = (keep, rs, r2, low, qo, vo, cosine, sine, *saved)
    shapes = [
        jax.ShapeDtypeStruct((2 * rank, wide * HEAD_SIZE), F32),
        jax.ShapeDtypeStruct((L, 2 * rank), BF16),
    ]
    return pl.pallas_call(
        functools.partial(attend_back_body, kv, len(saved)),
        grid=(1,),
        in_specs=[full(a) for a in inputs],
        out_specs=[full(a) for a in shapes],
        out_shape=shapes,
        compiler_params=params(32),
        cost_estimate=SMALL,
    )(*inputs)


def adapter_body(n, rows_each, scal, states, outer, *refs):
    mids = refs[:n]
    away, stay = refs[n:]
    src = pl.ds(pl.multiple_of(scal[0] * rows_each, rows_each), rows_each)
    own = states[:, src]
    total = None
    for mid in mids:
        term = dot(mid[...], own, ((0,), (0,)))
        total = term if total is None else total + term
    half = total.shape[0] // 2
    for low in range(2):
        rows = slice(low * half, (low + 1) * half)

        @pl.when(scal[1] == low)
        def _():
            stay[:, :rows_each] = total[rows]
            stay[:, rows_each:] = outer[rows]

        @pl.when(scal[1] != low)
        def _():
            away[:, :rows_each] = total[rows].astype(BF16)
            away[:, rows_each:] = outer[rows].astype(BF16)


def adapter_products(scal, states, mids, outer, rows_each):
    half = outer.shape[0] // 2
    cols = rows_each + outer.shape[1]
    shapes = [jax.ShapeDtypeStruct((half, cols), BF16), jax.ShapeDtypeStruct((half, cols), F32)]
    return pl.pallas_call(
        functools.partial(adapter_body, len(mids), rows_each),
        grid=(1,),
        in_specs=[smem()] + [full(a) for a in (states, outer, *mids)],
        out_specs=[full(a) for a in shapes],
        out_shape=shapes,
        compiler_params=params(32),
        cost_estimate=SMALL,
    )(scal, states, outer, *mids)


def assemble_body(rows_each, bit, own, other, q_inner, q_outer, v_inner, v_outer):
    low = jnp.where(bit[0] == 0, own[...], other[...]).astype(F32)
    high = jnp.where(bit[0] == 0, other[...], own[...]).astype(F32)
    q_inner[...] = low[:, :rows_each]
    v_inner[...] = high[:, :rows_each]
    outer = jnp.concatenate([low[:, rows_each:], high[:, rows_each:]], 1)
    cols = q_outer.shape[1]
    q_outer[...] = outer[:, :cols]
    v_outer[...] = outer[:, cols : cols + v_outer.shape[1]]


def assemble(bit, own, other, rows_each, q_cols, v_cols):
    rank = own.shape[0]
    shapes = [jax.ShapeDtypeStruct((rank, c), F32) for c in (rows_each, q_cols, rows_each, v_cols)]
    return pl.pallas_call(
        functools.partial(assemble_body, rows_each),
        grid=(1,),
        in_specs=[smem(), full(own), full(other)],
        out_specs=[full(a) for a in shapes],
        out_shape=shapes,
        compiler_params=params(32),
        cost_estimate=SMALL,
    )(bit, own, other)


def stats_body(counts, part, split, scal, xt_ref, xt_pol, tgt, gain, *refs):
    refs = list(refs)
    sums = []
    hidden_out, stats = refs[-2:]
    for which in range(2):
        xt = (xt_ref, xt_pol)[which]
        count = sum(counts)
        keeps = [r[i] for r in refs[: counts[0]] for i in range(r.shape[0])]
        recvs = [r[i] for r in refs[counts[0] : count] for i in range(r.shape[0])]
        refs = refs[count:]
        squares = jnp.zeros((L, HEAD_SIZE), F32)
        products = jnp.zeros((L, HEAD_SIZE), F32)
        for j, (keep, recv) in enumerate(zip(keeps, recvs)):
            src = pl.ds(pl.multiple_of((j * split + scal[0]) * part, part), part)
            hidden = xt[:, src].astype(F32) + keep.astype(F32) + recv.astype(F32)
            cols = slice(j * part, (j + 1) * part)
            if which == 1:
                hidden_out[0, :, cols] = hidden
            product = hidden * (gain[:, cols] * tgt[0, :, cols].astype(F32))
            square = hidden * hidden
            for s in range(part // HEAD_SIZE):
                lanes = slice(s * HEAD_SIZE, (s + 1) * HEAD_SIZE)
                squares += square[:, lanes]
                products += product[:, lanes]
        sums.append(
            [
                jnp.broadcast_to(jnp.sum(v, 1, keepdims=True), v.shape).T[:1]
                for v in (squares, products)
            ]
        )
    at = lax.broadcasted_iota(jnp.int32, (1, 2 * L), 1) % L
    own = (at >= scal[1]) & (pl.program_id(0) == 0)
    live = jnp.where(own, 1.0, 0.0).astype(F32)
    both = [jnp.concatenate([sums[0][i], sums[1][i]], 1) for i in range(2)]
    stats[...] = jnp.concatenate([*both, live, jnp.zeros((5, 2 * L), F32)], 0)


def norm_stats(scal, xt, tgt, gain, keeps, recvs, split):
    n = sum(a.shape[0] for a in keeps)
    part = keeps[0].shape[2]
    shared = []
    for which in range(2):
        at = functools.partial(lambda which, i: (0, 2 * i + which, 0), which)
        for a in (*keeps, *recvs):
            shared.append((a, pl.BlockSpec((a.shape[0], L, part), at)))
    return pl.pallas_call(
        functools.partial(stats_body, (len(keeps), len(recvs)), part, split),
        grid=(4,),
        in_specs=[
            smem(),
            pl.BlockSpec((L, xt.shape[1]), lambda i: ((i // 2) * 4 + i % 2, 0)),
            pl.BlockSpec((L, xt.shape[1]), lambda i: ((i // 2) * 4 + 2 + i % 2, 0)),
            pl.BlockSpec((1, L, n * part), lambda i: (i, 0, 0)),
            pl.BlockSpec((1, n * part), lambda i: (0, 0)),
        ]
        + [spec for _, spec in shared],
        out_specs=[
            pl.BlockSpec((1, L, n * part), lambda i: (i, 0, 0)),
            pl.BlockSpec((8, 2 * L), lambda i: (i, 0)),
        ],
        out_shape=[
            jax.ShapeDtypeStruct((4, L, n * part), F32),
            jax.ShapeDtypeStruct((32, 2 * L), F32),
        ],
        compiler_params=params(32),
        cost_estimate=SMALL,
    )(scal, xt, xt, tgt, gain, *[a for a, _ in shared])


def score_body(width, masks, ids, own, *refs):
    recvs = refs[: len(masks)]
    total_out, margin_out = refs[len(masks) :]
    lane = lax.broadcasted_iota(jnp.int32, (8, 128), 1)
    margins = jnp.zeros((8, 128), F32)
    for p in range(4):
        total = own[8 * p : 8 * p + 8]
        for recv, m in zip(recvs, masks):
            q = ORD.index(ORD[p] ^ m)
            total = total + recv[8 * q : 8 * q + 8]
        total_out[8 * p : 8 * p + 8] = total
        inverse = lax.rsqrt(total[0:1] * (1.0 / width) + norm_eps)
        score = total[1:2] * inverse * (width**-0.5)
        score = jnp.where(total[2:3] > 0.5, score, 0.0)
        margin = jnp.sum(score[:, L:], 1, keepdims=True) - jnp.sum(score[:, :L], 1, keepdims=True)
        margins = margins + jnp.where(lane == ids[p], margin, 0.0)
    margin_out[...] = margins


def scores(ids, own, recvs, masks, width):
    shapes = [jax.ShapeDtypeStruct(own.shape, F32), jax.ShapeDtypeStruct((8, 128), F32)]
    return pl.pallas_call(
        functools.partial(score_body, width, masks),
        grid=(1,),
        in_specs=[smem()] + [full(a) for a in (own, *recvs)],
        out_specs=[full(a) for a in shapes],
        out_shape=shapes,
        cost_estimate=SMALL,
    )(ids, own, *recvs)


def turn(i):
    return (2 * i + 1) % 5


def grad_body(width, seqs, n_vec, ids, pairs, total, hidden, tgt, gain, *refs):
    vecs = refs[:n_vec]
    grad_out, loss_out, slope = refs[n_vec:]
    lane = lax.broadcasted_iota(jnp.int32, (8, 128), 1)

    @pl.when(pl.program_id(0) == 0)
    def _():
        margin = vecs[0][...]
        for v in vecs[1:]:
            margin = margin + v[...]
        logits = jnp.zeros((8, 128), F32)
        for i in range(seqs // 2):
            sign = jnp.where(lane == pairs[2 * i], 1.0, 0.0) - jnp.where(
                lane == pairs[2 * i + 1], 1.0, 0.0
            )
            logit = dpo_beta * jnp.sum(margin * sign, 1, keepdims=True)
            logits = logits + jnp.where(lane == i, logit, 0.0)
        soft = jnp.maximum(-logits, 0.0) + jnp.log1p(jnp.exp(-jnp.abs(logits)))
        used = lane < seqs // 2
        loss = jnp.sum(jnp.where(used, soft, 0.0), 1, keepdims=True)
        loss_out[...] = jnp.broadcast_to(loss, (8, 128))
        slopes = jnp.where(used, -dpo_beta / (1.0 + jnp.exp(logits)), 0.0)
        gradient = jnp.zeros((8, 128), F32)
        for i in range(seqs // 2):
            each = jnp.sum(jnp.where(lane == i, slopes, 0.0), 1, keepdims=True)
            sign = jnp.where(lane == pairs[2 * i], 1.0, 0.0) - jnp.where(
                lane == pairs[2 * i + 1], 1.0, 0.0
            )
            gradient = gradient + each * sign
        slope[...] = gradient * loss_scale

    mine = lane == ids[turn(pl.program_id(0))]
    seq = jnp.sum(jnp.where(mine, slope[...], 0.0), 1, keepdims=True)[:1]
    rows = total[:, L:]
    token = jnp.where(rows[2:3] > 0.5, seq, 0.0) * (width**-0.5)
    inverse = lax.rsqrt(rows[0:1] * (1.0 / width) + norm_eps)
    first = inverse * token
    second = inverse * inverse * inverse * (token * rows[1:2] * (1.0 / width))
    first = jnp.broadcast_to(first, (L, L)).T
    second = jnp.broadcast_to(second, (L, L)).T
    for s in range(hidden.shape[2] // HEAD_SIZE):
        cols = slice(s * HEAD_SIZE, (s + 1) * HEAD_SIZE)
        weighted = gain[:, cols] * tgt[0, :, cols].astype(F32)
        grad_out[0, :, cols] = (first * weighted - second * hidden[0, :, cols]).astype(BF16)


def grad_hidden(ids, pairs, total, hidden, tgt, gain, vecs, width):
    n = hidden.shape[2]
    seqs = pairs.shape[0]
    return pl.pallas_call(
        functools.partial(grad_body, width, seqs, len(vecs)),
        grid=(4,),
        in_specs=[
            smem(),
            smem(),
            pl.BlockSpec((8, 2 * L), lambda i: (turn(i), 0)),
            pl.BlockSpec((1, L, n), lambda i: (turn(i), 0, 0)),
            pl.BlockSpec((1, L, n), lambda i: (turn(i), 0, 0)),
            pl.BlockSpec((1, n), lambda i: (0, 0)),
        ]
        + [pl.BlockSpec((8, 128), lambda i: (0, 0)) for _ in vecs],
        out_specs=[
            pl.BlockSpec((1, L, n), lambda i: (i, 0, 0)),
            pl.BlockSpec((8, 128), lambda i: (0, 0)),
        ],
        out_shape=[
            jax.ShapeDtypeStruct((4, L, n), BF16),
            jax.ShapeDtypeStruct((8, 128), F32),
        ],
        scratch_shapes=[pltpu.VMEM((8, 128), F32)],
        compiler_params=params(32),
        cost_estimate=SMALL,
    )(ids, pairs, total, hidden, tgt, gain, *vecs)


def per_device(
    fsdp_size,
    tensor_size,
    ref_states,
    pol_states,
    target_rows,
    norm_gain,
    wq,
    wk,
    wv,
    wo,
    qa,
    qo,
    va,
    vo,
    prompt_length,
    pairs,
):
    tokens, width = ref_states.shape
    groups = fsdp_size // 4
    near_z = fsdp_size // 4
    bits = []
    bit = 2
    while bit < fsdp_size:
        if bit != near_z:
            bits.append(bit)
        bit *= 2
    split = 2 if tensor_size == 2 and fsdp_size == 16 else 1
    kv_local = wk.shape[1] // HEAD_SIZE
    depth = wq.shape[0]
    part = depth // split
    rank = qa.shape[1]
    me = lax.axis_index("fsdp")
    x = lax.axis_index("tensor")
    side = x if split == 2 else 0

    def tmask(d):
        return (d & 1) | ((d >> 1) * near_z)

    def gmask(k):
        return sum(bit for i, bit in enumerate(bits) if (k >> i) & 1)

    def move(value, mask):
        return lax.ppermute(value, "fsdp", [(i, i ^ mask) for i in range(fsdp_size)])

    def swap_x(value):
        return lax.ppermute(value, "tensor", [(0, 1), (1, 0)])

    def move_both(value, mask, flip):
        pairs_list = [
            (2 * i + j, 2 * (i ^ mask) + (j ^ flip)) for i in range(fsdp_size) for j in range(2)
        ]
        return lax.ppermute(value, ("fsdp", "tensor"), pairs_list)

    def after(value, *others):
        return lax.optimization_barrier((value, *others))[0]

    def marker(*queue):
        return move(after(cosine[:16].astype(BF16), *queue), 1)

    cosine, sine = rope_tables(L, HEAD_SIZE)

    wide = groups == 4 and split == 2
    heads = wo.shape[0]

    def shard_of(j, *queue):
        q, k, v = wq, wk, wv
        if queue:
            q, k, v = lax.optimization_barrier((wq, wk, wv, *queue))[:3]
        pieces = [
            q[:, j * QCOLS : (j + 1) * QCOLS],
            k[:, j * HEAD_SIZE : (j + 1) * HEAD_SIZE],
            v[:, j * HEAD_SIZE : (j + 1) * HEAD_SIZE],
        ]
        return jnp.concatenate(pieces, 1)

    def gather(shard):
        return [shard] + [move(shard, gmask(k)) for k in range(1, groups)]

    if wide:
        over_y, over_z = gmask(1), gmask(2)
        shards = [shard_of(0)]
        zs = [move(shards[0], over_z)]
        ys = [move(shards[0], over_y)]
        corners = []

    parts = groups * split
    idx = []
    for d in range(4):
        for k in range(groups):
            for h in range(split):
                idx.append((me ^ tmask(d) ^ gmask(k)) * split + h)
    for d in range(4):
        for k in range(groups):
            idx.append((me ^ tmask(d) ^ gmask(k)) * split + side)
    idx.append(x)
    idx = jnp.stack(idx).astype(jnp.int32)
    marks = ()
    prepared = prep(
        idx,
        ref_states,
        pol_states,
        target_rows,
        norm_gain.astype(F32).reshape(1, width),
        parts,
        part,
        split,
        marks,
    )
    xs, ts, gain = prepared[:4], prepared[4:8], prepared[8]
    near = move(xs[1], 1)
    far = [move(xs[2], near_z)]
    far.append(move(xs[3], near_z | 1))

    if split == 2:
        other = [swap_x(a) for a in far]
        far = [
            [jnp.where(x == which, a[0], b[0]) for which in range(2)] for a, b in zip(far, other)
        ]
    states = jnp.concatenate(
        [
            *(xs[0][0], far[0][0], xs[0][1], far[0][1]),
            *(near[0], far[1][0], near[1], far[1][1]),
        ],
        0,
    )

    low = dot(pol_states, jnp.concatenate([qa, va], 1)).astype(BF16)
    cosine, sine = rope_tables(L, HEAD_SIZE)

    def own_columns(at, piece, *queue):
        return lax.dynamic_slice(
            after(wo, *queue), (piece * (heads // 2), at * part), (heads // 2, part)
        )

    def own_piece(step, *queue):
        at = (1 - x) if step < 2 else x
        return lax.dynamic_slice(
            after(wo, *queue), ((step % 2) * (heads // 2), at * part), (heads // 2, part)
        )

    def make_shard(j, *queue):
        if j < kv_local:
            shards.append(shard_of(j, *queue))
        elif j < kv_local + 4:
            shards.append(own_piece(j - kv_local, *queue))

    def next_shard(j, *more):
        queue = (zs[j - 1], ys[j - 1], *more)
        ys.append(move(after(shards[j], *queue), over_y))
        zs.append(move(after(shards[j], *queue), over_z))
        corners.append(move(after(*queue), over_y))

    saved = []
    parts_mixed = [[], [], []]

    def mix(j, keeps, came, sums, *queue, marks=()):
        results = []
        for which in range(2):
            total = sums[which * L : (which + 1) * L]
            result = attend(
                *(which == 1, keeps[which], came[which], total, low, qo, vo, j, cosine, sine),
                marks=marks,
            )
            saved.extend(result[1:])
            results.append(result[0])
        result = jnp.concatenate(results, 0)
        return result, move(after(result, *queue) if queue else result, near_z)

    def spread(result, other):
        far = move(jnp.concatenate([result, other], 0), 1)
        for part_mixed, value in zip(parts_mixed, (result, other, far)):
            part_mixed.append(value)
        return far

    if wide:
        make_shard(1, shards[0])
        next_shard(1)
        make_shard(2, zs[0])
    before = None
    ends = []
    for j in range(kv_local):
        if wide:
            marks = (marker(zs[j + 1], ys[j + 1]),)
            ws = [shards[j], ys[j], zs[j], corners[j]]
        else:
            ws = gather(shard_of(j))
        sends = mm(states, 1, ws, BF16, marks)
        came = [move(send, 1) for send in sends]
        keeps = mm(states, 0, ws, F32)
        if wide:
            next_shard(j + 2)
            make_shard(j + 3, zs[j + 1])
        over = jnp.concatenate(
            [(keeps[which][L:] + came[which][L:].astype(F32)).astype(BF16) for which in range(2)], 0
        )
        if before is not None:
            result, other = mix(j - 1, *before, *came, *ends)
            if j + 1 < kv_local:
                over = after(over, other)
            states = after(states, other)
            ends = [spread(result, other)]
        if wide:
            over = after(over, shards[-1])
        sums = move(over, near_z)
        if wide and j + 1 == kv_local:
            marks = (marker(zs[j + 2], ys[j + 2]),)
            make_shard(kv_local + 3, zs[-2])
        before = (keeps, came, sums)
    last = spread(*mix(kv_local - 1, *before, *ends, marks=marks))

    keeps, recvs = [], []
    if wide:
        next_shard(kv_local + 2, over)
        first = [a[kv_local : kv_local + 2] for a in (shards, ys, zs, corners)]
        marks = (marker(zs[-1], ys[-1]),)
        recvs.append(swap_x(out_mm(parts_mixed, first[:2], marks)))
        next_shard(kv_local + 3)
        recvs.append(swap_x(out_mm(parts_mixed, first[2:])))
        corners.append(move(after(zs[-1], ys[-1]), over_y))
        wo_send, wo_keep = first, [a[kv_local + 2 :] for a in (shards, ys, zs, corners)]
        keeps.append(out_mm(parts_mixed, wo_keep[:3]))
        keeps.append(out_mm(parts_mixed, wo_keep[3:]))
    else:
        wo_keep = [[w] for w in gather(wo)]
        product = out_mm(parts_mixed, wo_keep)
        if tensor_size > 1:
            product = lax.psum(product, "tensor")
        keeps.append(product)
        recvs.append(jnp.zeros_like(product))

    targets = [ts[0]] + [move(after(ts[d], last), tmask(d)) for d in (1, 2, 3)]
    tgt = jnp.stack([targets[d] for d in ORD])
    scal = jnp.stack([jnp.asarray(side, jnp.int32), prompt_length[0].astype(jnp.int32)])
    hidden, stats = norm_stats(scal, states, tgt, gain, keeps, recvs, split)
    masks, got = [], []
    for flip in range(split):
        for d in range(4):
            if d or flip:
                masks.append(d)
                if split == 2:
                    got.append(move_both(stats, tmask(d), flip))
                else:
                    got.append(move(stats, tmask(d)))
    ids = jnp.stack([me ^ tmask(d) for d in ORD]).astype(jnp.int32)
    total, margin = scores(ids, stats, got, tuple(masks), width)
    vecs = [margin] + [move(margin, gmask(k)) for k in range(1, groups)]
    grad, loss = grad_hidden(ids, pairs, total, hidden, tgt, gain, vecs, width)

    grad_rows = grad.reshape(4 * L, -1)
    other = None
    for half in range(2):
        if split == 2:
            leaving = grad_rows[2 * L * half : 2 * L * (half + 1)]
            other = swap_x(leaving if half == 0 else after(leaving, other))
            acc = back_mm(grad_rows, half, wo_keep, None)
            keep, send = back_mm(other, None, wo_send, acc)
        else:
            acc = jnp.zeros((2 * L, heads), F32)
            keep, send = back_mm(grad_rows, half, wo_keep, acc)
        rs = move(send if half == 0 else after(send, r2), 1)
        if half == 0:
            over = (keep + rs.astype(F32)).astype(BF16)
            r2 = move(over, near_z)
    outer, mid = attend_back(keep, rs, r2, low, qo, vo, cosine, sine, saved)

    rows_each = width // tensor_size
    if split == 2:
        mids = [mid, swap_x(mid)]
    elif tensor_size == 1:
        mids = [mid]
    else:
        gathered = lax.all_gather(mid, "tensor", axis=0, tiled=False)
        mids = [gathered[i] for i in range(tensor_size)]
    scal = jnp.stack([x, me & 1]).astype(jnp.int32)
    away, current = adapter_products(scal, pol_states, mids, outer, rows_each)
    current = current + move(away, 1).astype(F32)
    top = fsdp_size // 2
    g = (me // 2) % groups
    rows = current.shape[0] // groups
    pieces = [
        lax.dynamic_slice_in_dim(current, (g ^ k) * rows, rows, 0) for k in range(groups)
    ]
    current = pieces[0]
    for k in range(1, groups):
        current = current + move(pieces[k].astype(BF16), k << 1).astype(F32)
    rows //= 2
    high = me // top
    away = lax.dynamic_slice_in_dim(current, (1 - high) * rows, rows, 0).astype(BF16)
    current = lax.dynamic_slice_in_dim(current, high * rows, rows, 0)
    current = (current + move(away, top).astype(F32)).astype(BF16)

    def join(bit, own, other):
        return jnp.where(
            bit == 0, jnp.concatenate([own, other], 0), jnp.concatenate([other, own], 0)
        )

    current = join(high, current, move(current, top))
    pieces = [current] + [move(current, k << 1) for k in range(1, groups)]
    step = 1
    while step < groups:
        odd = (g & step) != 0
        pieces = [jnp.where(odd, pieces[k ^ step], pieces[k]) for k in range(groups)]
        step *= 2
    current = jnp.concatenate(pieces, 0)
    grads = assemble(
        (me & 1).reshape(1), current, move(current, 1), rows_each, qo.shape[1], vo.shape[1]
    )
    return (loss[0, 0], grads[0].T, grads[1], grads[2].T, grads[3])


def solution(mesh):
    in_specs = (
        P("fsdp", None),
        P("fsdp", None),
        P("fsdp", None),
        P(),
        P("fsdp", "tensor"),
        P("fsdp", "tensor"),
        P("fsdp", "tensor"),
        P("tensor", "fsdp"),
        P(),
        P(None, "tensor"),
        P(),
        P(None, "tensor"),
        P("fsdp"),
        P(),
    )
    out_specs = (P(), P("tensor", None), P(None, "tensor"), P("tensor", None), P(None, "tensor"))
    body = functools.partial(per_device, mesh.shape["fsdp"], mesh.shape["tensor"])
    return jax.shard_map(body, mesh=mesh, in_specs=in_specs, out_specs=out_specs, check_vma=False)
```

```python
import functools

import jax
import jax.numpy as jnp
from jax import lax
from jax.experimental import pallas as pl
from jax.experimental.pallas import tpu as pltpu
from jax.sharding import PartitionSpec as P

QUERY_HEADS = 32
KEY_VALUE_HEADS = 8
HEAD_SIZE = 128
L = 128
GROUP = QUERY_HEADS // KEY_VALUE_HEADS
QCOLS = GROUP * HEAD_SIZE

adapter_scale = 0.5
dpo_beta = 0.1
loss_scale = 256.0
rope_base = 500000.0
norm_eps = 1e-05

F32 = jnp.float32
BF16 = jnp.bfloat16
ORD = (0, 2, 1, 3)
MB = 1 << 20
SMALL = pl.CostEstimate(flops=1, bytes_accessed=1, transcendentals=0)


def rope_tables(length, head_dim):
    half_dim = head_dim // 2
    exponent = jnp.arange(half_dim, dtype=F32) * (2.0 / head_dim)
    inverse = jnp.power(F32(rope_base), -exponent)
    angles = jnp.arange(length, dtype=F32)[:, None] * inverse[None, :]
    cosine = jnp.concatenate([jnp.cos(angles), jnp.cos(angles)], 1)
    sine = jnp.concatenate([-jnp.sin(angles), jnp.sin(angles)], 1)
    return cosine, sine


def dot(a, b, dims=((1,), (0,))):
    return lax.dot_general(a, b, (dims, ((), ())), preferred_element_type=F32)


def params(limit_mb):
    return pltpu.CompilerParams(vmem_limit_bytes=limit_mb * MB)


def smem():
    return pl.BlockSpec(memory_space=pltpu.SMEM)


def full(a):
    return pl.BlockSpec(a.shape, lambda i: (0,) * len(a.shape))


def prep_body(parts, part, split, idx, ref, pol, tgt, gain, *outs):
    x0, x1, x2, x3, t0, t1, t2, t3, go = outs[-9:]
    groups = parts // split
    for d, (xo, to) in enumerate(((x0, t0), (x1, t1), (x2, t2), (x3, t3))):
        for j in range(parts):
            src = pl.ds(pl.multiple_of(idx[d * parts + j] * part, part), part)
            cols = slice(j * part, (j + 1) * part)
            if xo.shape[0] == 2:
                xo[0, :, cols] = ref[:, src]
                xo[1, :, cols] = pol[:, src]
            else:
                @pl.when(idx[4 * parts + 4 * groups] == 0)
                def _():
                    xo[0, :, cols] = ref[:, src]

                @pl.when(idx[4 * parts + 4 * groups] != 0)
                def _():
                    xo[0, :, cols] = pol[:, src]

        for j in range(groups):
            at = idx[4 * parts + d * groups + j] * part
            src = pl.ds(pl.multiple_of(at, part), part)
            to[:, j * part : (j + 1) * part] = tgt[:, src]
            if d == 0:
                go[:, j * part : (j + 1) * part] = gain[:, src]


def prep(idx, ref, pol, tgt, gain, parts, part, split):
    tokens = ref.shape[0]
    xs = lambda n: jax.ShapeDtypeStruct((n, tokens, parts * part), BF16)
    far = 1 if split == 2 else 2
    width = parts // split * part
    tile = 32
    shapes = [xs(2), xs(2), xs(far), xs(far)]
    shapes += [jax.ShapeDtypeStruct((tokens, width), BF16)] * 4
    shapes += [jax.ShapeDtypeStruct((1, width), F32)]
    return pl.pallas_call(
        functools.partial(prep_body, parts, part, split),
        grid=(tokens // tile,),
        in_specs=[smem()]
        + [pl.BlockSpec((tile, a.shape[1]), lambda i: (i, 0)) for a in (ref, pol, tgt)]
        + [full(gain)],
        out_specs=[
            pl.BlockSpec((a.shape[0], tile, a.shape[2]), lambda i: (0, i, 0)) for a in shapes[:4]
        ]
        + [pl.BlockSpec((tile, width), lambda i: (i, 0))] * 4
        + [full(shapes[8])],
        out_shape=shapes,
        compiler_params=params(60),
        cost_estimate=SMALL,
    )(idx, ref, pol, tgt, gain)


def tile_of(cols):
    for tile in (256, 128):
        if cols % tile == 0:
            return tile
    return cols


def mm_body(count, x_ref, *refs):
    ws, outs = refs[:count], refs[-2:]
    total = None
    at = 0
    for w in ws:
        depth = w.shape[0]
        term = dot(x_ref[:, at : at + depth], w[...])
        total = term if total is None else total + term
        at += depth
    rows = total.shape[0] // 2
    for i, out_ref in enumerate(outs):
        out_ref[...] = total[i * rows : (i + 1) * rows].astype(out_ref.dtype)


def mm(x, half, ws, out_dtype, marks=()):
    rows, depth = x.shape[0] // 2, x.shape[1]
    cols = ws[0].shape[1]
    tile = tile_of(cols)
    return pl.pallas_call(
        functools.partial(mm_body, len(ws)),
        grid=(cols // tile,),
        in_specs=[pl.BlockSpec((rows, depth), lambda i: (half, 0))]
        + [pl.BlockSpec((w.shape[0], tile), lambda i: (0, i)) for w in ws]
        + [full(a) for a in marks],
        out_specs=[pl.BlockSpec((rows // 2, tile), lambda i: (0, i))] * 2,
        out_shape=[jax.ShapeDtypeStruct((rows // 2, cols), out_dtype)] * 2,
        compiler_params=params(32),
        cost_estimate=pl.CostEstimate(
            flops=2 * rows * depth * cols,
            bytes_accessed=2 * (rows * (depth + cols) + depth * cols),
            transcendentals=0,
        ),
    )(x, *ws, *marks)


def out_body(n, row_parts, counts, *refs):
    ws = refs[row_parts * n :][: sum(counts)]
    out_ref, total = refs[-2:]
    for j in range(n):
        x = jnp.concatenate([refs[p * n + j][...] for p in range(row_parts)], 0)
        depth = x.shape[1]
        at = 0
        for k, count in enumerate(counts):
            row = j * depth
            piece = at
            while row >= ws[piece].shape[0]:
                row -= ws[piece].shape[0]
                piece += 1
            at += count
            term = dot(x, ws[piece][row : row + depth])
            if j:
                term = term + total[k]
            if j == n - 1:
                out_ref[k] = term.astype(BF16)
            else:
                total[k] = term


def out_mm(parts, ws, marks=()):
    n = len(parts[0])
    rows = sum(part[0].shape[0] for part in parts)
    cols = ws[0][0].shape[1]
    flat = [piece for w in ws for piece in w]
    inputs = [a for part in parts for a in part] + flat + list(marks)
    out_shape = jax.ShapeDtypeStruct((len(ws), rows, cols), BF16)
    return pl.pallas_call(
        functools.partial(out_body, n, len(parts), tuple(len(w) for w in ws)),
        grid=(1,),
        in_specs=[full(a) for a in inputs],
        out_specs=full(out_shape),
        out_shape=out_shape,
        scratch_shapes=[pltpu.VMEM(out_shape.shape, F32)],
        compiler_params=params(32),
        cost_estimate=SMALL,
    )(*inputs)


def back_body(counts, part, has_acc, x_ref, *refs):
    total = None
    at = 0
    for j, count in enumerate(counts):
        w = refs[at][...]
        if count == 2:
            w = jnp.where(pl.program_id(0) < pl.num_programs(0) // 2, w, refs[at + 1][...])
        at += count
        term = dot(x_ref[:, j * part : (j + 1) * part], w, ((1,), (1,)))
        total = term if total is None else total + term
    refs = refs[at:]
    if has_acc:
        total = total + refs[0][...]
        keep, send = refs[1:]
        half = total.shape[0] // 2
        keep[...] = total[:half]
        send[...] = total[half:].astype(send.dtype)
    else:
        refs[0][...] = total


def back_mm(x, half, ws, acc):
    rows = x.shape[0] // (1 if half is None else 2)
    depth = x.shape[1]
    part = ws[0][0].shape[1]
    heads = sum(piece.shape[0] for piece in ws[0])
    tile = min(512, heads)
    steps = heads // tile
    has_acc = acc is not None
    row = half or 0
    in_specs = [pl.BlockSpec((rows, depth), lambda i: (row, 0))]
    for w in ws:
        if len(w) == 1:
            in_specs.append(pl.BlockSpec((tile, part), lambda i: (i, 0)))
        else:
            in_specs.append(pl.BlockSpec((tile, part), lambda i: (jnp.minimum(i, steps // 2 - 1), 0)))
            in_specs.append(pl.BlockSpec((tile, part), lambda i: (jnp.maximum(i - steps // 2, 0), 0)))
    args = [x] + [piece for w in ws for piece in w]
    if has_acc:
        in_specs.append(pl.BlockSpec((rows, tile), lambda i: (0, i)))
        args.append(acc)
        out_specs = [pl.BlockSpec((rows // 2, tile), lambda i: (0, i))] * 2
        out_shape = [
            jax.ShapeDtypeStruct((rows // 2, heads), F32),
            jax.ShapeDtypeStruct((rows // 2, heads), BF16),
        ]
    else:
        out_specs = pl.BlockSpec((rows, tile), lambda i: (0, i))
        out_shape = jax.ShapeDtypeStruct((rows, heads), F32)
    return pl.pallas_call(
        functools.partial(back_body, tuple(len(w) for w in ws), part, has_acc),
        grid=(steps,),
        in_specs=in_specs,
        out_specs=out_specs,
        out_shape=out_shape,
        compiler_params=params(32),
        cost_estimate=SMALL,
    )(*args)


def causal(rows):
    at = lax.broadcasted_iota(jnp.int32, (rows, L), 0) % L
    return at >= lax.broadcasted_iota(jnp.int32, (rows, L), 1)


def probabilities(q4, keys):
    scores = dot(q4, keys, ((1,), (1,))) * (HEAD_SIZE**-0.5)
    weights = jnp.where(causal(q4.shape[0]), jnp.exp(scores), 0.0)
    return weights / jnp.sum(weights, -1, keepdims=True)


def stack_heads(values):
    return jnp.concatenate(
        [values[:, h * HEAD_SIZE : (h + 1) * HEAD_SIZE] for h in range(GROUP)], 0
    )


def attend_body(adapted, keep, rs, r2, low, qo, vo, cos_ref, sin_ref, *refs):
    mixed, *saved = refs[-1 - adapted :]
    cosine = cos_ref[...]
    sine = sin_ref[...]
    pre = keep[...] + rs[...].astype(F32) + r2[...].astype(F32)
    rank = qo.shape[0]
    q_pre = pre[:, :QCOLS]
    k_pre = pre[:, QCOLS : QCOLS + HEAD_SIZE]
    v_pre = pre[:, QCOLS + HEAD_SIZE :]
    if adapted:
        q_pre = q_pre + adapter_scale * dot(low[:, :rank], qo[...])
        v_pre = v_pre + adapter_scale * dot(low[:, rank:], vo[...])
    cos4 = jnp.concatenate([cosine] * GROUP, 0)
    sin4 = jnp.concatenate([sine] * GROUP, 0)
    q4 = stack_heads(q_pre)
    q4 = (q4 * cos4 + pltpu.roll(q4, HEAD_SIZE // 2, 1) * sin4).astype(BF16)
    keys = (k_pre * cosine + pltpu.roll(k_pre, HEAD_SIZE // 2, 1) * sine).astype(BF16)
    values = v_pre.astype(BF16)
    rounded = probabilities(q4, keys).astype(BF16)
    out = dot(rounded, values).astype(BF16)
    for h in range(GROUP):
        cols = slice(h * HEAD_SIZE, (h + 1) * HEAD_SIZE)
        mixed[:, cols] = out[h * L : (h + 1) * L]
        if saved:
            saved[0][:, cols] = q4[h * L : (h + 1) * L]
    if saved:
        saved[0][:, QCOLS : QCOLS + HEAD_SIZE] = keys
        saved[0][:, QCOLS + HEAD_SIZE :] = values


def attend(adapted, keep, rs, r2, low, qo, vo, group, cosine, sine, marks=()):
    each = QCOLS + 2 * HEAD_SIZE
    rank = qo.shape[0]
    top = lambda a: pl.BlockSpec((L, a.shape[1]), lambda i: (0, 0))
    return pl.pallas_call(
        functools.partial(attend_body, adapted),
        grid=(1,),
        in_specs=[
            top(keep),
            top(rs),
            top(r2),
            top(low),
            pl.BlockSpec((rank, QCOLS), lambda i: (0, group)),
            pl.BlockSpec((rank, HEAD_SIZE), lambda i: (0, group)),
            top(cosine),
            top(sine),
        ]
        + [full(a) for a in marks],
        out_specs=[pl.BlockSpec((L, w), lambda i: (0, 0)) for w in (QCOLS, each)[: 1 + adapted]],
        out_shape=[jax.ShapeDtypeStruct((L, w), BF16) for w in (QCOLS, each)[: 1 + adapted]],
        compiler_params=params(32),
        cost_estimate=SMALL,
    )(keep, rs, r2, low, qo, vo, cosine, sine, *marks)


def outer_place(block, rank, kv):
    wide = (kv * (GROUP + 1) + 1) // 2
    return (block // wide) * rank, (block % wide) * HEAD_SIZE, wide


def attend_back_body(kv, splits, keep, rs, r2, low, qo, vo, cos_ref, sin_ref, *refs):
    saved = refs[:splits]
    outer, mid = refs[splits:]
    rank = qo.shape[0]
    each = QCOLS + 2 * HEAD_SIZE
    cos4 = jnp.concatenate([cos_ref[...]] * GROUP, 0)
    sin4 = jnp.concatenate([sin_ref[...]] * GROUP, 0)
    low_q = low[:, :rank]
    low_v = low[:, rank:]
    q_mid = jnp.zeros((L, rank), F32)
    v_mid = jnp.zeros((L, rank), F32)

    def put(block, value):
        row, col, _ = outer_place(block, rank, kv)
        outer[row : row + rank, col : col + HEAD_SIZE] = adapter_scale * value

    if (kv * (GROUP + 1)) % 2:
        put(kv * (GROUP + 1), jnp.zeros((rank, HEAD_SIZE), F32))
    for j in range(kv):
        cols = slice(j * QCOLS, (j + 1) * QCOLS)
        at = (j % (kv // splits)) * each
        kept = saved[j // (kv // splits)]
        grad = keep[:, cols] + rs[:, cols].astype(F32) + r2[:, cols].astype(F32)
        grad4 = stack_heads(grad.astype(BF16))
        q4 = stack_heads(kept[:, at : at + QCOLS])
        keys = kept[:, at + QCOLS : at + QCOLS + HEAD_SIZE]
        values = kept[:, at + QCOLS + HEAD_SIZE : at + each]
        prob = probabilities(q4, keys)
        grad_prob = dot(grad4, values, ((1,), (1,)))
        grad_values = dot(prob.astype(BF16), grad4, ((0,), (0,))).astype(BF16)
        inner = jnp.sum(grad_prob * prob, -1, keepdims=True)
        grad_scores = (prob * (grad_prob - inner) * (HEAD_SIZE**-0.5)).astype(BF16)
        grad_query = dot(grad_scores, keys)
        back4 = (grad_query * cos4 - pltpu.roll(grad_query, HEAD_SIZE // 2, 1) * sin4).astype(BF16)
        for h in range(GROUP):
            at = j * GROUP + h
            back = back4[h * L : (h + 1) * L]
            put(at, dot(low_q, back, ((0,), (0,))))
            q_mid += dot(back, qo[:, at * HEAD_SIZE : (at + 1) * HEAD_SIZE], ((1,), (1,)))
        put(kv * GROUP + j, dot(low_v, grad_values, ((0,), (0,))))
        v_mid += dot(grad_values, vo[:, j * HEAD_SIZE : (j + 1) * HEAD_SIZE], ((1,), (1,)))
    mid[:, :rank] = (adapter_scale * q_mid).astype(BF16)
    mid[:, rank:] = (adapter_scale * v_mid).astype(BF16)


def attend_back(keep, rs, r2, low, qo, vo, cosine, sine, saved):
    rank = qo.shape[0]
    kv = vo.shape[1] // HEAD_SIZE
    wide = outer_place(0, rank, kv)[2]
    inputs = (keep, rs, r2, low, qo, vo, cosine, sine, *saved)
    shapes = [
        jax.ShapeDtypeStruct((2 * rank, wide * HEAD_SIZE), F32),
        jax.ShapeDtypeStruct((L, 2 * rank), BF16),
    ]
    return pl.pallas_call(
        functools.partial(attend_back_body, kv, len(saved)),
        grid=(1,),
        in_specs=[full(a) for a in inputs],
        out_specs=[full(a) for a in shapes],
        out_shape=shapes,
        compiler_params=params(60),
        cost_estimate=SMALL,
    )(*inputs)


def adapter_body(n, rows_each, scal, states, outer, *refs):
    mids = refs[:n]
    away, stay = refs[n:]
    src = pl.ds(pl.multiple_of(scal[0] * rows_each, rows_each), rows_each)
    own = states[:, src]
    total = None
    for mid in mids:
        term = dot(mid[...], own, ((0,), (0,)))
        total = term if total is None else total + term
    half = total.shape[0] // 2
    for low in range(2):
        rows = slice(low * half, (low + 1) * half)

        @pl.when(scal[1] == low)
        def _():
            stay[:, :rows_each] = total[rows]
            stay[:, rows_each:] = outer[rows]

        @pl.when(scal[1] != low)
        def _():
            away[:, :rows_each] = total[rows].astype(BF16)
            away[:, rows_each:] = outer[rows].astype(BF16)


def adapter_products(scal, states, mids, outer, rows_each):
    half = outer.shape[0] // 2
    cols = rows_each + outer.shape[1]
    shapes = [jax.ShapeDtypeStruct((half, cols), BF16), jax.ShapeDtypeStruct((half, cols), F32)]
    return pl.pallas_call(
        functools.partial(adapter_body, len(mids), rows_each),
        grid=(1,),
        in_specs=[smem()] + [full(a) for a in (states, outer, *mids)],
        out_specs=[full(a) for a in shapes],
        out_shape=shapes,
        compiler_params=params(32),
        cost_estimate=SMALL,
    )(scal, states, outer, *mids)


def assemble_body(rows_each, bit, own, other, q_inner, q_outer, v_inner, v_outer):
    low = jnp.where(bit[0] == 0, own[...], other[...]).astype(F32)
    high = jnp.where(bit[0] == 0, other[...], own[...]).astype(F32)
    q_inner[...] = low[:, :rows_each]
    v_inner[...] = high[:, :rows_each]
    outer = jnp.concatenate([low[:, rows_each:], high[:, rows_each:]], 1)
    cols = q_outer.shape[1]
    q_outer[...] = outer[:, :cols]
    v_outer[...] = outer[:, cols : cols + v_outer.shape[1]]


def assemble(bit, own, other, rows_each, q_cols, v_cols):
    rank = own.shape[0]
    shapes = [jax.ShapeDtypeStruct((rank, c), F32) for c in (rows_each, q_cols, rows_each, v_cols)]
    return pl.pallas_call(
        functools.partial(assemble_body, rows_each),
        grid=(1,),
        in_specs=[smem(), full(own), full(other)],
        out_specs=[full(a) for a in shapes],
        out_shape=shapes,
        compiler_params=params(32),
        cost_estimate=SMALL,
    )(bit, own, other)


def stats_body(counts, part, split, scal, xt_ref, xt_pol, tgt, gain, *refs):
    refs = list(refs)
    sums = []
    hidden_out, stats = refs[-2:]
    for which in range(2):
        xt = (xt_ref, xt_pol)[which]
        count = sum(counts)
        keeps = [r[i] for r in refs[: counts[0]] for i in range(r.shape[0])]
        recvs = [r[i] for r in refs[counts[0] : count] for i in range(r.shape[0])]
        refs = refs[count:]
        squares = jnp.zeros((L, HEAD_SIZE), F32)
        products = jnp.zeros((L, HEAD_SIZE), F32)
        for j, (keep, recv) in enumerate(zip(keeps, recvs)):
            src = pl.ds(pl.multiple_of((j * split + scal[0]) * part, part), part)
            hidden = xt[:, src].astype(F32) + keep.astype(F32) + recv.astype(F32)
            cols = slice(j * part, (j + 1) * part)
            if which == 1:
                hidden_out[0, :, cols] = hidden
            product = hidden * (gain[:, cols] * tgt[0, :, cols].astype(F32))
            square = hidden * hidden
            for s in range(part // HEAD_SIZE):
                lanes = slice(s * HEAD_SIZE, (s + 1) * HEAD_SIZE)
                squares += square[:, lanes]
                products += product[:, lanes]
        sums.append(
            [
                jnp.broadcast_to(jnp.sum(v, 1, keepdims=True), v.shape).T[:1]
                for v in (squares, products)
            ]
        )
    at = lax.broadcasted_iota(jnp.int32, (1, 2 * L), 1) % L
    own = (at >= scal[1]) & (pl.program_id(0) == 0)
    live = jnp.where(own, 1.0, 0.0).astype(F32)
    both = [jnp.concatenate([sums[0][i], sums[1][i]], 1) for i in range(2)]
    stats[...] = jnp.concatenate([*both, live, jnp.zeros((5, 2 * L), F32)], 0)


def norm_stats(scal, xt, tgt, gain, keeps, recvs, split):
    n = sum(a.shape[0] for a in keeps)
    part = keeps[0].shape[2]
    shared = []
    for which in range(2):
        at = functools.partial(lambda which, i: (0, 2 * i + which, 0), which)
        for a in (*keeps, *recvs):
            shared.append((a, pl.BlockSpec((a.shape[0], L, part), at)))
    return pl.pallas_call(
        functools.partial(stats_body, (len(keeps), len(recvs)), part, split),
        grid=(4,),
        in_specs=[
            smem(),
            pl.BlockSpec((L, xt.shape[1]), lambda i: ((i // 2) * 4 + i % 2, 0)),
            pl.BlockSpec((L, xt.shape[1]), lambda i: ((i // 2) * 4 + 2 + i % 2, 0)),
            pl.BlockSpec((1, L, n * part), lambda i: (i, 0, 0)),
            pl.BlockSpec((1, n * part), lambda i: (0, 0)),
        ]
        + [spec for _, spec in shared],
        out_specs=[
            pl.BlockSpec((1, L, n * part), lambda i: (i, 0, 0)),
            pl.BlockSpec((8, 2 * L), lambda i: (i, 0)),
        ],
        out_shape=[
            jax.ShapeDtypeStruct((4, L, n * part), F32),
            jax.ShapeDtypeStruct((32, 2 * L), F32),
        ],
        compiler_params=params(32),
        cost_estimate=SMALL,
    )(scal, xt, xt, tgt, gain, *[a for a, _ in shared])


def score_body(width, masks, ids, own, *refs):
    recvs = refs[: len(masks)]
    total_out, margin_out = refs[len(masks) :]
    lane = lax.broadcasted_iota(jnp.int32, (8, 128), 1)
    margins = jnp.zeros((8, 128), F32)
    for p in range(4):
        total = own[8 * p : 8 * p + 8]
        for recv, m in zip(recvs, masks):
            q = ORD.index(ORD[p] ^ m)
            total = total + recv[8 * q : 8 * q + 8]
        total_out[8 * p : 8 * p + 8] = total
        inverse = lax.rsqrt(total[0:1] * (1.0 / width) + norm_eps)
        score = total[1:2] * inverse * (width**-0.5)
        score = jnp.where(total[2:3] > 0.5, score, 0.0)
        margin = jnp.sum(score[:, L:], 1, keepdims=True) - jnp.sum(score[:, :L], 1, keepdims=True)
        margins = margins + jnp.where(lane == ids[p], margin, 0.0)
    margin_out[...] = margins


def scores(ids, own, recvs, masks, width):
    shapes = [jax.ShapeDtypeStruct(own.shape, F32), jax.ShapeDtypeStruct((8, 128), F32)]
    return pl.pallas_call(
        functools.partial(score_body, width, masks),
        grid=(1,),
        in_specs=[smem()] + [full(a) for a in (own, *recvs)],
        out_specs=[full(a) for a in shapes],
        out_shape=shapes,
        cost_estimate=SMALL,
    )(ids, own, *recvs)


def turn(i):
    return (2 * i + 1) % 5


def grad_body(width, seqs, n_vec, ids, pairs, total, hidden, tgt, gain, *refs):
    vecs = refs[:n_vec]
    grad_out, loss_out, slope = refs[n_vec:]
    lane = lax.broadcasted_iota(jnp.int32, (8, 128), 1)

    @pl.when(pl.program_id(0) == 0)
    def _():
        margin = vecs[0][...]
        for v in vecs[1:]:
            margin = margin + v[...]
        logits = jnp.zeros((8, 128), F32)
        for i in range(seqs // 2):
            sign = jnp.where(lane == pairs[2 * i], 1.0, 0.0) - jnp.where(
                lane == pairs[2 * i + 1], 1.0, 0.0
            )
            logit = dpo_beta * jnp.sum(margin * sign, 1, keepdims=True)
            logits = logits + jnp.where(lane == i, logit, 0.0)
        soft = jnp.maximum(-logits, 0.0) + jnp.log1p(jnp.exp(-jnp.abs(logits)))
        used = lane < seqs // 2
        loss = jnp.sum(jnp.where(used, soft, 0.0), 1, keepdims=True)
        loss_out[...] = jnp.broadcast_to(loss, (8, 128))
        slopes = jnp.where(used, -dpo_beta / (1.0 + jnp.exp(logits)), 0.0)
        gradient = jnp.zeros((8, 128), F32)
        for i in range(seqs // 2):
            each = jnp.sum(jnp.where(lane == i, slopes, 0.0), 1, keepdims=True)
            sign = jnp.where(lane == pairs[2 * i], 1.0, 0.0) - jnp.where(
                lane == pairs[2 * i + 1], 1.0, 0.0
            )
            gradient = gradient + each * sign
        slope[...] = gradient * loss_scale

    mine = lane == ids[turn(pl.program_id(0))]
    seq = jnp.sum(jnp.where(mine, slope[...], 0.0), 1, keepdims=True)[:1]
    rows = total[:, L:]
    token = jnp.where(rows[2:3] > 0.5, seq, 0.0) * (width**-0.5)
    inverse = lax.rsqrt(rows[0:1] * (1.0 / width) + norm_eps)
    first = inverse * token
    second = inverse * inverse * inverse * (token * rows[1:2] * (1.0 / width))
    first = jnp.broadcast_to(first, (L, L)).T
    second = jnp.broadcast_to(second, (L, L)).T
    for s in range(hidden.shape[2] // HEAD_SIZE):
        cols = slice(s * HEAD_SIZE, (s + 1) * HEAD_SIZE)
        weighted = gain[:, cols] * tgt[0, :, cols].astype(F32)
        grad_out[0, :, cols] = (first * weighted - second * hidden[0, :, cols]).astype(BF16)


def grad_hidden(ids, pairs, total, hidden, tgt, gain, vecs, width):
    n = hidden.shape[2]
    seqs = pairs.shape[0]
    return pl.pallas_call(
        functools.partial(grad_body, width, seqs, len(vecs)),
        grid=(4,),
        in_specs=[
            smem(),
            smem(),
            pl.BlockSpec((8, 2 * L), lambda i: (turn(i), 0)),
            pl.BlockSpec((1, L, n), lambda i: (turn(i), 0, 0)),
            pl.BlockSpec((1, L, n), lambda i: (turn(i), 0, 0)),
            pl.BlockSpec((1, n), lambda i: (0, 0)),
        ]
        + [pl.BlockSpec((8, 128), lambda i: (0, 0)) for _ in vecs],
        out_specs=[
            pl.BlockSpec((1, L, n), lambda i: (i, 0, 0)),
            pl.BlockSpec((8, 128), lambda i: (0, 0)),
        ],
        out_shape=[
            jax.ShapeDtypeStruct((4, L, n), BF16),
            jax.ShapeDtypeStruct((8, 128), F32),
        ],
        scratch_shapes=[pltpu.VMEM((8, 128), F32)],
        compiler_params=params(32),
        cost_estimate=SMALL,
    )(ids, pairs, total, hidden, tgt, gain, *vecs)


def per_device(
    fsdp_size,
    tensor_size,
    ref_states,
    pol_states,
    target_rows,
    norm_gain,
    wq,
    wk,
    wv,
    wo,
    qa,
    qo,
    va,
    vo,
    prompt_length,
    pairs,
):
    tokens, width = ref_states.shape
    groups = fsdp_size // 4
    near_z = fsdp_size // 4
    bits = []
    bit = 2
    while bit < fsdp_size:
        if bit != near_z:
            bits.append(bit)
        bit *= 2
    split = 2 if tensor_size == 2 and fsdp_size == 16 else 1
    kv_local = wk.shape[1] // HEAD_SIZE
    depth = wq.shape[0]
    part = depth // split
    rank = qa.shape[1]
    me = lax.axis_index("fsdp")
    x = lax.axis_index("tensor")
    side = x if split == 2 else 0

    def tmask(d):
        return (d & 1) | ((d >> 1) * near_z)

    def gmask(k):
        return sum(bit for i, bit in enumerate(bits) if (k >> i) & 1)

    def move(value, mask):
        return lax.ppermute(value, "fsdp", [(i, i ^ mask) for i in range(fsdp_size)])

    def swap_x(value):
        return lax.ppermute(value, "tensor", [(0, 1), (1, 0)])

    def move_both(value, mask, flip):
        pairs_list = [
            (2 * i + j, 2 * (i ^ mask) + (j ^ flip)) for i in range(fsdp_size) for j in range(2)
        ]
        return lax.ppermute(value, ("fsdp", "tensor"), pairs_list)

    def after(value, *others):
        return lax.optimization_barrier((value, *others))[0]

    def marker(*queue):
        return move(after(cosine[:16].astype(BF16), *queue), 1)

    cosine, sine = rope_tables(L, HEAD_SIZE)

    wide = groups == 4 and split == 2
    heads = wo.shape[0]

    def shard_of(j, *queue):
        q, k, v = wq, wk, wv
        if queue:
            q, k, v = lax.optimization_barrier((wq, wk, wv, *queue))[:3]
        pieces = [
            q[:, j * QCOLS : (j + 1) * QCOLS],
            k[:, j * HEAD_SIZE : (j + 1) * HEAD_SIZE],
            v[:, j * HEAD_SIZE : (j + 1) * HEAD_SIZE],
        ]
        return jnp.concatenate(pieces, 1)

    def gather(shard):
        return [shard] + [move(shard, gmask(k)) for k in range(1, groups)]

    if wide:
        over_y, over_z = gmask(1), gmask(2)
        shards = [shard_of(0)]
        zs = [move(shards[0], over_z)]
        ys = [move(shards[0], over_y)]
        corners = []

    parts = groups * split
    idx = []
    for d in range(4):
        for k in range(groups):
            for h in range(split):
                idx.append((me ^ tmask(d) ^ gmask(k)) * split + h)
    for d in range(4):
        for k in range(groups):
            idx.append((me ^ tmask(d) ^ gmask(k)) * split + side)
    idx.append(x)
    idx = jnp.stack(idx).astype(jnp.int32)
    prepared = prep(
        idx,
        ref_states,
        pol_states,
        target_rows,
        norm_gain.astype(F32).reshape(1, width),
        parts,
        part,
        split,
    )
    xs, ts, gain = prepared[:4], prepared[4:8], prepared[8]
    near = move(xs[1], 1)
    far = [move(xs[2], near_z)]
    far.append(move(xs[3], near_z | 1))

    if split == 2:
        other = [swap_x(a) for a in far]
        far = [
            [jnp.where(x == which, a[0], b[0]) for which in range(2)] for a, b in zip(far, other)
        ]
    states = jnp.concatenate(
        [
            *(xs[0][0], far[0][0], xs[0][1], far[0][1]),
            *(near[0], far[1][0], near[1], far[1][1]),
        ],
        0,
    )

    low = dot(pol_states, jnp.concatenate([qa, va], 1)).astype(BF16)
    cosine, sine = rope_tables(L, HEAD_SIZE)

    def own_columns(at, piece, *queue):
        return lax.dynamic_slice(
            after(wo, *queue), (piece * (heads // 2), at * part), (heads // 2, part)
        )

    def own_piece(step, *queue):
        at = (1 - x) if step < 2 else x
        return lax.dynamic_slice(
            after(wo, *queue), ((step % 2) * (heads // 2), at * part), (heads // 2, part)
        )

    def make_shard(j, *queue):
        if j < kv_local:
            shards.append(shard_of(j, *queue))
        elif j < kv_local + 4:
            shards.append(own_piece(j - kv_local, *queue))

    def next_shard(j, *more):
        queue = (zs[j - 1], ys[j - 1], *more)
        ys.append(move(after(shards[j], *queue), over_y))
        zs.append(move(after(shards[j], *queue), over_z))
        corners.append(move(after(*queue), over_y))

    saved = []
    parts_mixed = [[], [], []]

    def mix(j, keeps, came, sums, *queue, marks=()):
        results = []
        for which in range(2):
            total = sums[which * L : (which + 1) * L]
            result = attend(
                *(which == 1, keeps[which], came[which], total, low, qo, vo, j, cosine, sine),
                marks=marks,
            )
            saved.extend(result[1:])
            results.append(result[0])
        result = jnp.concatenate(results, 0)
        return result, move(after(result, *queue) if queue else result, near_z)

    def spread(result, other):
        far = move(jnp.concatenate([result, other], 0), 1)
        for part_mixed, value in zip(parts_mixed, (result, other, far)):
            part_mixed.append(value)
        return far

    if wide:
        make_shard(1, shards[0])
        next_shard(1)
        make_shard(2, zs[0])
    before = None
    ends = []
    marks = ()
    for j in range(kv_local):
        if wide:
            marks = (marker(zs[j + 1], ys[j + 1]),)
            ws = [shards[j], ys[j], zs[j], corners[j]]
        else:
            ws = gather(shard_of(j))
        sends = mm(states, 1, ws, BF16, marks)
        came = [move(send, 1) for send in sends]
        keeps = mm(states, 0, ws, F32)
        if wide:
            next_shard(j + 2)
            make_shard(j + 3, zs[j + 1])
        over = jnp.concatenate(
            [(keeps[which][L:] + came[which][L:].astype(F32)).astype(BF16) for which in range(2)], 0
        )
        if before is not None:
            result, other = mix(j - 1, *before, *came, *ends)
            if j + 1 < kv_local:
                over = after(over, other)
            states = after(states, other)
            ends = [spread(result, other)]
        if wide:
            over = after(over, shards[-1])
        sums = move(over, near_z)
        if wide and j + 1 == kv_local:
            marks = (marker(zs[j + 2], ys[j + 2]),)
            make_shard(kv_local + 3, zs[-2])
        before = (keeps, came, sums)
    last = spread(*mix(kv_local - 1, *before, *ends, marks=marks))

    keeps, recvs = [], []
    if wide:
        next_shard(kv_local + 2, over)
        first = [a[kv_local : kv_local + 2] for a in (shards, ys, zs, corners)]
        marks = (marker(zs[-1], ys[-1]),)
        recvs.append(swap_x(out_mm(parts_mixed, first[:2], marks)))
        next_shard(kv_local + 3)
        recvs.append(swap_x(out_mm(parts_mixed, first[2:])))
        corners.append(move(after(zs[-1], ys[-1]), over_y))
        wo_send, wo_keep = first, [a[kv_local + 2 :] for a in (shards, ys, zs, corners)]
        keeps.append(out_mm(parts_mixed, wo_keep[:3]))
        keeps.append(out_mm(parts_mixed, wo_keep[3:]))
    else:
        wo_keep = [[w] for w in gather(wo)]
        product = out_mm(parts_mixed, wo_keep)
        if tensor_size > 1:
            product = lax.psum(product, "tensor")
        keeps.append(product)
        recvs.append(jnp.zeros_like(product))

    targets = [ts[0]] + [move(after(ts[d], last), tmask(d)) for d in (1, 2, 3)]
    tgt = jnp.stack([targets[d] for d in ORD])
    scal = jnp.stack([jnp.asarray(side, jnp.int32), prompt_length[0].astype(jnp.int32)])
    hidden, stats = norm_stats(scal, states, tgt, gain, keeps, recvs, split)
    masks, got = [], []
    for flip in range(split):
        for d in range(4):
            if d or flip:
                masks.append(d)
                if split == 2:
                    got.append(move_both(stats, tmask(d), flip))
                else:
                    got.append(move(stats, tmask(d)))
    ids = jnp.stack([me ^ tmask(d) for d in ORD]).astype(jnp.int32)
    total, margin = scores(ids, stats, got, tuple(masks), width)
    vecs = [margin] + [move(margin, gmask(k)) for k in range(1, groups)]
    grad, loss = grad_hidden(ids, pairs, total, hidden, tgt, gain, vecs, width)

    grad_rows = grad.reshape(4 * L, -1)
    other = None
    for half in range(2):
        if split == 2:
            leaving = grad_rows[2 * L * half : 2 * L * (half + 1)]
            other = swap_x(leaving if half == 0 else after(leaving, other))
            acc = back_mm(grad_rows, half, wo_keep, None)
            keep, send = back_mm(other, None, wo_send, acc)
        else:
            acc = jnp.zeros((2 * L, heads), F32)
            keep, send = back_mm(grad_rows, half, wo_keep, acc)
        rs = move(send if half == 0 else after(send, r2), 1)
        if half == 0:
            over = (keep + rs.astype(F32)).astype(BF16)
            r2 = move(over, near_z)
    outer, mid = attend_back(keep, rs, r2, low, qo, vo, cosine, sine, saved)

    rows_each = width // tensor_size
    if split == 2:
        mids = [mid, swap_x(mid)]
    elif tensor_size == 1:
        mids = [mid]
    else:
        gathered = lax.all_gather(mid, "tensor", axis=0, tiled=False)
        mids = [gathered[i] for i in range(tensor_size)]
    scal = jnp.stack([x, me & 1]).astype(jnp.int32)
    away, current = adapter_products(scal, pol_states, mids, outer, rows_each)
    current = current + move(away, 1).astype(F32)
    top = fsdp_size // 2
    g = (me // 2) % groups
    rows = current.shape[0] // groups
    pieces = [
        lax.dynamic_slice_in_dim(current, (g ^ k) * rows, rows, 0) for k in range(groups)
    ]
    current = pieces[0]
    for k in range(1, groups):
        current = current + move(pieces[k].astype(BF16), k << 1).astype(F32)
    rows //= 2
    high = me // top
    away = lax.dynamic_slice_in_dim(current, (1 - high) * rows, rows, 0).astype(BF16)
    current = lax.dynamic_slice_in_dim(current, high * rows, rows, 0)
    current = (current + move(away, top).astype(F32)).astype(BF16)

    def join(bit, own, other):
        return jnp.where(
            bit == 0, jnp.concatenate([own, other], 0), jnp.concatenate([other, own], 0)
        )

    current = join(high, current, move(current, top))
    pieces = [current] + [move(current, k << 1) for k in range(1, groups)]
    step = 1
    while step < groups:
        odd = (g & step) != 0
        pieces = [jnp.where(odd, pieces[k ^ step], pieces[k]) for k in range(groups)]
        step *= 2
    current = jnp.concatenate(pieces, 0)
    grads = assemble(
        (me & 1).reshape(1), current, move(current, 1), rows_each, qo.shape[1], vo.shape[1]
    )
    return (loss[0, 0], grads[0].T, grads[1], grads[2].T, grads[3])


def solution(mesh):
    in_specs = (
        P("fsdp", None),
        P("fsdp", None),
        P("fsdp", None),
        P(),
        P("fsdp", "tensor"),
        P("fsdp", "tensor"),
        P("fsdp", "tensor"),
        P("tensor", "fsdp"),
        P(),
        P(None, "tensor"),
        P(),
        P(None, "tensor"),
        P("fsdp"),
        P(),
    )
    out_specs = (P(), P("tensor", None), P(None, "tensor"), P("tensor", None), P(None, "tensor"))
    body = functools.partial(per_device, mesh.shape["fsdp"], mesh.shape["tensor"])
    return jax.shard_map(body, mesh=mesh, in_specs=in_specs, out_specs=out_specs, check_vma=False)
```

```python
import functools

import jax
import jax.numpy as jnp
from jax import lax
from jax.experimental import pallas as pl
from jax.experimental.pallas import tpu as pltpu
from jax.sharding import PartitionSpec as P

QUERY_HEADS = 32
KEY_VALUE_HEADS = 8
HEAD_SIZE = 128
L = 128
GROUP = QUERY_HEADS // KEY_VALUE_HEADS
QCOLS = GROUP * HEAD_SIZE

adapter_scale = 0.5
dpo_beta = 0.1
loss_scale = 256.0
rope_base = 500000.0
norm_eps = 1e-05

F32 = jnp.float32
BF16 = jnp.bfloat16
ORD = (0, 2, 1, 3)
MB = 1 << 20
SMALL = pl.CostEstimate(flops=1, bytes_accessed=1, transcendentals=0)


def rope_tables(length, head_dim):
    half_dim = head_dim // 2
    exponent = jnp.arange(half_dim, dtype=F32) * (2.0 / head_dim)
    inverse = jnp.power(F32(rope_base), -exponent)
    angles = jnp.arange(length, dtype=F32)[:, None] * inverse[None, :]
    cosine = jnp.concatenate([jnp.cos(angles), jnp.cos(angles)], 1)
    sine = jnp.concatenate([-jnp.sin(angles), jnp.sin(angles)], 1)
    return cosine, sine


def dot(a, b, dims=((1,), (0,))):
    return lax.dot_general(a, b, (dims, ((), ())), preferred_element_type=F32)


def params(limit_mb):
    return pltpu.CompilerParams(vmem_limit_bytes=limit_mb * MB)


def smem():
    return pl.BlockSpec(memory_space=pltpu.SMEM)


def full(a):
    return pl.BlockSpec(a.shape, lambda i: (0,) * len(a.shape))


def prep_body(parts, part, split, idx, ref, pol, tgt, gain, *outs):
    x0, x1, x2, x3, t0, t1, t2, t3, go = outs[-9:]
    groups = parts // split
    for d, (xo, to) in enumerate(((x0, t0), (x1, t1), (x2, t2), (x3, t3))):
        for j in range(parts):
            src = pl.ds(pl.multiple_of(idx[d * parts + j] * part, part), part)
            cols = slice(j * part, (j + 1) * part)
            if xo.shape[0] == 2:
                xo[0, :, cols] = ref[:, src]
                xo[1, :, cols] = pol[:, src]
            else:
                @pl.when(idx[4 * parts + 4 * groups] == 0)
                def _():
                    xo[0, :, cols] = ref[:, src]

                @pl.when(idx[4 * parts + 4 * groups] != 0)
                def _():
                    xo[0, :, cols] = pol[:, src]

        for j in range(groups):
            at = idx[4 * parts + d * groups + j] * part
            src = pl.ds(pl.multiple_of(at, part), part)
            to[:, j * part : (j + 1) * part] = tgt[:, src]
            if d == 0:
                go[:, j * part : (j + 1) * part] = gain[:, src]


def prep(idx, ref, pol, tgt, gain, parts, part, split):
    tokens = ref.shape[0]
    xs = lambda n: jax.ShapeDtypeStruct((n, tokens, parts * part), BF16)
    far = 1 if split == 2 else 2
    width = parts // split * part
    tile = 32
    shapes = [xs(2), xs(2), xs(far), xs(far)]
    shapes += [jax.ShapeDtypeStruct((tokens, width), BF16)] * 4
    shapes += [jax.ShapeDtypeStruct((1, width), F32)]
    return pl.pallas_call(
        functools.partial(prep_body, parts, part, split),
        grid=(tokens // tile,),
        in_specs=[smem()]
        + [pl.BlockSpec((tile, a.shape[1]), lambda i: (i, 0)) for a in (ref, pol, tgt)]
        + [full(gain)],
        out_specs=[
            pl.BlockSpec((a.shape[0], tile, a.shape[2]), lambda i: (0, i, 0)) for a in shapes[:4]
        ]
        + [pl.BlockSpec((tile, width), lambda i: (i, 0))] * 4
        + [full(shapes[8])],
        out_shape=shapes,
        compiler_params=params(60),
        cost_estimate=SMALL,
    )(idx, ref, pol, tgt, gain)


def tile_of(cols):
    for tile in (256, 128):
        if cols % tile == 0:
            return tile
    return cols


def mm_body(count, x_ref, *refs):
    ws, outs = refs[:count], refs[-2:]
    total = None
    at = 0
    for w in ws:
        depth = w.shape[0]
        term = dot(x_ref[:, at : at + depth], w[...])
        total = term if total is None else total + term
        at += depth
    rows = total.shape[0] // 2
    for i, out_ref in enumerate(outs):
        out_ref[...] = total[i * rows : (i + 1) * rows].astype(out_ref.dtype)


def mm(x, half, ws, out_dtype, marks=()):
    rows, depth = x.shape[0] // 2, x.shape[1]
    cols = ws[0].shape[1]
    tile = tile_of(cols)
    return pl.pallas_call(
        functools.partial(mm_body, len(ws)),
        grid=(cols // tile,),
        in_specs=[pl.BlockSpec((rows, depth), lambda i: (half, 0))]
        + [pl.BlockSpec((w.shape[0], tile), lambda i: (0, i)) for w in ws]
        + [full(a) for a in marks],
        out_specs=[pl.BlockSpec((rows // 2, tile), lambda i: (0, i))] * 2,
        out_shape=[jax.ShapeDtypeStruct((rows // 2, cols), out_dtype)] * 2,
        compiler_params=params(32),
        cost_estimate=pl.CostEstimate(
            flops=2 * rows * depth * cols,
            bytes_accessed=2 * (rows * (depth + cols) + depth * cols),
            transcendentals=0,
        ),
    )(x, *ws, *marks)


def out_body(n, row_parts, counts, *refs):
    ws = refs[row_parts * n :][: sum(counts)]
    out_ref, total = refs[-2:]
    for j in range(n):
        x = jnp.concatenate([refs[p * n + j][...] for p in range(row_parts)], 0)
        depth = x.shape[1]
        at = 0
        for k, count in enumerate(counts):
            row = j * depth
            piece = at
            while row >= ws[piece].shape[0]:
                row -= ws[piece].shape[0]
                piece += 1
            at += count
            term = dot(x, ws[piece][row : row + depth])
            if j:
                term = term + total[k]
            if j == n - 1:
                out_ref[k] = term.astype(BF16)
            else:
                total[k] = term


def out_mm(parts, ws, marks=()):
    n = len(parts[0])
    rows = sum(part[0].shape[0] for part in parts)
    cols = ws[0][0].shape[1]
    flat = [piece for w in ws for piece in w]
    inputs = [a for part in parts for a in part] + flat + list(marks)
    out_shape = jax.ShapeDtypeStruct((len(ws), rows, cols), BF16)
    return pl.pallas_call(
        functools.partial(out_body, n, len(parts), tuple(len(w) for w in ws)),
        grid=(1,),
        in_specs=[full(a) for a in inputs],
        out_specs=full(out_shape),
        out_shape=out_shape,
        scratch_shapes=[pltpu.VMEM(out_shape.shape, F32)],
        compiler_params=params(32),
        cost_estimate=SMALL,
    )(*inputs)


def back_body(counts, part, has_acc, x_ref, *refs):
    total = None
    at = 0
    for j, count in enumerate(counts):
        w = refs[at][...]
        if count == 2:
            w = jnp.where(pl.program_id(0) < pl.num_programs(0) // 2, w, refs[at + 1][...])
        at += count
        term = dot(x_ref[:, j * part : (j + 1) * part], w, ((1,), (1,)))
        total = term if total is None else total + term
    refs = refs[at:]
    if has_acc:
        total = total + refs[0][...]
        keep, send = refs[1:]
        half = total.shape[0] // 2
        keep[...] = total[:half]
        send[...] = total[half:].astype(send.dtype)
    else:
        refs[0][...] = total


def back_mm(x, half, ws, acc):
    rows = x.shape[0] // (1 if half is None else 2)
    depth = x.shape[1]
    part = ws[0][0].shape[1]
    heads = sum(piece.shape[0] for piece in ws[0])
    tile = min(512, heads)
    steps = heads // tile
    has_acc = acc is not None
    row = half or 0
    in_specs = [pl.BlockSpec((rows, depth), lambda i: (row, 0))]
    for w in ws:
        if len(w) == 1:
            in_specs.append(pl.BlockSpec((tile, part), lambda i: (i, 0)))
        else:
            in_specs.append(pl.BlockSpec((tile, part), lambda i: (jnp.minimum(i, steps // 2 - 1), 0)))
            in_specs.append(pl.BlockSpec((tile, part), lambda i: (jnp.maximum(i - steps // 2, 0), 0)))
    args = [x] + [piece for w in ws for piece in w]
    if has_acc:
        in_specs.append(pl.BlockSpec((rows, tile), lambda i: (0, i)))
        args.append(acc)
        out_specs = [pl.BlockSpec((rows // 2, tile), lambda i: (0, i))] * 2
        out_shape = [
            jax.ShapeDtypeStruct((rows // 2, heads), F32),
            jax.ShapeDtypeStruct((rows // 2, heads), BF16),
        ]
    else:
        out_specs = pl.BlockSpec((rows, tile), lambda i: (0, i))
        out_shape = jax.ShapeDtypeStruct((rows, heads), F32)
    return pl.pallas_call(
        functools.partial(back_body, tuple(len(w) for w in ws), part, has_acc),
        grid=(steps,),
        in_specs=in_specs,
        out_specs=out_specs,
        out_shape=out_shape,
        compiler_params=params(32),
        cost_estimate=SMALL,
    )(*args)


def causal(rows):
    at = lax.broadcasted_iota(jnp.int32, (rows, L), 0) % L
    return at >= lax.broadcasted_iota(jnp.int32, (rows, L), 1)


def probabilities(q4, keys):
    scores = dot(q4, keys, ((1,), (1,))) * (HEAD_SIZE**-0.5)
    weights = jnp.where(causal(q4.shape[0]), jnp.exp(scores), 0.0)
    return weights / jnp.sum(weights, -1, keepdims=True)


def stack_heads(values):
    return jnp.concatenate(
        [values[:, h * HEAD_SIZE : (h + 1) * HEAD_SIZE] for h in range(GROUP)], 0
    )


def attend_body(adapted, keep, rs, r2, low, qo, vo, cos_ref, sin_ref, *refs):
    mixed, *saved = refs[-1 - adapted :]
    cosine = cos_ref[...]
    sine = sin_ref[...]
    pre = keep[...] + rs[...].astype(F32) + r2[...].astype(F32)
    rank = qo.shape[0]
    q_pre = pre[:, :QCOLS]
    k_pre = pre[:, QCOLS : QCOLS + HEAD_SIZE]
    v_pre = pre[:, QCOLS + HEAD_SIZE :]
    if adapted:
        q_pre = q_pre + adapter_scale * dot(low[:, :rank], qo[...])
        v_pre = v_pre + adapter_scale * dot(low[:, rank:], vo[...])
    cos4 = jnp.concatenate([cosine] * GROUP, 0)
    sin4 = jnp.concatenate([sine] * GROUP, 0)
    q4 = stack_heads(q_pre)
    q4 = (q4 * cos4 + pltpu.roll(q4, HEAD_SIZE // 2, 1) * sin4).astype(BF16)
    keys = (k_pre * cosine + pltpu.roll(k_pre, HEAD_SIZE // 2, 1) * sine).astype(BF16)
    values = v_pre.astype(BF16)
    rounded = probabilities(q4, keys).astype(BF16)
    out = dot(rounded, values).astype(BF16)
    for h in range(GROUP):
        cols = slice(h * HEAD_SIZE, (h + 1) * HEAD_SIZE)
        mixed[:, cols] = out[h * L : (h + 1) * L]
        if saved:
            saved[0][:, cols] = q4[h * L : (h + 1) * L]
    if saved:
        saved[0][:, QCOLS : QCOLS + HEAD_SIZE] = keys
        saved[0][:, QCOLS + HEAD_SIZE :] = values


def attend(adapted, keep, rs, r2, low, qo, vo, group, cosine, sine, marks=()):
    each = QCOLS + 2 * HEAD_SIZE
    rank = qo.shape[0]
    top = lambda a: pl.BlockSpec((L, a.shape[1]), lambda i: (0, 0))
    return pl.pallas_call(
        functools.partial(attend_body, adapted),
        grid=(1,),
        in_specs=[
            top(keep),
            top(rs),
            top(r2),
            top(low),
            pl.BlockSpec((rank, QCOLS), lambda i: (0, group)),
            pl.BlockSpec((rank, HEAD_SIZE), lambda i: (0, group)),
            top(cosine),
            top(sine),
        ]
        + [full(a) for a in marks],
        out_specs=[pl.BlockSpec((L, w), lambda i: (0, 0)) for w in (QCOLS, each)[: 1 + adapted]],
        out_shape=[jax.ShapeDtypeStruct((L, w), BF16) for w in (QCOLS, each)[: 1 + adapted]],
        compiler_params=params(32),
        cost_estimate=SMALL,
    )(keep, rs, r2, low, qo, vo, cosine, sine, *marks)


def outer_place(block, rank, kv):
    wide = (kv * (GROUP + 1) + 1) // 2
    return (block // wide) * rank, (block % wide) * HEAD_SIZE, wide


def attend_back_body(kv, splits, keep, rs, r2, low, qo, vo, cos_ref, sin_ref, *refs):
    saved = refs[:splits]
    outer, mid = refs[splits:]
    rank = qo.shape[0]
    each = QCOLS + 2 * HEAD_SIZE
    cos4 = jnp.concatenate([cos_ref[...]] * GROUP, 0)
    sin4 = jnp.concatenate([sin_ref[...]] * GROUP, 0)
    low_q = low[:, :rank]
    low_v = low[:, rank:]
    q_mid = jnp.zeros((L, rank), F32)
    v_mid = jnp.zeros((L, rank), F32)

    def put(block, value):
        row, col, _ = outer_place(block, rank, kv)
        outer[row : row + rank, col : col + HEAD_SIZE] = adapter_scale * value

    if (kv * (GROUP + 1)) % 2:
        put(kv * (GROUP + 1), jnp.zeros((rank, HEAD_SIZE), F32))
    for j in range(kv):
        cols = slice(j * QCOLS, (j + 1) * QCOLS)
        at = (j % (kv // splits)) * each
        kept = saved[j // (kv // splits)]
        grad = keep[:, cols] + rs[:, cols].astype(F32) + r2[:, cols].astype(F32)
        grad4 = stack_heads(grad.astype(BF16))
        q4 = stack_heads(kept[:, at : at + QCOLS])
        keys = kept[:, at + QCOLS : at + QCOLS + HEAD_SIZE]
        values = kept[:, at + QCOLS + HEAD_SIZE : at + each]
        prob = probabilities(q4, keys)
        grad_prob = dot(grad4, values, ((1,), (1,)))
        grad_values = dot(prob.astype(BF16), grad4, ((0,), (0,))).astype(BF16)
        inner = jnp.sum(grad_prob * prob, -1, keepdims=True)
        grad_scores = (prob * (grad_prob - inner) * (HEAD_SIZE**-0.5)).astype(BF16)
        grad_query = dot(grad_scores, keys)
        back4 = (grad_query * cos4 - pltpu.roll(grad_query, HEAD_SIZE // 2, 1) * sin4).astype(BF16)
        for h in range(GROUP):
            at = j * GROUP + h
            back = back4[h * L : (h + 1) * L]
            put(at, dot(low_q, back, ((0,), (0,))))
            q_mid += dot(back, qo[:, at * HEAD_SIZE : (at + 1) * HEAD_SIZE], ((1,), (1,)))
        put(kv * GROUP + j, dot(low_v, grad_values, ((0,), (0,))))
        v_mid += dot(grad_values, vo[:, j * HEAD_SIZE : (j + 1) * HEAD_SIZE], ((1,), (1,)))
    mid[:, :rank] = (adapter_scale * q_mid).astype(BF16)
    mid[:, rank:] = (adapter_scale * v_mid).astype(BF16)


def attend_back(keep, rs, r2, low, qo, vo, cosine, sine, saved):
    rank = qo.shape[0]
    kv = vo.shape[1] // HEAD_SIZE
    wide = outer_place(0, rank, kv)[2]
    inputs = (keep, rs, r2, low, qo, vo, cosine, sine, *saved)
    shapes = [
        jax.ShapeDtypeStruct((2 * rank, wide * HEAD_SIZE), F32),
        jax.ShapeDtypeStruct((L, 2 * rank), BF16),
    ]
    return pl.pallas_call(
        functools.partial(attend_back_body, kv, len(saved)),
        grid=(1,),
        in_specs=[full(a) for a in inputs],
        out_specs=[full(a) for a in shapes],
        out_shape=shapes,
        compiler_params=params(60),
        cost_estimate=SMALL,
    )(*inputs)


def adapter_body(n, rows_each, scal, states, outer, *refs):
    mids = refs[:n]
    away, stay = refs[n:]
    src = pl.ds(pl.multiple_of(scal[0] * rows_each, rows_each), rows_each)
    own = states[:, src]
    total = None
    for mid in mids:
        term = dot(mid[...], own, ((0,), (0,)))
        total = term if total is None else total + term
    half = total.shape[0] // 2
    for low in range(2):
        rows = slice(low * half, (low + 1) * half)

        @pl.when(scal[1] == low)
        def _():
            stay[:, :rows_each] = total[rows]
            stay[:, rows_each:] = outer[rows]

        @pl.when(scal[1] != low)
        def _():
            away[:, :rows_each] = total[rows].astype(BF16)
            away[:, rows_each:] = outer[rows].astype(BF16)


def adapter_products(scal, states, mids, outer, rows_each):
    half = outer.shape[0] // 2
    cols = rows_each + outer.shape[1]
    shapes = [jax.ShapeDtypeStruct((half, cols), BF16), jax.ShapeDtypeStruct((half, cols), F32)]
    return pl.pallas_call(
        functools.partial(adapter_body, len(mids), rows_each),
        grid=(1,),
        in_specs=[smem()] + [full(a) for a in (states, outer, *mids)],
        out_specs=[full(a) for a in shapes],
        out_shape=shapes,
        compiler_params=params(32),
        cost_estimate=SMALL,
    )(scal, states, outer, *mids)


def assemble_body(rows_each, bit, own, other, q_inner, q_outer, v_inner, v_outer):
    low = jnp.where(bit[0] == 0, own[...], other[...]).astype(F32)
    high = jnp.where(bit[0] == 0, other[...], own[...]).astype(F32)
    q_inner[...] = low[:, :rows_each]
    v_inner[...] = high[:, :rows_each]
    outer = jnp.concatenate([low[:, rows_each:], high[:, rows_each:]], 1)
    cols = q_outer.shape[1]
    q_outer[...] = outer[:, :cols]
    v_outer[...] = outer[:, cols : cols + v_outer.shape[1]]


def assemble(bit, own, other, rows_each, q_cols, v_cols):
    rank = own.shape[0]
    shapes = [jax.ShapeDtypeStruct((rank, c), F32) for c in (rows_each, q_cols, rows_each, v_cols)]
    return pl.pallas_call(
        functools.partial(assemble_body, rows_each),
        grid=(1,),
        in_specs=[smem(), full(own), full(other)],
        out_specs=[full(a) for a in shapes],
        out_shape=shapes,
        compiler_params=params(32),
        cost_estimate=SMALL,
    )(bit, own, other)


def stats_body(counts, part, split, scal, xt_ref, xt_pol, tgt, gain, *refs):
    refs = list(refs)
    sums = []
    hidden_out, stats = refs[-2:]
    for which in range(2):
        xt = (xt_ref, xt_pol)[which]
        count = sum(counts)
        keeps = [r[i] for r in refs[: counts[0]] for i in range(r.shape[0])]
        recvs = [r[i] for r in refs[counts[0] : count] for i in range(r.shape[0])]
        refs = refs[count:]
        squares = jnp.zeros((L, HEAD_SIZE), F32)
        products = jnp.zeros((L, HEAD_SIZE), F32)
        for j, (keep, recv) in enumerate(zip(keeps, recvs)):
            src = pl.ds(pl.multiple_of((j * split + scal[0]) * part, part), part)
            hidden = xt[:, src].astype(F32) + keep.astype(F32) + recv.astype(F32)
            cols = slice(j * part, (j + 1) * part)
            if which == 1:
                hidden_out[0, :, cols] = hidden
            product = hidden * (gain[:, cols] * tgt[0, :, cols].astype(F32))
            square = hidden * hidden
            for s in range(part // HEAD_SIZE):
                lanes = slice(s * HEAD_SIZE, (s + 1) * HEAD_SIZE)
                squares += square[:, lanes]
                products += product[:, lanes]
        sums.append(
            [
                jnp.broadcast_to(jnp.sum(v, 1, keepdims=True), v.shape).T[:1]
                for v in (squares, products)
            ]
        )
    at = lax.broadcasted_iota(jnp.int32, (1, 2 * L), 1) % L
    own = (at >= scal[1]) & (pl.program_id(0) == 0)
    live = jnp.where(own, 1.0, 0.0).astype(F32)
    both = [jnp.concatenate([sums[0][i], sums[1][i]], 1) for i in range(2)]
    stats[...] = jnp.concatenate([*both, live, jnp.zeros((5, 2 * L), F32)], 0)


def norm_stats(scal, xt, tgt, gain, keeps, recvs, split):
    n = sum(a.shape[0] for a in keeps)
    part = keeps[0].shape[2]
    shared = []
    for which in range(2):
        at = functools.partial(lambda which, i: (0, 2 * i + which, 0), which)
        for a in (*keeps, *recvs):
            shared.append((a, pl.BlockSpec((a.shape[0], L, part), at)))
    return pl.pallas_call(
        functools.partial(stats_body, (len(keeps), len(recvs)), part, split),
        grid=(4,),
        in_specs=[
            smem(),
            pl.BlockSpec((L, xt.shape[1]), lambda i: ((i // 2) * 4 + i % 2, 0)),
            pl.BlockSpec((L, xt.shape[1]), lambda i: ((i // 2) * 4 + 2 + i % 2, 0)),
            pl.BlockSpec((1, L, n * part), lambda i: (i, 0, 0)),
            pl.BlockSpec((1, n * part), lambda i: (0, 0)),
        ]
        + [spec for _, spec in shared],
        out_specs=[
            pl.BlockSpec((1, L, n * part), lambda i: (i, 0, 0)),
            pl.BlockSpec((8, 2 * L), lambda i: (i, 0)),
        ],
        out_shape=[
            jax.ShapeDtypeStruct((4, L, n * part), F32),
            jax.ShapeDtypeStruct((32, 2 * L), F32),
        ],
        compiler_params=params(32),
        cost_estimate=SMALL,
    )(scal, xt, xt, tgt, gain, *[a for a, _ in shared])


def score_body(width, masks, ids, own, *refs):
    recvs = refs[: len(masks)]
    total_out, margin_out = refs[len(masks) :]
    lane = lax.broadcasted_iota(jnp.int32, (8, 128), 1)
    margins = jnp.zeros((8, 128), F32)
    for p in range(4):
        total = own[8 * p : 8 * p + 8]
        for recv, m in zip(recvs, masks):
            q = ORD.index(ORD[p] ^ m)
            total = total + recv[8 * q : 8 * q + 8]
        total_out[8 * p : 8 * p + 8] = total
        inverse = lax.rsqrt(total[0:1] * (1.0 / width) + norm_eps)
        score = total[1:2] * inverse * (width**-0.5)
        score = jnp.where(total[2:3] > 0.5, score, 0.0)
        margin = jnp.sum(score[:, L:], 1, keepdims=True) - jnp.sum(score[:, :L], 1, keepdims=True)
        margins = margins + jnp.where(lane == ids[p], margin, 0.0)
    margin_out[...] = margins


def scores(ids, own, recvs, masks, width):
    shapes = [jax.ShapeDtypeStruct(own.shape, F32), jax.ShapeDtypeStruct((8, 128), F32)]
    return pl.pallas_call(
        functools.partial(score_body, width, masks),
        grid=(1,),
        in_specs=[smem()] + [full(a) for a in (own, *recvs)],
        out_specs=[full(a) for a in shapes],
        out_shape=shapes,
        cost_estimate=SMALL,
    )(ids, own, *recvs)


def turn(i):
    return (2 * i + 1) % 5


def grad_body(width, seqs, n_vec, ids, pairs, total, hidden, tgt, gain, *refs):
    vecs = refs[:n_vec]
    grad_out, loss_out, slope = refs[n_vec:]
    lane = lax.broadcasted_iota(jnp.int32, (8, 128), 1)

    @pl.when(pl.program_id(0) == 0)
    def _():
        margin = vecs[0][...]
        for v in vecs[1:]:
            margin = margin + v[...]
        logits = jnp.zeros((8, 128), F32)
        for i in range(seqs // 2):
            sign = jnp.where(lane == pairs[2 * i], 1.0, 0.0) - jnp.where(
                lane == pairs[2 * i + 1], 1.0, 0.0
            )
            logit = dpo_beta * jnp.sum(margin * sign, 1, keepdims=True)
            logits = logits + jnp.where(lane == i, logit, 0.0)
        soft = jnp.maximum(-logits, 0.0) + jnp.log1p(jnp.exp(-jnp.abs(logits)))
        used = lane < seqs // 2
        loss = jnp.sum(jnp.where(used, soft, 0.0), 1, keepdims=True)
        loss_out[...] = jnp.broadcast_to(loss, (8, 128))
        slopes = jnp.where(used, -dpo_beta / (1.0 + jnp.exp(logits)), 0.0)
        gradient = jnp.zeros((8, 128), F32)
        for i in range(seqs // 2):
            each = jnp.sum(jnp.where(lane == i, slopes, 0.0), 1, keepdims=True)
            sign = jnp.where(lane == pairs[2 * i], 1.0, 0.0) - jnp.where(
                lane == pairs[2 * i + 1], 1.0, 0.0
            )
            gradient = gradient + each * sign
        slope[...] = gradient * loss_scale

    mine = lane == ids[turn(pl.program_id(0))]
    seq = jnp.sum(jnp.where(mine, slope[...], 0.0), 1, keepdims=True)[:1]
    rows = total[:, L:]
    token = jnp.where(rows[2:3] > 0.5, seq, 0.0) * (width**-0.5)
    inverse = lax.rsqrt(rows[0:1] * (1.0 / width) + norm_eps)
    first = inverse * token
    second = inverse * inverse * inverse * (token * rows[1:2] * (1.0 / width))
    first = jnp.broadcast_to(first, (L, L)).T
    second = jnp.broadcast_to(second, (L, L)).T
    for s in range(hidden.shape[2] // HEAD_SIZE):
        cols = slice(s * HEAD_SIZE, (s + 1) * HEAD_SIZE)
        weighted = gain[:, cols] * tgt[0, :, cols].astype(F32)
        grad_out[0, :, cols] = (first * weighted - second * hidden[0, :, cols]).astype(BF16)


def grad_hidden(ids, pairs, total, hidden, tgt, gain, vecs, width):
    n = hidden.shape[2]
    seqs = pairs.shape[0]
    return pl.pallas_call(
        functools.partial(grad_body, width, seqs, len(vecs)),
        grid=(4,),
        in_specs=[
            smem(),
            smem(),
            pl.BlockSpec((8, 2 * L), lambda i: (turn(i), 0)),
            pl.BlockSpec((1, L, n), lambda i: (turn(i), 0, 0)),
            pl.BlockSpec((1, L, n), lambda i: (turn(i), 0, 0)),
            pl.BlockSpec((1, n), lambda i: (0, 0)),
        ]
        + [pl.BlockSpec((8, 128), lambda i: (0, 0)) for _ in vecs],
        out_specs=[
            pl.BlockSpec((1, L, n), lambda i: (i, 0, 0)),
            pl.BlockSpec((8, 128), lambda i: (0, 0)),
        ],
        out_shape=[
            jax.ShapeDtypeStruct((4, L, n), BF16),
            jax.ShapeDtypeStruct((8, 128), F32),
        ],
        scratch_shapes=[pltpu.VMEM((8, 128), F32)],
        compiler_params=params(32),
        cost_estimate=SMALL,
    )(ids, pairs, total, hidden, tgt, gain, *vecs)


def per_device(
    fsdp_size,
    tensor_size,
    ref_states,
    pol_states,
    target_rows,
    norm_gain,
    wq,
    wk,
    wv,
    wo,
    qa,
    qo,
    va,
    vo,
    prompt_length,
    pairs,
):
    tokens, width = ref_states.shape
    groups = fsdp_size // 4
    near_z = fsdp_size // 4
    bits = []
    bit = 2
    while bit < fsdp_size:
        if bit != near_z:
            bits.append(bit)
        bit *= 2
    split = 2 if tensor_size == 2 and fsdp_size == 16 else 1
    kv_local = wk.shape[1] // HEAD_SIZE
    depth = wq.shape[0]
    part = depth // split
    rank = qa.shape[1]
    me = lax.axis_index("fsdp")
    x = lax.axis_index("tensor")
    side = x if split == 2 else 0

    def tmask(d):
        return (d & 1) | ((d >> 1) * near_z)

    def gmask(k):
        return sum(bit for i, bit in enumerate(bits) if (k >> i) & 1)

    def move(value, mask):
        return lax.ppermute(value, "fsdp", [(i, i ^ mask) for i in range(fsdp_size)])

    def swap_x(value):
        return lax.ppermute(value, "tensor", [(0, 1), (1, 0)])

    def move_both(value, mask, flip):
        pairs_list = [
            (2 * i + j, 2 * (i ^ mask) + (j ^ flip)) for i in range(fsdp_size) for j in range(2)
        ]
        return lax.ppermute(value, ("fsdp", "tensor"), pairs_list)

    def after(value, *others):
        return lax.optimization_barrier((value, *others))[0]

    def marker(*queue):
        return move(after(cosine[:16].astype(BF16), *queue), 1)

    cosine, sine = rope_tables(L, HEAD_SIZE)

    wide = groups == 4 and split == 2
    heads = wo.shape[0]

    def shard_of(j, *queue):
        q, k, v = wq, wk, wv
        if queue:
            q, k, v = lax.optimization_barrier((wq, wk, wv, *queue))[:3]
        pieces = [
            q[:, j * QCOLS : (j + 1) * QCOLS],
            k[:, j * HEAD_SIZE : (j + 1) * HEAD_SIZE],
            v[:, j * HEAD_SIZE : (j + 1) * HEAD_SIZE],
        ]
        return jnp.concatenate(pieces, 1)

    def gather(shard):
        return [shard] + [move(shard, gmask(k)) for k in range(1, groups)]

    if wide:
        over_y, over_z = gmask(1), gmask(2)
        shards = [shard_of(0)]
        zs = [move(shards[0], over_z)]
        ys = [move(shards[0], over_y)]
        corners = []

    parts = groups * split
    idx = []
    for d in range(4):
        for k in range(groups):
            for h in range(split):
                idx.append((me ^ tmask(d) ^ gmask(k)) * split + h)
    for d in range(4):
        for k in range(groups):
            idx.append((me ^ tmask(d) ^ gmask(k)) * split + side)
    idx.append(x)
    idx = jnp.stack(idx).astype(jnp.int32)
    prepared = prep(
        idx,
        ref_states,
        pol_states,
        target_rows,
        norm_gain.astype(F32).reshape(1, width),
        parts,
        part,
        split,
    )
    xs, ts, gain = prepared[:4], prepared[4:8], prepared[8]
    near = move(xs[1], 1)
    far = [move(xs[2], near_z)]
    far.append(move(xs[3], near_z | 1))

    if split == 2:
        first = (zs[0], ys[0]) if wide else ()
        other = [swap_x(after(a, *first) if first else a) for a in far]
        far = [
            [jnp.where(x == which, a[0], b[0]) for which in range(2)] for a, b in zip(far, other)
        ]
    states = jnp.concatenate(
        [
            *(xs[0][0], far[0][0], xs[0][1], far[0][1]),
            *(near[0], far[1][0], near[1], far[1][1]),
        ],
        0,
    )

    low = dot(pol_states, jnp.concatenate([qa, va], 1)).astype(BF16)
    cosine, sine = rope_tables(L, HEAD_SIZE)

    def own_columns(at, piece, *queue):
        return lax.dynamic_slice(
            after(wo, *queue), (piece * (heads // 2), at * part), (heads // 2, part)
        )

    def own_piece(step, *queue):
        at = (1 - x) if step < 2 else x
        return lax.dynamic_slice(
            after(wo, *queue), ((step % 2) * (heads // 2), at * part), (heads // 2, part)
        )

    def make_shard(j, *queue):
        if j < kv_local:
            shards.append(shard_of(j, *queue))
        elif j < kv_local + 4:
            shards.append(own_piece(j - kv_local, *queue))

    def next_shard(j, *more):
        queue = (zs[j - 1], ys[j - 1], *more)
        ys.append(move(after(shards[j], *queue), over_y))
        zs.append(move(after(shards[j], *queue), over_z))
        corners.append(move(after(*queue), over_y))

    saved = []
    parts_mixed = [[], [], []]

    def mix(j, keeps, came, sums, *queue, marks=()):
        results = []
        for which in range(2):
            total = sums[which * L : (which + 1) * L]
            result = attend(
                *(which == 1, keeps[which], came[which], total, low, qo, vo, j, cosine, sine),
                marks=marks,
            )
            saved.extend(result[1:])
            results.append(result[0])
        result = jnp.concatenate(results, 0)
        return result, move(after(result, *queue) if queue else result, near_z)

    def spread(result, other):
        far = move(jnp.concatenate([result, other], 0), 1)
        for part_mixed, value in zip(parts_mixed, (result, other, far)):
            part_mixed.append(value)
        return far

    if wide:
        make_shard(1, shards[0])
        next_shard(1)
        make_shard(2, zs[0])
    before = None
    ends = []
    marks = ()
    for j in range(kv_local):
        if wide:
            marks = (marker(zs[j + 1], ys[j + 1]),)
            ws = [shards[j], ys[j], zs[j], corners[j]]
        else:
            ws = gather(shard_of(j))
        sends = mm(states, 1, ws, BF16, marks)
        came = [move(send, 1) for send in sends]
        keeps = mm(states, 0, ws, F32)
        if wide:
            next_shard(j + 2)
            make_shard(j + 3, zs[j + 1])
        over = jnp.concatenate(
            [(keeps[which][L:] + came[which][L:].astype(F32)).astype(BF16) for which in range(2)], 0
        )
        if before is not None:
            result, other = mix(j - 1, *before, *came, *ends)
            if j + 2 < kv_local:
                over = after(over, other)
            states = after(states, other)
            ends = [spread(result, other)]
        if wide:
            over = after(over, shards[-1])
        sums = move(over, near_z)
        if wide and j + 1 == kv_local:
            marks = (marker(zs[j + 2], ys[j + 2]),)
            make_shard(kv_local + 3, zs[-2])
        before = (keeps, came, sums)
    last = spread(*mix(kv_local - 1, *before, *ends, marks=marks))

    keeps, recvs = [], []
    if wide:
        next_shard(kv_local + 2, over)
        first = [a[kv_local : kv_local + 2] for a in (shards, ys, zs, corners)]
        marks = (marker(zs[-1], ys[-1]),)
        recvs.append(swap_x(out_mm(parts_mixed, first[:2], marks)))
        next_shard(kv_local + 3)
        recvs.append(swap_x(out_mm(parts_mixed, first[2:])))
        corners.append(move(after(zs[-1], ys[-1]), over_y))
        wo_send, wo_keep = first, [a[kv_local + 2 :] for a in (shards, ys, zs, corners)]
        keeps.append(out_mm(parts_mixed, wo_keep[:3]))
        keeps.append(out_mm(parts_mixed, wo_keep[3:]))
    else:
        wo_keep = [[w] for w in gather(wo)]
        product = out_mm(parts_mixed, wo_keep)
        if tensor_size > 1:
            product = lax.psum(product, "tensor")
        keeps.append(product)
        recvs.append(jnp.zeros_like(product))

    targets = [ts[0]] + [move(after(ts[d], last), tmask(d)) for d in (1, 2, 3)]
    tgt = jnp.stack([targets[d] for d in ORD])
    scal = jnp.stack([jnp.asarray(side, jnp.int32), prompt_length[0].astype(jnp.int32)])
    hidden, stats = norm_stats(scal, states, tgt, gain, keeps, recvs, split)
    masks, got = [], []
    for flip in range(split):
        for d in range(4):
            if d or flip:
                masks.append(d)
                if split == 2:
                    got.append(move_both(stats, tmask(d), flip))
                else:
                    got.append(move(stats, tmask(d)))
    ids = jnp.stack([me ^ tmask(d) for d in ORD]).astype(jnp.int32)
    total, margin = scores(ids, stats, got, tuple(masks), width)
    vecs = [margin] + [move(margin, gmask(k)) for k in range(1, groups)]
    grad, loss = grad_hidden(ids, pairs, total, hidden, tgt, gain, vecs, width)

    grad_rows = grad.reshape(4 * L, -1)
    other = None
    for half in range(2):
        if split == 2:
            leaving = grad_rows[2 * L * half : 2 * L * (half + 1)]
            other = swap_x(leaving if half == 0 else after(leaving, other))
            acc = back_mm(grad_rows, half, wo_keep, None)
            keep, send = back_mm(other, None, wo_send, acc)
        else:
            acc = jnp.zeros((2 * L, heads), F32)
            keep, send = back_mm(grad_rows, half, wo_keep, acc)
        rs = move(send if half == 0 else after(send, r2), 1)
        if half == 0:
            over = (keep + rs.astype(F32)).astype(BF16)
            r2 = move(over, near_z)
    outer, mid = attend_back(keep, rs, r2, low, qo, vo, cosine, sine, saved)

    rows_each = width // tensor_size
    if split == 2:
        mids = [mid, swap_x(mid)]
    elif tensor_size == 1:
        mids = [mid]
    else:
        gathered = lax.all_gather(mid, "tensor", axis=0, tiled=False)
        mids = [gathered[i] for i in range(tensor_size)]
    scal = jnp.stack([x, me & 1]).astype(jnp.int32)
    away, current = adapter_products(scal, pol_states, mids, outer, rows_each)
    current = current + move(away, 1).astype(F32)
    top = fsdp_size // 2
    g = (me // 2) % groups
    rows = current.shape[0] // groups
    pieces = [
        lax.dynamic_slice_in_dim(current, (g ^ k) * rows, rows, 0) for k in range(groups)
    ]
    current = pieces[0]
    for k in range(1, groups):
        current = current + move(pieces[k].astype(BF16), k << 1).astype(F32)
    rows //= 2
    high = me // top
    away = lax.dynamic_slice_in_dim(current, (1 - high) * rows, rows, 0).astype(BF16)
    current = lax.dynamic_slice_in_dim(current, high * rows, rows, 0)
    current = (current + move(away, top).astype(F32)).astype(BF16)

    def join(bit, own, other):
        return jnp.where(
            bit == 0, jnp.concatenate([own, other], 0), jnp.concatenate([other, own], 0)
        )

    current = join(high, current, move(current, top))
    pieces = [current] + [move(current, k << 1) for k in range(1, groups)]
    step = 1
    while step < groups:
        odd = (g & step) != 0
        pieces = [jnp.where(odd, pieces[k ^ step], pieces[k]) for k in range(groups)]
        step *= 2
    current = jnp.concatenate(pieces, 0)
    grads = assemble(
        (me & 1).reshape(1), current, move(current, 1), rows_each, qo.shape[1], vo.shape[1]
    )
    return (loss[0, 0], grads[0].T, grads[1], grads[2].T, grads[3])


def solution(mesh):
    in_specs = (
        P("fsdp", None),
        P("fsdp", None),
        P("fsdp", None),
        P(),
        P("fsdp", "tensor"),
        P("fsdp", "tensor"),
        P("fsdp", "tensor"),
        P("tensor", "fsdp"),
        P(),
        P(None, "tensor"),
        P(),
        P(None, "tensor"),
        P("fsdp"),
        P(),
    )
    out_specs = (P(), P("tensor", None), P(None, "tensor"), P("tensor", None), P(None, "tensor"))
    body = functools.partial(per_device, mesh.shape["fsdp"], mesh.shape["tensor"])
    return jax.shard_map(body, mesh=mesh, in_specs=in_specs, out_specs=out_specs, check_vma=False)
```

```python
import functools

import jax
import jax.numpy as jnp
from jax import lax
from jax.experimental import pallas as pl
from jax.experimental.pallas import tpu as pltpu
from jax.sharding import PartitionSpec as P

QUERY_HEADS = 32
KEY_VALUE_HEADS = 8
HEAD_SIZE = 128
L = 128
GROUP = QUERY_HEADS // KEY_VALUE_HEADS
QCOLS = GROUP * HEAD_SIZE

adapter_scale = 0.5
dpo_beta = 0.1
loss_scale = 256.0
rope_base = 500000.0
norm_eps = 1e-05

F32 = jnp.float32
BF16 = jnp.bfloat16
ORD = (0, 2, 1, 3)
MB = 1 << 20
SMALL = pl.CostEstimate(flops=1, bytes_accessed=1, transcendentals=0)


def rope_tables(length, head_dim):
    half_dim = head_dim // 2
    exponent = jnp.arange(half_dim, dtype=F32) * (2.0 / head_dim)
    inverse = jnp.power(F32(rope_base), -exponent)
    angles = jnp.arange(length, dtype=F32)[:, None] * inverse[None, :]
    cosine = jnp.concatenate([jnp.cos(angles), jnp.cos(angles)], 1)
    sine = jnp.concatenate([-jnp.sin(angles), jnp.sin(angles)], 1)
    return cosine, sine


def dot(a, b, dims=((1,), (0,))):
    return lax.dot_general(a, b, (dims, ((), ())), preferred_element_type=F32)


def params(limit_mb):
    return pltpu.CompilerParams(vmem_limit_bytes=limit_mb * MB)


def smem():
    return pl.BlockSpec(memory_space=pltpu.SMEM)


def full(a):
    return pl.BlockSpec(a.shape, lambda i: (0,) * len(a.shape))


def prep_body(parts, part, split, idx, ref, pol, tgt, gain, *outs):
    x0, x1, x2, x3, t0, t1, t2, t3, go = outs[-9:]
    groups = parts // split
    for d, (xo, to) in enumerate(((x0, t0), (x1, t1), (x2, t2), (x3, t3))):
        for j in range(parts):
            src = pl.ds(pl.multiple_of(idx[d * parts + j] * part, part), part)
            cols = slice(j * part, (j + 1) * part)
            if xo.shape[0] == 2:
                xo[0, :, cols] = ref[:, src]
                xo[1, :, cols] = pol[:, src]
            else:
                @pl.when(idx[4 * parts + 4 * groups] == 0)
                def _():
                    xo[0, :, cols] = ref[:, src]

                @pl.when(idx[4 * parts + 4 * groups] != 0)
                def _():
                    xo[0, :, cols] = pol[:, src]

        for j in range(groups):
            at = idx[4 * parts + d * groups + j] * part
            src = pl.ds(pl.multiple_of(at, part), part)
            to[:, j * part : (j + 1) * part] = tgt[:, src]
            if d == 0:
                go[:, j * part : (j + 1) * part] = gain[:, src]


def prep(idx, ref, pol, tgt, gain, parts, part, split):
    tokens = ref.shape[0]
    xs = lambda n: jax.ShapeDtypeStruct((n, tokens, parts * part), BF16)
    far = 1 if split == 2 else 2
    width = parts // split * part
    tile = 32
    shapes = [xs(2), xs(2), xs(far), xs(far)]
    shapes += [jax.ShapeDtypeStruct((tokens, width), BF16)] * 4
    shapes += [jax.ShapeDtypeStruct((1, width), F32)]
    return pl.pallas_call(
        functools.partial(prep_body, parts, part, split),
        grid=(tokens // tile,),
        in_specs=[smem()]
        + [pl.BlockSpec((tile, a.shape[1]), lambda i: (i, 0)) for a in (ref, pol, tgt)]
        + [full(gain)],
        out_specs=[
            pl.BlockSpec((a.shape[0], tile, a.shape[2]), lambda i: (0, i, 0)) for a in shapes[:4]
        ]
        + [pl.BlockSpec((tile, width), lambda i: (i, 0))] * 4
        + [full(shapes[8])],
        out_shape=shapes,
        compiler_params=params(60),
        cost_estimate=SMALL,
    )(idx, ref, pol, tgt, gain)


def tile_of(cols):
    for tile in (256, 128):
        if cols % tile == 0:
            return tile
    return cols


def mm_body(count, x_ref, *refs):
    ws, outs = refs[:count], refs[-2:]
    total = None
    at = 0
    for w in ws:
        depth = w.shape[0]
        term = dot(x_ref[:, at : at + depth], w[...])
        total = term if total is None else total + term
        at += depth
    rows = total.shape[0] // 2
    for i, out_ref in enumerate(outs):
        out_ref[...] = total[i * rows : (i + 1) * rows].astype(out_ref.dtype)


def mm(x, half, ws, out_dtype, marks=()):
    rows, depth = x.shape[0] // 2, x.shape[1]
    cols = ws[0].shape[1]
    tile = tile_of(cols)
    return pl.pallas_call(
        functools.partial(mm_body, len(ws)),
        grid=(cols // tile,),
        in_specs=[pl.BlockSpec((rows, depth), lambda i: (half, 0))]
        + [pl.BlockSpec((w.shape[0], tile), lambda i: (0, i)) for w in ws]
        + [full(a) for a in marks],
        out_specs=[pl.BlockSpec((rows // 2, tile), lambda i: (0, i))] * 2,
        out_shape=[jax.ShapeDtypeStruct((rows // 2, cols), out_dtype)] * 2,
        compiler_params=params(32),
        cost_estimate=pl.CostEstimate(
            flops=2 * rows * depth * cols,
            bytes_accessed=2 * (rows * (depth + cols) + depth * cols),
            transcendentals=0,
        ),
    )(x, *ws, *marks)


def out_body(n, row_parts, counts, *refs):
    ws = refs[row_parts * n :][: sum(counts)]
    out_ref, total = refs[-2:]
    for j in range(n):
        x = jnp.concatenate([refs[p * n + j][...] for p in range(row_parts)], 0)
        depth = x.shape[1]
        at = 0
        for k, count in enumerate(counts):
            row = j * depth
            piece = at
            while row >= ws[piece].shape[0]:
                row -= ws[piece].shape[0]
                piece += 1
            at += count
            term = dot(x, ws[piece][row : row + depth])
            if j:
                term = term + total[k]
            if j == n - 1:
                out_ref[k] = term.astype(BF16)
            else:
                total[k] = term


def out_mm(parts, ws, marks=()):
    n = len(parts[0])
    rows = sum(part[0].shape[0] for part in parts)
    cols = ws[0][0].shape[1]
    flat = [piece for w in ws for piece in w]
    inputs = [a for part in parts for a in part] + flat + list(marks)
    out_shape = jax.ShapeDtypeStruct((len(ws), rows, cols), BF16)
    return pl.pallas_call(
        functools.partial(out_body, n, len(parts), tuple(len(w) for w in ws)),
        grid=(1,),
        in_specs=[full(a) for a in inputs],
        out_specs=full(out_shape),
        out_shape=out_shape,
        scratch_shapes=[pltpu.VMEM(out_shape.shape, F32)],
        compiler_params=params(32),
        cost_estimate=SMALL,
    )(*inputs)


def back_body(counts, part, has_acc, x_ref, *refs):
    total = None
    at = 0
    for j, count in enumerate(counts):
        w = refs[at][...]
        if count == 2:
            w = jnp.where(pl.program_id(0) < pl.num_programs(0) // 2, w, refs[at + 1][...])
        at += count
        term = dot(x_ref[:, j * part : (j + 1) * part], w, ((1,), (1,)))
        total = term if total is None else total + term
    refs = refs[at:]
    if has_acc:
        total = total + refs[0][...]
        keep, send = refs[1:]
        half = total.shape[0] // 2
        keep[...] = total[:half]
        send[...] = total[half:].astype(send.dtype)
    else:
        refs[0][...] = total


def back_mm(x, half, ws, acc):
    rows = x.shape[0] // (1 if half is None else 2)
    depth = x.shape[1]
    part = ws[0][0].shape[1]
    heads = sum(piece.shape[0] for piece in ws[0])
    tile = min(512, heads)
    steps = heads // tile
    has_acc = acc is not None
    row = half or 0
    in_specs = [pl.BlockSpec((rows, depth), lambda i: (row, 0))]
    for w in ws:
        if len(w) == 1:
            in_specs.append(pl.BlockSpec((tile, part), lambda i: (i, 0)))
        else:
            in_specs.append(pl.BlockSpec((tile, part), lambda i: (jnp.minimum(i, steps // 2 - 1), 0)))
            in_specs.append(pl.BlockSpec((tile, part), lambda i: (jnp.maximum(i - steps // 2, 0), 0)))
    args = [x] + [piece for w in ws for piece in w]
    if has_acc:
        in_specs.append(pl.BlockSpec((rows, tile), lambda i: (0, i)))
        args.append(acc)
        out_specs = [pl.BlockSpec((rows // 2, tile), lambda i: (0, i))] * 2
        out_shape = [
            jax.ShapeDtypeStruct((rows // 2, heads), F32),
            jax.ShapeDtypeStruct((rows // 2, heads), BF16),
        ]
    else:
        out_specs = pl.BlockSpec((rows, tile), lambda i: (0, i))
        out_shape = jax.ShapeDtypeStruct((rows, heads), F32)
    return pl.pallas_call(
        functools.partial(back_body, tuple(len(w) for w in ws), part, has_acc),
        grid=(steps,),
        in_specs=in_specs,
        out_specs=out_specs,
        out_shape=out_shape,
        compiler_params=params(32),
        cost_estimate=SMALL,
    )(*args)


def causal(rows):
    at = lax.broadcasted_iota(jnp.int32, (rows, L), 0) % L
    return at >= lax.broadcasted_iota(jnp.int32, (rows, L), 1)


def probabilities(q4, keys):
    scores = dot(q4, keys, ((1,), (1,))) * (HEAD_SIZE**-0.5)
    weights = jnp.where(causal(q4.shape[0]), jnp.exp(scores), 0.0)
    return weights / jnp.sum(weights, -1, keepdims=True)


def stack_heads(values):
    return jnp.concatenate(
        [values[:, h * HEAD_SIZE : (h + 1) * HEAD_SIZE] for h in range(GROUP)], 0
    )


def attend_body(adapted, keep, rs, r2, low, qo, vo, cos_ref, sin_ref, *refs):
    mixed, *saved = refs[-1 - adapted :]
    cosine = cos_ref[...]
    sine = sin_ref[...]
    pre = keep[...] + rs[...].astype(F32) + r2[...].astype(F32)
    rank = qo.shape[0]
    q_pre = pre[:, :QCOLS]
    k_pre = pre[:, QCOLS : QCOLS + HEAD_SIZE]
    v_pre = pre[:, QCOLS + HEAD_SIZE :]
    if adapted:
        q_pre = q_pre + adapter_scale * dot(low[:, :rank], qo[...])
        v_pre = v_pre + adapter_scale * dot(low[:, rank:], vo[...])
    cos4 = jnp.concatenate([cosine] * GROUP, 0)
    sin4 = jnp.concatenate([sine] * GROUP, 0)
    q4 = stack_heads(q_pre)
    q4 = (q4 * cos4 + pltpu.roll(q4, HEAD_SIZE // 2, 1) * sin4).astype(BF16)
    keys = (k_pre * cosine + pltpu.roll(k_pre, HEAD_SIZE // 2, 1) * sine).astype(BF16)
    values = v_pre.astype(BF16)
    rounded = probabilities(q4, keys).astype(BF16)
    out = dot(rounded, values).astype(BF16)
    for h in range(GROUP):
        cols = slice(h * HEAD_SIZE, (h + 1) * HEAD_SIZE)
        mixed[:, cols] = out[h * L : (h + 1) * L]
        if saved:
            saved[0][:, cols] = q4[h * L : (h + 1) * L]
    if saved:
        saved[0][:, QCOLS : QCOLS + HEAD_SIZE] = keys
        saved[0][:, QCOLS + HEAD_SIZE :] = values


def attend(adapted, keep, rs, r2, low, qo, vo, group, cosine, sine, marks=()):
    each = QCOLS + 2 * HEAD_SIZE
    rank = qo.shape[0]
    top = lambda a: pl.BlockSpec((L, a.shape[1]), lambda i: (0, 0))
    return pl.pallas_call(
        functools.partial(attend_body, adapted),
        grid=(1,),
        in_specs=[
            top(keep),
            top(rs),
            top(r2),
            top(low),
            pl.BlockSpec((rank, QCOLS), lambda i: (0, group)),
            pl.BlockSpec((rank, HEAD_SIZE), lambda i: (0, group)),
            top(cosine),
            top(sine),
        ]
        + [full(a) for a in marks],
        out_specs=[pl.BlockSpec((L, w), lambda i: (0, 0)) for w in (QCOLS, each)[: 1 + adapted]],
        out_shape=[jax.ShapeDtypeStruct((L, w), BF16) for w in (QCOLS, each)[: 1 + adapted]],
        compiler_params=params(32),
        cost_estimate=SMALL,
    )(keep, rs, r2, low, qo, vo, cosine, sine, *marks)


def outer_place(block, rank, kv):
    wide = (kv * (GROUP + 1) + 1) // 2
    return (block // wide) * rank, (block % wide) * HEAD_SIZE, wide


def attend_back_body(kv, splits, keep, rs, r2, low, qo, vo, cos_ref, sin_ref, *refs):
    saved = refs[:splits]
    outer, mid = refs[splits:]
    rank = qo.shape[0]
    each = QCOLS + 2 * HEAD_SIZE
    cos4 = jnp.concatenate([cos_ref[...]] * GROUP, 0)
    sin4 = jnp.concatenate([sin_ref[...]] * GROUP, 0)
    low_q = low[:, :rank]
    low_v = low[:, rank:]
    q_mid = jnp.zeros((L, rank), F32)
    v_mid = jnp.zeros((L, rank), F32)

    def put(block, value):
        row, col, _ = outer_place(block, rank, kv)
        outer[row : row + rank, col : col + HEAD_SIZE] = adapter_scale * value

    if (kv * (GROUP + 1)) % 2:
        put(kv * (GROUP + 1), jnp.zeros((rank, HEAD_SIZE), F32))
    for j in range(kv):
        cols = slice(j * QCOLS, (j + 1) * QCOLS)
        at = (j % (kv // splits)) * each
        kept = saved[j // (kv // splits)]
        grad = keep[:, cols] + rs[:, cols].astype(F32) + r2[:, cols].astype(F32)
        grad4 = stack_heads(grad.astype(BF16))
        q4 = stack_heads(kept[:, at : at + QCOLS])
        keys = kept[:, at + QCOLS : at + QCOLS + HEAD_SIZE]
        values = kept[:, at + QCOLS + HEAD_SIZE : at + each]
        prob = probabilities(q4, keys)
        grad_prob = dot(grad4, values, ((1,), (1,)))
        grad_values = dot(prob.astype(BF16), grad4, ((0,), (0,))).astype(BF16)
        inner = jnp.sum(grad_prob * prob, -1, keepdims=True)
        grad_scores = (prob * (grad_prob - inner) * (HEAD_SIZE**-0.5)).astype(BF16)
        grad_query = dot(grad_scores, keys)
        back4 = (grad_query * cos4 - pltpu.roll(grad_query, HEAD_SIZE // 2, 1) * sin4).astype(BF16)
        for h in range(GROUP):
            at = j * GROUP + h
            back = back4[h * L : (h + 1) * L]
            put(at, dot(low_q, back, ((0,), (0,))))
            q_mid += dot(back, qo[:, at * HEAD_SIZE : (at + 1) * HEAD_SIZE], ((1,), (1,)))
        put(kv * GROUP + j, dot(low_v, grad_values, ((0,), (0,))))
        v_mid += dot(grad_values, vo[:, j * HEAD_SIZE : (j + 1) * HEAD_SIZE], ((1,), (1,)))
    mid[:, :rank] = (adapter_scale * q_mid).astype(BF16)
    mid[:, rank:] = (adapter_scale * v_mid).astype(BF16)


def attend_back(keep, rs, r2, low, qo, vo, cosine, sine, saved):
    rank = qo.shape[0]
    kv = vo.shape[1] // HEAD_SIZE
    wide = outer_place(0, rank, kv)[2]
    inputs = (keep, rs, r2, low, qo, vo, cosine, sine, *saved)
    shapes = [
        jax.ShapeDtypeStruct((2 * rank, wide * HEAD_SIZE), F32),
        jax.ShapeDtypeStruct((L, 2 * rank), BF16),
    ]
    return pl.pallas_call(
        functools.partial(attend_back_body, kv, len(saved)),
        grid=(1,),
        in_specs=[full(a) for a in inputs],
        out_specs=[full(a) for a in shapes],
        out_shape=shapes,
        compiler_params=params(60),
        cost_estimate=SMALL,
    )(*inputs)


def adapter_body(n, rows_each, scal, states, outer, *refs):
    mids = refs[:n]
    away, stay = refs[n:]
    src = pl.ds(pl.multiple_of(scal[0] * rows_each, rows_each), rows_each)
    own = states[:, src]
    total = None
    for mid in mids:
        term = dot(mid[...], own, ((0,), (0,)))
        total = term if total is None else total + term
    half = total.shape[0] // 2
    for low in range(2):
        rows = slice(low * half, (low + 1) * half)

        @pl.when(scal[1] == low)
        def _():
            stay[:, :rows_each] = total[rows]
            stay[:, rows_each:] = outer[rows]

        @pl.when(scal[1] != low)
        def _():
            away[:, :rows_each] = total[rows].astype(BF16)
            away[:, rows_each:] = outer[rows].astype(BF16)


def adapter_products(scal, states, mids, outer, rows_each):
    half = outer.shape[0] // 2
    cols = rows_each + outer.shape[1]
    shapes = [jax.ShapeDtypeStruct((half, cols), BF16), jax.ShapeDtypeStruct((half, cols), F32)]
    return pl.pallas_call(
        functools.partial(adapter_body, len(mids), rows_each),
        grid=(1,),
        in_specs=[smem()] + [full(a) for a in (states, outer, *mids)],
        out_specs=[full(a) for a in shapes],
        out_shape=shapes,
        compiler_params=params(32),
        cost_estimate=SMALL,
    )(scal, states, outer, *mids)


def assemble_body(rows_each, bit, own, other, q_inner, q_outer, v_inner, v_outer):
    low = jnp.where(bit[0] == 0, own[...], other[...]).astype(F32)
    high = jnp.where(bit[0] == 0, other[...], own[...]).astype(F32)
    q_inner[...] = low[:, :rows_each]
    v_inner[...] = high[:, :rows_each]
    outer = jnp.concatenate([low[:, rows_each:], high[:, rows_each:]], 1)
    cols = q_outer.shape[1]
    q_outer[...] = outer[:, :cols]
    v_outer[...] = outer[:, cols : cols + v_outer.shape[1]]


def assemble(bit, own, other, rows_each, q_cols, v_cols):
    rank = own.shape[0]
    shapes = [jax.ShapeDtypeStruct((rank, c), F32) for c in (rows_each, q_cols, rows_each, v_cols)]
    return pl.pallas_call(
        functools.partial(assemble_body, rows_each),
        grid=(1,),
        in_specs=[smem(), full(own), full(other)],
        out_specs=[full(a) for a in shapes],
        out_shape=shapes,
        compiler_params=params(32),
        cost_estimate=SMALL,
    )(bit, own, other)


def stats_body(counts, part, split, scal, xt_ref, xt_pol, tgt, gain, *refs):
    refs = list(refs)
    sums = []
    hidden_out, stats = refs[-2:]
    for which in range(2):
        xt = (xt_ref, xt_pol)[which]
        count = sum(counts)
        keeps = [r[i] for r in refs[: counts[0]] for i in range(r.shape[0])]
        recvs = [r[i] for r in refs[counts[0] : count] for i in range(r.shape[0])]
        refs = refs[count:]
        squares = jnp.zeros((L, HEAD_SIZE), F32)
        products = jnp.zeros((L, HEAD_SIZE), F32)
        for j, (keep, recv) in enumerate(zip(keeps, recvs)):
            src = pl.ds(pl.multiple_of((j * split + scal[0]) * part, part), part)
            hidden = xt[:, src].astype(F32) + keep.astype(F32) + recv.astype(F32)
            cols = slice(j * part, (j + 1) * part)
            if which == 1:
                hidden_out[0, :, cols] = hidden
            product = hidden * (gain[:, cols] * tgt[0, :, cols].astype(F32))
            square = hidden * hidden
            for s in range(part // HEAD_SIZE):
                lanes = slice(s * HEAD_SIZE, (s + 1) * HEAD_SIZE)
                squares += square[:, lanes]
                products += product[:, lanes]
        sums.append(
            [
                jnp.broadcast_to(jnp.sum(v, 1, keepdims=True), v.shape).T[:1]
                for v in (squares, products)
            ]
        )
    at = lax.broadcasted_iota(jnp.int32, (1, 2 * L), 1) % L
    own = (at >= scal[1]) & (pl.program_id(0) == 0)
    live = jnp.where(own, 1.0, 0.0).astype(F32)
    both = [jnp.concatenate([sums[0][i], sums[1][i]], 1) for i in range(2)]
    stats[...] = jnp.concatenate([*both, live, jnp.zeros((5, 2 * L), F32)], 0)


def norm_stats(scal, xt, tgt, gain, keeps, recvs, split):
    n = sum(a.shape[0] for a in keeps)
    part = keeps[0].shape[2]
    shared = []
    for which in range(2):
        at = functools.partial(lambda which, i: (0, 2 * i + which, 0), which)
        for a in (*keeps, *recvs):
            shared.append((a, pl.BlockSpec((a.shape[0], L, part), at)))
    return pl.pallas_call(
        functools.partial(stats_body, (len(keeps), len(recvs)), part, split),
        grid=(4,),
        in_specs=[
            smem(),
            pl.BlockSpec((L, xt.shape[1]), lambda i: ((i // 2) * 4 + i % 2, 0)),
            pl.BlockSpec((L, xt.shape[1]), lambda i: ((i // 2) * 4 + 2 + i % 2, 0)),
            pl.BlockSpec((1, L, n * part), lambda i: (i, 0, 0)),
            pl.BlockSpec((1, n * part), lambda i: (0, 0)),
        ]
        + [spec for _, spec in shared],
        out_specs=[
            pl.BlockSpec((1, L, n * part), lambda i: (i, 0, 0)),
            pl.BlockSpec((8, 2 * L), lambda i: (i, 0)),
        ],
        out_shape=[
            jax.ShapeDtypeStruct((4, L, n * part), F32),
            jax.ShapeDtypeStruct((32, 2 * L), F32),
        ],
        compiler_params=params(32),
        cost_estimate=SMALL,
    )(scal, xt, xt, tgt, gain, *[a for a, _ in shared])


def score_body(width, masks, ids, own, *refs):
    recvs = refs[: len(masks)]
    total_out, margin_out = refs[len(masks) :]
    lane = lax.broadcasted_iota(jnp.int32, (8, 128), 1)
    margins = jnp.zeros((8, 128), F32)
    for p in range(4):
        total = own[8 * p : 8 * p + 8]
        for recv, m in zip(recvs, masks):
            q = ORD.index(ORD[p] ^ m)
            total = total + recv[8 * q : 8 * q + 8]
        total_out[8 * p : 8 * p + 8] = total
        inverse = lax.rsqrt(total[0:1] * (1.0 / width) + norm_eps)
        score = total[1:2] * inverse * (width**-0.5)
        score = jnp.where(total[2:3] > 0.5, score, 0.0)
        margin = jnp.sum(score[:, L:], 1, keepdims=True) - jnp.sum(score[:, :L], 1, keepdims=True)
        margins = margins + jnp.where(lane == ids[p], margin, 0.0)
    margin_out[...] = margins


def scores(ids, own, recvs, masks, width):
    shapes = [jax.ShapeDtypeStruct(own.shape, F32), jax.ShapeDtypeStruct((8, 128), F32)]
    return pl.pallas_call(
        functools.partial(score_body, width, masks),
        grid=(1,),
        in_specs=[smem()] + [full(a) for a in (own, *recvs)],
        out_specs=[full(a) for a in shapes],
        out_shape=shapes,
        cost_estimate=SMALL,
    )(ids, own, *recvs)


def turn(i):
    return (2 * i + 1) % 5


def grad_body(width, seqs, n_vec, ids, pairs, total, hidden, tgt, gain, *refs):
    vecs = refs[:n_vec]
    grad_out, loss_out, slope = refs[n_vec:]
    lane = lax.broadcasted_iota(jnp.int32, (8, 128), 1)

    @pl.when(pl.program_id(0) == 0)
    def _():
        margin = vecs[0][...]
        for v in vecs[1:]:
            margin = margin + v[...]
        logits = jnp.zeros((8, 128), F32)
        for i in range(seqs // 2):
            sign = jnp.where(lane == pairs[2 * i], 1.0, 0.0) - jnp.where(
                lane == pairs[2 * i + 1], 1.0, 0.0
            )
            logit = dpo_beta * jnp.sum(margin * sign, 1, keepdims=True)
            logits = logits + jnp.where(lane == i, logit, 0.0)
        soft = jnp.maximum(-logits, 0.0) + jnp.log1p(jnp.exp(-jnp.abs(logits)))
        used = lane < seqs // 2
        loss = jnp.sum(jnp.where(used, soft, 0.0), 1, keepdims=True)
        loss_out[...] = jnp.broadcast_to(loss, (8, 128))
        slopes = jnp.where(used, -dpo_beta / (1.0 + jnp.exp(logits)), 0.0)
        gradient = jnp.zeros((8, 128), F32)
        for i in range(seqs // 2):
            each = jnp.sum(jnp.where(lane == i, slopes, 0.0), 1, keepdims=True)
            sign = jnp.where(lane == pairs[2 * i], 1.0, 0.0) - jnp.where(
                lane == pairs[2 * i + 1], 1.0, 0.0
            )
            gradient = gradient + each * sign
        slope[...] = gradient * loss_scale

    mine = lane == ids[turn(pl.program_id(0))]
    seq = jnp.sum(jnp.where(mine, slope[...], 0.0), 1, keepdims=True)[:1]
    rows = total[:, L:]
    token = jnp.where(rows[2:3] > 0.5, seq, 0.0) * (width**-0.5)
    inverse = lax.rsqrt(rows[0:1] * (1.0 / width) + norm_eps)
    first = inverse * token
    second = inverse * inverse * inverse * (token * rows[1:2] * (1.0 / width))
    first = jnp.broadcast_to(first, (L, L)).T
    second = jnp.broadcast_to(second, (L, L)).T
    for s in range(hidden.shape[2] // HEAD_SIZE):
        cols = slice(s * HEAD_SIZE, (s + 1) * HEAD_SIZE)
        weighted = gain[:, cols] * tgt[0, :, cols].astype(F32)
        grad_out[0, :, cols] = (first * weighted - second * hidden[0, :, cols]).astype(BF16)


def grad_hidden(ids, pairs, total, hidden, tgt, gain, vecs, width):
    n = hidden.shape[2]
    seqs = pairs.shape[0]
    return pl.pallas_call(
        functools.partial(grad_body, width, seqs, len(vecs)),
        grid=(4,),
        in_specs=[
            smem(),
            smem(),
            pl.BlockSpec((8, 2 * L), lambda i: (turn(i), 0)),
            pl.BlockSpec((1, L, n), lambda i: (turn(i), 0, 0)),
            pl.BlockSpec((1, L, n), lambda i: (turn(i), 0, 0)),
            pl.BlockSpec((1, n), lambda i: (0, 0)),
        ]
        + [pl.BlockSpec((8, 128), lambda i: (0, 0)) for _ in vecs],
        out_specs=[
            pl.BlockSpec((1, L, n), lambda i: (i, 0, 0)),
            pl.BlockSpec((8, 128), lambda i: (0, 0)),
        ],
        out_shape=[
            jax.ShapeDtypeStruct((4, L, n), BF16),
            jax.ShapeDtypeStruct((8, 128), F32),
        ],
        scratch_shapes=[pltpu.VMEM((8, 128), F32)],
        compiler_params=params(32),
        cost_estimate=SMALL,
    )(ids, pairs, total, hidden, tgt, gain, *vecs)


def per_device(
    fsdp_size,
    tensor_size,
    ref_states,
    pol_states,
    target_rows,
    norm_gain,
    wq,
    wk,
    wv,
    wo,
    qa,
    qo,
    va,
    vo,
    prompt_length,
    pairs,
):
    tokens, width = ref_states.shape
    groups = fsdp_size // 4
    near_z = fsdp_size // 4
    bits = []
    bit = 2
    while bit < fsdp_size:
        if bit != near_z:
            bits.append(bit)
        bit *= 2
    split = 2 if tensor_size == 2 and fsdp_size == 16 else 1
    kv_local = wk.shape[1] // HEAD_SIZE
    depth = wq.shape[0]
    part = depth // split
    rank = qa.shape[1]
    me = lax.axis_index("fsdp")
    x = lax.axis_index("tensor")
    side = x if split == 2 else 0

    def tmask(d):
        return (d & 1) | ((d >> 1) * near_z)

    def gmask(k):
        return sum(bit for i, bit in enumerate(bits) if (k >> i) & 1)

    def move(value, mask):
        return lax.ppermute(value, "fsdp", [(i, i ^ mask) for i in range(fsdp_size)])

    def swap_x(value):
        return lax.ppermute(value, "tensor", [(0, 1), (1, 0)])

    def move_both(value, mask, flip):
        pairs_list = [
            (2 * i + j, 2 * (i ^ mask) + (j ^ flip)) for i in range(fsdp_size) for j in range(2)
        ]
        return lax.ppermute(value, ("fsdp", "tensor"), pairs_list)

    def after(value, *others):
        return lax.optimization_barrier((value, *others))[0]

    def marker(*queue):
        return move(after(cosine[:16].astype(BF16), *queue), 1)

    cosine, sine = rope_tables(L, HEAD_SIZE)

    wide = groups == 4 and split == 2
    heads = wo.shape[0]

    def shard_of(j, *queue):
        q, k, v = wq, wk, wv
        if queue:
            q, k, v = lax.optimization_barrier((wq, wk, wv, *queue))[:3]
        pieces = [
            q[:, j * QCOLS : (j + 1) * QCOLS],
            k[:, j * HEAD_SIZE : (j + 1) * HEAD_SIZE],
            v[:, j * HEAD_SIZE : (j + 1) * HEAD_SIZE],
        ]
        return jnp.concatenate(pieces, 1)

    def gather(shard):
        return [shard] + [move(shard, gmask(k)) for k in range(1, groups)]

    if wide:
        over_y, over_z = gmask(1), gmask(2)
        shards = [shard_of(0)]
        zs = [move(shards[0], over_z)]
        ys = [move(shards[0], over_y)]
        corners = []

    parts = groups * split
    idx = []
    for d in range(4):
        for k in range(groups):
            for h in range(split):
                idx.append((me ^ tmask(d) ^ gmask(k)) * split + h)
    for d in range(4):
        for k in range(groups):
            idx.append((me ^ tmask(d) ^ gmask(k)) * split + side)
    idx.append(x)
    idx = jnp.stack(idx).astype(jnp.int32)
    prepared = prep(
        idx,
        ref_states,
        pol_states,
        target_rows,
        norm_gain.astype(F32).reshape(1, width),
        parts,
        part,
        split,
    )
    xs, ts, gain = prepared[:4], prepared[4:8], prepared[8]
    near = move(xs[1], 1)
    far = [move(xs[2], near_z)]
    far.append(move(xs[3], near_z | 1))

    if split == 2:
        first = (zs[0], ys[0]) if wide else ()
        other = [swap_x(after(a, *first) if first else a) for a in far]
        far = [
            [jnp.where(x == which, a[0], b[0]) for which in range(2)] for a, b in zip(far, other)
        ]
    states = jnp.concatenate(
        [
            *(xs[0][0], far[0][0], xs[0][1], far[0][1]),
            *(near[0], far[1][0], near[1], far[1][1]),
        ],
        0,
    )

    low = dot(pol_states, jnp.concatenate([qa, va], 1)).astype(BF16)
    cosine, sine = rope_tables(L, HEAD_SIZE)

    def own_columns(at, piece, *queue):
        return lax.dynamic_slice(
            after(wo, *queue), (piece * (heads // 2), at * part), (heads // 2, part)
        )

    def own_piece(step, *queue):
        at = (1 - x) if step < 2 else x
        return lax.dynamic_slice(
            after(wo, *queue), ((step % 2) * (heads // 2), at * part), (heads // 2, part)
        )

    def make_shard(j, *queue):
        if j < kv_local:
            shards.append(shard_of(j, *queue))
        elif j < kv_local + 4:
            shards.append(own_piece(j - kv_local, *queue))

    def next_shard(j, *more):
        queue = (zs[j - 1], ys[j - 1], *more)
        ys.append(move(after(shards[j], *queue), over_y))
        zs.append(move(after(shards[j], *queue), over_z))
        corners.append(move(after(*queue), over_y))

    saved = []
    parts_mixed = [[], [], []]

    def mix(j, keeps, came, sums, *queue, marks=()):
        results = []
        for which in range(2):
            total = sums[which * L : (which + 1) * L]
            result = attend(
                *(which == 1, keeps[which], came[which], total, low, qo, vo, j, cosine, sine),
                marks=marks,
            )
            saved.extend(result[1:])
            results.append(result[0])
        result = jnp.concatenate(results, 0)
        return result, move(after(result, *queue) if queue else result, near_z)

    def spread(result, other):
        far = move(jnp.concatenate([result, other], 0), 1)
        for part_mixed, value in zip(parts_mixed, (result, other, far)):
            part_mixed.append(value)
        return far

    if wide:
        make_shard(1, shards[0])
        next_shard(1)
        make_shard(2, zs[0])
    before = None
    ends = []
    marks = ()
    for j in range(kv_local):
        if wide:
            marks = (marker(zs[j + 1], ys[j + 1]),)
            ws = [shards[j], ys[j], zs[j], corners[j]]
        else:
            ws = gather(shard_of(j))
        sends = mm(states, 1, ws, BF16, marks)
        came = [move(send, 1) for send in sends]
        keeps = mm(states, 0, ws, F32)
        if wide:
            next_shard(j + 2)
            make_shard(j + 3, zs[j + 1])
        over = jnp.concatenate(
            [(keeps[which][L:] + came[which][L:].astype(F32)).astype(BF16) for which in range(2)], 0
        )
        if before is not None:
            result, other = mix(j - 1, *before, *came, *ends)
            if j + 2 < kv_local:
                over = after(over, other)
            states = after(states, other)
            ends = [spread(result, other)]
        if wide:
            over = after(over, shards[-1])
        sums = move(over, near_z)
        if wide and j + 1 == kv_local:
            marks = (marker(zs[j + 2], ys[j + 2]),)
            make_shard(kv_local + 3, zs[-2])
        before = (keeps, came, sums)
    last = spread(*mix(kv_local - 1, *before, *ends, marks=marks))

    keeps, recvs = [], []
    if wide:
        next_shard(kv_local + 2, over)
        first = [a[kv_local : kv_local + 2] for a in (shards, ys, zs, corners)]
        marks = (marker(zs[-1], ys[-1]),)
        recvs.append(swap_x(out_mm(parts_mixed, first[:2], marks)))
        next_shard(kv_local + 3)
        recvs.append(swap_x(out_mm(parts_mixed, first[2:])))
        corners.append(move(after(zs[-1], ys[-1]), over_y))
        wo_send, wo_keep = first, [a[kv_local + 2 :] for a in (shards, ys, zs, corners)]
        keeps.append(out_mm(parts_mixed, wo_keep[:3]))
        keeps.append(out_mm(parts_mixed, wo_keep[3:]))
    else:
        wo_keep = [[w] for w in gather(wo)]
        product = out_mm(parts_mixed, wo_keep)
        if tensor_size > 1:
            product = lax.psum(product, "tensor")
        keeps.append(product)
        recvs.append(jnp.zeros_like(product))

    from_neighbour = move(after(jnp.stack(ts[2:]), last), near_z)
    from_core = move(jnp.stack([ts[1], from_neighbour[1]]), 1)
    tgt = jnp.stack([ts[0], from_neighbour[0], *from_core])
    scal = jnp.stack([jnp.asarray(side, jnp.int32), prompt_length[0].astype(jnp.int32)])
    hidden, stats = norm_stats(scal, states, tgt, gain, keeps, recvs, split)
    masks, got = [], []
    for flip in range(split):
        for d in range(4):
            if d or flip:
                masks.append(d)
                if split == 2:
                    got.append(move_both(stats, tmask(d), flip))
                else:
                    got.append(move(stats, tmask(d)))
    ids = jnp.stack([me ^ tmask(d) for d in ORD]).astype(jnp.int32)
    total, margin = scores(ids, stats, got, tuple(masks), width)
    vecs = [margin] + [move(margin, gmask(k)) for k in range(1, groups)]
    grad, loss = grad_hidden(ids, pairs, total, hidden, tgt, gain, vecs, width)

    grad_rows = grad.reshape(4 * L, -1)
    other = None
    for half in range(2):
        if split == 2:
            leaving = grad_rows[2 * L * half : 2 * L * (half + 1)]
            other = swap_x(leaving if half == 0 else after(leaving, other))
            acc = back_mm(grad_rows, half, wo_keep, None)
            keep, send = back_mm(other, None, wo_send, acc)
        else:
            acc = jnp.zeros((2 * L, heads), F32)
            keep, send = back_mm(grad_rows, half, wo_keep, acc)
        rs = move(send if half == 0 else after(send, r2), 1)
        if half == 0:
            over = (keep + rs.astype(F32)).astype(BF16)
            r2 = move(over, near_z)
    outer, mid = attend_back(keep, rs, r2, low, qo, vo, cosine, sine, saved)

    rows_each = width // tensor_size
    if split == 2:
        mids = [mid, swap_x(mid)]
    elif tensor_size == 1:
        mids = [mid]
    else:
        gathered = lax.all_gather(mid, "tensor", axis=0, tiled=False)
        mids = [gathered[i] for i in range(tensor_size)]
    scal = jnp.stack([x, me & 1]).astype(jnp.int32)
    away, current = adapter_products(scal, pol_states, mids, outer, rows_each)
    current = current + move(away, 1).astype(F32)
    top = fsdp_size // 2
    g = (me // 2) % groups
    rows = current.shape[0] // groups
    pieces = [
        lax.dynamic_slice_in_dim(current, (g ^ k) * rows, rows, 0) for k in range(groups)
    ]
    current = pieces[0]
    for k in range(1, groups):
        current = current + move(pieces[k].astype(BF16), k << 1).astype(F32)
    rows //= 2
    high = me // top
    away = lax.dynamic_slice_in_dim(current, (1 - high) * rows, rows, 0).astype(BF16)
    current = lax.dynamic_slice_in_dim(current, high * rows, rows, 0)
    current = (current + move(away, top).astype(F32)).astype(BF16)

    def join(bit, own, other):
        return jnp.where(
            bit == 0, jnp.concatenate([own, other], 0), jnp.concatenate([other, own], 0)
        )

    current = join(high, current, move(current, top))
    pieces = [current] + [move(current, k << 1) for k in range(1, groups)]
    step = 1
    while step < groups:
        odd = (g & step) != 0
        pieces = [jnp.where(odd, pieces[k ^ step], pieces[k]) for k in range(groups)]
        step *= 2
    current = jnp.concatenate(pieces, 0)
    grads = assemble(
        (me & 1).reshape(1), current, move(current, 1), rows_each, qo.shape[1], vo.shape[1]
    )
    return (loss[0, 0], grads[0].T, grads[1], grads[2].T, grads[3])


def solution(mesh):
    in_specs = (
        P("fsdp", None),
        P("fsdp", None),
        P("fsdp", None),
        P(),
        P("fsdp", "tensor"),
        P("fsdp", "tensor"),
        P("fsdp", "tensor"),
        P("tensor", "fsdp"),
        P(),
        P(None, "tensor"),
        P(),
        P(None, "tensor"),
        P("fsdp"),
        P(),
    )
    out_specs = (P(), P("tensor", None), P(None, "tensor"), P("tensor", None), P(None, "tensor"))
    body = functools.partial(per_device, mesh.shape["fsdp"], mesh.shape["tensor"])
    return jax.shard_map(body, mesh=mesh, in_specs=in_specs, out_specs=out_specs, check_vma=False)
```

```python
import functools

import jax
import jax.numpy as jnp
from jax import lax
from jax.experimental import pallas as pl
from jax.experimental.pallas import tpu as pltpu
from jax.sharding import PartitionSpec as P

QUERY_HEADS = 32
KEY_VALUE_HEADS = 8
HEAD_SIZE = 128
L = 128
GROUP = QUERY_HEADS // KEY_VALUE_HEADS
QCOLS = GROUP * HEAD_SIZE

adapter_scale = 0.5
dpo_beta = 0.1
loss_scale = 256.0
rope_base = 500000.0
norm_eps = 1e-05

F32 = jnp.float32
BF16 = jnp.bfloat16
ORD = (0, 2, 1, 3)
MB = 1 << 20
SMALL = pl.CostEstimate(flops=1, bytes_accessed=1, transcendentals=0)


def rope_tables(length, head_dim):
    half_dim = head_dim // 2
    exponent = jnp.arange(half_dim, dtype=F32) * (2.0 / head_dim)
    inverse = jnp.power(F32(rope_base), -exponent)
    angles = jnp.arange(length, dtype=F32)[:, None] * inverse[None, :]
    cosine = jnp.concatenate([jnp.cos(angles), jnp.cos(angles)], 1)
    sine = jnp.concatenate([-jnp.sin(angles), jnp.sin(angles)], 1)
    return cosine, sine


def dot(a, b, dims=((1,), (0,))):
    return lax.dot_general(a, b, (dims, ((), ())), preferred_element_type=F32)


def params(limit_mb):
    return pltpu.CompilerParams(vmem_limit_bytes=limit_mb * MB)


def smem():
    return pl.BlockSpec(memory_space=pltpu.SMEM)


def full(a):
    return pl.BlockSpec(a.shape, lambda i: (0,) * len(a.shape))


def prep_body(parts, part, split, idx, ref, pol, tgt, gain, *outs):
    x0, x1, x2, x3, t0, t1, t2, t3, go = outs[-9:]
    groups = parts // split
    for d, (xo, to) in enumerate(((x0, t0), (x1, t1), (x2, t2), (x3, t3))):
        for j in range(parts):
            src = pl.ds(pl.multiple_of(idx[d * parts + j] * part, part), part)
            cols = slice(j * part, (j + 1) * part)
            if xo.shape[0] == 2:
                xo[0, :, cols] = ref[:, src]
                xo[1, :, cols] = pol[:, src]
            else:
                @pl.when(idx[4 * parts + 4 * groups] == 0)
                def _():
                    xo[0, :, cols] = ref[:, src]

                @pl.when(idx[4 * parts + 4 * groups] != 0)
                def _():
                    xo[0, :, cols] = pol[:, src]

        for j in range(groups):
            at = idx[4 * parts + d * groups + j] * part
            src = pl.ds(pl.multiple_of(at, part), part)
            to[:, j * part : (j + 1) * part] = tgt[:, src]
            if d == 0:
                go[:, j * part : (j + 1) * part] = gain[:, src]


def prep(idx, ref, pol, tgt, gain, parts, part, split):
    tokens = ref.shape[0]
    xs = lambda n: jax.ShapeDtypeStruct((n, tokens, parts * part), BF16)
    far = 1 if split == 2 else 2
    width = parts // split * part
    tile = 32
    shapes = [xs(2), xs(2), xs(far), xs(far)]
    shapes += [jax.ShapeDtypeStruct((tokens, width), BF16)] * 4
    shapes += [jax.ShapeDtypeStruct((1, width), F32)]
    return pl.pallas_call(
        functools.partial(prep_body, parts, part, split),
        grid=(tokens // tile,),
        in_specs=[smem()]
        + [pl.BlockSpec((tile, a.shape[1]), lambda i: (i, 0)) for a in (ref, pol, tgt)]
        + [full(gain)],
        out_specs=[
            pl.BlockSpec((a.shape[0], tile, a.shape[2]), lambda i: (0, i, 0)) for a in shapes[:4]
        ]
        + [pl.BlockSpec((tile, width), lambda i: (i, 0))] * 4
        + [full(shapes[8])],
        out_shape=shapes,
        compiler_params=params(60),
        cost_estimate=SMALL,
    )(idx, ref, pol, tgt, gain)


def tile_of(cols):
    for tile in (256, 128):
        if cols % tile == 0:
            return tile
    return cols


def mm_body(count, x_ref, *refs):
    ws, outs = refs[:count], refs[-2:]
    total = None
    at = 0
    for w in ws:
        depth = w.shape[0]
        term = dot(x_ref[:, at : at + depth], w[...])
        total = term if total is None else total + term
        at += depth
    rows = total.shape[0] // 2
    for i, out_ref in enumerate(outs):
        out_ref[...] = total[i * rows : (i + 1) * rows].astype(out_ref.dtype)


def mm(x, half, ws, out_dtype, marks=()):
    rows, depth = x.shape[0] // 2, x.shape[1]
    cols = ws[0].shape[1]
    tile = tile_of(cols)
    return pl.pallas_call(
        functools.partial(mm_body, len(ws)),
        grid=(cols // tile,),
        in_specs=[pl.BlockSpec((rows, depth), lambda i: (half, 0))]
        + [pl.BlockSpec((w.shape[0], tile), lambda i: (0, i)) for w in ws]
        + [full(a) for a in marks],
        out_specs=[pl.BlockSpec((rows // 2, tile), lambda i: (0, i))] * 2,
        out_shape=[jax.ShapeDtypeStruct((rows // 2, cols), out_dtype)] * 2,
        compiler_params=params(32),
        cost_estimate=pl.CostEstimate(
            flops=2 * rows * depth * cols,
            bytes_accessed=2 * (rows * (depth + cols) + depth * cols),
            transcendentals=0,
        ),
    )(x, *ws, *marks)


def out_body(n, row_parts, counts, *refs):
    ws = refs[row_parts * n :][: sum(counts)]
    out_ref, total = refs[-2:]
    for j in range(n):
        x = jnp.concatenate([refs[p * n + j][...] for p in range(row_parts)], 0)
        depth = x.shape[1]
        at = 0
        for k, count in enumerate(counts):
            row = j * depth
            piece = at
            while row >= ws[piece].shape[0]:
                row -= ws[piece].shape[0]
                piece += 1
            at += count
            term = dot(x, ws[piece][row : row + depth])
            if j:
                term = term + total[k]
            if j == n - 1:
                out_ref[k] = term.astype(BF16)
            else:
                total[k] = term


def out_mm(parts, ws, marks=()):
    n = len(parts[0])
    rows = sum(part[0].shape[0] for part in parts)
    cols = ws[0][0].shape[1]
    flat = [piece for w in ws for piece in w]
    inputs = [a for part in parts for a in part] + flat + list(marks)
    out_shape = jax.ShapeDtypeStruct((len(ws), rows, cols), BF16)
    return pl.pallas_call(
        functools.partial(out_body, n, len(parts), tuple(len(w) for w in ws)),
        grid=(1,),
        in_specs=[full(a) for a in inputs],
        out_specs=full(out_shape),
        out_shape=out_shape,
        scratch_shapes=[pltpu.VMEM(out_shape.shape, F32)],
        compiler_params=params(32),
        cost_estimate=SMALL,
    )(*inputs)


def back_body(counts, part, has_acc, x_ref, *refs):
    total = None
    at = 0
    for j, count in enumerate(counts):
        w = refs[at][...]
        if count == 2:
            w = jnp.where(pl.program_id(0) < pl.num_programs(0) // 2, w, refs[at + 1][...])
        at += count
        term = dot(x_ref[:, j * part : (j + 1) * part], w, ((1,), (1,)))
        total = term if total is None else total + term
    refs = refs[at:]
    if has_acc:
        total = total + refs[0][...]
        keep, send = refs[1:]
        half = total.shape[0] // 2
        keep[...] = total[:half]
        send[...] = total[half:].astype(send.dtype)
    else:
        refs[0][...] = total


def back_mm(x, half, ws, acc):
    rows = x.shape[0] // (1 if half is None else 2)
    depth = x.shape[1]
    part = ws[0][0].shape[1]
    heads = sum(piece.shape[0] for piece in ws[0])
    tile = min(512, heads)
    steps = heads // tile
    has_acc = acc is not None
    row = half or 0
    in_specs = [pl.BlockSpec((rows, depth), lambda i: (row, 0))]
    for w in ws:
        if len(w) == 1:
            in_specs.append(pl.BlockSpec((tile, part), lambda i: (i, 0)))
        else:
            in_specs.append(pl.BlockSpec((tile, part), lambda i: (jnp.minimum(i, steps // 2 - 1), 0)))
            in_specs.append(pl.BlockSpec((tile, part), lambda i: (jnp.maximum(i - steps // 2, 0), 0)))
    args = [x] + [piece for w in ws for piece in w]
    if has_acc:
        in_specs.append(pl.BlockSpec((rows, tile), lambda i: (0, i)))
        args.append(acc)
        out_specs = [pl.BlockSpec((rows // 2, tile), lambda i: (0, i))] * 2
        out_shape = [
            jax.ShapeDtypeStruct((rows // 2, heads), F32),
            jax.ShapeDtypeStruct((rows // 2, heads), BF16),
        ]
    else:
        out_specs = pl.BlockSpec((rows, tile), lambda i: (0, i))
        out_shape = jax.ShapeDtypeStruct((rows, heads), F32)
    return pl.pallas_call(
        functools.partial(back_body, tuple(len(w) for w in ws), part, has_acc),
        grid=(steps,),
        in_specs=in_specs,
        out_specs=out_specs,
        out_shape=out_shape,
        compiler_params=params(32),
        cost_estimate=SMALL,
    )(*args)


def causal(rows):
    at = lax.broadcasted_iota(jnp.int32, (rows, L), 0) % L
    return at >= lax.broadcasted_iota(jnp.int32, (rows, L), 1)


def probabilities(q4, keys):
    scores = dot(q4, keys, ((1,), (1,))) * (HEAD_SIZE**-0.5)
    weights = jnp.where(causal(q4.shape[0]), jnp.exp(scores), 0.0)
    return weights / jnp.sum(weights, -1, keepdims=True)


def stack_heads(values):
    return jnp.concatenate(
        [values[:, h * HEAD_SIZE : (h + 1) * HEAD_SIZE] for h in range(GROUP)], 0
    )


def attend_body(adapted, keep, rs, r2, low, qo, vo, cos_ref, sin_ref, *refs):
    mixed, *saved = refs[-1 - adapted :]
    cosine = cos_ref[...]
    sine = sin_ref[...]
    pre = keep[...] + rs[...].astype(F32) + r2[...].astype(F32)
    rank = qo.shape[0]
    q_pre = pre[:, :QCOLS]
    k_pre = pre[:, QCOLS : QCOLS + HEAD_SIZE]
    v_pre = pre[:, QCOLS + HEAD_SIZE :]
    if adapted:
        q_pre = q_pre + adapter_scale * dot(low[:, :rank], qo[...])
        v_pre = v_pre + adapter_scale * dot(low[:, rank:], vo[...])
    cos4 = jnp.concatenate([cosine] * GROUP, 0)
    sin4 = jnp.concatenate([sine] * GROUP, 0)
    q4 = stack_heads(q_pre)
    q4 = (q4 * cos4 + pltpu.roll(q4, HEAD_SIZE // 2, 1) * sin4).astype(BF16)
    keys = (k_pre * cosine + pltpu.roll(k_pre, HEAD_SIZE // 2, 1) * sine).astype(BF16)
    values = v_pre.astype(BF16)
    rounded = probabilities(q4, keys).astype(BF16)
    out = dot(rounded, values).astype(BF16)
    for h in range(GROUP):
        cols = slice(h * HEAD_SIZE, (h + 1) * HEAD_SIZE)
        mixed[:, cols] = out[h * L : (h + 1) * L]
        if saved:
            saved[0][:, cols] = q4[h * L : (h + 1) * L]
    if saved:
        saved[0][:, QCOLS : QCOLS + HEAD_SIZE] = keys
        saved[0][:, QCOLS + HEAD_SIZE :] = values


def attend(adapted, keep, rs, r2, low, qo, vo, group, cosine, sine, marks=()):
    each = QCOLS + 2 * HEAD_SIZE
    rank = qo.shape[0]
    top = lambda a: pl.BlockSpec((L, a.shape[1]), lambda i: (0, 0))
    return pl.pallas_call(
        functools.partial(attend_body, adapted),
        grid=(1,),
        in_specs=[
            top(keep),
            top(rs),
            top(r2),
            top(low),
            pl.BlockSpec((rank, QCOLS), lambda i: (0, group)),
            pl.BlockSpec((rank, HEAD_SIZE), lambda i: (0, group)),
            top(cosine),
            top(sine),
        ]
        + [full(a) for a in marks],
        out_specs=[pl.BlockSpec((L, w), lambda i: (0, 0)) for w in (QCOLS, each)[: 1 + adapted]],
        out_shape=[jax.ShapeDtypeStruct((L, w), BF16) for w in (QCOLS, each)[: 1 + adapted]],
        compiler_params=params(32),
        cost_estimate=SMALL,
    )(keep, rs, r2, low, qo, vo, cosine, sine, *marks)


def outer_place(block, rank, kv):
    wide = (kv * (GROUP + 1) + 1) // 2
    return (block // wide) * rank, (block % wide) * HEAD_SIZE, wide


def attend_back_body(kv, splits, keep, rs, r2, low, qo, vo, cos_ref, sin_ref, *refs):
    saved = refs[:splits]
    outer, mid = refs[splits:]
    rank = qo.shape[0]
    each = QCOLS + 2 * HEAD_SIZE
    cos4 = jnp.concatenate([cos_ref[...]] * GROUP, 0)
    sin4 = jnp.concatenate([sin_ref[...]] * GROUP, 0)
    low_q = low[:, :rank]
    low_v = low[:, rank:]
    q_mid = jnp.zeros((L, rank), F32)
    v_mid = jnp.zeros((L, rank), F32)

    def put(block, value):
        row, col, _ = outer_place(block, rank, kv)
        outer[row : row + rank, col : col + HEAD_SIZE] = adapter_scale * value

    if (kv * (GROUP + 1)) % 2:
        put(kv * (GROUP + 1), jnp.zeros((rank, HEAD_SIZE), F32))
    for j in range(kv):
        cols = slice(j * QCOLS, (j + 1) * QCOLS)
        at = (j % (kv // splits)) * each
        kept = saved[j // (kv // splits)]
        grad = keep[:, cols] + rs[:, cols].astype(F32) + r2[:, cols].astype(F32)
        grad4 = stack_heads(grad.astype(BF16))
        q4 = stack_heads(kept[:, at : at + QCOLS])
        keys = kept[:, at + QCOLS : at + QCOLS + HEAD_SIZE]
        values = kept[:, at + QCOLS + HEAD_SIZE : at + each]
        prob = probabilities(q4, keys)
        grad_prob = dot(grad4, values, ((1,), (1,)))
        grad_values = dot(prob.astype(BF16), grad4, ((0,), (0,))).astype(BF16)
        inner = jnp.sum(grad_prob * prob, -1, keepdims=True)
        grad_scores = (prob * (grad_prob - inner) * (HEAD_SIZE**-0.5)).astype(BF16)
        grad_query = dot(grad_scores, keys)
        back4 = (grad_query * cos4 - pltpu.roll(grad_query, HEAD_SIZE // 2, 1) * sin4).astype(BF16)
        for h in range(GROUP):
            at = j * GROUP + h
            back = back4[h * L : (h + 1) * L]
            put(at, dot(low_q, back, ((0,), (0,))))
            q_mid += dot(back, qo[:, at * HEAD_SIZE : (at + 1) * HEAD_SIZE], ((1,), (1,)))
        put(kv * GROUP + j, dot(low_v, grad_values, ((0,), (0,))))
        v_mid += dot(grad_values, vo[:, j * HEAD_SIZE : (j + 1) * HEAD_SIZE], ((1,), (1,)))
    mid[:, :rank] = (adapter_scale * q_mid).astype(BF16)
    mid[:, rank:] = (adapter_scale * v_mid).astype(BF16)


def attend_back(keep, rs, r2, low, qo, vo, cosine, sine, saved):
    rank = qo.shape[0]
    kv = vo.shape[1] // HEAD_SIZE
    wide = outer_place(0, rank, kv)[2]
    inputs = (keep, rs, r2, low, qo, vo, cosine, sine, *saved)
    shapes = [
        jax.ShapeDtypeStruct((2 * rank, wide * HEAD_SIZE), F32),
        jax.ShapeDtypeStruct((L, 2 * rank), BF16),
    ]
    return pl.pallas_call(
        functools.partial(attend_back_body, kv, len(saved)),
        grid=(1,),
        in_specs=[full(a) for a in inputs],
        out_specs=[full(a) for a in shapes],
        out_shape=shapes,
        compiler_params=params(60),
        cost_estimate=SMALL,
    )(*inputs)


def adapter_body(n, rows_each, scal, states, outer, *refs):
    mids = refs[:n]
    away, stay = refs[n:]
    src = pl.ds(pl.multiple_of(scal[0] * rows_each, rows_each), rows_each)
    own = states[:, src]
    total = None
    for mid in mids:
        term = dot(mid[...], own, ((0,), (0,)))
        total = term if total is None else total + term
    half = total.shape[0] // 2
    for low in range(2):
        rows = slice(low * half, (low + 1) * half)

        @pl.when(scal[1] == low)
        def _():
            stay[:, :rows_each] = total[rows]
            stay[:, rows_each:] = outer[rows]

        @pl.when(scal[1] != low)
        def _():
            away[:, :rows_each] = total[rows].astype(BF16)
            away[:, rows_each:] = outer[rows].astype(BF16)


def adapter_products(scal, states, mids, outer, rows_each):
    half = outer.shape[0] // 2
    cols = rows_each + outer.shape[1]
    shapes = [jax.ShapeDtypeStruct((half, cols), BF16), jax.ShapeDtypeStruct((half, cols), F32)]
    return pl.pallas_call(
        functools.partial(adapter_body, len(mids), rows_each),
        grid=(1,),
        in_specs=[smem()] + [full(a) for a in (states, outer, *mids)],
        out_specs=[full(a) for a in shapes],
        out_shape=shapes,
        compiler_params=params(32),
        cost_estimate=SMALL,
    )(scal, states, outer, *mids)


def assemble_body(rows_each, bit, own, other, q_inner, q_outer, v_inner, v_outer):
    low = jnp.where(bit[0] == 0, own[...], other[...]).astype(F32)
    high = jnp.where(bit[0] == 0, other[...], own[...]).astype(F32)
    q_inner[...] = low[:, :rows_each]
    v_inner[...] = high[:, :rows_each]
    outer = jnp.concatenate([low[:, rows_each:], high[:, rows_each:]], 1)
    cols = q_outer.shape[1]
    q_outer[...] = outer[:, :cols]
    v_outer[...] = outer[:, cols : cols + v_outer.shape[1]]


def assemble(bit, own, other, rows_each, q_cols, v_cols):
    rank = own.shape[0]
    shapes = [jax.ShapeDtypeStruct((rank, c), F32) for c in (rows_each, q_cols, rows_each, v_cols)]
    return pl.pallas_call(
        functools.partial(assemble_body, rows_each),
        grid=(1,),
        in_specs=[smem(), full(own), full(other)],
        out_specs=[full(a) for a in shapes],
        out_shape=shapes,
        compiler_params=params(32),
        cost_estimate=SMALL,
    )(bit, own, other)


def stats_body(counts, part, split, scal, xt_ref, xt_pol, tgt, gain, *refs):
    refs = list(refs)
    sums = []
    hidden_out, stats = refs[-2:]
    for which in range(2):
        xt = (xt_ref, xt_pol)[which]
        count = sum(counts)
        keeps = [r[i] for r in refs[: counts[0]] for i in range(r.shape[0])]
        recvs = [r[i] for r in refs[counts[0] : count] for i in range(r.shape[0])]
        refs = refs[count:]
        squares = jnp.zeros((L, HEAD_SIZE), F32)
        products = jnp.zeros((L, HEAD_SIZE), F32)
        for j, (keep, recv) in enumerate(zip(keeps, recvs)):
            src = pl.ds(pl.multiple_of((j * split + scal[0]) * part, part), part)
            hidden = xt[:, src].astype(F32) + keep.astype(F32) + recv.astype(F32)
            cols = slice(j * part, (j + 1) * part)
            if which == 1:
                hidden_out[0, :, cols] = hidden
            product = hidden * (gain[:, cols] * tgt[0, :, cols].astype(F32))
            square = hidden * hidden
            for s in range(part // HEAD_SIZE):
                lanes = slice(s * HEAD_SIZE, (s + 1) * HEAD_SIZE)
                squares += square[:, lanes]
                products += product[:, lanes]
        sums.append(
            [
                jnp.broadcast_to(jnp.sum(v, 1, keepdims=True), v.shape).T[:1]
                for v in (squares, products)
            ]
        )
    at = lax.broadcasted_iota(jnp.int32, (1, 2 * L), 1) % L
    own = (at >= scal[1]) & (pl.program_id(0) == 0)
    live = jnp.where(own, 1.0, 0.0).astype(F32)
    both = [jnp.concatenate([sums[0][i], sums[1][i]], 1) for i in range(2)]
    stats[...] = jnp.concatenate([*both, live, jnp.zeros((5, 2 * L), F32)], 0)


def norm_stats(scal, xt, tgt, gain, keeps, recvs, split):
    n = sum(a.shape[0] for a in keeps)
    part = keeps[0].shape[2]
    shared = []
    for which in range(2):
        at = functools.partial(lambda which, i: (0, 2 * i + which, 0), which)
        for a in (*keeps, *recvs):
            shared.append((a, pl.BlockSpec((a.shape[0], L, part), at)))
    return pl.pallas_call(
        functools.partial(stats_body, (len(keeps), len(recvs)), part, split),
        grid=(4,),
        in_specs=[
            smem(),
            pl.BlockSpec((L, xt.shape[1]), lambda i: ((i // 2) * 4 + i % 2, 0)),
            pl.BlockSpec((L, xt.shape[1]), lambda i: ((i // 2) * 4 + 2 + i % 2, 0)),
            pl.BlockSpec((1, L, n * part), lambda i: (i // 2 + i % 2 * 2, 0, 0)),
            pl.BlockSpec((1, n * part), lambda i: (0, 0)),
        ]
        + [spec for _, spec in shared],
        out_specs=[
            pl.BlockSpec((1, L, n * part), lambda i: (i, 0, 0)),
            pl.BlockSpec((8, 2 * L), lambda i: (i, 0)),
        ],
        out_shape=[
            jax.ShapeDtypeStruct((4, L, n * part), F32),
            jax.ShapeDtypeStruct((32, 2 * L), F32),
        ],
        compiler_params=params(32),
        cost_estimate=SMALL,
    )(scal, xt, xt, tgt, gain, *[a for a, _ in shared])


def score_body(width, masks, ids, own, *refs):
    recvs = refs[: len(masks)]
    total_out, margin_out = refs[len(masks) :]
    lane = lax.broadcasted_iota(jnp.int32, (8, 128), 1)
    margins = jnp.zeros((8, 128), F32)
    for p in range(4):
        total = own[8 * p : 8 * p + 8]
        for recv, m in zip(recvs, masks):
            q = ORD.index(ORD[p] ^ m)
            total = total + recv[8 * q : 8 * q + 8]
        total_out[8 * p : 8 * p + 8] = total
        inverse = lax.rsqrt(total[0:1] * (1.0 / width) + norm_eps)
        score = total[1:2] * inverse * (width**-0.5)
        score = jnp.where(total[2:3] > 0.5, score, 0.0)
        margin = jnp.sum(score[:, L:], 1, keepdims=True) - jnp.sum(score[:, :L], 1, keepdims=True)
        margins = margins + jnp.where(lane == ids[p], margin, 0.0)
    margin_out[...] = margins


def scores(ids, own, recvs, masks, width):
    shapes = [jax.ShapeDtypeStruct(own.shape, F32), jax.ShapeDtypeStruct((8, 128), F32)]
    return pl.pallas_call(
        functools.partial(score_body, width, masks),
        grid=(1,),
        in_specs=[smem()] + [full(a) for a in (own, *recvs)],
        out_specs=[full(a) for a in shapes],
        out_shape=shapes,
        cost_estimate=SMALL,
    )(ids, own, *recvs)


def turn(i):
    return (2 * i + 1) % 5


def grad_body(width, seqs, n_vec, ids, pairs, total, hidden, tgt, gain, *refs):
    vecs = refs[:n_vec]
    grad_out, loss_out, slope = refs[n_vec:]
    lane = lax.broadcasted_iota(jnp.int32, (8, 128), 1)

    @pl.when(pl.program_id(0) == 0)
    def _():
        margin = vecs[0][...]
        for v in vecs[1:]:
            margin = margin + v[...]
        logits = jnp.zeros((8, 128), F32)
        for i in range(seqs // 2):
            sign = jnp.where(lane == pairs[2 * i], 1.0, 0.0) - jnp.where(
                lane == pairs[2 * i + 1], 1.0, 0.0
            )
            logit = dpo_beta * jnp.sum(margin * sign, 1, keepdims=True)
            logits = logits + jnp.where(lane == i, logit, 0.0)
        soft = jnp.maximum(-logits, 0.0) + jnp.log1p(jnp.exp(-jnp.abs(logits)))
        used = lane < seqs // 2
        loss = jnp.sum(jnp.where(used, soft, 0.0), 1, keepdims=True)
        loss_out[...] = jnp.broadcast_to(loss, (8, 128))
        slopes = jnp.where(used, -dpo_beta / (1.0 + jnp.exp(logits)), 0.0)
        gradient = jnp.zeros((8, 128), F32)
        for i in range(seqs // 2):
            each = jnp.sum(jnp.where(lane == i, slopes, 0.0), 1, keepdims=True)
            sign = jnp.where(lane == pairs[2 * i], 1.0, 0.0) - jnp.where(
                lane == pairs[2 * i + 1], 1.0, 0.0
            )
            gradient = gradient + each * sign
        slope[...] = gradient * loss_scale

    mine = lane == ids[turn(pl.program_id(0))]
    seq = jnp.sum(jnp.where(mine, slope[...], 0.0), 1, keepdims=True)[:1]
    rows = total[:, L:]
    token = jnp.where(rows[2:3] > 0.5, seq, 0.0) * (width**-0.5)
    inverse = lax.rsqrt(rows[0:1] * (1.0 / width) + norm_eps)
    first = inverse * token
    second = inverse * inverse * inverse * (token * rows[1:2] * (1.0 / width))
    first = jnp.broadcast_to(first, (L, L)).T
    second = jnp.broadcast_to(second, (L, L)).T
    for s in range(hidden.shape[2] // HEAD_SIZE):
        cols = slice(s * HEAD_SIZE, (s + 1) * HEAD_SIZE)
        weighted = gain[:, cols] * tgt[0, :, cols].astype(F32)
        grad_out[0, :, cols] = (first * weighted - second * hidden[0, :, cols]).astype(BF16)


def grad_hidden(ids, pairs, total, hidden, tgt, gain, vecs, width):
    n = hidden.shape[2]
    seqs = pairs.shape[0]
    return pl.pallas_call(
        functools.partial(grad_body, width, seqs, len(vecs)),
        grid=(4,),
        in_specs=[
            smem(),
            smem(),
            pl.BlockSpec((8, 2 * L), lambda i: (turn(i), 0)),
            pl.BlockSpec((1, L, n), lambda i: (turn(i), 0, 0)),
            pl.BlockSpec((1, L, n), lambda i: (turn(i) // 2 + turn(i) % 2 * 2, 0, 0)),
            pl.BlockSpec((1, n), lambda i: (0, 0)),
        ]
        + [pl.BlockSpec((8, 128), lambda i: (0, 0)) for _ in vecs],
        out_specs=[
            pl.BlockSpec((1, L, n), lambda i: (i, 0, 0)),
            pl.BlockSpec((8, 128), lambda i: (0, 0)),
        ],
        out_shape=[
            jax.ShapeDtypeStruct((4, L, n), BF16),
            jax.ShapeDtypeStruct((8, 128), F32),
        ],
        scratch_shapes=[pltpu.VMEM((8, 128), F32)],
        compiler_params=params(32),
        cost_estimate=SMALL,
    )(ids, pairs, total, hidden, tgt, gain, *vecs)


def per_device(
    fsdp_size,
    tensor_size,
    ref_states,
    pol_states,
    target_rows,
    norm_gain,
    wq,
    wk,
    wv,
    wo,
    qa,
    qo,
    va,
    vo,
    prompt_length,
    pairs,
):
    tokens, width = ref_states.shape
    groups = fsdp_size // 4
    near_z = fsdp_size // 4
    bits = []
    bit = 2
    while bit < fsdp_size:
        if bit != near_z:
            bits.append(bit)
        bit *= 2
    split = 2 if tensor_size == 2 and fsdp_size == 16 else 1
    kv_local = wk.shape[1] // HEAD_SIZE
    depth = wq.shape[0]
    part = depth // split
    rank = qa.shape[1]
    me = lax.axis_index("fsdp")
    x = lax.axis_index("tensor")
    side = x if split == 2 else 0

    def tmask(d):
        return (d & 1) | ((d >> 1) * near_z)

    def gmask(k):
        return sum(bit for i, bit in enumerate(bits) if (k >> i) & 1)

    def move(value, mask):
        return lax.ppermute(value, "fsdp", [(i, i ^ mask) for i in range(fsdp_size)])

    def swap_x(value):
        return lax.ppermute(value, "tensor", [(0, 1), (1, 0)])

    def move_both(value, mask, flip):
        pairs_list = [
            (2 * i + j, 2 * (i ^ mask) + (j ^ flip)) for i in range(fsdp_size) for j in range(2)
        ]
        return lax.ppermute(value, ("fsdp", "tensor"), pairs_list)

    def after(value, *others):
        return lax.optimization_barrier((value, *others))[0]

    def marker(*queue):
        return move(after(cosine[:16].astype(BF16), *queue), 1)

    cosine, sine = rope_tables(L, HEAD_SIZE)

    wide = groups == 4 and split == 2
    heads = wo.shape[0]

    def shard_of(j, *queue):
        q, k, v = wq, wk, wv
        if queue:
            q, k, v = lax.optimization_barrier((wq, wk, wv, *queue))[:3]
        pieces = [
            q[:, j * QCOLS : (j + 1) * QCOLS],
            k[:, j * HEAD_SIZE : (j + 1) * HEAD_SIZE],
            v[:, j * HEAD_SIZE : (j + 1) * HEAD_SIZE],
        ]
        return jnp.concatenate(pieces, 1)

    def gather(shard):
        return [shard] + [move(shard, gmask(k)) for k in range(1, groups)]

    if wide:
        over_y, over_z = gmask(1), gmask(2)
        shards = [shard_of(0)]
        zs = [move(shards[0], over_z)]
        ys = [move(shards[0], over_y)]
        corners = []

    parts = groups * split
    idx = []
    for d in range(4):
        for k in range(groups):
            for h in range(split):
                idx.append((me ^ tmask(d) ^ gmask(k)) * split + h)
    for d in range(4):
        for k in range(groups):
            idx.append((me ^ tmask(d) ^ gmask(k)) * split + side)
    idx.append(x)
    idx = jnp.stack(idx).astype(jnp.int32)
    prepared = prep(
        idx,
        ref_states,
        pol_states,
        target_rows,
        norm_gain.astype(F32).reshape(1, width),
        parts,
        part,
        split,
    )
    xs, ts, gain = prepared[:4], prepared[4:8], prepared[8]
    near = move(xs[1], 1)
    far = [move(xs[2], near_z)]
    far.append(move(xs[3], near_z | 1))

    if split == 2:
        first = (zs[0], ys[0]) if wide else ()
        other = [swap_x(after(a, *first) if first else a) for a in far]
        far = [
            [jnp.where(x == which, a[0], b[0]) for which in range(2)] for a, b in zip(far, other)
        ]
    states = jnp.concatenate(
        [
            *(xs[0][0], far[0][0], xs[0][1], far[0][1]),
            *(near[0], far[1][0], near[1], far[1][1]),
        ],
        0,
    )

    low = dot(pol_states, jnp.concatenate([qa, va], 1)).astype(BF16)
    cosine, sine = rope_tables(L, HEAD_SIZE)

    def own_columns(at, piece, *queue):
        return lax.dynamic_slice(
            after(wo, *queue), (piece * (heads // 2), at * part), (heads // 2, part)
        )

    def own_piece(step, *queue):
        at = (1 - x) if step < 2 else x
        return lax.dynamic_slice(
            after(wo, *queue), ((step % 2) * (heads // 2), at * part), (heads // 2, part)
        )

    def make_shard(j, *queue):
        if j < kv_local:
            shards.append(shard_of(j, *queue))
        elif j < kv_local + 4:
            shards.append(own_piece(j - kv_local, *queue))

    def next_shard(j, *more):
        queue = (zs[j - 1], ys[j - 1], *more)
        ys.append(move(after(shards[j], *queue), over_y))
        zs.append(move(after(shards[j], *queue), over_z))
        corners.append(move(after(*queue), over_y))

    saved = []
    parts_mixed = [[], [], []]

    def mix(j, keeps, came, sums, *queue, marks=()):
        results = []
        for which in range(2):
            total = sums[which * L : (which + 1) * L]
            result = attend(
                *(which == 1, keeps[which], came[which], total, low, qo, vo, j, cosine, sine),
                marks=marks,
            )
            saved.extend(result[1:])
            results.append(result[0])
        result = jnp.concatenate(results, 0)
        return result, move(after(result, *queue) if queue else result, near_z)

    def spread(result, other):
        far = move(jnp.concatenate([result, other], 0), 1)
        for part_mixed, value in zip(parts_mixed, (result, other, far)):
            part_mixed.append(value)
        return far

    if wide:
        make_shard(1, shards[0])
        next_shard(1)
        make_shard(2, zs[0])
    before = None
    ends = []
    marks = ()
    for j in range(kv_local):
        if wide:
            marks = (marker(zs[j + 1], ys[j + 1]),)
            ws = [shards[j], ys[j], zs[j], corners[j]]
        else:
            ws = gather(shard_of(j))
        sends = mm(states, 1, ws, BF16, marks)
        came = [move(send, 1) for send in sends]
        keeps = mm(states, 0, ws, F32)
        if wide:
            next_shard(j + 2)
            make_shard(j + 3, zs[j + 1])
        over = jnp.concatenate(
            [(keeps[which][L:] + came[which][L:].astype(F32)).astype(BF16) for which in range(2)], 0
        )
        if before is not None:
            result, other = mix(j - 1, *before, *came, *ends)
            if j + 2 < kv_local:
                over = after(over, other)
            states = after(states, other)
            ends = [spread(result, other)]
        if wide:
            over = after(over, shards[-1])
        sums = move(over, near_z)
        if wide and j + 1 == kv_local:
            marks = (marker(zs[j + 2], ys[j + 2]),)
            make_shard(kv_local + 3, zs[-2])
        before = (keeps, came, sums)
    last = spread(*mix(kv_local - 1, *before, *ends, marks=marks))

    keeps, recvs = [], []
    if wide:
        next_shard(kv_local + 2, over)
        first = [a[kv_local : kv_local + 2] for a in (shards, ys, zs, corners)]
        marks = (marker(zs[-1], ys[-1]),)
        recvs.append(swap_x(out_mm(parts_mixed, first[:2], marks)))
        next_shard(kv_local + 3)
        recvs.append(swap_x(out_mm(parts_mixed, first[2:])))
        corners.append(move(after(zs[-1], ys[-1]), over_y))
        wo_send, wo_keep = first, [a[kv_local + 2 :] for a in (shards, ys, zs, corners)]
        keeps.append(out_mm(parts_mixed, wo_keep[:3]))
        keeps.append(out_mm(parts_mixed, wo_keep[3:]))
    else:
        wo_keep = [[w] for w in gather(wo)]
        product = out_mm(parts_mixed, wo_keep)
        if tensor_size > 1:
            product = lax.psum(product, "tensor")
        keeps.append(product)
        recvs.append(jnp.zeros_like(product))

    targets = [ts[0]] + [move(after(ts[d], last), tmask(d)) for d in (1, 2, 3)]
    tgt = jnp.stack(targets)
    scal = jnp.stack([jnp.asarray(side, jnp.int32), prompt_length[0].astype(jnp.int32)])
    hidden, stats = norm_stats(scal, states, tgt, gain, keeps, recvs, split)
    masks, got = [], []
    for flip in reversed(range(split)):
        for d in (3, 2, 1, 0):
            if d or flip:
                masks.append(d)
                if split == 2:
                    got.append(move_both(stats, tmask(d), flip))
                else:
                    got.append(move(stats, tmask(d)))
    ids = jnp.stack([me ^ tmask(d) for d in ORD]).astype(jnp.int32)
    total, margin = scores(ids, stats, got, tuple(masks), width)
    vecs = [margin] + [move(margin, gmask(k)) for k in reversed(range(1, groups))]
    grad, loss = grad_hidden(ids, pairs, total, hidden, tgt, gain, vecs, width)

    grad_rows = grad.reshape(4 * L, -1)
    other = None
    for half in range(2):
        if split == 2:
            leaving = grad_rows[2 * L * half : 2 * L * (half + 1)]
            other = swap_x(leaving if half == 0 else after(leaving, other))
            acc = back_mm(grad_rows, half, wo_keep, None)
            keep, send = back_mm(other, None, wo_send, acc)
        else:
            acc = jnp.zeros((2 * L, heads), F32)
            keep, send = back_mm(grad_rows, half, wo_keep, acc)
        rs = move(send if half == 0 else after(send, r2), 1)
        if half == 0:
            over = (keep + rs.astype(F32)).astype(BF16)
            r2 = move(over, near_z)
    outer, mid = attend_back(keep, rs, r2, low, qo, vo, cosine, sine, saved)

    rows_each = width // tensor_size
    if split == 2:
        mids = [mid, swap_x(mid)]
    elif tensor_size == 1:
        mids = [mid]
    else:
        gathered = lax.all_gather(mid, "tensor", axis=0, tiled=False)
        mids = [gathered[i] for i in range(tensor_size)]
    scal = jnp.stack([x, me & 1]).astype(jnp.int32)
    away, current = adapter_products(scal, pol_states, mids, outer, rows_each)
    current = current + move(away, 1).astype(F32)
    top = fsdp_size // 2
    g = (me // 2) % groups
    rows = current.shape[0] // groups
    pieces = [
        lax.dynamic_slice_in_dim(current, (g ^ k) * rows, rows, 0) for k in range(groups)
    ]
    current = pieces[0]
    for k in range(1, groups):
        current = current + move(pieces[k].astype(BF16), k << 1).astype(F32)
    rows //= 2
    high = me // top
    away = lax.dynamic_slice_in_dim(current, (1 - high) * rows, rows, 0).astype(BF16)
    current = lax.dynamic_slice_in_dim(current, high * rows, rows, 0)
    current = (current + move(away, top).astype(F32)).astype(BF16)

    def join(bit, own, other):
        return jnp.where(
            bit == 0, jnp.concatenate([own, other], 0), jnp.concatenate([other, own], 0)
        )

    current = join(high, current, move(current, top))
    pieces = [current] + [move(current, k << 1) for k in range(1, groups)]
    step = 1
    while step < groups:
        odd = (g & step) != 0
        pieces = [jnp.where(odd, pieces[k ^ step], pieces[k]) for k in range(groups)]
        step *= 2
    current = jnp.concatenate(pieces, 0)
    grads = assemble(
        (me & 1).reshape(1), current, move(current, 1), rows_each, qo.shape[1], vo.shape[1]
    )
    return (loss[0, 0], grads[0].T, grads[1], grads[2].T, grads[3])


def solution(mesh):
    in_specs = (
        P("fsdp", None),
        P("fsdp", None),
        P("fsdp", None),
        P(),
        P("fsdp", "tensor"),
        P("fsdp", "tensor"),
        P("fsdp", "tensor"),
        P("tensor", "fsdp"),
        P(),
        P(None, "tensor"),
        P(),
        P(None, "tensor"),
        P("fsdp"),
        P(),
    )
    out_specs = (P(), P("tensor", None), P(None, "tensor"), P("tensor", None), P(None, "tensor"))
    body = functools.partial(per_device, mesh.shape["fsdp"], mesh.shape["tensor"])
    return jax.shard_map(body, mesh=mesh, in_specs=in_specs, out_specs=out_specs, check_vma=False)
```

```python
import functools

import jax
import jax.numpy as jnp
from jax import lax
from jax.experimental import pallas as pl
from jax.experimental.pallas import tpu as pltpu
from jax.sharding import PartitionSpec as P

QUERY_HEADS = 32
KEY_VALUE_HEADS = 8
HEAD_SIZE = 128
L = 128
GROUP = QUERY_HEADS // KEY_VALUE_HEADS
QCOLS = GROUP * HEAD_SIZE

adapter_scale = 0.5
dpo_beta = 0.1
loss_scale = 256.0
rope_base = 500000.0
norm_eps = 1e-05

F32 = jnp.float32
BF16 = jnp.bfloat16
ORD = (0, 2, 1, 3)
MB = 1 << 20
SMALL = pl.CostEstimate(flops=1, bytes_accessed=1, transcendentals=0)


def rope_tables(length, head_dim):
    half_dim = head_dim // 2
    exponent = jnp.arange(half_dim, dtype=F32) * (2.0 / head_dim)
    inverse = jnp.power(F32(rope_base), -exponent)
    angles = jnp.arange(length, dtype=F32)[:, None] * inverse[None, :]
    cosine = jnp.concatenate([jnp.cos(angles), jnp.cos(angles)], 1)
    sine = jnp.concatenate([-jnp.sin(angles), jnp.sin(angles)], 1)
    return cosine, sine


def dot(a, b, dims=((1,), (0,))):
    return lax.dot_general(a, b, (dims, ((), ())), preferred_element_type=F32)


def params(limit_mb):
    return pltpu.CompilerParams(vmem_limit_bytes=limit_mb * MB)


def smem():
    return pl.BlockSpec(memory_space=pltpu.SMEM)


def full(a):
    return pl.BlockSpec(a.shape, lambda i: (0,) * len(a.shape))


def prep_body(parts, part, split, idx, ref, pol, tgt, gain, *outs):
    x0, x1, x2, x3, t0, t1, t2, t3, go = outs[-9:]
    groups = parts // split
    for d, (xo, to) in enumerate(((x0, t0), (x1, t1), (x2, t2), (x3, t3))):
        for j in range(parts):
            src = pl.ds(pl.multiple_of(idx[d * parts + j] * part, part), part)
            cols = slice(j * part, (j + 1) * part)
            if xo.shape[0] == 2:
                xo[0, :, cols] = ref[:, src]
                xo[1, :, cols] = pol[:, src]
            else:
                @pl.when(idx[4 * parts + 4 * groups] == 0)
                def _():
                    xo[0, :, cols] = ref[:, src]

                @pl.when(idx[4 * parts + 4 * groups] != 0)
                def _():
                    xo[0, :, cols] = pol[:, src]

        for j in range(groups):
            at = idx[4 * parts + d * groups + j] * part
            src = pl.ds(pl.multiple_of(at, part), part)
            to[:, j * part : (j + 1) * part] = tgt[:, src]
            if d == 0:
                go[:, j * part : (j + 1) * part] = gain[:, src]


def prep(idx, ref, pol, tgt, gain, parts, part, split):
    tokens = ref.shape[0]
    xs = lambda n: jax.ShapeDtypeStruct((n, tokens, parts * part), BF16)
    far = 1 if split == 2 else 2
    width = parts // split * part
    tile = 32
    shapes = [xs(2), xs(2), xs(far), xs(far)]
    shapes += [jax.ShapeDtypeStruct((tokens, width), BF16)] * 4
    shapes += [jax.ShapeDtypeStruct((1, width), F32)]
    return pl.pallas_call(
        functools.partial(prep_body, parts, part, split),
        grid=(tokens // tile,),
        in_specs=[smem()]
        + [pl.BlockSpec((tile, a.shape[1]), lambda i: (i, 0)) for a in (ref, pol, tgt)]
        + [full(gain)],
        out_specs=[
            pl.BlockSpec((a.shape[0], tile, a.shape[2]), lambda i: (0, i, 0)) for a in shapes[:4]
        ]
        + [pl.BlockSpec((tile, width), lambda i: (i, 0))] * 4
        + [full(shapes[8])],
        out_shape=shapes,
        compiler_params=params(60),
        cost_estimate=SMALL,
    )(idx, ref, pol, tgt, gain)


def tile_of(cols):
    for tile in (256, 128):
        if cols % tile == 0:
            return tile
    return cols


def mm_body(count, x_ref, *refs):
    ws, outs = refs[:count], refs[-2:]
    total = None
    at = 0
    for w in ws:
        depth = w.shape[0]
        term = dot(x_ref[:, at : at + depth], w[...])
        total = term if total is None else total + term
        at += depth
    rows = total.shape[0] // 2
    for i, out_ref in enumerate(outs):
        out_ref[...] = total[i * rows : (i + 1) * rows].astype(out_ref.dtype)


def mm(x, half, ws, out_dtype, marks=()):
    rows, depth = x.shape[0] // 2, x.shape[1]
    cols = ws[0].shape[1]
    tile = tile_of(cols)
    return pl.pallas_call(
        functools.partial(mm_body, len(ws)),
        grid=(cols // tile,),
        in_specs=[pl.BlockSpec((rows, depth), lambda i: (half, 0))]
        + [pl.BlockSpec((w.shape[0], tile), lambda i: (0, i)) for w in ws]
        + [full(a) for a in marks],
        out_specs=[pl.BlockSpec((rows // 2, tile), lambda i: (0, i))] * 2,
        out_shape=[jax.ShapeDtypeStruct((rows // 2, cols), out_dtype)] * 2,
        compiler_params=params(32),
        cost_estimate=pl.CostEstimate(
            flops=2 * rows * depth * cols,
            bytes_accessed=2 * (rows * (depth + cols) + depth * cols),
            transcendentals=0,
        ),
    )(x, *ws, *marks)


def out_body(n, row_parts, counts, *refs):
    ws = refs[row_parts * n :][: sum(counts)]
    out_ref, total = refs[-2:]
    for j in range(n):
        x = jnp.concatenate([refs[p * n + j][...] for p in range(row_parts)], 0)
        depth = x.shape[1]
        at = 0
        for k, count in enumerate(counts):
            row = j * depth
            piece = at
            while row >= ws[piece].shape[0]:
                row -= ws[piece].shape[0]
                piece += 1
            at += count
            term = dot(x, ws[piece][row : row + depth])
            if j:
                term = term + total[k]
            if j == n - 1:
                out_ref[k] = term.astype(BF16)
            else:
                total[k] = term


def out_mm(parts, ws, marks=()):
    n = len(parts[0])
    rows = sum(part[0].shape[0] for part in parts)
    cols = ws[0][0].shape[1]
    flat = [piece for w in ws for piece in w]
    inputs = [a for part in parts for a in part] + flat + list(marks)
    out_shape = jax.ShapeDtypeStruct((len(ws), rows, cols), BF16)
    return pl.pallas_call(
        functools.partial(out_body, n, len(parts), tuple(len(w) for w in ws)),
        grid=(1,),
        in_specs=[full(a) for a in inputs],
        out_specs=full(out_shape),
        out_shape=out_shape,
        scratch_shapes=[pltpu.VMEM(out_shape.shape, F32)],
        compiler_params=params(32),
        cost_estimate=SMALL,
    )(*inputs)


def back_body(counts, part, has_acc, x_ref, *refs):
    total = None
    at = 0
    for j, count in enumerate(counts):
        w = refs[at][...]
        if count == 2:
            w = jnp.where(pl.program_id(0) < pl.num_programs(0) // 2, w, refs[at + 1][...])
        at += count
        term = dot(x_ref[:, j * part : (j + 1) * part], w, ((1,), (1,)))
        total = term if total is None else total + term
    refs = refs[at:]
    if has_acc:
        total = total + refs[0][...]
        keep, send = refs[1:]
        half = total.shape[0] // 2
        keep[...] = total[:half]
        send[...] = total[half:].astype(send.dtype)
    else:
        refs[0][...] = total


def back_mm(x, half, ws, acc):
    rows = x.shape[0] // (1 if half is None else 2)
    depth = x.shape[1]
    part = ws[0][0].shape[1]
    heads = sum(piece.shape[0] for piece in ws[0])
    tile = min(512, heads)
    steps = heads // tile
    has_acc = acc is not None
    row = half or 0
    in_specs = [pl.BlockSpec((rows, depth), lambda i: (row, 0))]
    for w in ws:
        if len(w) == 1:
            in_specs.append(pl.BlockSpec((tile, part), lambda i: (i, 0)))
        else:
            in_specs.append(pl.BlockSpec((tile, part), lambda i: (jnp.minimum(i, steps // 2 - 1), 0)))
            in_specs.append(pl.BlockSpec((tile, part), lambda i: (jnp.maximum(i - steps // 2, 0), 0)))
    args = [x] + [piece for w in ws for piece in w]
    if has_acc:
        in_specs.append(pl.BlockSpec((rows, tile), lambda i: (0, i)))
        args.append(acc)
        out_specs = [pl.BlockSpec((rows // 2, tile), lambda i: (0, i))] * 2
        out_shape = [
            jax.ShapeDtypeStruct((rows // 2, heads), F32),
            jax.ShapeDtypeStruct((rows // 2, heads), BF16),
        ]
    else:
        out_specs = pl.BlockSpec((rows, tile), lambda i: (0, i))
        out_shape = jax.ShapeDtypeStruct((rows, heads), F32)
    return pl.pallas_call(
        functools.partial(back_body, tuple(len(w) for w in ws), part, has_acc),
        grid=(steps,),
        in_specs=in_specs,
        out_specs=out_specs,
        out_shape=out_shape,
        compiler_params=params(32),
        cost_estimate=SMALL,
    )(*args)


def causal(rows):
    at = lax.broadcasted_iota(jnp.int32, (rows, L), 0) % L
    return at >= lax.broadcasted_iota(jnp.int32, (rows, L), 1)


def probabilities(q4, keys):
    scores = dot(q4, keys, ((1,), (1,))) * (HEAD_SIZE**-0.5)
    weights = jnp.where(causal(q4.shape[0]), jnp.exp(scores), 0.0)
    return weights / jnp.sum(weights, -1, keepdims=True)


def stack_heads(values):
    return jnp.concatenate(
        [values[:, h * HEAD_SIZE : (h + 1) * HEAD_SIZE] for h in range(GROUP)], 0
    )


def attend_body(adapted, keep, rs, r2, low, qo, vo, cos_ref, sin_ref, *refs):
    mixed, *saved = refs[-1 - adapted :]
    cosine = cos_ref[...]
    sine = sin_ref[...]
    pre = keep[...] + rs[...].astype(F32) + r2[...].astype(F32)
    rank = qo.shape[0]
    q_pre = pre[:, :QCOLS]
    k_pre = pre[:, QCOLS : QCOLS + HEAD_SIZE]
    v_pre = pre[:, QCOLS + HEAD_SIZE :]
    if adapted:
        q_pre = q_pre + adapter_scale * dot(low[:, :rank], qo[...])
        v_pre = v_pre + adapter_scale * dot(low[:, rank:], vo[...])
    cos4 = jnp.concatenate([cosine] * GROUP, 0)
    sin4 = jnp.concatenate([sine] * GROUP, 0)
    q4 = stack_heads(q_pre)
    q4 = (q4 * cos4 + pltpu.roll(q4, HEAD_SIZE // 2, 1) * sin4).astype(BF16)
    keys = (k_pre * cosine + pltpu.roll(k_pre, HEAD_SIZE // 2, 1) * sine).astype(BF16)
    values = v_pre.astype(BF16)
    rounded = probabilities(q4, keys).astype(BF16)
    out = dot(rounded, values).astype(BF16)
    for h in range(GROUP):
        cols = slice(h * HEAD_SIZE, (h + 1) * HEAD_SIZE)
        mixed[:, cols] = out[h * L : (h + 1) * L]
        if saved:
            saved[0][:, cols] = q4[h * L : (h + 1) * L]
    if saved:
        saved[0][:, QCOLS : QCOLS + HEAD_SIZE] = keys
        saved[0][:, QCOLS + HEAD_SIZE :] = values


def attend(adapted, keep, rs, r2, low, qo, vo, group, cosine, sine, marks=()):
    each = QCOLS + 2 * HEAD_SIZE
    rank = qo.shape[0]
    top = lambda a: pl.BlockSpec((L, a.shape[1]), lambda i: (0, 0))
    return pl.pallas_call(
        functools.partial(attend_body, adapted),
        grid=(1,),
        in_specs=[
            top(keep),
            top(rs),
            top(r2),
            top(low),
            pl.BlockSpec((rank, QCOLS), lambda i: (0, group)),
            pl.BlockSpec((rank, HEAD_SIZE), lambda i: (0, group)),
            top(cosine),
            top(sine),
        ]
        + [full(a) for a in marks],
        out_specs=[pl.BlockSpec((L, w), lambda i: (0, 0)) for w in (QCOLS, each)[: 1 + adapted]],
        out_shape=[jax.ShapeDtypeStruct((L, w), BF16) for w in (QCOLS, each)[: 1 + adapted]],
        compiler_params=params(32),
        cost_estimate=SMALL,
    )(keep, rs, r2, low, qo, vo, cosine, sine, *marks)


def outer_place(block, rank, kv):
    wide = (kv * (GROUP + 1) + 1) // 2
    return (block // wide) * rank, (block % wide) * HEAD_SIZE, wide


def attend_back_body(kv, splits, keep, rs, r2, low, qo, vo, cos_ref, sin_ref, *refs):
    saved = refs[:splits]
    outer, mid = refs[splits:]
    rank = qo.shape[0]
    each = QCOLS + 2 * HEAD_SIZE
    cos4 = jnp.concatenate([cos_ref[...]] * GROUP, 0)
    sin4 = jnp.concatenate([sin_ref[...]] * GROUP, 0)
    low_q = low[:, :rank]
    low_v = low[:, rank:]
    q_mid = jnp.zeros((L, rank), F32)
    v_mid = jnp.zeros((L, rank), F32)

    def put(block, value):
        row, col, _ = outer_place(block, rank, kv)
        outer[row : row + rank, col : col + HEAD_SIZE] = adapter_scale * value

    if (kv * (GROUP + 1)) % 2:
        put(kv * (GROUP + 1), jnp.zeros((rank, HEAD_SIZE), F32))
    for j in range(kv):
        cols = slice(j * QCOLS, (j + 1) * QCOLS)
        at = (j % (kv // splits)) * each
        kept = saved[j // (kv // splits)]
        grad = keep[:, cols] + rs[:, cols].astype(F32) + r2[:, cols].astype(F32)
        grad4 = stack_heads(grad.astype(BF16))
        q4 = stack_heads(kept[:, at : at + QCOLS])
        keys = kept[:, at + QCOLS : at + QCOLS + HEAD_SIZE]
        values = kept[:, at + QCOLS + HEAD_SIZE : at + each]
        prob = probabilities(q4, keys)
        grad_prob = dot(grad4, values, ((1,), (1,)))
        grad_values = dot(prob.astype(BF16), grad4, ((0,), (0,))).astype(BF16)
        inner = jnp.sum(grad_prob * prob, -1, keepdims=True)
        grad_scores = (prob * (grad_prob - inner) * (HEAD_SIZE**-0.5)).astype(BF16)
        grad_query = dot(grad_scores, keys)
        back4 = (grad_query * cos4 - pltpu.roll(grad_query, HEAD_SIZE // 2, 1) * sin4).astype(BF16)
        for h in range(GROUP):
            at = j * GROUP + h
            back = back4[h * L : (h + 1) * L]
            put(at, dot(low_q, back, ((0,), (0,))))
            q_mid += dot(back, qo[:, at * HEAD_SIZE : (at + 1) * HEAD_SIZE], ((1,), (1,)))
        put(kv * GROUP + j, dot(low_v, grad_values, ((0,), (0,))))
        v_mid += dot(grad_values, vo[:, j * HEAD_SIZE : (j + 1) * HEAD_SIZE], ((1,), (1,)))
    mid[:, :rank] = (adapter_scale * q_mid).astype(BF16)
    mid[:, rank:] = (adapter_scale * v_mid).astype(BF16)


def attend_back(keep, rs, r2, low, qo, vo, cosine, sine, saved):
    rank = qo.shape[0]
    kv = vo.shape[1] // HEAD_SIZE
    wide = outer_place(0, rank, kv)[2]
    inputs = (keep, rs, r2, low, qo, vo, cosine, sine, *saved)
    shapes = [
        jax.ShapeDtypeStruct((2 * rank, wide * HEAD_SIZE), F32),
        jax.ShapeDtypeStruct((L, 2 * rank), BF16),
    ]
    return pl.pallas_call(
        functools.partial(attend_back_body, kv, len(saved)),
        grid=(1,),
        in_specs=[full(a) for a in inputs],
        out_specs=[full(a) for a in shapes],
        out_shape=shapes,
        compiler_params=params(60),
        cost_estimate=SMALL,
    )(*inputs)


def adapter_body(n, rows_each, scal, states, outer, *refs):
    mids = refs[:n]
    away, stay = refs[n:]
    src = pl.ds(pl.multiple_of(scal[0] * rows_each, rows_each), rows_each)
    own = states[:, src]
    total = None
    for mid in mids:
        term = dot(mid[...], own, ((0,), (0,)))
        total = term if total is None else total + term
    half = total.shape[0] // 2
    for low in range(2):
        rows = slice(low * half, (low + 1) * half)

        @pl.when(scal[1] == low)
        def _():
            stay[:, :rows_each] = total[rows]
            stay[:, rows_each:] = outer[rows]

        @pl.when(scal[1] != low)
        def _():
            away[:, :rows_each] = total[rows].astype(BF16)
            away[:, rows_each:] = outer[rows].astype(BF16)


def adapter_products(scal, states, mids, outer, rows_each):
    half = outer.shape[0] // 2
    cols = rows_each + outer.shape[1]
    shapes = [jax.ShapeDtypeStruct((half, cols), BF16), jax.ShapeDtypeStruct((half, cols), F32)]
    return pl.pallas_call(
        functools.partial(adapter_body, len(mids), rows_each),
        grid=(1,),
        in_specs=[smem()] + [full(a) for a in (states, outer, *mids)],
        out_specs=[full(a) for a in shapes],
        out_shape=shapes,
        compiler_params=params(32),
        cost_estimate=SMALL,
    )(scal, states, outer, *mids)


def assemble_body(rows_each, bit, own, other, q_inner, q_outer, v_inner, v_outer):
    low = jnp.where(bit[0] == 0, own[...], other[...]).astype(F32)
    high = jnp.where(bit[0] == 0, other[...], own[...]).astype(F32)
    q_inner[...] = low[:, :rows_each]
    v_inner[...] = high[:, :rows_each]
    outer = jnp.concatenate([low[:, rows_each:], high[:, rows_each:]], 1)
    cols = q_outer.shape[1]
    q_outer[...] = outer[:, :cols]
    v_outer[...] = outer[:, cols : cols + v_outer.shape[1]]


def assemble(bit, own, other, rows_each, q_cols, v_cols):
    rank = own.shape[0]
    shapes = [jax.ShapeDtypeStruct((rank, c), F32) for c in (rows_each, q_cols, rows_each, v_cols)]
    return pl.pallas_call(
        functools.partial(assemble_body, rows_each),
        grid=(1,),
        in_specs=[smem(), full(own), full(other)],
        out_specs=[full(a) for a in shapes],
        out_shape=shapes,
        compiler_params=params(32),
        cost_estimate=SMALL,
    )(bit, own, other)


def stats_body(counts, part, split, scal, xt_ref, xt_pol, tgt, gain, *refs):
    refs = list(refs)
    sums = []
    hidden_out, stats = refs[-2:]
    for which in range(2):
        xt = (xt_ref, xt_pol)[which]
        count = sum(counts)
        keeps = [r[i] for r in refs[: counts[0]] for i in range(r.shape[0])]
        recvs = [r[i] for r in refs[counts[0] : count] for i in range(r.shape[0])]
        refs = refs[count:]
        squares = jnp.zeros((L, HEAD_SIZE), F32)
        products = jnp.zeros((L, HEAD_SIZE), F32)
        for j, (keep, recv) in enumerate(zip(keeps, recvs)):
            src = pl.ds(pl.multiple_of((j * split + scal[0]) * part, part), part)
            hidden = xt[:, src].astype(F32) + keep.astype(F32) + recv.astype(F32)
            cols = slice(j * part, (j + 1) * part)
            if which == 1:
                hidden_out[0, :, cols] = hidden
            product = hidden * (gain[:, cols] * tgt[0, :, cols].astype(F32))
            square = hidden * hidden
            for s in range(part // HEAD_SIZE):
                lanes = slice(s * HEAD_SIZE, (s + 1) * HEAD_SIZE)
                squares += square[:, lanes]
                products += product[:, lanes]
        sums.append(
            [
                jnp.broadcast_to(jnp.sum(v, 1, keepdims=True), v.shape).T[:1]
                for v in (squares, products)
            ]
        )
    at = lax.broadcasted_iota(jnp.int32, (1, 2 * L), 1) % L
    own = (at >= scal[1]) & (pl.program_id(0) == 0)
    live = jnp.where(own, 1.0, 0.0).astype(F32)
    both = [jnp.concatenate([sums[0][i], sums[1][i]], 1) for i in range(2)]
    stats[...] = jnp.concatenate([*both, live, jnp.zeros((5, 2 * L), F32)], 0)


def norm_stats(scal, xt, tgt, gain, keeps, recvs, split):
    n = sum(a.shape[0] for a in keeps)
    part = keeps[0].shape[2]
    shared = []
    for which in range(2):
        at = functools.partial(lambda which, i: (0, 2 * i + which, 0), which)
        for a in (*keeps, *recvs):
            shared.append((a, pl.BlockSpec((a.shape[0], L, part), at)))
    return pl.pallas_call(
        functools.partial(stats_body, (len(keeps), len(recvs)), part, split),
        grid=(4,),
        in_specs=[
            smem(),
            pl.BlockSpec((L, xt.shape[1]), lambda i: ((i // 2) * 4 + i % 2, 0)),
            pl.BlockSpec((L, xt.shape[1]), lambda i: ((i // 2) * 4 + 2 + i % 2, 0)),
            pl.BlockSpec((1, L, n * part), lambda i: (i // 2 + i % 2 * 2, 0, 0)),
            pl.BlockSpec((1, n * part), lambda i: (0, 0)),
        ]
        + [spec for _, spec in shared],
        out_specs=[
            pl.BlockSpec((1, L, n * part), lambda i: (i, 0, 0)),
            pl.BlockSpec((8, 2 * L), lambda i: (i, 0)),
        ],
        out_shape=[
            jax.ShapeDtypeStruct((4, L, n * part), F32),
            jax.ShapeDtypeStruct((32, 2 * L), F32),
        ],
        compiler_params=params(32),
        cost_estimate=SMALL,
    )(scal, xt, xt, tgt, gain, *[a for a, _ in shared])


def score_body(width, masks, ids, own, *refs):
    recvs = refs[: len(masks)]
    total_out, margin_out = refs[len(masks) :]
    lane = lax.broadcasted_iota(jnp.int32, (8, 128), 1)
    margins = jnp.zeros((8, 128), F32)
    for p in range(4):
        total = own[8 * p : 8 * p + 8]
        for recv, m in zip(recvs, masks):
            q = ORD.index(ORD[p] ^ m)
            total = total + recv[8 * q : 8 * q + 8]
        total_out[8 * p : 8 * p + 8] = total
        inverse = lax.rsqrt(total[0:1] * (1.0 / width) + norm_eps)
        score = total[1:2] * inverse * (width**-0.5)
        score = jnp.where(total[2:3] > 0.5, score, 0.0)
        margin = jnp.sum(score[:, L:], 1, keepdims=True) - jnp.sum(score[:, :L], 1, keepdims=True)
        margins = margins + jnp.where(lane == ids[p], margin, 0.0)
    margin_out[...] = margins


def scores(ids, own, recvs, masks, width):
    shapes = [jax.ShapeDtypeStruct(own.shape, F32), jax.ShapeDtypeStruct((8, 128), F32)]
    return pl.pallas_call(
        functools.partial(score_body, width, masks),
        grid=(1,),
        in_specs=[smem()] + [full(a) for a in (own, *recvs)],
        out_specs=[full(a) for a in shapes],
        out_shape=shapes,
        cost_estimate=SMALL,
    )(ids, own, *recvs)


def turn(i):
    return (2 * i + 1) % 5


def grad_body(width, seqs, n_vec, ids, pairs, total, hidden, tgt, gain, *refs):
    vecs = refs[:n_vec]
    grad_out, loss_out, slope = refs[n_vec:]
    lane = lax.broadcasted_iota(jnp.int32, (8, 128), 1)

    @pl.when(pl.program_id(0) == 0)
    def _():
        margin = vecs[0][...]
        for v in vecs[1:]:
            margin = margin + v[...]
        logits = jnp.zeros((8, 128), F32)
        for i in range(seqs // 2):
            sign = jnp.where(lane == pairs[2 * i], 1.0, 0.0) - jnp.where(
                lane == pairs[2 * i + 1], 1.0, 0.0
            )
            logit = dpo_beta * jnp.sum(margin * sign, 1, keepdims=True)
            logits = logits + jnp.where(lane == i, logit, 0.0)
        soft = jnp.maximum(-logits, 0.0) + jnp.log1p(jnp.exp(-jnp.abs(logits)))
        used = lane < seqs // 2
        loss = jnp.sum(jnp.where(used, soft, 0.0), 1, keepdims=True)
        loss_out[...] = jnp.broadcast_to(loss, (8, 128))
        slopes = jnp.where(used, -dpo_beta / (1.0 + jnp.exp(logits)), 0.0)
        gradient = jnp.zeros((8, 128), F32)
        for i in range(seqs // 2):
            each = jnp.sum(jnp.where(lane == i, slopes, 0.0), 1, keepdims=True)
            sign = jnp.where(lane == pairs[2 * i], 1.0, 0.0) - jnp.where(
                lane == pairs[2 * i + 1], 1.0, 0.0
            )
            gradient = gradient + each * sign
        slope[...] = gradient * loss_scale

    mine = lane == ids[turn(pl.program_id(0))]
    seq = jnp.sum(jnp.where(mine, slope[...], 0.0), 1, keepdims=True)[:1]
    rows = total[:, L:]
    token = jnp.where(rows[2:3] > 0.5, seq, 0.0) * (width**-0.5)
    inverse = lax.rsqrt(rows[0:1] * (1.0 / width) + norm_eps)
    first = inverse * token
    second = inverse * inverse * inverse * (token * rows[1:2] * (1.0 / width))
    first = jnp.broadcast_to(first, (L, L)).T
    second = jnp.broadcast_to(second, (L, L)).T
    for s in range(hidden.shape[2] // HEAD_SIZE):
        cols = slice(s * HEAD_SIZE, (s + 1) * HEAD_SIZE)
        weighted = gain[:, cols] * tgt[0, :, cols].astype(F32)
        grad_out[0, :, cols] = (first * weighted - second * hidden[0, :, cols]).astype(BF16)


def grad_hidden(ids, pairs, total, hidden, tgt, gain, vecs, width):
    n = hidden.shape[2]
    seqs = pairs.shape[0]
    return pl.pallas_call(
        functools.partial(grad_body, width, seqs, len(vecs)),
        grid=(4,),
        in_specs=[
            smem(),
            smem(),
            pl.BlockSpec((8, 2 * L), lambda i: (turn(i), 0)),
            pl.BlockSpec((1, L, n), lambda i: (turn(i), 0, 0)),
            pl.BlockSpec((1, L, n), lambda i: (turn(i) // 2 + turn(i) % 2 * 2, 0, 0)),
            pl.BlockSpec((1, n), lambda i: (0, 0)),
        ]
        + [pl.BlockSpec((8, 128), lambda i: (0, 0)) for _ in vecs],
        out_specs=[
            pl.BlockSpec((1, L, n), lambda i: (i, 0, 0)),
            pl.BlockSpec((8, 128), lambda i: (0, 0)),
        ],
        out_shape=[
            jax.ShapeDtypeStruct((4, L, n), BF16),
            jax.ShapeDtypeStruct((8, 128), F32),
        ],
        scratch_shapes=[pltpu.VMEM((8, 128), F32)],
        compiler_params=params(32),
        cost_estimate=SMALL,
    )(ids, pairs, total, hidden, tgt, gain, *vecs)


def per_device(
    fsdp_size,
    tensor_size,
    ref_states,
    pol_states,
    target_rows,
    norm_gain,
    wq,
    wk,
    wv,
    wo,
    qa,
    qo,
    va,
    vo,
    prompt_length,
    pairs,
):
    tokens, width = ref_states.shape
    groups = fsdp_size // 4
    near_z = fsdp_size // 4
    bits = []
    bit = 2
    while bit < fsdp_size:
        if bit != near_z:
            bits.append(bit)
        bit *= 2
    split = 2 if tensor_size == 2 and fsdp_size == 16 else 1
    kv_local = wk.shape[1] // HEAD_SIZE
    depth = wq.shape[0]
    part = depth // split
    rank = qa.shape[1]
    me = lax.axis_index("fsdp")
    x = lax.axis_index("tensor")
    side = x if split == 2 else 0

    def tmask(d):
        return (d & 1) | ((d >> 1) * near_z)

    def gmask(k):
        return sum(bit for i, bit in enumerate(bits) if (k >> i) & 1)

    def move(value, mask):
        return lax.ppermute(value, "fsdp", [(i, i ^ mask) for i in range(fsdp_size)])

    def swap_x(value):
        return lax.ppermute(value, "tensor", [(0, 1), (1, 0)])

    def move_both(value, mask, flip):
        pairs_list = [
            (2 * i + j, 2 * (i ^ mask) + (j ^ flip)) for i in range(fsdp_size) for j in range(2)
        ]
        return lax.ppermute(value, ("fsdp", "tensor"), pairs_list)

    def after(value, *others):
        return lax.optimization_barrier((value, *others))[0]

    def marker(*queue):
        return move(after(cosine[:16].astype(BF16), *queue), 1)

    cosine, sine = rope_tables(L, HEAD_SIZE)

    wide = groups == 4 and split == 2
    heads = wo.shape[0]

    def shard_of(j, *queue):
        q, k, v = wq, wk, wv
        if queue:
            q, k, v = lax.optimization_barrier((wq, wk, wv, *queue))[:3]
        pieces = [
            q[:, j * QCOLS : (j + 1) * QCOLS],
            k[:, j * HEAD_SIZE : (j + 1) * HEAD_SIZE],
            v[:, j * HEAD_SIZE : (j + 1) * HEAD_SIZE],
        ]
        return jnp.concatenate(pieces, 1)

    def gather(shard):
        return [shard] + [move(shard, gmask(k)) for k in range(1, groups)]

    if wide:
        over_y, over_z = gmask(1), gmask(2)
        shards = [shard_of(0)]
        zs = [move(shards[0], over_z)]
        ys = [move(shards[0], over_y)]
        corners = []

    parts = groups * split
    idx = []
    for d in range(4):
        for k in range(groups):
            for h in range(split):
                idx.append((me ^ tmask(d) ^ gmask(k)) * split + h)
    for d in range(4):
        for k in range(groups):
            idx.append((me ^ tmask(d) ^ gmask(k)) * split + side)
    idx.append(x)
    idx = jnp.stack(idx).astype(jnp.int32)
    prepared = prep(
        idx,
        ref_states,
        pol_states,
        target_rows,
        norm_gain.astype(F32).reshape(1, width),
        parts,
        part,
        split,
    )
    xs, ts, gain = prepared[:4], prepared[4:8], prepared[8]
    near = move(xs[1], 1)
    far = [move(xs[2], near_z)]
    far.append(move(xs[3], near_z | 1))

    if split == 2:
        first = (zs[0], ys[0]) if wide else ()
        other = [swap_x(after(a, *first) if first else a) for a in far]
        far = [
            [jnp.where(x == which, a[0], b[0]) for which in range(2)] for a, b in zip(far, other)
        ]
    states = jnp.concatenate(
        [
            *(xs[0][0], far[0][0], xs[0][1], far[0][1]),
            *(near[0], far[1][0], near[1], far[1][1]),
        ],
        0,
    )

    low = dot(pol_states, jnp.concatenate([qa, va], 1)).astype(BF16)
    cosine, sine = rope_tables(L, HEAD_SIZE)

    def own_columns(at, piece, *queue):
        return lax.dynamic_slice(
            after(wo, *queue), (piece * (heads // 2), at * part), (heads // 2, part)
        )

    def own_piece(step, *queue):
        at = (1 - x) if step < 2 else x
        return lax.dynamic_slice(
            after(wo, *queue), ((step % 2) * (heads // 2), at * part), (heads // 2, part)
        )

    def make_shard(j, *queue):
        if j < kv_local:
            shards.append(shard_of(j, *queue))
        elif j < kv_local + 4:
            shards.append(own_piece(j - kv_local, *queue))

    def next_shard(j, *more):
        queue = (zs[j - 1], ys[j - 1], *more)
        ys.append(move(after(shards[j], *queue), over_y))
        zs.append(move(after(shards[j], *queue), over_z))
        corners.append(move(after(*queue), over_y))

    saved = []
    parts_mixed = [[], [], []]

    def mix(j, keeps, came, sums, *queue, marks=()):
        results = []
        for which in range(2):
            total = sums[which * L : (which + 1) * L]
            result = attend(
                *(which == 1, keeps[which], came[which], total, low, qo, vo, j, cosine, sine),
                marks=marks,
            )
            saved.extend(result[1:])
            results.append(result[0])
        result = jnp.concatenate(results, 0)
        return result, move(after(result, *queue) if queue else result, near_z)

    def spread(result, other):
        far = move(jnp.concatenate([result, other], 0), 1)
        for part_mixed, value in zip(parts_mixed, (result, other, far)):
            part_mixed.append(value)
        return far

    if wide:
        make_shard(1, shards[0])
        next_shard(1)
        make_shard(2, zs[0])
    before = None
    ends = []
    marks = ()
    for j in range(kv_local):
        if wide:
            marks = (marker(zs[j + 1], ys[j + 1]),)
            ws = [shards[j], ys[j], zs[j], corners[j]]
        else:
            ws = gather(shard_of(j))
        sends = mm(states, 1, ws, BF16, marks)
        came = [move(send, 1) for send in sends]
        keeps = mm(states, 0, ws, F32)
        if wide:
            next_shard(j + 2)
            make_shard(j + 3, zs[j + 1])
        over = jnp.concatenate(
            [(keeps[which][L:] + came[which][L:].astype(F32)).astype(BF16) for which in range(2)], 0
        )
        if before is not None:
            result, other = mix(j - 1, *before, *came, *ends)
            if j + 2 < kv_local:
                over = after(over, other)
            states = after(states, other)
            ends = [spread(result, other)]
        if wide:
            over = after(over, shards[-1])
        sums = move(over, near_z)
        if wide and j + 1 == kv_local:
            marks = (marker(zs[j + 2], ys[j + 2]),)
            make_shard(kv_local + 3, zs[-2])
        before = (keeps, came, sums)
    last = spread(*mix(kv_local - 1, *before, *ends, marks=marks))

    keeps, recvs = [], []
    if wide:
        next_shard(kv_local + 2, over)
        first = [a[kv_local : kv_local + 2] for a in (shards, ys, zs, corners)]
        marks = (marker(zs[-1], ys[-1]),)
        recvs.append(swap_x(out_mm(parts_mixed, first[:2], marks)))
        next_shard(kv_local + 3)
        recvs.append(swap_x(out_mm(parts_mixed, first[2:])))
        corners.append(move(after(zs[-1], ys[-1]), over_y))
        wo_send, wo_keep = first, [a[kv_local + 2 :] for a in (shards, ys, zs, corners)]
        keeps.append(out_mm(parts_mixed, wo_keep[:3]))
        keeps.append(out_mm(parts_mixed, wo_keep[3:]))
    else:
        wo_keep = [[w] for w in gather(wo)]
        product = out_mm(parts_mixed, wo_keep)
        if tensor_size > 1:
            product = lax.psum(product, "tensor")
        keeps.append(product)
        recvs.append(jnp.zeros_like(product))

    targets = [ts[0], move(after(ts[1], last, keeps[0]), 1)]
    targets += [move(after(ts[d], last), tmask(d)) for d in (2, 3)]
    tgt = jnp.stack(targets)
    scal = jnp.stack([jnp.asarray(side, jnp.int32), prompt_length[0].astype(jnp.int32)])
    hidden, stats = norm_stats(scal, states, tgt, gain, keeps, recvs, split)
    masks, got = [], []
    for flip in reversed(range(split)):
        for d in (3, 2, 1, 0):
            if d or flip:
                masks.append(d)
                if split == 2:
                    got.append(move_both(stats, tmask(d), flip))
                else:
                    got.append(move(stats, tmask(d)))
    ids = jnp.stack([me ^ tmask(d) for d in ORD]).astype(jnp.int32)
    total, margin = scores(ids, stats, got, tuple(masks), width)
    vecs = [margin] + [move(margin, gmask(k)) for k in reversed(range(1, groups))]
    grad, loss = grad_hidden(ids, pairs, total, hidden, tgt, gain, vecs, width)

    grad_rows = grad.reshape(4 * L, -1)
    other = None
    for half in range(2):
        if split == 2:
            leaving = grad_rows[2 * L * half : 2 * L * (half + 1)]
            other = swap_x(leaving if half == 0 else after(leaving, other))
            acc = back_mm(grad_rows, half, wo_keep, None)
            keep, send = back_mm(other, None, wo_send, acc)
        else:
            acc = jnp.zeros((2 * L, heads), F32)
            keep, send = back_mm(grad_rows, half, wo_keep, acc)
        rs = move(send if half == 0 else after(send, r2), 1)
        if half == 0:
            over = (keep + rs.astype(F32)).astype(BF16)
            r2 = move(over, near_z)
    outer, mid = attend_back(keep, rs, r2, low, qo, vo, cosine, sine, saved)

    rows_each = width // tensor_size
    if split == 2:
        mids = [mid, swap_x(mid)]
    elif tensor_size == 1:
        mids = [mid]
    else:
        gathered = lax.all_gather(mid, "tensor", axis=0, tiled=False)
        mids = [gathered[i] for i in range(tensor_size)]
    scal = jnp.stack([x, me & 1]).astype(jnp.int32)
    away, current = adapter_products(scal, pol_states, mids, outer, rows_each)
    current = current + move(away, 1).astype(F32)
    top = fsdp_size // 2
    g = (me // 2) % groups
    rows = current.shape[0] // groups
    pieces = [
        lax.dynamic_slice_in_dim(current, (g ^ k) * rows, rows, 0) for k in range(groups)
    ]
    current = pieces[0]
    for k in range(1, groups):
        current = current + move(pieces[k].astype(BF16), k << 1).astype(F32)
    rows //= 2
    high = me // top
    away = lax.dynamic_slice_in_dim(current, (1 - high) * rows, rows, 0).astype(BF16)
    current = lax.dynamic_slice_in_dim(current, high * rows, rows, 0)
    current = (current + move(away, top).astype(F32)).astype(BF16)

    def join(bit, own, other):
        return jnp.where(
            bit == 0, jnp.concatenate([own, other], 0), jnp.concatenate([other, own], 0)
        )

    current = join(high, current, move(current, top))
    pieces = [current] + [move(current, k << 1) for k in range(1, groups)]
    step = 1
    while step < groups:
        odd = (g & step) != 0
        pieces = [jnp.where(odd, pieces[k ^ step], pieces[k]) for k in range(groups)]
        step *= 2
    current = jnp.concatenate(pieces, 0)
    grads = assemble(
        (me & 1).reshape(1), current, move(current, 1), rows_each, qo.shape[1], vo.shape[1]
    )
    return (loss[0, 0], grads[0].T, grads[1], grads[2].T, grads[3])


def solution(mesh):
    in_specs = (
        P("fsdp", None),
        P("fsdp", None),
        P("fsdp", None),
        P(),
        P("fsdp", "tensor"),
        P("fsdp", "tensor"),
        P("fsdp", "tensor"),
        P("tensor", "fsdp"),
        P(),
        P(None, "tensor"),
        P(),
        P(None, "tensor"),
        P("fsdp"),
        P(),
    )
    out_specs = (P(), P("tensor", None), P(None, "tensor"), P("tensor", None), P(None, "tensor"))
    body = functools.partial(per_device, mesh.shape["fsdp"], mesh.shape["tensor"])
    return jax.shard_map(body, mesh=mesh, in_specs=in_specs, out_specs=out_specs, check_vma=False)
```
